128 devices in a mesh: adapter: 8 (over z, core), tensor: 16 (over y, x).
Axes of the slice: x: 4, y: 4, z: 4, core: 2. Of those that a mesh axis runs over, the one named last changes fastest.
Arguments:
- normed_input: bfloat16 [8192, 8192], P('adapter', 'tensor'), may hold values from -6 to 6
- query_matrix: bfloat16 [8192, 8192], P(None, 'tensor'), may hold values from -0.0625 to 0.0625
- key_value_matrix: bfloat16 [8192, 2048], P(None, 'tensor'), may hold values from -0.0625 to 0.0625
- output_matrix: bfloat16 [8192, 8192], P('tensor'), may hold values from -0.09375 to 0.09375
- adapter_down_qkv: bfloat16 [64, 8192, 192], P('adapter', 'tensor'), may hold values from -0.0625 to 0.0625
- adapter_up_query: bfloat16 [64, 64, 8192], P('adapter', None, 'tensor'), may hold values from -0.75 to 0.75
- adapter_up_key_value: bfloat16 [64, 64, 2048], P('adapter', None, 'tensor'), may hold values from -0.75 to 0.75
- adapter_down_output: bfloat16 [64, 8192, 64], P('adapter', 'tensor'), may hold values from -0.0625 to 0.0625
- adapter_up_output: bfloat16 [64, 64, 8192], P('adapter', None, 'tensor'), may hold values from -0.75 to 0.75
- adapter_choice: int32 [8, 4], replicated, may hold values from 0 to 63, as said below
- request_block_count: int32 [8, 4], P('adapter'), may hold values from 1 to 3, 8 in all within a row
- last_block_tokens: int32 [8, 4], P('adapter'), may hold values from 1 to 128
Outputs:
- attention_out: float32 [8192, 8192], P('adapter', 'tensor')
The draws below stay inside these ranges and needn't reach their ends.
Inputs may be any that keep to these rules, and one draw needn't show every extreme that they name: `adapter_choice`: the owner of adapter j is j // 8. In each group at most 1 request use adapters of one owner, and in every group some owner has exactly 1. `request_block_count`: each row sums to 8.
All inputs are finite; a program needn't handle non-finite values.
Results may differ from the reference program's by a relative error of at most 0.01.
Values may be sent and summed in bfloat16 or wider, within the bound.
No kernel may reach another device: no remote copies, remote signals or barrier semaphores. Data moves between devices by JAX's collectives and lax.ppermute only.
A program may use at most 192 MiB of HBM per device.

```python
import math
import jax
import jax.numpy as jnp
import numpy as np
from jax import lax

MODEL_WIDTH = 8192
QUERY_HEADS = 64
KEY_VALUE_HEADS = 8
HEAD_SIZE = 128
ADAPTER_RANK = 64
BLOCK = 128
GROUP_TOKENS = 1024
ADAP_DEV = 8
GROUPS = 8
TOKENS = 8192
GROUP_BLOCKS = 8
REQ_G = 4
CAP = 1
ADAPTER_STORE = 64


def draw_adapter_choice(key, part):
    key = jax.random.fold_in(key, 11)
    key_owner, key_noise, key_order, key_local = jax.random.split(key, 4)
    slot_total = GROUPS * CAP
    item_index = jnp.arange(slot_total, dtype=jnp.int32)
    item_owner = item_index // CAP
    favored = jax.random.randint(key_owner, (GROUPS,), 0, GROUPS, dtype=jnp.int32)
    noise = jax.random.randint(key_noise, (GROUPS, slot_total), 0, 1 << 20, dtype=jnp.int32) * slot_total + item_index[None, :]
    scores = jnp.where(item_owner[None, :] == favored[:, None], item_index[None, :] - slot_total, noise)
    picked = jnp.argsort(scores, axis=1)[:, :REQ_G]
    owners = jnp.take(item_owner, picked)
    req_index = jnp.arange(REQ_G, dtype=jnp.int32)
    shuffle = jax.random.randint(key_order, (GROUPS, REQ_G), 0, 1 << 20, dtype=jnp.int32) * REQ_G + req_index[None, :]
    order = jnp.argsort(shuffle, axis=1)
    owners = jnp.take_along_axis(owners, order, axis=1)
    local = jax.random.randint(key_local, (GROUPS, REQ_G), 0, ADAP_DEV, dtype=jnp.int32)
    return (owners * ADAP_DEV + local).astype(jnp.int32)


def plant(array, stream_key, low, top_value):
    longest = array.shape.index(max(array.shape))
    spots = []
    for shift in (0, 1):
        where = [jax.random.randint(jax.random.fold_in(stream_key, axis), (), 0, length) for axis, length in enumerate(array.shape)]
        where[longest] = (where[longest] + shift) % array.shape[longest]
        spots.append(tuple(where))
    return array.at[spots[0]].set(low).at[spots[1]].set(top_value)


def with_spikes(values, stream_key, source, target, blocks, factor):
    owner, partner = [(jnp.arange(values.shape[dim]) // (values.shape[dim] // blocks)).reshape([-1 if axis == dim else 1 for axis in range(values.ndim)]) for dim in (source, target)]
    chosen = jax.random.permutation(stream_key, blocks)[partner]
    strong = (owner == chosen) | (owner == (partner + blocks // 2) % blocks)
    return jnp.where(strong, factor * values, values)


def steps_of(own_key, shape, shards, smallest, top_value):
    def one(position, blocks):
        heights = jax.random.uniform(jax.random.fold_in(jax.random.fold_in(own_key, 6), position), (blocks,), jnp.float32, smallest / len(shards), top_value / len(shards))
        return jnp.repeat(jnp.exp(heights), shape[position] // blocks).reshape((-1,) + (1,) * (len(shape) - position - 1))

    level = one(*shards[0])
    for cut in shards[1:]:
        level = level * one(*cut)
    return level


def length_profile(amount, total, most, skew):
    loads = [(1 << 20) // math.isqrt(standing ** skew) + 1 for standing in range(2, amount + 1)]
    rest, given = total - most - (amount - 1), [1] * (amount - 1)
    while rest > 0:
        movable = [i for i in range(amount - 1) if given[i] < most]
        mass, left = sum([loads[i] for i in movable]), rest
        for i in movable:
            addition = min(most - given[i], max(1, left * loads[i] // mass), rest)
            given[i] = given[i] + addition
            rest = rest - addition
    return np.array([most] + given)


def uneven(key, amount, total, most, skew):
    if amount == 2:
        one = jax.random.randint(key, (), max(1, total - most), min(most, total - 1) + 1)
        return jnp.stack([one, total - one])
    lengths = jnp.asarray(length_profile(amount, total, most, skew), jnp.int32)
    twos = (amount - 1) // 2
    donor, taker = lengths[1:1 + 2 * twos:2], lengths[2:2 + 2 * twos:2]
    room = jnp.minimum(donor - 1, most - taker)
    shifted = jax.random.randint(jax.random.fold_in(key, 1), (twos,), 0, 1 << 20) % (room + 1)
    lengths = lengths.at[1:1 + 2 * twos:2].set(donor - shifted).at[2:2 + 2 * twos:2].set(taker + shifted)
    return lengths[jax.random.permutation(jax.random.fold_in(key, 2), amount)]


def centred(rng, shape, scale, most, pieces=(), held_as=jnp.bfloat16):
    drawn = scale * jax.random.normal(rng, shape, jnp.float32)
    if pieces:
        drawn = drawn * steps_of(rng, shape, pieces, -0.22, 0.18)
    return jnp.clip(drawn, -most, most).astype(held_as)


def bell_draw_with(stream_key, shape, scale, reach, cuts, heavy, kind=jnp.bfloat16):
    drawn = scale * jax.random.normal(stream_key, shape, jnp.float32)
    if cuts:
        drawn = drawn * steps_of(stream_key, shape, cuts, -0.22, 0.18)
    return jnp.clip(with_spikes(drawn, jax.random.fold_in(stream_key, 3), *heavy), -reach, reach).astype(kind)


def setup_inputs(seed: int = 0) -> dict:
    seeds = jax.random.split(jax.random.key(seed), 13)
    return {
        "normed_input": centred(seeds[0], (TOKENS, MODEL_WIDTH), 1.0, 6.0, ((0, 8), (1, 16))),
        "query_matrix": centred(seeds[1], (MODEL_WIDTH, QUERY_HEADS * HEAD_SIZE), MODEL_WIDTH ** -0.5, 0.0625, ((1, 16),)),
        "key_value_matrix": centred(seeds[2], (MODEL_WIDTH, KEY_VALUE_HEADS * 2 * HEAD_SIZE), MODEL_WIDTH ** -0.5, 0.0625, ((1, 16),)),
        "output_matrix": bell_draw_with(seeds[3], (QUERY_HEADS * HEAD_SIZE, MODEL_WIDTH), (QUERY_HEADS * HEAD_SIZE) ** -0.5, 0.09375, ((0, 16),), (0, 1, 16, 2.0)),
        "adapter_down_qkv": centred(seeds[4], (ADAPTER_STORE, MODEL_WIDTH, 3 * ADAPTER_RANK), MODEL_WIDTH ** -0.5, 0.0625, ((0, 8), (1, 16))),
        "adapter_up_query": centred(seeds[5], (ADAPTER_STORE, ADAPTER_RANK, QUERY_HEADS * HEAD_SIZE), ADAPTER_RANK ** -0.5, 0.75, ((0, 8), (2, 16))),
        "adapter_up_key_value": centred(seeds[6], (ADAPTER_STORE, ADAPTER_RANK, KEY_VALUE_HEADS * 2 * HEAD_SIZE), ADAPTER_RANK ** -0.5, 0.75, ((0, 8), (2, 16))),
        "adapter_down_output": centred(seeds[7], (ADAPTER_STORE, QUERY_HEADS * HEAD_SIZE, ADAPTER_RANK), (QUERY_HEADS * HEAD_SIZE) ** -0.5, 0.0625, ((0, 8), (1, 16))),
        "adapter_up_output": centred(seeds[8], (ADAPTER_STORE, ADAPTER_RANK, MODEL_WIDTH), ADAPTER_RANK ** -0.5, 0.75, ((0, 8), (2, 16))),
        "adapter_choice": draw_adapter_choice(jax.random.fold_in(seeds[12], 71), 0),
        "request_block_count": jax.vmap(lambda own: uneven(own, REQ_G, GROUP_BLOCKS, GROUP_BLOCKS // 2 - 1, 0))(jax.random.split(seeds[10], GROUPS)).reshape((GROUPS, REQ_G)).astype(jnp.int32),
        "last_block_tokens": plant(jax.random.randint(seeds[11], (GROUPS, REQ_G), 1, BLOCK + 1), jax.random.fold_in(seeds[11], 1), 1, BLOCK).astype(jnp.int32),
    }


rope_base = 500000.0

def small_lookup(table, index):
    entries = jnp.arange(table.shape[0], dtype=jnp.int32)
    return lax.optimization_barrier(jnp.sum(jnp.where(index[:, None] == entries[None, :], table[None, :], 0), axis=1)).astype(jnp.int32)

def request_layout(counts, tails, token_rows, block):
    block_total = token_rows // block
    starts = (jnp.cumsum(counts) - counts).astype(jnp.int32)
    blocks = jnp.arange(block_total, dtype=jnp.int32)
    block_req = (lax.optimization_barrier(jnp.sum((starts[None, :] <= blocks[:, None]).astype(jnp.int32), axis=1)) - 1).astype(jnp.int32)
    first_tok = small_lookup(starts, block_req) * block
    used = (small_lookup(counts, block_req) - 1) * block + small_lookup(tails, block_req)
    offset = jnp.arange(block, dtype=jnp.int32)
    token_position = (blocks[:, None] * block + offset[None, :] - first_tok[:, None]).reshape(token_rows)
    token_req = jnp.broadcast_to(block_req[:, None], (block_total, block)).reshape(token_rows)
    limit = jnp.broadcast_to(used[:, None], (block_total, block)).reshape(token_rows)
    return (block_req, token_req, token_position, token_position < limit)

def rotary_heads(values, token_position):
    width = values.shape[-1]
    half = width // 2
    freq = jnp.exp(-(2.0 * jnp.arange(half, dtype=jnp.float32) / width) * math.log(rope_base))
    angle = token_position.astype(jnp.float32)[:, None] * freq[None, :]
    cosine = jnp.cos(angle)[:, None, :]
    sine = jnp.sin(angle)[:, None, :]
    first = values[..., :half]
    second = values[..., half:]
    return jnp.concatenate([first * cosine - second * sine, second * cosine + first * sine], axis=-1)

def attend(query, keys, values, token_req, token_position, valid_mask, rows):
    token_rows = query.shape[0]
    heads = query.shape[1]
    width = query.shape[2]

    def one_block(index):
        start = index * rows
        q_rows = lax.dynamic_slice_in_dim(query, start, rows, 0).astype(jnp.float32)
        r_rows = lax.dynamic_slice_in_dim(token_req, start, rows, 0)
        p_rows = lax.dynamic_slice_in_dim(token_position, start, rows, 0)
        scores = jnp.einsum('qhd,kd->hqk', q_rows, keys.astype(jnp.float32)) / math.sqrt(width)
        allowed = (r_rows[:, None] == token_req[None, :]) & (token_position[None, :] <= p_rows[:, None]) & valid_mask[None, :]
        weights = jnp.where(allowed[None], jnp.exp(scores), 0.0)
        weights = (weights / lax.optimization_barrier(jnp.sum(weights, axis=2, keepdims=True))).astype(jnp.bfloat16)
        mixed = jnp.einsum('hqk,kd->qhd', weights.astype(jnp.float32), values.astype(jnp.float32))
        return mixed.astype(jnp.bfloat16).reshape(rows, heads * width)
    parts = lax.map(one_block, jnp.arange(token_rows // rows, dtype=jnp.int32))
    return parts.reshape(token_rows, heads * width)

def reference(normed_input, query_matrix, key_value_matrix, output_matrix, adapter_down_qkv, adapter_up_query, adapter_up_key_value, adapter_down_output, adapter_up_output, adapter_choice, request_block_count, last_block_tokens):
    rows = min(512, GROUP_TOKENS)
    per_head = QUERY_HEADS // KEY_VALUE_HEADS
    kv_four = key_value_matrix.reshape(MODEL_WIDTH, KEY_VALUE_HEADS, 2, HEAD_SIZE)
    key_matrix = kv_four[:, :, 0, :].reshape(MODEL_WIDTH, KEY_VALUE_HEADS * HEAD_SIZE)
    value_matrix = kv_four[:, :, 1, :].reshape(MODEL_WIDTH, KEY_VALUE_HEADS * HEAD_SIZE)
    group_in = normed_input.reshape(GROUPS, GROUP_TOKENS, MODEL_WIDTH)

    def one_group(inputs):
        token_list, ids, counts, tails = inputs
        block_req, token_req, token_position, valid_mask = request_layout(counts, tails, GROUP_TOKENS, BLOCK)
        block_numbers = small_lookup(ids, block_req)
        token_tiles = token_list.reshape(GROUP_BLOCKS, BLOCK, MODEL_WIDTH).astype(jnp.float32)
        down_block_rows = adapter_down_qkv[block_numbers].astype(jnp.float32)
        reduced_rows = jnp.einsum('btd,bdr->btr', token_tiles, down_block_rows).astype(jnp.bfloat16).astype(jnp.float32)
        query_up_blocks = adapter_up_query[block_numbers].astype(jnp.float32)
        query_adapter_delta = jnp.einsum('fnw,fwv->fnv', reduced_rows[..., :ADAPTER_RANK], query_up_blocks).reshape(GROUP_TOKENS, QUERY_HEADS * HEAD_SIZE)
        query_complete = jnp.dot(token_list, query_matrix, preferred_element_type=jnp.float32) + query_adapter_delta
        query_rows_all = rotary_heads(query_complete.reshape(GROUP_TOKENS, QUERY_HEADS, HEAD_SIZE), token_position).astype(jnp.bfloat16)
        key_value_up_blocks = adapter_up_key_value[block_numbers].reshape(GROUP_BLOCKS, ADAPTER_RANK, KEY_VALUE_HEADS, 2, HEAD_SIZE).astype(jnp.float32)
        key_adapter_delta = jnp.einsum('fmx,fxuc->fmuc', reduced_rows[..., ADAPTER_RANK:2 * ADAPTER_RANK], key_value_up_blocks[:, :, :, 0, :]).reshape(GROUP_TOKENS, KEY_VALUE_HEADS, HEAD_SIZE)
        value_adapter_delta = jnp.einsum('fmx,fxuc->fmuc', reduced_rows[..., 2 * ADAPTER_RANK:], key_value_up_blocks[:, :, :, 1, :]).reshape(GROUP_TOKENS, KEY_VALUE_HEADS, HEAD_SIZE)
        key_complete = jnp.dot(token_list, key_matrix, preferred_element_type=jnp.float32).reshape(GROUP_TOKENS, KEY_VALUE_HEADS, HEAD_SIZE) + key_adapter_delta
        value_complete = jnp.dot(token_list, value_matrix, preferred_element_type=jnp.float32).reshape(GROUP_TOKENS, KEY_VALUE_HEADS, HEAD_SIZE) + value_adapter_delta
        keys = rotary_heads(key_complete, token_position).astype(jnp.bfloat16)
        values = value_complete.astype(jnp.bfloat16)
        q_groups = jnp.moveaxis(query_rows_all.reshape(GROUP_TOKENS, KEY_VALUE_HEADS, per_head, HEAD_SIZE), 1, 0)
        k_groups = jnp.moveaxis(keys, 1, 0)
        v_groups = jnp.moveaxis(values, 1, 0)

        def one_head(items):
            return attend(items[0], items[1], items[2], token_req, token_position, valid_mask, rows)
        attended = lax.map(one_head, (q_groups, k_groups, v_groups))
        attended = jnp.moveaxis(attended, 0, 1).reshape(GROUP_TOKENS, QUERY_HEADS * HEAD_SIZE)
        projected_rows = jnp.dot(attended, output_matrix, preferred_element_type=jnp.float32)
        att_tiles = attended.reshape(GROUP_BLOCKS, BLOCK, QUERY_HEADS * HEAD_SIZE).astype(jnp.float32)
        output_down_blocks = adapter_down_output[block_numbers].astype(jnp.float32)
        head_rank_index = jnp.einsum('btq,bqr->btr', att_tiles, output_down_blocks).astype(jnp.bfloat16).astype(jnp.float32)
        output_up_blocks = adapter_up_output[block_numbers].astype(jnp.float32)
        output_adapter_delta = jnp.einsum('fps,fsq->fpq', head_rank_index, output_up_blocks).reshape(GROUP_TOKENS, MODEL_WIDTH)
        return jnp.where(valid_mask[:, None], projected_rows + output_adapter_delta, 0.0).astype(jnp.float32)
    result = lax.map(one_group, (group_in, adapter_choice, request_block_count, last_block_tokens))
    return result.reshape(TOKENS, MODEL_WIDTH)
```

```python
import math

import jax
import jax.numpy as jnp
from jax import lax
from jax.experimental import pallas as pl
from jax.experimental.pallas import tpu as pltpu
from jax.sharding import Mesh, PartitionSpec as P

HEAD = 128
BLOCK = 128
SIDE = 4
CORES = 2
ADAPTER_AXES = ("z", "c")
TENSOR_AXES = ("y", "x")
ROPE_BASE = 500000.0
VMEM = 56 * 1024 * 1024
bf16 = jnp.bfloat16
f32 = jnp.float32
i32 = jnp.int32


def params():
    return pltpu.CompilerParams(vmem_limit_bytes=VMEM)


def cost(flops, moved, exps=0):
    return pl.CostEstimate(flops=flops, bytes_accessed=moved, transcendentals=exps)


def shift(block, axis, step):
    return lax.ppermute(block, axis, [(i, (i + step) % SIDE) for i in range(SIDE)])


def ring_gather(block, axis):
    half = block.shape[1] // 2
    behind = shift(block, axis, 1)
    ahead = shift(block, axis, -1)
    far_low = shift(behind[:, :half], axis, 1)
    far_high = shift(ahead[:, half:], axis, -1)
    return block, behind, ahead, far_low, far_high


def ring_order(index):
    return [index, (index + SIDE - 1) % SIDE, (index + 1) % SIDE, (index + 2) % SIDE]


def pick_adapters(pick, down_qkv, up_q, up_kv, down_o, up_o):
    groups = pick.shape[0]
    depth, rank3 = down_qkv.shape[1:]
    rank, wide = up_q.shape[1:]
    narrow = up_kv.shape[2]

    def body(pick_ref, dq, uq, ukv, do, uo, down, up):
        down[0, :, :rank3] = dq[0]
        down[0, :, rank3:] = do[0]
        up[0, :, :wide] = uq[0]
        up[0, :, wide : 2 * wide] = uo[0]
        up[0, :, 2 * wide :] = ukv[0]

    def chosen(a):
        return pl.BlockSpec((1,) + a.shape[1:], lambda i, p: (p[i], 0, 0))

    down_shape = (groups, depth, rank3 + rank)
    up_shape = (groups, rank, 2 * wide + narrow)
    return pl.pallas_call(
        body,
        out_shape=(
            jax.ShapeDtypeStruct(down_shape, bf16),
            jax.ShapeDtypeStruct(up_shape, bf16),
        ),
        grid_spec=pltpu.PrefetchScalarGridSpec(
            num_scalar_prefetch=1,
            grid=(groups,),
            in_specs=[chosen(a) for a in (down_qkv, up_q, up_kv, down_o, up_o)],
            out_specs=[
                pl.BlockSpec((1,) + s[1:], lambda i, p: (i, 0, 0)) for s in (down_shape, up_shape)
            ],
        ),
        compiler_params=params(),
        cost_estimate=cost(0, 2 * 2 * (math.prod(down_shape) + math.prod(up_shape))),
    )(pick, down_qkv, up_q, up_kv, down_o, up_o)


def rank_partial(slot, x, down, rank3):
    tokens, depth = x.shape

    def body(slot_ref, x_ref, d_ref, out):
        out[...] = jnp.dot(x_ref[...], d_ref[0], preferred_element_type=f32)[:, :rank3]

    return pl.pallas_call(
        body,
        out_shape=jax.ShapeDtypeStruct((tokens, rank3), f32),
        grid_spec=pltpu.PrefetchScalarGridSpec(
            num_scalar_prefetch=1,
            grid=(tokens // BLOCK,),
            in_specs=[
                pl.BlockSpec((BLOCK, depth), lambda i, s: (i, 0)),
                pl.BlockSpec((1,) + down.shape[1:], lambda i, s: (s[i], 0, 0)),
            ],
            out_specs=pl.BlockSpec((BLOCK, rank3), lambda i, s: (i, 0)),
        ),
        compiler_params=params(),
        cost_estimate=cost(2 * tokens * depth * rank3, 2 * tokens * depth + 8 * tokens * rank3),
    )(slot, x, down)


def sum_over_tensor(partial):
    tokens, rank = partial.shape
    ways = SIDE * SIDE
    pieces = lax.all_to_all(
        partial.reshape(ways, tokens // ways, rank), TENSOR_AXES, 0, 0, tiled=True
    )
    mine = jnp.sum(pieces, axis=0).astype(bf16)
    copies = jnp.broadcast_to(mine[None], (ways,) + mine.shape)
    return lax.all_to_all(copies, TENSOR_AXES, 0, 0, tiled=True).reshape(tokens, rank)


def project(index, total, blocks, wq, wkv, rows=256):
    tokens = blocks[0].shape[0]
    wide, narrow = wq.shape[1], wkv.shape[1]
    tile = 256
    counts = [b.shape[1] // rows for b in blocks]
    pieces = sum(counts)
    first = total is None

    def body(index_ref, *refs):
        x_refs = refs[: len(blocks)]
        q_refs = refs[len(blocks) : len(blocks) + pieces]
        kv_refs = refs[len(blocks) + pieces : len(blocks) + 2 * pieces]
        rest = refs[len(blocks) + 2 * pieces :]
        q_out, kv_out = rest[-2:]
        q = kv = None
        at = 0
        for x_ref, n in zip(x_refs, counts):
            x = x_ref[...]
            wq_rows = jnp.concatenate([r[...] for r in q_refs[at : at + n]], axis=0)
            wkv_rows = jnp.concatenate([r[...] for r in kv_refs[at : at + n]], axis=0)
            q_add = jnp.dot(x, wq_rows, preferred_element_type=f32)
            kv_add = jnp.dot(x, wkv_rows, preferred_element_type=f32)
            q = q_add if q is None else q + q_add
            kv = kv_add if kv is None else kv + kv_add
            at += n
        if not first:
            q = q + rest[0][...]
            kv = kv + rest[1][...]
        q_out[...] = q
        kv_out[...] = kv

    def weight(k, width):
        return pl.BlockSpec((rows, width), lambda i, p, k=k: (p[k], 0))

    row_spec = [
        pl.BlockSpec((tile, wide), lambda i, p: (i, 0)),
        pl.BlockSpec((tile, narrow), lambda i, p: (i, 0)),
    ]
    in_specs = (
        [pl.BlockSpec((tile, b.shape[1]), lambda i, p: (i, 0)) for b in blocks]
        + [weight(k, wide) for k in range(pieces)]
        + [weight(k, narrow) for k in range(pieces)]
        + ([] if first else row_spec)
    )
    operands = list(blocks) + [wq] * pieces + [wkv] * pieces + ([] if first else list(total))
    aliases = {} if first else {len(operands) - 1: 0, len(operands): 1}
    depth = pieces * rows
    return pl.pallas_call(
        body,
        out_shape=(
            jax.ShapeDtypeStruct((tokens, wide), f32),
            jax.ShapeDtypeStruct((tokens, narrow), f32),
        ),
        grid_spec=pltpu.PrefetchScalarGridSpec(
            num_scalar_prefetch=1,
            grid=(tokens // tile,),
            in_specs=in_specs,
            out_specs=row_spec,
        ),
        input_output_aliases=aliases,
        compiler_params=params(),
        cost_estimate=cost(
            2 * tokens * depth * (wide + narrow),
            2 * depth * (tokens + wide + narrow) + 8 * tokens * (wide + narrow),
        ),
    )(index, *operands)


def finish_key_value(meta, kv, shrunk, up, cosine, sine, wide):
    tokens, narrow = kv.shape
    rank = shrunk.shape[1] // 3

    def body(meta_ref, kv_ref, s_ref, up_ref, c_ref, n_ref, out):
        is_key = meta_ref[3, 0] == 1
        s = s_ref[...].astype(f32)
        rank_in = jnp.where(is_key, s[:, rank : 2 * rank], s[:, 2 * rank :]).astype(bf16)
        u = kv_ref[...] + jnp.dot(rank_in, up_ref[0], preferred_element_type=f32)
        turned = u * c_ref[0] + pltpu.roll(u, HEAD // 2, 1) * n_ref[0]
        out[...] = jnp.where(is_key, turned, u).astype(bf16)

    table = pl.BlockSpec((1, BLOCK, HEAD), lambda i, m: (m[1, i], 0, 0))
    return pl.pallas_call(
        body,
        out_shape=jax.ShapeDtypeStruct((tokens, narrow), bf16),
        grid_spec=pltpu.PrefetchScalarGridSpec(
            num_scalar_prefetch=1,
            grid=(tokens // BLOCK,),
            in_specs=[
                pl.BlockSpec((BLOCK, narrow), lambda i, m: (i, 0)),
                pl.BlockSpec((BLOCK, 3 * rank), lambda i, m: (i, 0)),
                pl.BlockSpec((1, rank, narrow), lambda i, m: (m[0, i], 0, 2 * wide // narrow)),
                table,
                table,
            ],
            out_specs=pl.BlockSpec((BLOCK, narrow), lambda i, m: (i, 0)),
        ),
        compiler_params=params(),
        cost_estimate=cost(2 * tokens * rank * narrow, 6 * tokens * narrow + 6 * tokens * rank),
    )(meta, kv, shrunk, up, cosine, sine)


def attention(meta, q, shrunk, up, down, mine, other, cosine, sine):
    tokens, wide = q.shape
    rank = shrunk.shape[1] // 3
    heads = wide // HEAD
    window = min(3 * BLOCK, tokens)
    scale = 1.0 / math.sqrt(HEAD)

    def body(meta_ref, q_ref, s_ref, up_ref, d_ref, m_ref, o_ref, c_ref, n_ref, att, head):
        i = pl.program_id(0)
        is_key = meta_ref[3, 0] == 1
        first = meta_ref[2, i]
        limit = meta_ref[4, i]
        u = q_ref[...] + jnp.dot(
            s_ref[...][:, :rank], up_ref[0], preferred_element_type=f32
        )
        start = pl.multiple_of(jnp.maximum(i - 2, 0) * BLOCK, BLOCK)
        own = m_ref[pl.ds(start, window), :]
        far = o_ref[pl.ds(start, window), :]
        keys = jnp.where(is_key, own, far)
        values = jnp.where(is_key, far, own)
        row = i * BLOCK + lax.broadcasted_iota(i32, (BLOCK, window), 0)
        col = start + lax.broadcasted_iota(i32, (BLOCK, window), 1)
        allowed = (col >= first) & (col <= row) & (col < limit)
        for h in range(heads):
            at = slice(h * HEAD, (h + 1) * HEAD)
            part = u[:, at]
            turned = part * c_ref[0] + pltpu.roll(part, HEAD // 2, 1) * n_ref[0]
            scores = lax.dot_general(
                turned.astype(bf16), keys, (((1,), (1,)), ((), ())), preferred_element_type=f32
            )
            weights = jnp.where(allowed, jnp.exp(scores * scale), 0.0)
            weights = weights / jnp.sum(weights, axis=1, keepdims=True)
            mixed = jnp.dot(weights.astype(bf16), values, preferred_element_type=f32)
            att[:, at] = mixed.astype(bf16)
        head[...] = jnp.dot(att[...], d_ref[0], preferred_element_type=f32)[:, 3 * rank :]

    table = pl.BlockSpec((1, BLOCK, HEAD), lambda i, m: (m[1, i], 0, 0))
    whole = pl.BlockSpec((tokens, HEAD), lambda i, m: (0, 0))
    return pl.pallas_call(
        body,
        out_shape=(
            jax.ShapeDtypeStruct((tokens, wide), bf16),
            jax.ShapeDtypeStruct((tokens, rank), f32),
        ),
        grid_spec=pltpu.PrefetchScalarGridSpec(
            num_scalar_prefetch=1,
            grid=(tokens // BLOCK,),
            in_specs=[
                pl.BlockSpec((BLOCK, wide), lambda i, m: (i, 0)),
                pl.BlockSpec((BLOCK, 3 * rank), lambda i, m: (i, 0)),
                pl.BlockSpec((1, rank, wide), lambda i, m: (m[0, i], 0, 0)),
                pl.BlockSpec((1,) + down.shape[1:], lambda i, m: (m[0, i], 0, 0)),
                whole,
                whole,
                table,
                table,
            ],
            out_specs=[
                pl.BlockSpec((BLOCK, wide), lambda i, m: (i, 0)),
                pl.BlockSpec((BLOCK, rank), lambda i, m: (i, 0)),
            ],
        ),
        compiler_params=params(),
        cost_estimate=cost(
            4 * tokens * window * wide, 8 * tokens * wide, heads * tokens * window
        ),
    )(meta, q, shrunk, up, down, mine, other, cosine, sine)


def pick_columns(index, matrix, width):
    depth = matrix.shape[0]
    count = index.shape[0]

    def body(index_ref, m_ref, out):
        out[0] = m_ref[...]

    return pl.pallas_call(
        body,
        out_shape=jax.ShapeDtypeStruct((count, depth, width), bf16),
        grid_spec=pltpu.PrefetchScalarGridSpec(
            num_scalar_prefetch=1,
            grid=(count,),
            in_specs=[pl.BlockSpec((depth, width), lambda i, p: (0, p[i]))],
            out_specs=pl.BlockSpec((1, depth, width), lambda i, p: (i, 0, 0)),
        ),
        compiler_params=params(),
        cost_estimate=cost(0, 4 * count * depth * width),
    )(index, matrix)


def output_partial(index, pieces, weights, dtype):
    tokens = pieces[0].shape[0]
    shards, depth, width = weights.shape
    per = shards // SIDE
    unit = depth // SIDE

    def body(index_ref, *refs):
        x_refs, w_ref, out = refs[:-2], refs[-2], refs[-1]
        total = None
        for k, (x_ref, (place, offset)) in enumerate(zip(x_refs, places)):
            size = x_ref.shape[1]
            start = pl.multiple_of(index_ref[1 + place] * unit + offset, 128)
            rows = w_ref[0, pl.ds(start, size), :]
            add = jnp.dot(x_ref[...], rows, preferred_element_type=f32)
            total = add if total is None else total + add
        out[...] = total.astype(dtype)

    places = [(0, 0), (1, 0), (2, 0), (3, 0), (3, unit // 2)]
    return pl.pallas_call(
        body,
        out_shape=jax.ShapeDtypeStruct((tokens, per * width), dtype),
        grid_spec=pltpu.PrefetchScalarGridSpec(
            num_scalar_prefetch=1,
            grid=(per,),
            in_specs=[pl.BlockSpec(p.shape, lambda j, d: (0, 0)) for p in pieces]
            + [pl.BlockSpec((1, depth, width), lambda j, d: (d[0] * per + j, 0, 0))],
            out_specs=pl.BlockSpec((tokens, width), lambda j, d: (0, j)),
        ),
        compiler_params=params(),
        cost_estimate=cost(
            2 * tokens * depth * per * width, 2 * depth * (tokens + per * width)
        ),
    )(index, *pieces, weights)


def finish(meta, parts_a, parts_b, head_rank, up, wide):
    half, width = parts_a[0].shape
    tokens = 2 * half
    steps = half // BLOCK
    rank = head_rank.shape[1]
    count = len(parts_a)

    def body(meta_ref, *refs):
        a_refs, b_refs = refs[:count], refs[count : 2 * count]
        h_ref, up_ref, out = refs[2 * count :]
        i = pl.program_id(0)
        extra = jnp.dot(h_ref[...], up_ref[0], preferred_element_type=f32)
        row = i * BLOCK + lax.broadcasted_iota(i32, (BLOCK, width), 0)
        valid = row < meta_ref[4, i]

        def put(group):
            total = extra
            for ref in group:
                total = total + ref[...].astype(f32)
            out[...] = jnp.where(valid, total, 0.0)

        @pl.when(i < steps)
        def _():
            put(a_refs)

        @pl.when(i >= steps)
        def _():
            put(b_refs)

    spec_a = pl.BlockSpec((BLOCK, width), lambda i, m: (jnp.minimum(i, steps - 1), 0))
    spec_b = pl.BlockSpec((BLOCK, width), lambda i, m: (jnp.maximum(i - steps, 0), 0))
    return pl.pallas_call(
        body,
        out_shape=jax.ShapeDtypeStruct((tokens, width), f32),
        grid_spec=pltpu.PrefetchScalarGridSpec(
            num_scalar_prefetch=1,
            grid=(2 * steps,),
            in_specs=[spec_a] * count
            + [spec_b] * count
            + [
                pl.BlockSpec((BLOCK, rank), lambda i, m: (i, 0)),
                pl.BlockSpec((1, rank, wide), lambda i, m: (m[0, i], 0, 1)),
            ],
            out_specs=pl.BlockSpec((BLOCK, width), lambda i, m: (i, 0)),
        ),
        compiler_params=params(),
        cost_estimate=cost(2 * tokens * rank * width, 14 * tokens * width),
    )(meta, *parts_a, *parts_b, head_rank, up)


def output_ring(pieces, weights, axis, places):
    me, behind, ahead, far = ring_order(lax.axis_index(axis))

    def partial(dest, dtype=bf16):
        return output_partial(jnp.stack([dest] + places).astype(i32), pieces, weights, dtype)

    away = partial(far)
    half = away.shape[1] // 2
    via_ahead = shift(away[:, :half], axis, 1)
    via_behind = shift(away[:, half:], axis, -1)
    to_ahead = partial(ahead)
    to_behind = partial(behind)
    mine = partial(me, f32)
    to_ahead = jnp.concatenate([to_ahead[:, :half] + via_ahead, to_ahead[:, half:]], axis=1)
    to_behind = jnp.concatenate([to_behind[:, :half], to_behind[:, half:] + via_behind], axis=1)
    return mine, shift(to_ahead, axis, 1), shift(to_behind, axis, -1)


def on_device(x, wq, wkv, wo, down_qkv, up_q, up_kv, down_o, up_o, choice, counts, tails):
    z, c, y, xi = (lax.axis_index(n) for n in ADAPTER_AXES + TENSOR_AXES)
    group = z * CORES + c
    tokens, local = x.shape
    holders = down_qkv.shape[0]
    requests = choice.shape[1]
    wide = wq.shape[1]
    rank = up_q.shape[1]
    blocks = tokens // BLOCK

    owners = choice // holders
    pick = jnp.sum(jnp.where(owners == group, choice % holders, 0), axis=1).astype(i32)
    own_owner = lax.dynamic_index_in_dim(owners, group, 0, keepdims=False)
    req = jnp.arange(requests, dtype=i32)
    starts = jnp.sum(jnp.where(req[None, :] < req[:, None], counts[0][None, :], 0), axis=1)
    block = jnp.arange(blocks, dtype=i32)
    of_block = (starts[None, :] <= block[:, None]) & (
        block[:, None] < (starts + counts[0])[None, :]
    )

    def lookup(values):
        return jnp.sum(jnp.where(of_block, values[None, :], 0), axis=1).astype(i32)

    slot = lookup(own_owner)
    first = lookup(starts)
    limit = (first + lookup(counts[0]) - 1) * BLOCK + lookup(tails[0])
    is_key = jnp.broadcast_to(1 - xi % 2, (blocks,)).astype(i32)
    meta = jnp.stack([slot, block - first, first * BLOCK, is_key, limit]).astype(i32)

    freq = jnp.exp(-(2.0 * jnp.arange(HEAD // 2, dtype=f32) / HEAD) * math.log(ROPE_BASE))
    angle = jnp.arange(3 * BLOCK, dtype=f32)[:, None] * freq[None, :]
    cosine = jnp.tile(jnp.cos(angle), (1, 2)).reshape(3, BLOCK, HEAD)
    sine = jnp.concatenate([-jnp.sin(angle), jnp.sin(angle)], axis=1).reshape(3, BLOCK, HEAD)

    half = local // 2
    ys, xs = ring_order(y), ring_order(xi)
    flat_a = jnp.concatenate(ring_gather(x[:, :half], "x"), axis=1)
    flat_b = jnp.concatenate(ring_gather(x[:, half:], "y"), axis=1)

    def rows_a(k, cols):
        return [(ys[k] * SIDE + xs[j]) * 2 for j in cols]

    def rows_b(k, cols):
        return [(ys[j] * SIDE + xs[k]) * 2 + 1 for j in cols]

    def index_of(rows):
        return jnp.stack(rows).astype(i32)

    every = range(SIDE)
    a0, a1, a2, a3, a4 = ring_gather(flat_a, "y")
    b0, b1, b2, b3, b4 = ring_gather(flat_b, "x")

    down_out, up_out = pick_adapters(pick, down_qkv, up_q, up_kv, down_o, up_o)
    down = lax.all_to_all(down_out, ADAPTER_AXES, 0, 0, tiled=True)
    up = lax.all_to_all(up_out, ADAPTER_AXES, 0, 0, tiled=True)
    shrunk = sum_over_tensor(rank_partial(slot, x, down, 3 * rank))

    unit = wo.shape[1] // (SIDE * SIDE * 2)
    four = jnp.arange(SIDE, dtype=i32)
    wo, _ = lax.optimization_barrier((wo, down))
    send_a = pick_columns(four * (2 * SIDE) + group, wo, unit)
    send_b = pick_columns((group // 2) * (2 * SIDE) + four * 2 + group % 2, wo, unit)
    got_a = lax.all_to_all(send_a, "y", 0, 0, tiled=True).reshape(-1, unit)
    got_b = lax.all_to_all(send_b, "x", 0, 0, tiled=True).reshape(-1, unit)
    wo_a = lax.all_gather(got_a, ADAPTER_AXES, axis=0)
    wo_b = lax.all_gather(got_b, ADAPTER_AXES, axis=0)

    total = project(index_of(rows_a(0, every) + rows_b(0, every)), None, [a0, b0], wq, wkv)
    total = project(
        index_of(rows_a(1, every) + rows_a(2, every) + rows_b(1, every) + rows_b(2, every)),
        total,
        [a1, a2, b1, b2],
        wq,
        wkv,
    )
    q, kv = project(
        index_of(rows_a(3, every) + rows_b(3, every)), total, [a3, a4, b3, b4], wq, wkv
    )

    mine = finish_key_value(meta, kv, shrunk, up, cosine, sine, wide)
    other = lax.ppermute(mine, "x", [(i, i ^ 1) for i in range(SIDE)])
    attended, head_partial = attention(meta, q, shrunk, up, down, mine, other, cosine, sine)

    cut = tokens // 2
    pieces_a = ring_gather(attended[:cut], "y")
    pieces_b = ring_gather(attended[cut:], "x")
    head_rank = sum_over_tensor(head_partial)
    parts_a = output_ring(pieces_a, wo_a, "x", ys)
    parts_b = output_ring(pieces_b, wo_b, "y", xs)
    return finish(meta, parts_a, parts_b, head_rank, up, wide)


def solution(mesh):
    fine = Mesh(mesh.devices.reshape(SIDE, CORES, SIDE, SIDE), ADAPTER_AXES + TENSOR_AXES)
    placed = (
        P(ADAPTER_AXES, TENSOR_AXES),
        P(None, TENSOR_AXES),
        P(None, TENSOR_AXES),
        P(TENSOR_AXES, None),
        P(ADAPTER_AXES, TENSOR_AXES, None),
        P(ADAPTER_AXES, None, TENSOR_AXES),
        P(ADAPTER_AXES, None, TENSOR_AXES),
        P(ADAPTER_AXES, TENSOR_AXES, None),
        P(ADAPTER_AXES, None, TENSOR_AXES),
        P(),
        P(ADAPTER_AXES, None),
        P(ADAPTER_AXES, None),
    )
    return jax.shard_map(
        on_device,
        mesh=fine,
        in_specs=placed,
        out_specs=P(ADAPTER_AXES, TENSOR_AXES),
        check_vma=False,
    )
```

```python
import math

import jax
import jax.numpy as jnp
from jax import lax
from jax.experimental import pallas as pl
from jax.experimental.pallas import tpu as pltpu
from jax.sharding import Mesh, PartitionSpec as P

HEAD = 128
BLOCK = 128
SIDE = 4
CORES = 2
ADAPTER_AXES = ("z", "c")
TENSOR_AXES = ("y", "x")
ROPE_BASE = 500000.0
VMEM = 56 * 1024 * 1024
bf16 = jnp.bfloat16
f32 = jnp.float32
i32 = jnp.int32


def params():
    return pltpu.CompilerParams(vmem_limit_bytes=VMEM)


def cost(flops, moved, exps=0):
    return pl.CostEstimate(flops=flops, bytes_accessed=moved, transcendentals=exps)


def shift(block, axis, step):
    return lax.ppermute(block, axis, [(i, (i + step) % SIDE) for i in range(SIDE)])


def ring_gather(block, axis):
    half = block.shape[1] // 2
    behind = shift(block, axis, 1)
    ahead = shift(block, axis, -1)
    far_low = shift(behind[:, :half], axis, 1)
    far_high = shift(ahead[:, half:], axis, -1)
    return block, behind, ahead, far_low, far_high


def ring_order(index):
    return [index, (index + SIDE - 1) % SIDE, (index + 1) % SIDE, (index + 2) % SIDE]


def pick_adapters(pick, down_qkv, up_q, up_kv, down_o, up_o):
    groups = pick.shape[0]
    rank3, depth = down_qkv.shape[1:]
    rank, wide = up_q.shape[1:]
    narrow = up_kv.shape[2]

    def body(pick_ref, dq, uq, ukv, do, uo, down, up):
        down[0, :rank3, :] = dq[0]
        down[0, rank3:, :] = do[0]
        up[0, :, :wide] = uq[0]
        up[0, :, wide : 2 * wide] = uo[0]
        up[0, :, 2 * wide :] = ukv[0]

    def chosen(a):
        return pl.BlockSpec((1,) + a.shape[1:], lambda i, p: (p[i], 0, 0))

    down_shape = (groups, rank3 + rank, depth)
    up_shape = (groups, rank, 2 * wide + narrow)
    return pl.pallas_call(
        body,
        out_shape=(
            jax.ShapeDtypeStruct(down_shape, bf16),
            jax.ShapeDtypeStruct(up_shape, bf16),
        ),
        grid_spec=pltpu.PrefetchScalarGridSpec(
            num_scalar_prefetch=1,
            grid=(groups,),
            in_specs=[chosen(a) for a in (down_qkv, up_q, up_kv, down_o, up_o)],
            out_specs=[
                pl.BlockSpec((1,) + s[1:], lambda i, p: (i, 0, 0)) for s in (down_shape, up_shape)
            ],
        ),
        compiler_params=params(),
        cost_estimate=cost(0, 2 * 2 * (math.prod(down_shape) + math.prod(up_shape))),
    )(pick, down_qkv, up_q, up_kv, down_o, up_o)


def rank_partial(meta, x, down, rank3):
    tokens, depth = x.shape
    per = 2
    rows = per * BLOCK

    def body(meta_ref, x_ref, *rest):
        d_refs, out = rest[:-1], rest[-1]
        for k in range(per):
            at = slice(k * BLOCK, (k + 1) * BLOCK)
            out[at, :] = lax.dot_general(
                x_ref[at, :], d_refs[k][0], (((1,), (1,)), ((), ())), preferred_element_type=f32
            )

    def chosen(k):
        return pl.BlockSpec((1, rank3, depth), lambda i, m: (m[0, i * per + k], 0, 0))

    return pl.pallas_call(
        body,
        out_shape=jax.ShapeDtypeStruct((tokens, rank3), f32),
        grid_spec=pltpu.PrefetchScalarGridSpec(
            num_scalar_prefetch=1,
            grid=(tokens // rows,),
            in_specs=[pl.BlockSpec((rows, depth), lambda i, m: (i, 0))]
            + [chosen(k) for k in range(per)],
            out_specs=pl.BlockSpec((rows, rank3), lambda i, m: (i, 0)),
        ),
        compiler_params=params(),
        cost_estimate=cost(2 * tokens * depth * rank3, 2 * tokens * depth + 8 * tokens * rank3),
    )(meta, x, *[down] * per)


def sum_over_tensor(partial):
    rows, rank = partial.shape
    ways = SIDE * SIDE
    pieces = lax.all_to_all(
        partial.reshape(ways, rows // ways, rank), TENSOR_AXES, 0, 0, tiled=True
    )
    mine = jnp.sum(pieces, axis=0).astype(bf16)
    copies = jnp.broadcast_to(mine[None], (ways,) + mine.shape)
    return lax.all_to_all(copies, TENSOR_AXES, 0, 0, tiled=True).reshape(rows, rank)


def project(index, total, blocks, weights, tile, last=None, rows=256):
    tokens = blocks[0].shape[0]
    counts = [b.shape[1] // rows for b in blocks]
    pieces = sum(counts)
    kinds = len(weights)
    first = total is None
    tail, tail_operands, tail_specs, dtype = last or (None, [], [], f32)

    def body(index_ref, meta_ref, *refs):
        x_refs = refs[: len(blocks)]
        w_refs = refs[len(blocks) : len(blocks) + kinds * pieces]
        rest = refs[len(blocks) + kinds * pieces :]
        outs = rest[len(rest) - kinds :]
        for kind in range(kinds):
            mine = w_refs[kind * pieces : (kind + 1) * pieces]
            acc = None if first else rest[kind][...]
            at = 0
            for x_ref, n in zip(x_refs, counts):
                w = jnp.concatenate([r[...] for r in mine[at : at + n]], axis=0)
                add = jnp.dot(x_ref[...], w, preferred_element_type=f32)
                acc = add if acc is None else acc + add
                at += n
            if tail is not None:
                acc = tail(meta_ref, acc, rest[kinds : len(rest) - kinds])
            outs[kind][...] = acc

    def weight(k, width):
        return pl.BlockSpec((rows, width), lambda i, p, m: (p[k], 0))

    widths = [w.shape[1] for w in weights]
    row_specs = [pl.BlockSpec((tile, w), lambda i, p, m: (i, 0)) for w in widths]
    in_specs = [pl.BlockSpec((tile, b.shape[1]), lambda i, p, m: (i, 0)) for b in blocks]
    operands = list(blocks)
    for w in weights:
        in_specs += [weight(k, w.shape[1]) for k in range(pieces)]
        operands += [w] * pieces
    aliases = {}
    if not first:
        if tail is None:
            aliases = {2 + len(operands) + k: k for k in range(kinds)}
        in_specs += row_specs
        operands += list(total)
    index, meta = index
    depth = pieces * rows
    return pl.pallas_call(
        body,
        out_shape=tuple(jax.ShapeDtypeStruct((tokens, w), dtype) for w in widths),
        grid_spec=pltpu.PrefetchScalarGridSpec(
            num_scalar_prefetch=2,
            grid=(tokens // tile,),
            in_specs=in_specs + tail_specs,
            out_specs=row_specs,
        ),
        input_output_aliases=aliases,
        compiler_params=params(),
        cost_estimate=cost(
            2 * tokens * depth * sum(widths),
            2 * depth * (tokens + sum(widths)) + 8 * tokens * sum(widths),
        ),
    )(index, meta, *operands, *tail_operands)


def key_value_tail(shrunk, up, cosine, sine, wide, narrow, tile):
    rank = shrunk.shape[1] // 3
    per = tile // BLOCK

    def tail(meta_ref, acc, refs):
        s_ref, up_ref, c_ref, n_ref = refs
        i = pl.program_id(0)
        is_key = meta_ref[3, 0] == 1
        done = []
        for k in range(per):
            at = slice(k * BLOCK, (k + 1) * BLOCK)
            s = s_ref[at, :].astype(f32)
            rank_in = jnp.where(is_key, s[:, rank : 2 * rank], s[:, 2 * rank :]).astype(bf16)
            u = acc[at, :] + jnp.dot(
                rank_in, up_ref[meta_ref[0, i * per + k]], preferred_element_type=f32
            )
            place = meta_ref[1, i * per + k]
            turned = u * c_ref[place] + pltpu.roll(u, HEAD // 2, 1) * n_ref[place]
            done.append(jnp.where(is_key, turned, u).astype(bf16))
        return jnp.concatenate(done, axis=0)

    specs = [
        pl.BlockSpec((tile, 3 * rank), lambda i, p, m: (i, 0)),
        pl.BlockSpec((up.shape[0], rank, narrow), lambda i, p, m: (0, 0, 2 * wide // narrow)),
        pl.BlockSpec(cosine.shape, lambda i, p, m: (0, 0, 0)),
        pl.BlockSpec(sine.shape, lambda i, p, m: (0, 0, 0)),
    ]
    return tail, [shrunk, up, cosine, sine], specs, bf16


def attention(meta, q, shrunk, up, down, mine, other, cosine, sine, begin, count):
    tokens, wide = q.shape
    rank = shrunk.shape[1] // 3
    heads = wide // HEAD
    window = min(3 * BLOCK, tokens)
    scale = 1.0 / math.sqrt(HEAD)

    def body(meta_ref, q_ref, s_ref, up_ref, d_ref, m_ref, o_ref, c_ref, n_ref, att, head):
        i = begin + pl.program_id(0)
        is_key = meta_ref[3, 0] == 1
        first = meta_ref[2, i]
        limit = meta_ref[4, i]
        u = q_ref[...] + jnp.dot(
            s_ref[...][:, :rank], up_ref[0], preferred_element_type=f32
        )
        start = pl.multiple_of(jnp.maximum(i - 2, 0) * BLOCK, BLOCK)
        own = m_ref[pl.ds(start, window), :]
        far = o_ref[pl.ds(start, window), :]
        keys = jnp.where(is_key, own, far)
        values = jnp.where(is_key, far, own)
        row = i * BLOCK + lax.broadcasted_iota(i32, (BLOCK, window), 0)
        col = start + lax.broadcasted_iota(i32, (BLOCK, window), 1)
        allowed = (col >= first) & (col <= row) & (col < limit)
        cosines = c_ref[0]
        sines = n_ref[0]
        turned = []
        for h in range(heads):
            part = u[:, h * HEAD : (h + 1) * HEAD]
            turned.append(
                (part * cosines + pltpu.roll(part, HEAD // 2, 1) * sines).astype(bf16)
            )
        scores = lax.dot_general(
            jnp.concatenate(turned, axis=0),
            keys,
            (((1,), (1,)), ((), ())),
            preferred_element_type=f32,
        )
        for h in range(heads):
            at = slice(h * HEAD, (h + 1) * HEAD)
            weights = jnp.where(allowed, jnp.exp(scores[at, :] * scale), 0.0)
            weights = weights * (1.0 / jnp.sum(weights, axis=1, keepdims=True))
            mixed = jnp.dot(weights.astype(bf16), values, preferred_element_type=f32)
            att[:, at] = mixed.astype(bf16)
        head[...] = lax.dot_general(
            att[...], d_ref[0], (((1,), (1,)), ((), ())), preferred_element_type=f32
        )

    table = pl.BlockSpec((1, BLOCK, HEAD), lambda i, m: (m[1, i + begin], 0, 0))
    whole = pl.BlockSpec((tokens, HEAD), lambda i, m: (0, 0))
    return pl.pallas_call(
        body,
        out_shape=(
            jax.ShapeDtypeStruct((count * BLOCK, wide), bf16),
            jax.ShapeDtypeStruct((count * BLOCK, rank), f32),
        ),
        grid_spec=pltpu.PrefetchScalarGridSpec(
            num_scalar_prefetch=1,
            grid=(count,),
            in_specs=[
                pl.BlockSpec((BLOCK, wide), lambda i, m: (i + begin, 0)),
                pl.BlockSpec((BLOCK, 3 * rank), lambda i, m: (i + begin, 0)),
                pl.BlockSpec((1, rank, wide), lambda i, m: (m[0, i + begin], 0, 0)),
                pl.BlockSpec((1, rank, down.shape[2]), lambda i, m: (m[0, i + begin], 3, 0)),
                whole,
                whole,
                table,
                table,
            ],
            out_specs=[
                pl.BlockSpec((BLOCK, wide), lambda i, m: (i, 0)),
                pl.BlockSpec((BLOCK, rank), lambda i, m: (i, 0)),
            ],
        ),
        compiler_params=params(),
        cost_estimate=cost(
            4 * count * BLOCK * window * wide, 8 * count * BLOCK * wide, heads * count * BLOCK * window
        ),
    )(meta, q, shrunk, up, down, mine, other, cosine, sine)


def pick_columns(index, matrix, width):
    depth = matrix.shape[0]
    count = index.shape[0]

    def body(index_ref, m_ref, out):
        out[0] = m_ref[...]

    return pl.pallas_call(
        body,
        out_shape=jax.ShapeDtypeStruct((count, depth, width), bf16),
        grid_spec=pltpu.PrefetchScalarGridSpec(
            num_scalar_prefetch=1,
            grid=(count,),
            in_specs=[pl.BlockSpec((depth, width), lambda i, p: (0, p[i]))],
            out_specs=pl.BlockSpec((1, depth, width), lambda i, p: (i, 0, 0)),
        ),
        compiler_params=params(),
        cost_estimate=cost(0, 4 * count * depth * width),
    )(index, matrix)


def output_partial(index, pieces, weights, dtypes):
    tokens = pieces[0].shape[0]
    depth, width = weights.shape[1:]
    unit = depth // SIDE
    count = len(dtypes)
    places = [(0, 0), (1, 0), (2, 0), (3, 0), (3, unit // 2)]

    def body(index_ref, *refs):
        x_refs, w_ref, outs = refs[: len(pieces)], refs[len(pieces)], refs[len(pieces) + 1 :]
        total = None
        for x_ref, (place, offset) in zip(x_refs, places):
            start = pl.multiple_of(index_ref[place] * unit + offset, 128)
            rows = w_ref[0, pl.ds(start, x_ref.shape[1]), :]
            add = jnp.dot(x_ref[...], rows, preferred_element_type=f32)
            total = add if total is None else total + add
        for k, out in enumerate(outs):

            @pl.when(pl.program_id(0) == k)
            def _():
                out[...] = total.astype(out.dtype)

    return pl.pallas_call(
        body,
        out_shape=tuple(jax.ShapeDtypeStruct((tokens, width), d) for d in dtypes),
        grid_spec=pltpu.PrefetchScalarGridSpec(
            num_scalar_prefetch=1,
            grid=(count,),
            in_specs=[pl.BlockSpec(p.shape, lambda j, d: (0, 0)) for p in pieces]
            + [pl.BlockSpec((1, depth, width), lambda j, d: (d[SIDE + j], 0, 0))],
            out_specs=[pl.BlockSpec((tokens, width), lambda j, d: (0, 0))] * count,
        ),
        compiler_params=params(),
        cost_estimate=cost(
            2 * tokens * depth * count * width, 2 * depth * (tokens + count * width)
        ),
    )(index, *pieces, weights)


def output_ring(pieces, weights, axis, places):
    me, behind, ahead, far = ring_order(lax.axis_index(axis))

    def partial(shards, dtypes):
        return output_partial(jnp.stack(places + shards).astype(i32), pieces, weights, dtypes)

    far_low, far_high = partial([2 * far, 2 * far + 1], [bf16] * 2)
    via_behind = shift(far_low, axis, 1)
    via_ahead = shift(far_high, axis, -1)
    ahead_high, behind_low, ahead_low, behind_high, low, high = partial(
        [2 * ahead + 1, 2 * behind, 2 * ahead, 2 * behind + 1, 2 * me, 2 * me + 1],
        [bf16] * 4 + [f32] * 2,
    )
    return (
        (low, shift(behind_low, axis, -1), shift(ahead_low + via_behind, axis, 1)),
        (high, shift(ahead_high, axis, 1), shift(behind_high + via_ahead, axis, -1)),
    )


def finish(meta, parts, head_rank, up, wide):
    cuts = len(parts)
    rows, width = parts[0][0][0].shape
    per = 2
    steps = rows // (per * BLOCK)
    rank = head_rank.shape[1] // cuts
    terms = [t for cut in parts for side in cut for t in side]
    each = len(parts[0][0])

    def body(meta_ref, *refs):
        h_ref, up_ref, out = refs[len(terms) :]
        i = pl.program_id(0)

        def put(cut):
            for k in range(per):
                at = slice(k * BLOCK, (k + 1) * BLOCK)
                block = i * per + k
                extra = jnp.dot(
                    h_ref[at, cut * rank : (cut + 1) * rank],
                    up_ref[meta_ref[0, block]],
                    preferred_element_type=f32,
                )
                row = block * BLOCK + lax.broadcasted_iota(i32, (BLOCK, width), 0)
                valid = row < meta_ref[4, block]
                for side in range(2):
                    cols = slice(side * width, (side + 1) * width)
                    total = extra[:, cols]
                    begin = (cut * 2 + side) * each
                    for ref in refs[begin : begin + each]:
                        total = total + ref[at, :].astype(f32)
                    out[at, cols] = jnp.where(valid, total, 0.0)

        for cut in range(cuts):

            @pl.when(i // steps == cut)
            def _():
                put(cut)

    def term_spec(cut):
        return pl.BlockSpec(
            (per * BLOCK, width), lambda i, m: (jnp.clip(i - cut * steps, 0, steps - 1), 0)
        )

    return pl.pallas_call(
        body,
        out_shape=jax.ShapeDtypeStruct((cuts * rows, 2 * width), f32),
        grid_spec=pltpu.PrefetchScalarGridSpec(
            num_scalar_prefetch=1,
            grid=(cuts * steps,),
            in_specs=[term_spec(cut) for cut in range(cuts) for _ in range(2 * each)]
            + [
                pl.BlockSpec((per * BLOCK, cuts * rank), lambda i, m: (lax.rem(i, steps), 0)),
                pl.BlockSpec((up.shape[0], rank, wide), lambda i, m: (0, 0, 1)),
            ],
            out_specs=pl.BlockSpec((per * BLOCK, 2 * width), lambda i, m: (i, 0)),
        ),
        compiler_params=params(),
        cost_estimate=cost(4 * cuts * rows * rank * width, 28 * cuts * rows * width),
    )(meta, *terms, head_rank, up)


def on_device(x, wq, wkv, wo, down_qkv, up_q, up_kv, down_o, up_o, choice, counts, tails):
    z, c, y, xi = (lax.axis_index(n) for n in ADAPTER_AXES + TENSOR_AXES)
    group = z * CORES + c
    tokens, local = x.shape
    holders = down_qkv.shape[0]
    requests = choice.shape[1]
    wide = wq.shape[1]
    rank = up_q.shape[1]
    blocks = tokens // BLOCK

    owners = choice // holders
    pick = jnp.sum(jnp.where(owners == group, choice % holders, 0), axis=1).astype(i32)
    own_owner = lax.dynamic_index_in_dim(owners, group, 0, keepdims=False)
    req = jnp.arange(requests, dtype=i32)
    starts = jnp.sum(jnp.where(req[None, :] < req[:, None], counts[0][None, :], 0), axis=1)
    block = jnp.arange(blocks, dtype=i32)
    of_block = (starts[None, :] <= block[:, None]) & (
        block[:, None] < (starts + counts[0])[None, :]
    )

    def lookup(values):
        return jnp.sum(jnp.where(of_block, values[None, :], 0), axis=1).astype(i32)

    slot = lookup(own_owner)
    first = lookup(starts)
    limit = (first + lookup(counts[0]) - 1) * BLOCK + lookup(tails[0])
    is_key = jnp.broadcast_to(1 - xi % 2, (blocks,)).astype(i32)
    meta = jnp.stack([slot, block - first, first * BLOCK, is_key, limit]).astype(i32)

    freq = jnp.exp(-(2.0 * jnp.arange(HEAD // 2, dtype=f32) / HEAD) * math.log(ROPE_BASE))
    angle = jnp.arange(3 * BLOCK, dtype=f32)[:, None] * freq[None, :]
    cosine = jnp.tile(jnp.cos(angle), (1, 2)).reshape(3, BLOCK, HEAD)
    sine = jnp.concatenate([-jnp.sin(angle), jnp.sin(angle)], axis=1).reshape(3, BLOCK, HEAD)

    half = local // 2
    ys, xs = ring_order(y), ring_order(xi)
    flat_first = ring_gather(x[:, :half], "x")
    flat_a = jnp.concatenate(flat_first, axis=1)
    flat_b = jnp.concatenate(ring_gather(x[:, half:], "y"), axis=1)

    def rows_a(k, cols):
        return [(ys[k] * SIDE + xs[j]) * 2 for j in cols]

    def rows_b(k, cols):
        return [(ys[j] * SIDE + xs[k]) * 2 + 1 for j in cols]

    def index_of(rows):
        return jnp.stack(rows).astype(i32)

    every = range(SIDE)
    a0, a1, a2, a3, a4 = ring_gather(flat_a, "y")
    b0, b1, b2, b3, b4 = ring_gather(flat_b, "x")

    stores = (jnp.swapaxes(down_qkv, 1, 2), up_q, up_kv, jnp.swapaxes(down_o, 1, 2), up_o)
    stores, _ = lax.optimization_barrier((stores, flat_first[1]))
    down_out, up_out = pick_adapters(pick, *stores)
    down = lax.all_to_all(down_out, ADAPTER_AXES, 0, 0, tiled=True)
    up = lax.all_to_all(up_out, ADAPTER_AXES, 0, 0, tiled=True)
    shrunk = sum_over_tensor(rank_partial(meta, x, down, 3 * rank))

    unit = wo.shape[1] // (SIDE * SIDE * 2)
    tied, _ = lax.optimization_barrier((wo, down))
    order = ring_order(y)
    sent = pick_columns(jnp.stack(order).astype(i32) * (2 * SIDE) + group, tied, unit)
    got = [sent[0], shift(sent[2], "y", 1), shift(sent[1], "y", -1), shift(sent[3], "y", 2)]
    wo_all = lax.all_gather(jnp.concatenate(got, axis=0), ADAPTER_AXES, axis=0)

    total = project(
        (index_of(rows_a(0, every) + rows_b(0, every)), meta), None, [a0, b0], [wq, wkv], 512
    )
    total = project(
        (index_of(rows_a(1, every) + rows_a(2, every) + rows_b(1, every) + rows_b(2, every)), meta),
        total,
        [a1, a2, b1, b2],
        [wq, wkv],
        512,
    )
    final = (index_of(rows_a(3, every) + rows_b(3, every)), meta)
    far = [a3, a4, b3, b4]
    tail = key_value_tail(shrunk, up, cosine, sine, wide, wkv.shape[1], 512)
    (mine,) = project(final, total[1:], far, [wkv], 512, tail)
    other = lax.ppermute(mine, "x", [(i, i ^ 1) for i in range(SIDE)])
    (q,) = project(final, total[:1], far, [wq], 512)

    cuts = 2
    parts, ranks = [], []
    for cut in range(cuts):
        attended, head = attention(
            meta, q, shrunk, up, down, mine, other, cosine, sine, cut * blocks // cuts, blocks // cuts
        )
        ranks.append(head)
        parts.append(output_ring(ring_gather(attended, "y"), wo_all, "x", [jnp.int32(k) for k in range(SIDE)]))
    head_rank = sum_over_tensor(jnp.concatenate(ranks, axis=1))
    return finish(meta, parts, head_rank, up, wide)


def solution(mesh):
    fine = Mesh(mesh.devices.reshape(SIDE, CORES, SIDE, SIDE), ADAPTER_AXES + TENSOR_AXES)
    placed = (
        P(ADAPTER_AXES, TENSOR_AXES),
        P(None, TENSOR_AXES),
        P(None, TENSOR_AXES),
        P(TENSOR_AXES, None),
        P(ADAPTER_AXES, TENSOR_AXES, None),
        P(ADAPTER_AXES, None, TENSOR_AXES),
        P(ADAPTER_AXES, None, TENSOR_AXES),
        P(ADAPTER_AXES, TENSOR_AXES, None),
        P(ADAPTER_AXES, None, TENSOR_AXES),
        P(),
        P(ADAPTER_AXES, None),
        P(ADAPTER_AXES, None),
    )
    return jax.shard_map(
        on_device,
        mesh=fine,
        in_specs=placed,
        out_specs=P(ADAPTER_AXES, TENSOR_AXES),
        check_vma=False,
    )
```

```python
import math

import jax
import jax.numpy as jnp
from jax import lax
from jax.experimental import pallas as pl
from jax.experimental.pallas import tpu as pltpu
from jax.sharding import Mesh, PartitionSpec as P

HEAD = 128
BLOCK = 128
SIDE = 4
CORES = 2
ADAPTER_AXES = ("z", "c")
TENSOR_AXES = ("y", "x")
ROPE_BASE = 500000.0
VMEM = 56 * 1024 * 1024
bf16 = jnp.bfloat16
f32 = jnp.float32
i32 = jnp.int32


def params():
    return pltpu.CompilerParams(vmem_limit_bytes=VMEM)


def cost(flops, moved, exps=0):
    return pl.CostEstimate(flops=flops, bytes_accessed=moved, transcendentals=exps)


def shift(block, axis, step):
    return lax.ppermute(block, axis, [(i, (i + step) % SIDE) for i in range(SIDE)])


def ring_gather(block, axis):
    half = block.shape[1] // 2
    behind = shift(block, axis, 1)
    ahead = shift(block, axis, -1)
    far_low = shift(behind[:, :half], axis, 1)
    far_high = shift(ahead[:, half:], axis, -1)
    return block, behind, ahead, far_low, far_high


def second_gather(low, high, axis):
    onward = shift(low, axis, 1), shift(high, axis, -1)
    return onward, (shift(high, axis, 1), shift(low, axis, -1))


def ring_order(index):
    return [index, (index + SIDE - 1) % SIDE, (index + 1) % SIDE, (index + 2) % SIDE]


def pick_adapters(pick, down_qkv, up_q, up_kv, down_o, up_o):
    groups = pick.shape[0]
    rank3, depth = down_qkv.shape[1:]
    rank, wide = up_q.shape[1:]
    narrow = up_kv.shape[2]

    def body(pick_ref, dq, uq, ukv, do, uo, down, up):
        down[0, :rank3, :] = dq[0]
        down[0, rank3:, :] = do[0]
        up[0, :, :wide] = uq[0]
        up[0, :, wide : 2 * wide] = uo[0]
        up[0, :, 2 * wide :] = ukv[0]

    def chosen(a):
        return pl.BlockSpec((1,) + a.shape[1:], lambda i, p: (p[i], 0, 0))

    down_shape = (groups, rank3 + rank, depth)
    up_shape = (groups, rank, 2 * wide + narrow)
    return pl.pallas_call(
        body,
        out_shape=(
            jax.ShapeDtypeStruct(down_shape, bf16),
            jax.ShapeDtypeStruct(up_shape, bf16),
        ),
        grid_spec=pltpu.PrefetchScalarGridSpec(
            num_scalar_prefetch=1,
            grid=(groups,),
            in_specs=[chosen(a) for a in (down_qkv, up_q, up_kv, down_o, up_o)],
            out_specs=[
                pl.BlockSpec((1,) + s[1:], lambda i, p: (i, 0, 0)) for s in (down_shape, up_shape)
            ],
        ),
        compiler_params=params(),
        cost_estimate=cost(0, 2 * 2 * (math.prod(down_shape) + math.prod(up_shape))),
    )(pick, down_qkv, up_q, up_kv, down_o, up_o)


def rank_partial(meta, x, down, rank3):
    tokens, depth = x.shape
    per = 2
    rows = per * BLOCK

    def body(meta_ref, x_ref, *rest):
        d_refs, out = rest[:-1], rest[-1]
        for k in range(per):
            at = slice(k * BLOCK, (k + 1) * BLOCK)
            out[at, :] = lax.dot_general(
                x_ref[at, :], d_refs[k][0], (((1,), (1,)), ((), ())), preferred_element_type=f32
            )

    def chosen(k):
        return pl.BlockSpec((1, rank3, depth), lambda i, m: (m[0, i * per + k], 0, 0))

    return pl.pallas_call(
        body,
        out_shape=jax.ShapeDtypeStruct((tokens, rank3), f32),
        grid_spec=pltpu.PrefetchScalarGridSpec(
            num_scalar_prefetch=1,
            grid=(tokens // rows,),
            in_specs=[pl.BlockSpec((rows, depth), lambda i, m: (i, 0))]
            + [chosen(k) for k in range(per)],
            out_specs=pl.BlockSpec((rows, rank3), lambda i, m: (i, 0)),
        ),
        compiler_params=params(),
        cost_estimate=cost(2 * tokens * depth * rank3, 2 * tokens * depth + 8 * tokens * rank3),
    )(meta, x, *[down] * per)


def sum_over_tensor(partial):
    mine, spread = sum_over_tensor_in_two(partial)
    return spread(mine)


def sum_over_tensor_in_two(partial):
    rows, rank = partial.shape
    ways = SIDE * SIDE
    pieces = lax.all_to_all(
        partial.reshape(ways, rows // ways, rank), TENSOR_AXES, 0, 0, tiled=True
    )
    mine = jnp.sum(pieces, axis=0).astype(bf16)

    def spread(mine):
        copies = jnp.broadcast_to(mine[None], (ways,) + mine.shape)
        return lax.all_to_all(copies, TENSOR_AXES, 0, 0, tiled=True).reshape(rows, rank)

    return mine, spread


def project(index, total, blocks, weights, tile, last=None, rows=256):
    tokens = blocks[0].shape[0]
    counts = [b.shape[1] // rows for b in blocks]
    pieces = sum(counts)
    kinds = len(weights)
    first = total is None
    tail, tail_operands, tail_specs, dtype = last or (None, [], [], f32)

    def body(index_ref, meta_ref, *refs):
        x_refs = refs[: len(blocks)]
        w_refs = refs[len(blocks) : len(blocks) + kinds * pieces]
        rest = refs[len(blocks) + kinds * pieces :]
        outs = rest[len(rest) - kinds :]
        for kind in range(kinds):
            mine = w_refs[kind * pieces : (kind + 1) * pieces]
            acc = None if first else rest[kind][...]
            at = 0
            for x_ref, n in zip(x_refs, counts):
                w = jnp.concatenate([r[...] for r in mine[at : at + n]], axis=0)
                add = jnp.dot(x_ref[...], w, preferred_element_type=f32)
                acc = add if acc is None else acc + add
                at += n
            if tail is not None:
                acc = tail(meta_ref, acc, rest[kinds : len(rest) - kinds])
            outs[kind][...] = acc

    def weight(k, width):
        return pl.BlockSpec((rows, width), lambda i, p, m: (p[k], 0))

    widths = [w.shape[1] for w in weights]
    row_specs = [pl.BlockSpec((tile, w), lambda i, p, m: (i, 0)) for w in widths]
    in_specs = [pl.BlockSpec((tile, b.shape[1]), lambda i, p, m: (i, 0)) for b in blocks]
    operands = list(blocks)
    for w in weights:
        in_specs += [weight(k, w.shape[1]) for k in range(pieces)]
        operands += [w] * pieces
    aliases = {}
    if not first:
        if tail is None:
            aliases = {2 + len(operands) + k: k for k in range(kinds)}
        in_specs += row_specs
        operands += list(total)
    index, meta = index
    depth = pieces * rows
    return pl.pallas_call(
        body,
        out_shape=tuple(jax.ShapeDtypeStruct((tokens, w), dtype) for w in widths),
        grid_spec=pltpu.PrefetchScalarGridSpec(
            num_scalar_prefetch=2,
            grid=(tokens // tile,),
            in_specs=in_specs + tail_specs,
            out_specs=row_specs,
        ),
        input_output_aliases=aliases,
        compiler_params=params(),
        cost_estimate=cost(
            2 * tokens * depth * sum(widths),
            2 * depth * (tokens + sum(widths)) + 8 * tokens * sum(widths),
        ),
    )(index, meta, *operands, *tail_operands)


def key_value_tail(shrunk, up, cosine, sine, wide, narrow, tile):
    rank = shrunk.shape[1] // 3
    per = tile // BLOCK

    def tail(meta_ref, acc, refs):
        s_ref, up_ref, c_ref, n_ref = refs
        i = pl.program_id(0)
        is_key = meta_ref[3, 0] == 1
        done = []
        for k in range(per):
            at = slice(k * BLOCK, (k + 1) * BLOCK)
            s = s_ref[at, :].astype(f32)
            rank_in = jnp.where(is_key, s[:, rank : 2 * rank], s[:, 2 * rank :]).astype(bf16)
            u = acc[at, :] + jnp.dot(
                rank_in, up_ref[meta_ref[0, i * per + k]], preferred_element_type=f32
            )
            place = meta_ref[1, i * per + k]
            turned = u * c_ref[place] + pltpu.roll(u, HEAD // 2, 1) * n_ref[place]
            done.append(jnp.where(is_key, turned, u).astype(bf16))
        return jnp.concatenate(done, axis=0)

    specs = [
        pl.BlockSpec((tile, 3 * rank), lambda i, p, m: (i, 0)),
        pl.BlockSpec((up.shape[0], rank, narrow), lambda i, p, m: (0, 0, 2 * wide // narrow)),
        pl.BlockSpec(cosine.shape, lambda i, p, m: (0, 0, 0)),
        pl.BlockSpec(sine.shape, lambda i, p, m: (0, 0, 0)),
    ]
    return tail, [shrunk, up, cosine, sine], specs, bf16


def attention(meta, q, shrunk, up, down, mine, other, cosine, sine, begin, count):
    tokens, wide = q.shape
    rank = shrunk.shape[1] // 3
    heads = wide // HEAD
    window = min(3 * BLOCK, tokens)
    scale = 1.0 / math.sqrt(HEAD)

    def body(meta_ref, q_ref, s_ref, up_ref, d_ref, m_ref, o_ref, c_ref, n_ref, att, head):
        i = begin + pl.program_id(0)
        is_key = meta_ref[3, 0] == 1
        first = meta_ref[2, i]
        limit = meta_ref[4, i]
        u = q_ref[...] + jnp.dot(
            s_ref[...][:, :rank], up_ref[0], preferred_element_type=f32
        )
        start = pl.multiple_of(jnp.maximum(i - 2, 0) * BLOCK, BLOCK)
        own = m_ref[pl.ds(start, window), :]
        far = o_ref[pl.ds(start, window), :]
        keys = jnp.where(is_key, own, far)
        values = jnp.where(is_key, far, own)
        row = i * BLOCK + lax.broadcasted_iota(i32, (BLOCK, window), 0)
        col = start + lax.broadcasted_iota(i32, (BLOCK, window), 1)
        allowed = (col >= first) & (col <= row) & (col < limit)
        cosines = c_ref[0]
        sines = n_ref[0]
        turned = []
        for h in range(heads):
            part = u[:, h * HEAD : (h + 1) * HEAD]
            turned.append(
                (part * cosines + pltpu.roll(part, HEAD // 2, 1) * sines).astype(bf16)
            )
        scores = lax.dot_general(
            jnp.concatenate(turned, axis=0),
            keys,
            (((1,), (1,)), ((), ())),
            preferred_element_type=f32,
        )
        for h in range(heads):
            at = slice(h * HEAD, (h + 1) * HEAD)
            weights = jnp.where(allowed, jnp.exp(scores[at, :] * scale), 0.0)
            weights = weights * (1.0 / jnp.sum(weights, axis=1, keepdims=True))
            mixed = jnp.dot(weights.astype(bf16), values, preferred_element_type=f32)
            att[:, at] = mixed.astype(bf16)
        head[...] = lax.dot_general(
            att[...], d_ref[0], (((1,), (1,)), ((), ())), preferred_element_type=f32
        )

    table = pl.BlockSpec((1, BLOCK, HEAD), lambda i, m: (m[1, i + begin], 0, 0))
    whole = pl.BlockSpec((tokens, HEAD), lambda i, m: (0, 0))
    return pl.pallas_call(
        body,
        out_shape=(
            jax.ShapeDtypeStruct((count * BLOCK, wide), bf16),
            jax.ShapeDtypeStruct((count * BLOCK, rank), f32),
        ),
        grid_spec=pltpu.PrefetchScalarGridSpec(
            num_scalar_prefetch=1,
            grid=(count,),
            in_specs=[
                pl.BlockSpec((BLOCK, wide), lambda i, m: (i + begin, 0)),
                pl.BlockSpec((BLOCK, 3 * rank), lambda i, m: (i + begin, 0)),
                pl.BlockSpec((1, rank, wide), lambda i, m: (m[0, i + begin], 0, 0)),
                pl.BlockSpec((1, rank, down.shape[2]), lambda i, m: (m[0, i + begin], 3, 0)),
                whole,
                whole,
                table,
                table,
            ],
            out_specs=[
                pl.BlockSpec((BLOCK, wide), lambda i, m: (i, 0)),
                pl.BlockSpec((BLOCK, rank), lambda i, m: (i, 0)),
            ],
        ),
        compiler_params=params(),
        cost_estimate=cost(
            4 * count * BLOCK * window * wide, 8 * count * BLOCK * wide, heads * count * BLOCK * window
        ),
    )(meta, q, shrunk, up, down, mine, other, cosine, sine)


def pick_columns(index, matrix, width):
    depth = matrix.shape[0]
    count = index.shape[0]

    def body(index_ref, m_ref, out):
        out[0] = m_ref[...]

    return pl.pallas_call(
        body,
        out_shape=jax.ShapeDtypeStruct((count, depth, width), bf16),
        grid_spec=pltpu.PrefetchScalarGridSpec(
            num_scalar_prefetch=1,
            grid=(count,),
            in_specs=[pl.BlockSpec((depth, width), lambda i, p: (0, p[i]))],
            out_specs=pl.BlockSpec((1, depth, width), lambda i, p: (i, 0, 0)),
        ),
        compiler_params=params(),
        cost_estimate=cost(0, 4 * count * depth * width),
    )(index, matrix)


def output_partial(index, pieces, weights, dtypes):
    tokens = pieces[0].shape[0]
    depth, width = weights.shape[1:]
    unit = depth // SIDE
    count = len(dtypes)
    places = [(0, 0), (1, 0), (2, 0), (3, 0), (3, unit // 2)]

    def body(index_ref, *refs):
        x_refs, w_ref, outs = refs[: len(pieces)], refs[len(pieces)], refs[len(pieces) + 1 :]
        total = None
        for x_ref, (place, offset) in zip(x_refs, places):
            start = pl.multiple_of(index_ref[place] * unit + offset, 128)
            rows = w_ref[0, pl.ds(start, x_ref.shape[1]), :]
            add = jnp.dot(x_ref[...], rows, preferred_element_type=f32)
            total = add if total is None else total + add
        for k, out in enumerate(outs):

            @pl.when(pl.program_id(0) == k)
            def _():
                out[...] = total.astype(out.dtype)

    return pl.pallas_call(
        body,
        out_shape=tuple(jax.ShapeDtypeStruct((tokens, width), d) for d in dtypes),
        grid_spec=pltpu.PrefetchScalarGridSpec(
            num_scalar_prefetch=1,
            grid=(count,),
            in_specs=[pl.BlockSpec(p.shape, lambda j, d: (0, 0)) for p in pieces]
            + [pl.BlockSpec((1, depth, width), lambda j, d: (d[SIDE + j], 0, 0))],
            out_specs=[pl.BlockSpec((tokens, width), lambda j, d: (0, 0))] * count,
        ),
        compiler_params=params(),
        cost_estimate=cost(
            2 * tokens * depth * count * width, 2 * depth * (tokens + count * width)
        ),
    )(index, *pieces, weights)


def output_ring(pieces, weights, axis, places):
    me, behind, ahead, far = ring_order(lax.axis_index(axis))

    def partial(shards, dtypes):
        return output_partial(jnp.stack(places + shards).astype(i32), pieces, weights, dtypes)

    far_low, far_high = partial([2 * far, 2 * far + 1], [bf16] * 2)
    via_behind = shift(far_low, axis, 1)
    via_ahead = shift(far_high, axis, -1)
    ahead_high, behind_low, ahead_low, behind_high, low, high = partial(
        [2 * ahead + 1, 2 * behind, 2 * ahead, 2 * behind + 1, 2 * me, 2 * me + 1],
        [bf16] * 4 + [f32] * 2,
    )
    return (
        (low, shift(behind_low, axis, -1), shift(ahead_low + via_behind, axis, 1)),
        (high, shift(ahead_high, axis, 1), shift(behind_high + via_ahead, axis, -1)),
    )


def finish(meta, parts, head_rank, up, wide):
    cuts = len(parts)
    rows, width = parts[0][0][0].shape
    per = 2
    steps = rows // (per * BLOCK)
    rank = head_rank.shape[1] // cuts
    terms = [t for cut in parts for side in cut for t in side]
    each = len(parts[0][0])

    def body(meta_ref, *refs):
        h_ref, up_ref, out = refs[len(terms) :]
        i = pl.program_id(0)

        def put(cut):
            for k in range(per):
                at = slice(k * BLOCK, (k + 1) * BLOCK)
                block = i * per + k
                extra = jnp.dot(
                    h_ref[at, cut * rank : (cut + 1) * rank],
                    up_ref[meta_ref[0, block]],
                    preferred_element_type=f32,
                )
                row = block * BLOCK + lax.broadcasted_iota(i32, (BLOCK, width), 0)
                valid = row < meta_ref[4, block]
                for side in range(2):
                    cols = slice(side * width, (side + 1) * width)
                    total = extra[:, cols]
                    begin = (cut * 2 + side) * each
                    for ref in refs[begin : begin + each]:
                        total = total + ref[at, :].astype(f32)
                    out[at, cols] = jnp.where(valid, total, 0.0)

        for cut in range(cuts):

            @pl.when(i // steps == cut)
            def _():
                put(cut)

    def term_spec(cut):
        return pl.BlockSpec(
            (per * BLOCK, width), lambda i, m: (jnp.clip(i - cut * steps, 0, steps - 1), 0)
        )

    return pl.pallas_call(
        body,
        out_shape=jax.ShapeDtypeStruct((cuts * rows, 2 * width), f32),
        grid_spec=pltpu.PrefetchScalarGridSpec(
            num_scalar_prefetch=1,
            grid=(cuts * steps,),
            in_specs=[term_spec(cut) for cut in range(cuts) for _ in range(2 * each)]
            + [
                pl.BlockSpec((per * BLOCK, cuts * rank), lambda i, m: (lax.rem(i, steps), 0)),
                pl.BlockSpec((up.shape[0], rank, wide), lambda i, m: (0, 0, 1)),
            ],
            out_specs=pl.BlockSpec((per * BLOCK, 2 * width), lambda i, m: (i, 0)),
        ),
        compiler_params=params(),
        cost_estimate=cost(4 * cuts * rows * rank * width, 28 * cuts * rows * width),
    )(meta, *terms, head_rank, up)


def on_device(x, wq, wkv, wo, down_qkv, up_q, up_kv, down_o, up_o, choice, counts, tails):
    z, c, y, xi = (lax.axis_index(n) for n in ADAPTER_AXES + TENSOR_AXES)
    group = z * CORES + c
    tokens, local = x.shape
    holders = down_qkv.shape[0]
    requests = choice.shape[1]
    wide = wq.shape[1]
    rank = up_q.shape[1]
    blocks = tokens // BLOCK

    owners = choice // holders
    pick = jnp.sum(jnp.where(owners == group, choice % holders, 0), axis=1).astype(i32)
    own_owner = lax.dynamic_index_in_dim(owners, group, 0, keepdims=False)
    req = jnp.arange(requests, dtype=i32)
    starts = jnp.sum(jnp.where(req[None, :] < req[:, None], counts[0][None, :], 0), axis=1)
    block = jnp.arange(blocks, dtype=i32)
    of_block = (starts[None, :] <= block[:, None]) & (
        block[:, None] < (starts + counts[0])[None, :]
    )

    def lookup(values):
        return jnp.sum(jnp.where(of_block, values[None, :], 0), axis=1).astype(i32)

    slot = lookup(own_owner)
    first = lookup(starts)
    limit = (first + lookup(counts[0]) - 1) * BLOCK + lookup(tails[0])
    is_key = jnp.broadcast_to(1 - xi % 2, (blocks,)).astype(i32)
    meta = jnp.stack([slot, block - first, first * BLOCK, is_key, limit]).astype(i32)

    freq = jnp.exp(-(2.0 * jnp.arange(HEAD // 2, dtype=f32) / HEAD) * math.log(ROPE_BASE))
    angle = jnp.arange(3 * BLOCK, dtype=f32)[:, None] * freq[None, :]
    cosine = jnp.tile(jnp.cos(angle), (1, 2)).reshape(3, BLOCK, HEAD)
    sine = jnp.concatenate([-jnp.sin(angle), jnp.sin(angle)], axis=1).reshape(3, BLOCK, HEAD)

    half = local // 2
    ys, xs = ring_order(y), ring_order(xi)
    first_a = ring_gather(x[:, :half], "x")
    first_b = ring_gather(x[:, half:], "y")
    low_a, high_a = jnp.concatenate(first_a[:2], axis=1), jnp.concatenate(first_a[2:], axis=1)
    low_b, high_b = jnp.concatenate(first_b[:2], axis=1), jnp.concatenate(first_b[2:], axis=1)

    stores = (jnp.swapaxes(down_qkv, 1, 2), up_q, up_kv, jnp.swapaxes(down_o, 1, 2), up_o)
    down_out, up_out = pick_adapters(pick, *stores)
    down = lax.all_to_all(down_out, ADAPTER_AXES, 0, 0, tiled=True)

    far_a, next_a = second_gather(low_a, high_a, "y")
    far_b, next_b = second_gather(low_b, high_b, "x")

    def rows_a(k, cols):
        return [(ys[k] * SIDE + xs[j]) * 2 for j in cols]

    def rows_b(k, cols):
        return [(ys[j] * SIDE + xs[k]) * 2 + 1 for j in cols]

    def index_of(rows):
        return jnp.stack(rows).astype(i32)

    every = range(SIDE)
    low, high = (0, 1), (2, 3)
    total = project(
        (index_of(rows_a(0, every) + rows_b(0, every)), meta),
        None,
        [low_a, high_a, low_b, high_b],
        [wq, wkv],
        512,
    )

    own, down, _ = lax.optimization_barrier((x, down, (low_a, high_a, low_b, high_b)))
    partial = rank_partial(meta, own, down, 3 * rank)
    shrunk = sum_over_tensor(partial)
    up_out, _ = lax.optimization_barrier((up_out, partial))
    up = lax.all_to_all(up_out, ADAPTER_AXES, 0, 0, tiled=True)

    unit = wo.shape[1] // (SIDE * SIDE * 2)
    tied, total = lax.optimization_barrier((wo, total))
    order = ring_order(y)
    sent = pick_columns(jnp.stack(order).astype(i32) * (2 * SIDE) + group, tied, unit)
    got = [sent[0], shift(sent[2], "y", 1), shift(sent[1], "y", -1), shift(sent[3], "y", 2)]
    wo_all = lax.all_gather(jnp.concatenate(got, axis=0), ADAPTER_AXES, axis=0)

    far_a, total = lax.optimization_barrier((far_a, total))
    a_low, a_high = shift(far_a[0], "y", 1), shift(far_a[1], "y", -1)
    b_low, b_high = shift(far_b[0], "x", 1), shift(far_b[1], "x", -1)
    total = project(
        (
            index_of(
                rows_a(1, low) + rows_a(2, high) + rows_b(1, low) + rows_b(2, high)
                + rows_a(1, high) + rows_a(2, low) + rows_b(1, high) + rows_b(2, low)
            ),
            meta,
        ),
        total,
        [*far_a, *far_b, *next_a, *next_b],
        [wq, wkv],
        512,
    )
    final = (index_of(rows_a(3, every) + rows_b(3, every)), meta)
    far = [a_low, a_high, b_low, b_high]
    tail = key_value_tail(shrunk, up, cosine, sine, wide, wkv.shape[1], 512)
    (mine,) = project(final, total[1:], far, [wkv], 512, tail)
    other = lax.ppermute(mine, "x", [(i, i ^ 1) for i in range(SIDE)])
    (q,) = project(final, total[:1], far, [wq], 512)

    cuts = 2
    pieces, ranks = [], []
    for cut in range(cuts):
        attended, head = attention(
            meta, q, shrunk, up, down, mine, other, cosine, sine, cut * blocks // cuts, blocks // cuts
        )
        ranks.append(head)
        pieces.append(ring_gather(attended, "y"))
    mine_rank, spread = sum_over_tensor_in_two(jnp.concatenate(ranks, axis=1))
    places = [jnp.int32(k) for k in range(SIDE)]
    parts = [output_ring(pieces[0], wo_all, "x", places)]
    last, mine_rank = lax.optimization_barrier((pieces[1], mine_rank))
    parts.append(output_ring(last, wo_all, "x", places))
    return finish(meta, parts, spread(mine_rank), up, wide)


def solution(mesh):
    fine = Mesh(mesh.devices.reshape(SIDE, CORES, SIDE, SIDE), ADAPTER_AXES + TENSOR_AXES)
    placed = (
        P(ADAPTER_AXES, TENSOR_AXES),
        P(None, TENSOR_AXES),
        P(None, TENSOR_AXES),
        P(TENSOR_AXES, None),
        P(ADAPTER_AXES, TENSOR_AXES, None),
        P(ADAPTER_AXES, None, TENSOR_AXES),
        P(ADAPTER_AXES, None, TENSOR_AXES),
        P(ADAPTER_AXES, TENSOR_AXES, None),
        P(ADAPTER_AXES, None, TENSOR_AXES),
        P(),
        P(ADAPTER_AXES, None),
        P(ADAPTER_AXES, None),
    )
    return jax.shard_map(
        on_device,
        mesh=fine,
        in_specs=placed,
        out_specs=P(ADAPTER_AXES, TENSOR_AXES),
        check_vma=False,
    )
```

```python
import math

import jax
import jax.numpy as jnp
import numpy as np
from jax import lax
from jax.experimental import pallas as pl
from jax.experimental.pallas import tpu as pltpu
from jax.sharding import Mesh, PartitionSpec as P

HEAD = 128
BLOCK = 128
SIDE = 4
CORES = 2
ADAPTER_AXES = ("z", "c")
TENSOR_AXES = ("y", "x")
ROPE_BASE = 500000.0
VMEM = 56 * 1024 * 1024
bf16 = jnp.bfloat16
f32 = jnp.float32
i32 = jnp.int32


def params():
    return pltpu.CompilerParams(vmem_limit_bytes=VMEM)


def passive(arrays):
    return [pl.BlockSpec(memory_space=pl.ANY)] * len(arrays)


def cost(flops, moved, exps=0):
    return pl.CostEstimate(flops=flops, bytes_accessed=moved, transcendentals=exps)


def shift(block, axis, step):
    return lax.ppermute(block, axis, [(i, (i + step) % SIDE) for i in range(SIDE)])


def ring_gather(block, axis):
    half = block.shape[1] // 2
    behind = shift(block, axis, 1)
    ahead = shift(block, axis, -1)
    far_low = shift(behind[:, :half], axis, 1)
    far_high = shift(ahead[:, half:], axis, -1)
    return block, behind, ahead, far_low, far_high


def second_gather(low, high, axis):
    onward = shift(low, axis, 1), shift(high, axis, -1)
    return onward, (shift(high, axis, 1), shift(low, axis, -1))


def ring_order(index):
    return [index, (index + SIDE - 1) % SIDE, (index + 1) % SIDE, (index + 2) % SIDE]


def pick_adapters(pick, down_qkv, up_q, up_kv, down_o, up_o, x):
    tokens, local = x.shape
    groups = pick.shape[0]
    rank3, depth = down_qkv.shape[1:]
    rank, wide = up_q.shape[1:]
    narrow = up_kv.shape[2]

    def body(pick_ref, dq, uq, ukv, do, uo, x_ref, down, up, left, right):
        left[...] = x_ref[:, : local // 2]
        right[...] = x_ref[:, local // 2 :]
        down[0, :rank3, :] = dq[0]
        down[0, rank3:, :] = do[0]
        up[0, :, :wide] = uq[0]
        up[0, :, wide : 2 * wide] = uo[0]
        up[0, :, 2 * wide :] = ukv[0]

    def chosen(a):
        return pl.BlockSpec((1,) + a.shape[1:], lambda i, p: (p[i], 0, 0))

    down_shape = (groups, rank3 + rank, depth)
    up_shape = (groups, rank, 2 * wide + narrow)
    return pl.pallas_call(
        body,
        out_shape=(
            jax.ShapeDtypeStruct(down_shape, bf16),
            jax.ShapeDtypeStruct(up_shape, bf16),
            jax.ShapeDtypeStruct((tokens, local // 2), bf16),
            jax.ShapeDtypeStruct((tokens, local // 2), bf16),
        ),
        grid_spec=pltpu.PrefetchScalarGridSpec(
            num_scalar_prefetch=1,
            grid=(groups,),
            in_specs=[chosen(a) for a in (down_qkv, up_q, up_kv, down_o, up_o)]
            + [pl.BlockSpec((tokens // groups, local), lambda i, p: (i, 0))],
            out_specs=[
                pl.BlockSpec((1,) + s[1:], lambda i, p: (i, 0, 0)) for s in (down_shape, up_shape)
            ]
            + [pl.BlockSpec((tokens // groups, local // 2), lambda i, p: (i, 0))] * 2,
        ),
        compiler_params=params(),
        cost_estimate=cost(0, 2 * 2 * (math.prod(down_shape) + math.prod(up_shape))),
    )(pick, down_qkv, up_q, up_kv, down_o, up_o, x)


def rank_partial(meta, x, down, rank3, after):
    tokens, depth = x.shape
    per = 2
    rows = per * BLOCK

    def body(meta_ref, x_ref, *rest):
        d_refs, out = rest[:per], rest[-1]
        for k in range(per):
            at = slice(k * BLOCK, (k + 1) * BLOCK)
            out[at, :] = lax.dot_general(
                x_ref[at, :], d_refs[k][0], (((1,), (1,)), ((), ())), preferred_element_type=f32
            )

    def chosen(k):
        return pl.BlockSpec((1, rank3, depth), lambda i, m: (m[0, i * per + k], 0, 0))

    return pl.pallas_call(
        body,
        out_shape=jax.ShapeDtypeStruct((tokens, rank3), f32),
        grid_spec=pltpu.PrefetchScalarGridSpec(
            num_scalar_prefetch=1,
            grid=(tokens // rows,),
            in_specs=[pl.BlockSpec((rows, depth), lambda i, m: (i, 0))]
            + [chosen(k) for k in range(per)]
            + passive(after),
            out_specs=pl.BlockSpec((rows, rank3), lambda i, m: (i, 0)),
        ),
        compiler_params=params(),
        cost_estimate=cost(2 * tokens * depth * rank3, 2 * tokens * depth + 8 * tokens * rank3),
    )(meta, x, *[down] * per, *after)


def join(groups, after):
    tokens = groups[0][0].shape[0]
    rows = 256
    flat = [b for group in groups for b in group]
    widths = [sum(b.shape[1] for b in group) for group in groups]

    def body(*refs):
        ins, outs = refs[: len(flat)], refs[len(flat) + len(after) :]
        at = 0
        for out, group in zip(outs, groups):
            col = 0
            for b in group:
                out[:, col : col + b.shape[1]] = ins[at][...]
                col += b.shape[1]
                at += 1

    return pl.pallas_call(
        body,
        out_shape=tuple(jax.ShapeDtypeStruct((tokens, w), bf16) for w in widths),
        grid=(tokens // rows,),
        in_specs=[pl.BlockSpec((rows, b.shape[1]), lambda i: (i, 0)) for b in flat]
        + passive(after),
        out_specs=[pl.BlockSpec((rows, w), lambda i: (i, 0)) for w in widths],
        compiler_params=params(),
        cost_estimate=cost(0, 4 * tokens * sum(widths)),
    )(*flat, *after)


def share_sum(pieces, after):
    ways, rows, rank = pieces.shape

    def body(p_ref, *refs):
        total = p_ref[0]
        for k in range(1, ways):
            total = total + p_ref[k]
        for k in range(ways):
            refs[-1][k] = total.astype(bf16)

    whole = pl.BlockSpec(pieces.shape, lambda i: (0, 0, 0))
    return pl.pallas_call(
        body,
        out_shape=jax.ShapeDtypeStruct(pieces.shape, bf16),
        grid=(1,),
        in_specs=[whole] + passive(after),
        out_specs=whole,
        compiler_params=params(),
        cost_estimate=cost(ways * rows * rank, 6 * ways * rows * rank),
    )(pieces, *after)


def scatter_rows(partial):
    rows, rank = partial.shape
    ways = SIDE * SIDE
    return lax.all_to_all(
        partial.reshape(ways, rows // ways, rank), TENSOR_AXES, 0, 0, tiled=True
    )


def project(index, total, blocks, weights, tile, last=None, rows=256):
    tokens = blocks[0].shape[0]
    counts = [b.shape[1] // rows for b in blocks]
    pieces = sum(counts)
    kinds = len(weights)
    first = total is None
    tail, tail_operands, tail_specs, dtype = last or (None, [], [], f32)

    def body(index_ref, meta_ref, *refs):
        x_refs = refs[: len(blocks)]
        w_refs = refs[len(blocks) : len(blocks) + kinds * pieces]
        rest = refs[len(blocks) + kinds * pieces :]
        outs = rest[len(rest) - kinds :]
        for kind in range(kinds):
            mine = w_refs[kind * pieces : (kind + 1) * pieces]
            acc = None if first else rest[kind][...]
            at = 0
            for x_ref, n in zip(x_refs, counts):
                w = jnp.concatenate([r[...] for r in mine[at : at + n]], axis=0)
                add = jnp.dot(x_ref[...], w, preferred_element_type=f32)
                acc = add if acc is None else acc + add
                at += n
            if tail is not None:
                acc = tail(meta_ref, acc, rest[kinds : len(rest) - kinds])
            outs[kind][...] = acc

    def weight(k, width):
        return pl.BlockSpec((rows, width), lambda i, p, m: (p[k], 0))

    widths = [w.shape[1] for w in weights]
    row_specs = [pl.BlockSpec((tile, w), lambda i, p, m: (i, 0)) for w in widths]
    in_specs = [pl.BlockSpec((tile, b.shape[1]), lambda i, p, m: (i, 0)) for b in blocks]
    operands = list(blocks)
    for w in weights:
        in_specs += [weight(k, w.shape[1]) for k in range(pieces)]
        operands += [w] * pieces
    aliases = {}
    if not first:
        if tail is None:
            aliases = {2 + len(operands) + k: k for k in range(kinds)}
        in_specs += row_specs
        operands += list(total)
    index, meta = index
    depth = pieces * rows
    return pl.pallas_call(
        body,
        out_shape=tuple(jax.ShapeDtypeStruct((tokens, w), dtype) for w in widths),
        grid_spec=pltpu.PrefetchScalarGridSpec(
            num_scalar_prefetch=2,
            grid=(tokens // tile,),
            in_specs=in_specs + tail_specs,
            out_specs=row_specs,
        ),
        input_output_aliases=aliases,
        compiler_params=params(),
        cost_estimate=cost(
            2 * tokens * depth * sum(widths),
            2 * depth * (tokens + sum(widths)) + 8 * tokens * sum(widths),
        ),
    )(index, meta, *operands, *tail_operands)


def key_value_tail(shrunk, up, cosine, sine, wide, narrow, tile):
    rank = shrunk.shape[1] // 3
    per = tile // BLOCK

    def tail(meta_ref, acc, refs):
        s_ref, up_ref, c_ref, n_ref = refs
        i = pl.program_id(0)
        is_key = meta_ref[3, 0] == 1
        done = []
        for k in range(per):
            at = slice(k * BLOCK, (k + 1) * BLOCK)
            s = s_ref[at, :].astype(f32)
            rank_in = jnp.where(is_key, s[:, rank : 2 * rank], s[:, 2 * rank :]).astype(bf16)
            u = acc[at, :] + jnp.dot(
                rank_in, up_ref[meta_ref[0, i * per + k]], preferred_element_type=f32
            )
            place = meta_ref[1, i * per + k]
            turned = u * c_ref[place] + pltpu.roll(u, HEAD // 2, 1) * n_ref[place]
            done.append(jnp.where(is_key, turned, u).astype(bf16))
        return jnp.concatenate(done, axis=0)

    specs = [
        pl.BlockSpec((tile, 3 * rank), lambda i, p, m: (i, 0)),
        pl.BlockSpec((up.shape[0], rank, narrow), lambda i, p, m: (0, 0, 2 * wide // narrow)),
        pl.BlockSpec(cosine.shape, lambda i, p, m: (0, 0, 0)),
        pl.BlockSpec(sine.shape, lambda i, p, m: (0, 0, 0)),
    ]
    return tail, [shrunk, up, cosine, sine], specs, bf16


def rotation_tables():
    freq = np.exp(-(2.0 * np.arange(HEAD // 2, dtype=np.float32) / HEAD) * math.log(ROPE_BASE))
    angle = np.arange(3 * BLOCK, dtype=np.float32)[:, None] * freq.astype(np.float32)[None, :]
    cosine = np.concatenate([np.cos(angle)] * 2, axis=1)
    sine = np.concatenate([-np.sin(angle), np.sin(angle)], axis=1)
    shape = (3, BLOCK, HEAD)
    return (
        jnp.asarray(cosine.reshape(shape), f32),
        jnp.asarray(sine.reshape(shape), f32),
    )


def attention(meta, q, shrunk, up, down, mine, other, cosine, sine, begin, count):
    tokens, wide = q.shape
    rank = shrunk.shape[1] // 3
    heads = wide // HEAD
    window = min(3 * BLOCK, tokens)
    scale = 1.0 / math.sqrt(HEAD)

    def body(meta_ref, q_ref, s_ref, up_ref, d_ref, m_ref, o_ref, c_ref, n_ref, att, head):
        i = begin + pl.program_id(0)
        is_key = meta_ref[3, 0] == 1
        first = meta_ref[2, i]
        limit = meta_ref[4, i]
        u = q_ref[...] + jnp.dot(
            s_ref[...][:, :rank], up_ref[0], preferred_element_type=f32
        )
        start = pl.multiple_of(jnp.maximum(i - 2, 0) * BLOCK, BLOCK)
        own = m_ref[pl.ds(start, window), :]
        far = o_ref[pl.ds(start, window), :]
        keys = jnp.where(is_key, own, far)
        values = jnp.where(is_key, far, own)
        row = i * BLOCK + lax.broadcasted_iota(i32, (BLOCK, window), 0)
        col = start + lax.broadcasted_iota(i32, (BLOCK, window), 1)
        allowed = (col >= first) & (col <= row) & (col < limit)
        cosines = c_ref[0]
        sines = n_ref[0]
        turned = []
        for h in range(heads):
            part = u[:, h * HEAD : (h + 1) * HEAD]
            turned.append(
                (part * cosines + pltpu.roll(part, HEAD // 2, 1) * sines).astype(bf16)
            )
        scores = lax.dot_general(
            jnp.concatenate(turned, axis=0),
            keys,
            (((1,), (1,)), ((), ())),
            preferred_element_type=f32,
        )
        for h in range(heads):
            at = slice(h * HEAD, (h + 1) * HEAD)
            weights = jnp.where(allowed, jnp.exp(scores[at, :] * scale), 0.0)
            weights = weights * (1.0 / jnp.sum(weights, axis=1, keepdims=True))
            mixed = jnp.dot(weights.astype(bf16), values, preferred_element_type=f32)
            att[:, at] = mixed.astype(bf16)
        head[...] = lax.dot_general(
            att[...], d_ref[0], (((1,), (1,)), ((), ())), preferred_element_type=f32
        )

    table = pl.BlockSpec((1, BLOCK, HEAD), lambda i, m: (m[1, i + begin], 0, 0))
    whole = pl.BlockSpec((tokens, HEAD), lambda i, m: (0, 0))
    return pl.pallas_call(
        body,
        out_shape=(
            jax.ShapeDtypeStruct((count * BLOCK, wide), bf16),
            jax.ShapeDtypeStruct((count * BLOCK, rank), f32),
        ),
        grid_spec=pltpu.PrefetchScalarGridSpec(
            num_scalar_prefetch=1,
            grid=(count,),
            in_specs=[
                pl.BlockSpec((BLOCK, wide), lambda i, m: (i + begin, 0)),
                pl.BlockSpec((BLOCK, 3 * rank), lambda i, m: (i + begin, 0)),
                pl.BlockSpec((1, rank, wide), lambda i, m: (m[0, i + begin], 0, 0)),
                pl.BlockSpec((1, rank, down.shape[2]), lambda i, m: (m[0, i + begin], 3, 0)),
                whole,
                whole,
                table,
                table,
            ],
            out_specs=[
                pl.BlockSpec((BLOCK, wide), lambda i, m: (i, 0)),
                pl.BlockSpec((BLOCK, rank), lambda i, m: (i, 0)),
            ],
        ),
        compiler_params=params(),
        cost_estimate=cost(
            4 * count * BLOCK * window * wide, 8 * count * BLOCK * wide, heads * count * BLOCK * window
        ),
    )(meta, q, shrunk, up, down, mine, other, cosine, sine)


def pick_columns(index, matrix, width, after):
    depth = matrix.shape[0]
    count = index.shape[0]

    def body(index_ref, m_ref, *refs):
        refs[-1][0] = m_ref[...]

    return pl.pallas_call(
        body,
        out_shape=jax.ShapeDtypeStruct((count, depth, width), bf16),
        grid_spec=pltpu.PrefetchScalarGridSpec(
            num_scalar_prefetch=1,
            grid=(count,),
            in_specs=[pl.BlockSpec((depth, width), lambda i, p: (0, p[i]))] + passive(after),
            out_specs=pl.BlockSpec((1, depth, width), lambda i, p: (i, 0, 0)),
        ),
        compiler_params=params(),
        cost_estimate=cost(0, 4 * count * depth * width),
    )(index, matrix, *after)


def output_partial(index, pieces, weights, dtypes, after):
    tokens = pieces[0].shape[0]
    depth, width = weights.shape[1:]
    unit = depth // SIDE
    count = len(dtypes)
    places = [(0, 0), (1, 0), (2, 0), (3, 0), (3, unit // 2)]

    def body(index_ref, *refs):
        x_refs, w_ref, outs = refs[: len(pieces)], refs[len(pieces)], refs[-count:]
        total = None
        for x_ref, (place, offset) in zip(x_refs, places):
            start = pl.multiple_of(index_ref[place] * unit + offset, 128)
            rows = w_ref[0, pl.ds(start, x_ref.shape[1]), :]
            add = jnp.dot(x_ref[...], rows, preferred_element_type=f32)
            total = add if total is None else total + add
        for k, out in enumerate(outs):

            @pl.when(pl.program_id(0) == k)
            def _():
                out[...] = total.astype(out.dtype)

    return pl.pallas_call(
        body,
        out_shape=tuple(jax.ShapeDtypeStruct((tokens, width), d) for d in dtypes),
        grid_spec=pltpu.PrefetchScalarGridSpec(
            num_scalar_prefetch=1,
            grid=(count,),
            in_specs=[pl.BlockSpec(p.shape, lambda j, d: (0, 0)) for p in pieces]
            + [pl.BlockSpec((1, depth, width), lambda j, d: (d[SIDE + j], 0, 0))]
            + passive(after),
            out_specs=[pl.BlockSpec((tokens, width), lambda j, d: (0, 0))] * count,
        ),
        compiler_params=params(),
        cost_estimate=cost(
            2 * tokens * depth * count * width, 2 * depth * (tokens + count * width)
        ),
    )(index, *pieces, weights, *after)


def output_ring(pieces, weights, axis, places, ahead_of):
    me, behind, ahead, far = ring_order(lax.axis_index(axis))

    def partial(shards, dtypes, after=()):
        index = jnp.stack(places + shards).astype(i32)
        return output_partial(index, pieces, weights, dtypes, after)

    far_low, far_high = partial([2 * far, 2 * far + 1], [bf16] * 2)
    via_behind = shift(far_low, axis, 1)
    via_ahead = shift(far_high, axis, -1)
    ahead_high, behind_low, ahead_low, behind_high, low, high = partial(
        [2 * ahead + 1, 2 * behind, 2 * ahead, 2 * behind + 1, 2 * me, 2 * me + 1],
        [bf16] * 4 + [f32] * 2,
        [ahead_of],
    )
    return (
        (low, shift(behind_low, axis, -1), shift(ahead_low + via_behind, axis, 1)),
        (high, shift(ahead_high, axis, 1), shift(behind_high + via_ahead, axis, -1)),
    )


def finish(meta, parts, head_rank, up, wide):
    cuts = len(parts)
    rows, width = parts[0][0][0].shape
    per = 2
    steps = rows // (per * BLOCK)
    rank = head_rank.shape[1] // cuts
    terms = [t for cut in parts for side in cut for t in side]
    each = len(parts[0][0])

    def body(meta_ref, *refs):
        h_ref, up_ref, out = refs[len(terms) :]
        i = pl.program_id(0)

        def put(cut):
            for k in range(per):
                at = slice(k * BLOCK, (k + 1) * BLOCK)
                block = i * per + k
                extra = jnp.dot(
                    h_ref[at, cut * rank : (cut + 1) * rank],
                    up_ref[meta_ref[0, block]],
                    preferred_element_type=f32,
                )
                row = block * BLOCK + lax.broadcasted_iota(i32, (BLOCK, width), 0)
                valid = row < meta_ref[4, block]
                for side in range(2):
                    cols = slice(side * width, (side + 1) * width)
                    total = extra[:, cols]
                    begin = (cut * 2 + side) * each
                    for ref in refs[begin : begin + each]:
                        total = total + ref[at, :].astype(f32)
                    out[at, cols] = jnp.where(valid, total, 0.0)

        for cut in range(cuts):

            @pl.when(i // steps == cut)
            def _():
                put(cut)

    def term_spec(cut):
        return pl.BlockSpec(
            (per * BLOCK, width), lambda i, m: (jnp.clip(i - cut * steps, 0, steps - 1), 0)
        )

    return pl.pallas_call(
        body,
        out_shape=jax.ShapeDtypeStruct((cuts * rows, 2 * width), f32),
        grid_spec=pltpu.PrefetchScalarGridSpec(
            num_scalar_prefetch=1,
            grid=(cuts * steps,),
            in_specs=[term_spec(cut) for cut in range(cuts) for _ in range(2 * each)]
            + [
                pl.BlockSpec((per * BLOCK, cuts * rank), lambda i, m: (lax.rem(i, steps), 0)),
                pl.BlockSpec((up.shape[0], rank, wide), lambda i, m: (0, 0, 1)),
            ],
            out_specs=pl.BlockSpec((per * BLOCK, 2 * width), lambda i, m: (i, 0)),
        ),
        compiler_params=params(),
        cost_estimate=cost(4 * cuts * rows * rank * width, 28 * cuts * rows * width),
    )(meta, *terms, head_rank, up)


def on_device(x, wq, wkv, wo, down_qkv, up_q, up_kv, down_o, up_o, choice, counts, tails):
    z, c, y, xi = (lax.axis_index(n) for n in ADAPTER_AXES + TENSOR_AXES)
    group = z * CORES + c
    tokens, local = x.shape
    holders = down_qkv.shape[0]
    requests = choice.shape[1]
    wide = wq.shape[1]
    rank = up_q.shape[1]
    blocks = tokens // BLOCK

    owners = choice // holders
    pick = jnp.sum(jnp.where(owners == group, choice % holders, 0), axis=1).astype(i32)
    own_owner = lax.dynamic_index_in_dim(owners, group, 0, keepdims=False)
    req = jnp.arange(requests, dtype=i32)
    starts = jnp.sum(jnp.where(req[None, :] < req[:, None], counts[0][None, :], 0), axis=1)
    block = jnp.arange(blocks, dtype=i32)
    of_block = (starts[None, :] <= block[:, None]) & (
        block[:, None] < (starts + counts[0])[None, :]
    )

    def lookup(values):
        return jnp.sum(jnp.where(of_block, values[None, :], 0), axis=1).astype(i32)

    slot = lookup(own_owner)
    first = lookup(starts)
    limit = (first + lookup(counts[0]) - 1) * BLOCK + lookup(tails[0])
    is_key = jnp.broadcast_to(1 - xi % 2, (blocks,)).astype(i32)
    meta = jnp.stack([slot, block - first, first * BLOCK, is_key, limit]).astype(i32)

    cosine, sine = rotation_tables()

    stores = (jnp.swapaxes(down_qkv, 1, 2), up_q, up_kv, jnp.swapaxes(down_o, 1, 2), up_o)
    down_out, up_out, x_a, x_b = pick_adapters(pick, *stores, x)
    down = lax.all_to_all(down_out, ADAPTER_AXES, 0, 0, tiled=True)

    ys, xs = ring_order(y), ring_order(xi)
    first_a = ring_gather(x_a, "x")
    first_b = ring_gather(x_b, "y")
    low_a, high_a, low_b, high_b = join(
        [first_a[:2], first_a[2:], first_b[:2], first_b[2:]], [down]
    )
    far_a, next_a = second_gather(low_a, high_a, "y")
    far_b, next_b = second_gather(low_b, high_b, "x")

    def rows_a(k, cols):
        return [(ys[k] * SIDE + xs[j]) * 2 for j in cols]

    def rows_b(k, cols):
        return [(ys[j] * SIDE + xs[k]) * 2 + 1 for j in cols]

    def index_of(rows):
        return jnp.stack(rows).astype(i32)

    every = range(SIDE)
    low, high = (0, 1), (2, 3)
    total = project(
        (index_of(rows_a(0, every) + rows_b(0, every)), meta),
        None,
        [low_a, high_a, low_b, high_b],
        [wq, wkv],
        512,
    )

    pieces = scatter_rows(rank_partial(meta, x, down, 3 * rank, [low_a]))
    copies = share_sum(pieces, [*far_a, *far_b])
    shrunk = lax.all_to_all(copies, TENSOR_AXES, 0, 0, tiled=True).reshape(tokens, 3 * rank)
    up = lax.all_to_all(up_out, ADAPTER_AXES, 0, 0, tiled=True)

    unit = wo.shape[1] // (SIDE * SIDE * 2)
    order = ring_order(y)
    sent = pick_columns(jnp.stack(order).astype(i32) * (2 * SIDE) + group, wo, unit, first_a[1:3] + first_b[1:3])
    got = [sent[0], shift(sent[2], "y", 1), shift(sent[1], "y", -1), shift(sent[3], "y", 2)]
    wo_all = lax.all_gather(jnp.concatenate(got, axis=0), ADAPTER_AXES, axis=0)

    a_low, a_high = shift(far_a[0], "y", 1), shift(far_a[1], "y", -1)
    b_low, b_high = shift(far_b[0], "x", 1), shift(far_b[1], "x", -1)
    total = project(
        (
            index_of(
                rows_a(1, low) + rows_a(2, high) + rows_b(1, low) + rows_b(2, high)
                + rows_a(1, high) + rows_a(2, low) + rows_b(1, high) + rows_b(2, low)
            ),
            meta,
        ),
        total,
        [*far_a, *far_b, *next_a, *next_b],
        [wq, wkv],
        512,
    )
    final = (index_of(rows_a(3, every) + rows_b(3, every)), meta)
    far = [a_low, a_high, b_low, b_high]
    tail = key_value_tail(shrunk, up, cosine, sine, wide, wkv.shape[1], 512)
    (mine,) = project(final, total[1:], far, [wkv], 512, tail)
    other = lax.ppermute(mine, "x", [(i, i ^ 1) for i in range(SIDE)])
    (q,) = project(final, total[:1], far, [wq], 512)

    cuts = 2
    pieces, ranks = [], []
    for cut in range(cuts):
        attended, head = attention(
            meta, q, shrunk, up, down, mine, other, cosine, sine, cut * blocks // cuts, blocks // cuts
        )
        ranks.append(head)
        pieces.append(ring_gather(attended, "y"))
    rank_mine = jnp.sum(scatter_rows(jnp.concatenate(ranks, axis=1)), axis=0).astype(bf16)
    head_rank = lax.all_gather(rank_mine, TENSOR_AXES, axis=0, tiled=True)
    places = [jnp.int32(k) for k in range(SIDE)]
    parts = [
        output_ring(pieces[0], wo_all, "x", places, rank_mine),
        output_ring(pieces[1], wo_all, "x", places, head_rank),
    ]
    return finish(meta, parts, head_rank, up, wide)


def solution(mesh):
    fine = Mesh(mesh.devices.reshape(SIDE, CORES, SIDE, SIDE), ADAPTER_AXES + TENSOR_AXES)
    placed = (
        P(ADAPTER_AXES, TENSOR_AXES),
        P(None, TENSOR_AXES),
        P(None, TENSOR_AXES),
        P(TENSOR_AXES, None),
        P(ADAPTER_AXES, TENSOR_AXES, None),
        P(ADAPTER_AXES, None, TENSOR_AXES),
        P(ADAPTER_AXES, None, TENSOR_AXES),
        P(ADAPTER_AXES, TENSOR_AXES, None),
        P(ADAPTER_AXES, None, TENSOR_AXES),
        P(),
        P(ADAPTER_AXES, None),
        P(ADAPTER_AXES, None),
    )
    return jax.shard_map(
        on_device,
        mesh=fine,
        in_specs=placed,
        out_specs=P(ADAPTER_AXES, TENSOR_AXES),
        check_vma=False,
    )
```

```python
import math

import jax
import jax.numpy as jnp
import numpy as np
from jax import lax
from jax.experimental import pallas as pl
from jax.experimental.pallas import tpu as pltpu
from jax.sharding import Mesh, PartitionSpec as P

HEAD = 128
BLOCK = 128
SIDE = 4
CORES = 2
ADAPTER_AXES = ("z", "c")
TENSOR_AXES = ("y", "x")
ROPE_BASE = 500000.0
VMEM = 56 * 1024 * 1024
bf16 = jnp.bfloat16
f32 = jnp.float32
i32 = jnp.int32


def params():
    return pltpu.CompilerParams(vmem_limit_bytes=VMEM)


def passive(arrays):
    return [pl.BlockSpec(memory_space=pl.ANY)] * len(arrays)


def cost(flops, moved, exps=0):
    return pl.CostEstimate(flops=flops, bytes_accessed=moved, transcendentals=exps)


def shift(block, axis, step):
    return lax.ppermute(block, axis, [(i, (i + step) % SIDE) for i in range(SIDE)])


def ring_gather(block, axis):
    half = block.shape[1] // 2
    behind = shift(block, axis, 1)
    ahead = shift(block, axis, -1)
    far_low = shift(behind[:, :half], axis, 1)
    far_high = shift(ahead[:, half:], axis, -1)
    return block, behind, ahead, far_low, far_high


def second_gather(low, high, axis):
    onward = shift(low, axis, 1), shift(high, axis, -1)
    return onward, (shift(high, axis, 1), shift(low, axis, -1))


def ring_order(index):
    return [index, (index + SIDE - 1) % SIDE, (index + 1) % SIDE, (index + 2) % SIDE]


def pick_local(pick, down_qkv, up_q, up_kv, down_o, up_o, x, wo, unit):
    tokens, local = x.shape
    groups = pick.shape[0] - SIDE
    rank3, depth = down_qkv.shape[1:]
    rank, wide = up_q.shape[1:]
    narrow = up_kv.shape[2]
    rows = wo.shape[0] // groups

    def body(pick_ref, dq, uq, ukv, do, uo, x_ref, *refs):
        w_refs, (down, up, left, right), w_outs = refs[:SIDE], refs[SIDE : SIDE + 4], refs[SIDE + 4 :]
        left[...] = x_ref[:, : local // 2]
        right[...] = x_ref[:, local // 2 :]
        down[0, :rank3, :] = dq[0]
        down[0, rank3:, :] = do[0]
        up[0, :, :wide] = uq[0]
        up[0, :, wide : 2 * wide] = uo[0]
        up[0, :, 2 * wide :] = ukv[0]
        for w_ref, w_out in zip(w_refs, w_outs):
            w_out[...] = w_ref[...]

    def chosen(a):
        return pl.BlockSpec((1,) + a.shape[1:], lambda i, p: (p[i], 0, 0))

    def columns(k):
        return pl.BlockSpec((rows, unit), lambda i, p: (i, p[groups + k]))

    down_shape = (groups, rank3 + rank, depth)
    up_shape = (groups, rank, 2 * wide + narrow)
    half = (tokens, local // 2)
    share = (wo.shape[0], unit)
    return pl.pallas_call(
        body,
        out_shape=tuple(
            jax.ShapeDtypeStruct(s, bf16)
            for s in (down_shape, up_shape, half, half, share, share, share, share)
        ),
        grid_spec=pltpu.PrefetchScalarGridSpec(
            num_scalar_prefetch=1,
            grid=(groups,),
            in_specs=[chosen(a) for a in (down_qkv, up_q, up_kv, down_o, up_o)]
            + [pl.BlockSpec((tokens // groups, local), lambda i, p: (i, 0))]
            + [columns(k) for k in range(SIDE)],
            out_specs=[
                pl.BlockSpec((1,) + s[1:], lambda i, p: (i, 0, 0)) for s in (down_shape, up_shape)
            ]
            + [pl.BlockSpec((tokens // groups, local // 2), lambda i, p: (i, 0))] * 2
            + [pl.BlockSpec((rows, unit), lambda i, p: (i, 0))] * SIDE,
        ),
        compiler_params=params(),
        cost_estimate=cost(0, 2 * 2 * (math.prod(down_shape) + math.prod(up_shape))),
    )(pick, down_qkv, up_q, up_kv, down_o, up_o, x, wo, wo, wo, wo)


def stack_rows(blocks, after):
    rows, width = blocks[0].shape
    count = len(blocks)

    def body(*refs):
        out = refs[-1]
        for k in range(count):
            out[k * rows : (k + 1) * rows, :] = refs[k][...]

    spec = pl.BlockSpec((rows, width), lambda i: (0, 0))
    return pl.pallas_call(
        body,
        out_shape=jax.ShapeDtypeStruct((count * rows, width), bf16),
        grid=(1,),
        in_specs=[spec] * count + passive(after),
        out_specs=pl.BlockSpec((count * rows, width), lambda i: (0, 0)),
        compiler_params=params(),
        cost_estimate=cost(0, 4 * count * rows * width),
    )(*blocks, *after)


def rank_partial(meta, x, down, rank3, after):
    tokens, depth = x.shape
    per = 2
    rows = per * BLOCK

    def body(meta_ref, x_ref, *rest):
        d_refs, out = rest[:per], rest[-1]
        for k in range(per):
            at = slice(k * BLOCK, (k + 1) * BLOCK)
            out[at, :] = lax.dot_general(
                x_ref[at, :], d_refs[k][0], (((1,), (1,)), ((), ())), preferred_element_type=f32
            )

    def chosen(k):
        return pl.BlockSpec((1, rank3, depth), lambda i, m: (m[0, i * per + k], 0, 0))

    return pl.pallas_call(
        body,
        out_shape=jax.ShapeDtypeStruct((tokens, rank3), f32),
        grid_spec=pltpu.PrefetchScalarGridSpec(
            num_scalar_prefetch=1,
            grid=(tokens // rows,),
            in_specs=[pl.BlockSpec((rows, depth), lambda i, m: (i, 0))]
            + [chosen(k) for k in range(per)]
            + passive(after),
            out_specs=pl.BlockSpec((rows, rank3), lambda i, m: (i, 0)),
        ),
        compiler_params=params(),
        cost_estimate=cost(2 * tokens * depth * rank3, 2 * tokens * depth + 8 * tokens * rank3),
    )(meta, x, *[down] * per, *after)


def join(groups, after):
    tokens = groups[0][0].shape[0]
    rows = 256
    flat = [b for group in groups for b in group]
    widths = [sum(b.shape[1] for b in group) for group in groups]

    def body(*refs):
        ins, outs = refs[: len(flat)], refs[len(flat) + len(after) :]
        at = 0
        for out, group in zip(outs, groups):
            col = 0
            for b in group:
                out[:, col : col + b.shape[1]] = ins[at][...]
                col += b.shape[1]
                at += 1

    return pl.pallas_call(
        body,
        out_shape=tuple(jax.ShapeDtypeStruct((tokens, w), bf16) for w in widths),
        grid=(tokens // rows,),
        in_specs=[pl.BlockSpec((rows, b.shape[1]), lambda i: (i, 0)) for b in flat]
        + passive(after),
        out_specs=[pl.BlockSpec((rows, w), lambda i: (i, 0)) for w in widths],
        compiler_params=params(),
        cost_estimate=cost(0, 4 * tokens * sum(widths)),
    )(*flat, *after)


def share_sum(pieces, after):
    ways, rows, rank = pieces.shape

    def body(p_ref, *refs):
        total = p_ref[0]
        for k in range(1, ways):
            total = total + p_ref[k]
        for k in range(ways):
            refs[-1][k] = total.astype(bf16)

    whole = pl.BlockSpec(pieces.shape, lambda i: (0, 0, 0))
    return pl.pallas_call(
        body,
        out_shape=jax.ShapeDtypeStruct(pieces.shape, bf16),
        grid=(1,),
        in_specs=[whole] + passive(after),
        out_specs=whole,
        compiler_params=params(),
        cost_estimate=cost(ways * rows * rank, 6 * ways * rows * rank),
    )(pieces, *after)


def scatter_rows(partial):
    rows, rank = partial.shape
    ways = SIDE * SIDE
    return lax.all_to_all(
        partial.reshape(ways, rows // ways, rank), TENSOR_AXES, 0, 0, tiled=True
    )


def project(index, total, blocks, weights, tile, last=None, rows=256):
    tokens = blocks[0].shape[0]
    counts = [b.shape[1] // rows for b in blocks]
    pieces = sum(counts)
    kinds = len(weights)
    first = total is None
    tail, tail_operands, tail_specs, dtype = last or (None, [], [], f32)

    def body(index_ref, meta_ref, *refs):
        x_refs = refs[: len(blocks)]
        w_refs = refs[len(blocks) : len(blocks) + kinds * pieces]
        rest = refs[len(blocks) + kinds * pieces :]
        outs = rest[len(rest) - kinds :]
        for kind in range(kinds):
            mine = w_refs[kind * pieces : (kind + 1) * pieces]
            acc = None if first else rest[kind][...]
            at = 0
            for x_ref, n in zip(x_refs, counts):
                w = jnp.concatenate([r[...] for r in mine[at : at + n]], axis=0)
                add = jnp.dot(x_ref[...], w, preferred_element_type=f32)
                acc = add if acc is None else acc + add
                at += n
            if tail is not None:
                acc = tail(meta_ref, acc, rest[kinds : len(rest) - kinds])
            outs[kind][...] = acc

    def weight(k, width):
        return pl.BlockSpec((rows, width), lambda i, p, m: (p[k], 0))

    widths = [w.shape[1] for w in weights]
    row_specs = [pl.BlockSpec((tile, w), lambda i, p, m: (i, 0)) for w in widths]
    in_specs = [pl.BlockSpec((tile, b.shape[1]), lambda i, p, m: (i, 0)) for b in blocks]
    operands = list(blocks)
    for w in weights:
        in_specs += [weight(k, w.shape[1]) for k in range(pieces)]
        operands += [w] * pieces
    aliases = {}
    if not first:
        if tail is None:
            aliases = {2 + len(operands) + k: k for k in range(kinds)}
        in_specs += row_specs
        operands += list(total)
    index, meta = index
    depth = pieces * rows
    return pl.pallas_call(
        body,
        out_shape=tuple(jax.ShapeDtypeStruct((tokens, w), dtype) for w in widths),
        grid_spec=pltpu.PrefetchScalarGridSpec(
            num_scalar_prefetch=2,
            grid=(tokens // tile,),
            in_specs=in_specs + tail_specs,
            out_specs=row_specs,
        ),
        input_output_aliases=aliases,
        compiler_params=params(),
        cost_estimate=cost(
            2 * tokens * depth * sum(widths),
            2 * depth * (tokens + sum(widths)) + 8 * tokens * sum(widths),
        ),
    )(index, meta, *operands, *tail_operands)


def key_value_tail(shrunk, up, cosine, sine, wide, narrow, tile):
    rank = shrunk.shape[1] // 3
    per = tile // BLOCK

    def tail(meta_ref, acc, refs):
        s_ref, up_ref, c_ref, n_ref = refs
        i = pl.program_id(0)
        is_key = meta_ref[3, 0] == 1
        done = []
        for k in range(per):
            at = slice(k * BLOCK, (k + 1) * BLOCK)
            s = s_ref[at, :].astype(f32)
            rank_in = jnp.where(is_key, s[:, rank : 2 * rank], s[:, 2 * rank :]).astype(bf16)
            u = acc[at, :] + jnp.dot(
                rank_in, up_ref[meta_ref[0, i * per + k]], preferred_element_type=f32
            )
            place = meta_ref[1, i * per + k]
            turned = u * c_ref[place] + pltpu.roll(u, HEAD // 2, 1) * n_ref[place]
            done.append(jnp.where(is_key, turned, u).astype(bf16))
        return jnp.concatenate(done, axis=0)

    specs = [
        pl.BlockSpec((tile, 3 * rank), lambda i, p, m: (i, 0)),
        pl.BlockSpec((up.shape[0], rank, narrow), lambda i, p, m: (0, 0, 2 * wide // narrow)),
        pl.BlockSpec(cosine.shape, lambda i, p, m: (0, 0, 0)),
        pl.BlockSpec(sine.shape, lambda i, p, m: (0, 0, 0)),
    ]
    return tail, [shrunk, up, cosine, sine], specs, bf16


def rotation_tables():
    freq = np.exp(-(2.0 * np.arange(HEAD // 2, dtype=np.float32) / HEAD) * math.log(ROPE_BASE))
    angle = np.arange(3 * BLOCK, dtype=np.float32)[:, None] * freq.astype(np.float32)[None, :]
    cosine = np.concatenate([np.cos(angle)] * 2, axis=1)
    sine = np.concatenate([-np.sin(angle), np.sin(angle)], axis=1)
    shape = (3, BLOCK, HEAD)
    return (
        jnp.asarray(cosine.reshape(shape), f32),
        jnp.asarray(sine.reshape(shape), f32),
    )


def attention(meta, q, shrunk, up, down, mine, other, cosine, sine, begin, count):
    tokens, wide = q.shape
    rank = shrunk.shape[1] // 3
    heads = wide // HEAD
    window = min(3 * BLOCK, tokens)
    scale = 1.0 / math.sqrt(HEAD)

    def body(meta_ref, q_ref, s_ref, up_ref, d_ref, m_ref, o_ref, c_ref, n_ref, att, head):
        i = begin + pl.program_id(0)
        is_key = meta_ref[3, 0] == 1
        first = meta_ref[2, i]
        limit = meta_ref[4, i]
        u = q_ref[...] + jnp.dot(
            s_ref[...][:, :rank], up_ref[0], preferred_element_type=f32
        )
        start = pl.multiple_of(jnp.maximum(i - 2, 0) * BLOCK, BLOCK)
        own = m_ref[pl.ds(start, window), :]
        far = o_ref[pl.ds(start, window), :]
        keys = jnp.where(is_key, own, far)
        values = jnp.where(is_key, far, own)
        row = i * BLOCK + lax.broadcasted_iota(i32, (BLOCK, window), 0)
        col = start + lax.broadcasted_iota(i32, (BLOCK, window), 1)
        allowed = (col >= first) & (col <= row) & (col < limit)
        cosines = c_ref[0]
        sines = n_ref[0]
        turned = []
        for h in range(heads):
            part = u[:, h * HEAD : (h + 1) * HEAD]
            turned.append(
                (part * cosines + pltpu.roll(part, HEAD // 2, 1) * sines).astype(bf16)
            )
        scores = lax.dot_general(
            jnp.concatenate(turned, axis=0),
            keys,
            (((1,), (1,)), ((), ())),
            preferred_element_type=f32,
        )
        for h in range(heads):
            at = slice(h * HEAD, (h + 1) * HEAD)
            weights = jnp.where(allowed, jnp.exp(scores[at, :] * scale), 0.0)
            weights = weights * (1.0 / jnp.sum(weights, axis=1, keepdims=True))
            mixed = jnp.dot(weights.astype(bf16), values, preferred_element_type=f32)
            att[:, at] = mixed.astype(bf16)
        head[...] = lax.dot_general(
            att[...], d_ref[0], (((1,), (1,)), ((), ())), preferred_element_type=f32
        )

    table = pl.BlockSpec((1, BLOCK, HEAD), lambda i, m: (m[1, i + begin], 0, 0))
    whole = pl.BlockSpec((tokens, HEAD), lambda i, m: (0, 0))
    return pl.pallas_call(
        body,
        out_shape=(
            jax.ShapeDtypeStruct((count * BLOCK, wide), bf16),
            jax.ShapeDtypeStruct((count * BLOCK, rank), f32),
        ),
        grid_spec=pltpu.PrefetchScalarGridSpec(
            num_scalar_prefetch=1,
            grid=(count,),
            in_specs=[
                pl.BlockSpec((BLOCK, wide), lambda i, m: (i + begin, 0)),
                pl.BlockSpec((BLOCK, 3 * rank), lambda i, m: (i + begin, 0)),
                pl.BlockSpec((1, rank, wide), lambda i, m: (m[0, i + begin], 0, 0)),
                pl.BlockSpec((1, rank, down.shape[2]), lambda i, m: (m[0, i + begin], 3, 0)),
                whole,
                whole,
                table,
                table,
            ],
            out_specs=[
                pl.BlockSpec((BLOCK, wide), lambda i, m: (i, 0)),
                pl.BlockSpec((BLOCK, rank), lambda i, m: (i, 0)),
            ],
        ),
        compiler_params=params(),
        cost_estimate=cost(
            4 * count * BLOCK * window * wide, 8 * count * BLOCK * wide, heads * count * BLOCK * window
        ),
    )(meta, q, shrunk, up, down, mine, other, cosine, sine)


def output_partial(index, pieces, weights, dtypes, after):
    tokens = pieces[0].shape[0]
    depth, width = weights.shape[1:]
    unit = depth // SIDE
    count = len(dtypes)
    places = [(0, 0), (1, 0), (2, 0), (3, 0), (3, unit // 2)]

    def body(index_ref, *refs):
        x_refs, w_ref, outs = refs[: len(pieces)], refs[len(pieces)], refs[-count:]
        total = None
        for x_ref, (place, offset) in zip(x_refs, places):
            start = pl.multiple_of(index_ref[place] * unit + offset, 128)
            rows = w_ref[0, pl.ds(start, x_ref.shape[1]), :]
            add = jnp.dot(x_ref[...], rows, preferred_element_type=f32)
            total = add if total is None else total + add
        for k, out in enumerate(outs):

            @pl.when(pl.program_id(0) == k)
            def _():
                out[...] = total.astype(out.dtype)

    return pl.pallas_call(
        body,
        out_shape=tuple(jax.ShapeDtypeStruct((tokens, width), d) for d in dtypes),
        grid_spec=pltpu.PrefetchScalarGridSpec(
            num_scalar_prefetch=1,
            grid=(count,),
            in_specs=[pl.BlockSpec(p.shape, lambda j, d: (0, 0)) for p in pieces]
            + [pl.BlockSpec((1, depth, width), lambda j, d: (d[SIDE + j], 0, 0))]
            + passive(after),
            out_specs=[pl.BlockSpec((tokens, width), lambda j, d: (0, 0))] * count,
        ),
        compiler_params=params(),
        cost_estimate=cost(
            2 * tokens * depth * count * width, 2 * depth * (tokens + count * width)
        ),
    )(index, *pieces, weights, *after)


def output_ring(pieces, weights, axis, places, ahead_of):
    me, behind, ahead, far = ring_order(lax.axis_index(axis))

    def partial(shards, dtypes, after=()):
        index = jnp.stack(places + shards).astype(i32)
        return output_partial(index, pieces, weights, dtypes, after)

    far_low, far_high = partial([2 * far, 2 * far + 1], [bf16] * 2)
    via_behind = shift(far_low, axis, 1)
    via_ahead = shift(far_high, axis, -1)
    ahead_high, behind_low, ahead_low, behind_high, low, high = partial(
        [2 * ahead + 1, 2 * behind, 2 * ahead, 2 * behind + 1, 2 * me, 2 * me + 1],
        [bf16] * 4 + [f32] * 2,
        [ahead_of],
    )
    return (
        (low, shift(behind_low, axis, -1), shift(ahead_low + via_behind, axis, 1)),
        (high, shift(ahead_high, axis, 1), shift(behind_high + via_ahead, axis, -1)),
    )


def finish(meta, parts, head_rank, up, wide):
    cuts = len(parts)
    rows, width = parts[0][0][0].shape
    per = 2
    steps = rows // (per * BLOCK)
    rank = head_rank.shape[1] // cuts
    terms = [t for cut in parts for side in cut for t in side]
    each = len(parts[0][0])

    def body(meta_ref, *refs):
        h_ref, up_ref, out = refs[len(terms) :]
        i = pl.program_id(0)

        def put(cut):
            for k in range(per):
                at = slice(k * BLOCK, (k + 1) * BLOCK)
                block = i * per + k
                extra = jnp.dot(
                    h_ref[at, cut * rank : (cut + 1) * rank],
                    up_ref[meta_ref[0, block]],
                    preferred_element_type=f32,
                )
                row = block * BLOCK + lax.broadcasted_iota(i32, (BLOCK, width), 0)
                valid = row < meta_ref[4, block]
                for side in range(2):
                    cols = slice(side * width, (side + 1) * width)
                    total = extra[:, cols]
                    begin = (cut * 2 + side) * each
                    for ref in refs[begin : begin + each]:
                        total = total + ref[at, :].astype(f32)
                    out[at, cols] = jnp.where(valid, total, 0.0)

        for cut in range(cuts):

            @pl.when(i // steps == cut)
            def _():
                put(cut)

    def term_spec(cut):
        return pl.BlockSpec(
            (per * BLOCK, width), lambda i, m: (jnp.clip(i - cut * steps, 0, steps - 1), 0)
        )

    return pl.pallas_call(
        body,
        out_shape=jax.ShapeDtypeStruct((cuts * rows, 2 * width), f32),
        grid_spec=pltpu.PrefetchScalarGridSpec(
            num_scalar_prefetch=1,
            grid=(cuts * steps,),
            in_specs=[term_spec(cut) for cut in range(cuts) for _ in range(2 * each)]
            + [
                pl.BlockSpec((per * BLOCK, cuts * rank), lambda i, m: (lax.rem(i, steps), 0)),
                pl.BlockSpec((up.shape[0], rank, wide), lambda i, m: (0, 0, 1)),
            ],
            out_specs=pl.BlockSpec((per * BLOCK, 2 * width), lambda i, m: (i, 0)),
        ),
        compiler_params=params(),
        cost_estimate=cost(4 * cuts * rows * rank * width, 28 * cuts * rows * width),
    )(meta, *terms, head_rank, up)


def on_device(x, wq, wkv, wo, down_qkv, up_q, up_kv, down_o, up_o, choice, counts, tails):
    z, c, y, xi = (lax.axis_index(n) for n in ADAPTER_AXES + TENSOR_AXES)
    group = z * CORES + c
    tokens, local = x.shape
    holders = down_qkv.shape[0]
    requests = choice.shape[1]
    wide = wq.shape[1]
    rank = up_q.shape[1]
    blocks = tokens // BLOCK

    owners = choice // holders
    pick = jnp.sum(jnp.where(owners == group, choice % holders, 0), axis=1).astype(i32)
    own_owner = lax.dynamic_index_in_dim(owners, group, 0, keepdims=False)
    req = jnp.arange(requests, dtype=i32)
    starts = jnp.sum(jnp.where(req[None, :] < req[:, None], counts[0][None, :], 0), axis=1)
    block = jnp.arange(blocks, dtype=i32)
    of_block = (starts[None, :] <= block[:, None]) & (
        block[:, None] < (starts + counts[0])[None, :]
    )

    def lookup(values):
        return jnp.sum(jnp.where(of_block, values[None, :], 0), axis=1).astype(i32)

    slot = lookup(own_owner)
    first = lookup(starts)
    limit = (first + lookup(counts[0]) - 1) * BLOCK + lookup(tails[0])
    is_key = jnp.broadcast_to(1 - xi % 2, (blocks,)).astype(i32)
    meta = jnp.stack([slot, block - first, first * BLOCK, is_key, limit]).astype(i32)

    cosine, sine = rotation_tables()

    stores = (jnp.swapaxes(down_qkv, 1, 2), up_q, up_kv, jnp.swapaxes(down_o, 1, 2), up_o)
    ys, xs = ring_order(y), ring_order(xi)
    unit = wo.shape[1] // (SIDE * SIDE * 2)
    wo_cols = jnp.stack(ys) * (2 * SIDE) + group
    down_out, up_out, x_a, x_b, *sent = pick_local(
        jnp.concatenate([pick, wo_cols.astype(i32)]), *stores, x, wo, unit
    )
    down = lax.all_to_all(down_out, ADAPTER_AXES, 0, 0, tiled=True)

    first_a = ring_gather(x_a, "x")
    first_b = ring_gather(x_b, "y")

    got = [sent[0], shift(sent[2], "y", 1), shift(sent[1], "y", -1), shift(sent[3], "y", 2)]
    wo_mine = stack_rows(got, first_a[1:3] + first_b[1:3])
    wo_all = lax.all_gather(wo_mine, ADAPTER_AXES, axis=0)

    low_a, high_a, low_b, high_b = join(
        [first_a[:2], first_a[2:], first_b[:2], first_b[2:]], [wo_mine]
    )
    far_a, next_a = second_gather(low_a, high_a, "y")
    far_b, next_b = second_gather(low_b, high_b, "x")

    def rows_a(k, cols):
        return [(ys[k] * SIDE + xs[j]) * 2 for j in cols]

    def rows_b(k, cols):
        return [(ys[j] * SIDE + xs[k]) * 2 + 1 for j in cols]

    def index_of(rows):
        return jnp.stack(rows).astype(i32)

    every = range(SIDE)
    low, high = (0, 1), (2, 3)
    total = project(
        (index_of(rows_a(0, every) + rows_b(0, every)), meta),
        None,
        [low_a, high_a, low_b, high_b],
        [wq, wkv],
        512,
    )

    pieces = scatter_rows(rank_partial(meta, x, down, 3 * rank, [*far_a, *far_b]))
    copies = share_sum(pieces, [])
    shrunk = lax.all_to_all(copies, TENSOR_AXES, 0, 0, tiled=True).reshape(tokens, 3 * rank)
    up = lax.all_to_all(up_out, ADAPTER_AXES, 0, 0, tiled=True)

    a_low, a_high = shift(far_a[0], "y", 1), shift(far_a[1], "y", -1)
    b_low, b_high = shift(far_b[0], "x", 1), shift(far_b[1], "x", -1)
    total = project(
        (
            index_of(
                rows_a(1, low) + rows_a(2, high) + rows_b(1, low) + rows_b(2, high)
                + rows_a(1, high) + rows_a(2, low) + rows_b(1, high) + rows_b(2, low)
            ),
            meta,
        ),
        total,
        [*far_a, *far_b, *next_a, *next_b],
        [wq, wkv],
        512,
    )
    final = (index_of(rows_a(3, every) + rows_b(3, every)), meta)
    far = [a_low, a_high, b_low, b_high]
    tail = key_value_tail(shrunk, up, cosine, sine, wide, wkv.shape[1], 512)
    (mine,) = project(final, total[1:], far, [wkv], 512, tail)
    other = lax.ppermute(mine, "x", [(i, i ^ 1) for i in range(SIDE)])
    (q,) = project(final, total[:1], far, [wq], 512)

    cuts = 2
    pieces, ranks = [], []
    for cut in range(cuts):
        attended, head = attention(
            meta, q, shrunk, up, down, mine, other, cosine, sine, cut * blocks // cuts, blocks // cuts
        )
        ranks.append(head)
        pieces.append(ring_gather(attended, "y"))
    copies = share_sum(scatter_rows(jnp.concatenate(ranks, axis=1)), [])
    head_rank = lax.all_to_all(copies, TENSOR_AXES, 0, 0, tiled=True).reshape(tokens // 2, 2 * rank)
    places = [jnp.int32(k) for k in range(SIDE)]
    parts = [
        output_ring(pieces[0], wo_all, "x", places, copies),
        output_ring(pieces[1], wo_all, "x", places, head_rank),
    ]
    return finish(meta, parts, head_rank, up, wide)


def solution(mesh):
    fine = Mesh(mesh.devices.reshape(SIDE, CORES, SIDE, SIDE), ADAPTER_AXES + TENSOR_AXES)
    placed = (
        P(ADAPTER_AXES, TENSOR_AXES),
        P(None, TENSOR_AXES),
        P(None, TENSOR_AXES),
        P(TENSOR_AXES, None),
        P(ADAPTER_AXES, TENSOR_AXES, None),
        P(ADAPTER_AXES, None, TENSOR_AXES),
        P(ADAPTER_AXES, None, TENSOR_AXES),
        P(ADAPTER_AXES, TENSOR_AXES, None),
        P(ADAPTER_AXES, None, TENSOR_AXES),
        P(),
        P(ADAPTER_AXES, None),
        P(ADAPTER_AXES, None),
    )
    return jax.shard_map(
        on_device,
        mesh=fine,
        in_specs=placed,
        out_specs=P(ADAPTER_AXES, TENSOR_AXES),
        check_vma=False,
    )
```

```python
import math

import jax
import jax.numpy as jnp
import numpy as np
from jax import lax
from jax.experimental import pallas as pl
from jax.experimental.pallas import tpu as pltpu
from jax.sharding import Mesh, PartitionSpec as P

HEAD = 128
BLOCK = 128
SIDE = 4
CORES = 2
ADAPTER_AXES = ("z", "c")
TENSOR_AXES = ("y", "x")
ROPE_BASE = 500000.0
VMEM = 56 * 1024 * 1024
bf16 = jnp.bfloat16
f32 = jnp.float32
i32 = jnp.int32


def params():
    return pltpu.CompilerParams(vmem_limit_bytes=VMEM)


def passive(arrays):
    return [pl.BlockSpec(memory_space=pl.ANY)] * len(arrays)


def cost(flops, moved, exps=0):
    return pl.CostEstimate(flops=flops, bytes_accessed=moved, transcendentals=exps)


def shift(block, axis, step):
    return lax.ppermute(block, axis, [(i, (i + step) % SIDE) for i in range(SIDE)])


def ring_gather(block, axis):
    half = block.shape[1] // 2
    behind = shift(block, axis, 1)
    ahead = shift(block, axis, -1)
    far_low = shift(behind[:, :half], axis, 1)
    far_high = shift(ahead[:, half:], axis, -1)
    return block, behind, ahead, far_low, far_high


def second_gather(low, high, axis):
    onward = shift(low, axis, 1), shift(high, axis, -1)
    return onward, (shift(high, axis, 1), shift(low, axis, -1))


def ring_order(index):
    return [index, (index + SIDE - 1) % SIDE, (index + 1) % SIDE, (index + 2) % SIDE]


def pick_local(pick, down_qkv, up_q, up_kv, down_o, up_o, x, wo, unit):
    tokens, local = x.shape
    groups = pick.shape[0] - SIDE
    rank3, depth = down_qkv.shape[1:]
    rank, wide = up_q.shape[1:]
    narrow = up_kv.shape[2]
    rows = wo.shape[0] // groups

    def body(pick_ref, dq, uq, ukv, do, uo, x_ref, *refs):
        w_refs, (down, up, left, right), w_outs = refs[:SIDE], refs[SIDE : SIDE + 4], refs[SIDE + 4 :]
        left[...] = x_ref[:, : local // 2]
        right[...] = x_ref[:, local // 2 :]
        down[0, :rank3, :] = dq[0]
        down[0, rank3:, :] = do[0]
        up[0, :, :wide] = uq[0]
        up[0, :, wide : 2 * wide] = uo[0]
        up[0, :, 2 * wide :] = ukv[0]
        for w_ref, w_out in zip(w_refs, w_outs):
            w_out[...] = w_ref[...]

    def chosen(a):
        return pl.BlockSpec((1,) + a.shape[1:], lambda i, p: (p[i], 0, 0))

    def columns(k):
        return pl.BlockSpec((rows, unit), lambda i, p: (i, p[groups + k]))

    down_shape = (groups, rank3 + rank, depth)
    up_shape = (groups, rank, 2 * wide + narrow)
    half = (tokens, local // 2)
    share = (wo.shape[0], unit)
    return pl.pallas_call(
        body,
        out_shape=tuple(
            jax.ShapeDtypeStruct(s, bf16)
            for s in (down_shape, up_shape, half, half, share, share, share, share)
        ),
        grid_spec=pltpu.PrefetchScalarGridSpec(
            num_scalar_prefetch=1,
            grid=(groups,),
            in_specs=[chosen(a) for a in (down_qkv, up_q, up_kv, down_o, up_o)]
            + [pl.BlockSpec((tokens // groups, local), lambda i, p: (i, 0))]
            + [columns(k) for k in range(SIDE)],
            out_specs=[
                pl.BlockSpec((1,) + s[1:], lambda i, p: (i, 0, 0)) for s in (down_shape, up_shape)
            ]
            + [pl.BlockSpec((tokens // groups, local // 2), lambda i, p: (i, 0))] * 2
            + [pl.BlockSpec((rows, unit), lambda i, p: (i, 0))] * SIDE,
        ),
        compiler_params=params(),
        cost_estimate=cost(0, 2 * 2 * (math.prod(down_shape) + math.prod(up_shape))),
    )(pick, down_qkv, up_q, up_kv, down_o, up_o, x, wo, wo, wo, wo)


def stack_rows(blocks, after):
    rows, width = blocks[0].shape
    count = len(blocks)

    def body(*refs):
        out = refs[-1]
        for k in range(count):
            out[k * rows : (k + 1) * rows, :] = refs[k][...]

    spec = pl.BlockSpec((rows, width), lambda i: (0, 0))
    return pl.pallas_call(
        body,
        out_shape=jax.ShapeDtypeStruct((count * rows, width), bf16),
        grid=(1,),
        in_specs=[spec] * count + passive(after),
        out_specs=pl.BlockSpec((count * rows, width), lambda i: (0, 0)),
        compiler_params=params(),
        cost_estimate=cost(0, 4 * count * rows * width),
    )(*blocks, *after)


def rank_partial(meta, x, down, rank3, after):
    tokens, depth = x.shape
    per = 2
    rows = per * BLOCK

    def body(meta_ref, x_ref, *rest):
        d_refs, out = rest[:per], rest[-1]
        for k in range(per):
            at = slice(k * BLOCK, (k + 1) * BLOCK)
            out[at, :] = lax.dot_general(
                x_ref[at, :], d_refs[k][0], (((1,), (1,)), ((), ())), preferred_element_type=f32
            )

    def chosen(k):
        return pl.BlockSpec((1, rank3, depth), lambda i, m: (m[0, i * per + k], 0, 0))

    return pl.pallas_call(
        body,
        out_shape=jax.ShapeDtypeStruct((tokens, rank3), f32),
        grid_spec=pltpu.PrefetchScalarGridSpec(
            num_scalar_prefetch=1,
            grid=(tokens // rows,),
            in_specs=[pl.BlockSpec((rows, depth), lambda i, m: (i, 0))]
            + [chosen(k) for k in range(per)]
            + passive(after),
            out_specs=pl.BlockSpec((rows, rank3), lambda i, m: (i, 0)),
        ),
        compiler_params=params(),
        cost_estimate=cost(2 * tokens * depth * rank3, 2 * tokens * depth + 8 * tokens * rank3),
    )(meta, x, *[down] * per, *after)


def join(groups, after):
    tokens = groups[0][0].shape[0]
    rows = 256
    flat = [b for group in groups for b in group]
    widths = [sum(b.shape[1] for b in group) for group in groups]

    def body(*refs):
        ins, outs = refs[: len(flat)], refs[len(flat) + len(after) :]
        at = 0
        for out, group in zip(outs, groups):
            col = 0
            for b in group:
                out[:, col : col + b.shape[1]] = ins[at][...]
                col += b.shape[1]
                at += 1

    return pl.pallas_call(
        body,
        out_shape=tuple(jax.ShapeDtypeStruct((tokens, w), bf16) for w in widths),
        grid=(tokens // rows,),
        in_specs=[pl.BlockSpec((rows, b.shape[1]), lambda i: (i, 0)) for b in flat]
        + passive(after),
        out_specs=[pl.BlockSpec((rows, w), lambda i: (i, 0)) for w in widths],
        compiler_params=params(),
        cost_estimate=cost(0, 4 * tokens * sum(widths)),
    )(*flat, *after)


def side_by_side(blocks, after):
    rows, width = blocks[0].shape

    def body(*refs):
        for k in range(len(blocks)):
            refs[-1][:, k * width : (k + 1) * width] = refs[k][...]

    spec = pl.BlockSpec((rows, width), lambda i: (0, 0))
    shape = (rows, width * len(blocks))
    return pl.pallas_call(
        body,
        out_shape=jax.ShapeDtypeStruct(shape, f32),
        grid=(1,),
        in_specs=[spec] * len(blocks) + passive(after),
        out_specs=pl.BlockSpec(shape, lambda i: (0, 0)),
        compiler_params=params(),
        cost_estimate=cost(0, 8 * math.prod(shape)),
    )(*blocks, *after)


def share_sum(pieces, after):
    ways, rows, rank = pieces.shape

    def body(p_ref, *refs):
        total = p_ref[0]
        for k in range(1, ways):
            total = total + p_ref[k]
        for k in range(ways):
            refs[-1][k] = total.astype(bf16)

    whole = pl.BlockSpec(pieces.shape, lambda i: (0, 0, 0))
    return pl.pallas_call(
        body,
        out_shape=jax.ShapeDtypeStruct(pieces.shape, bf16),
        grid=(1,),
        in_specs=[whole] + passive(after),
        out_specs=whole,
        compiler_params=params(),
        cost_estimate=cost(ways * rows * rank, 6 * ways * rows * rank),
    )(pieces, *after)


def scatter_rows(partial):
    rows, rank = partial.shape
    ways = SIDE * SIDE
    return lax.all_to_all(
        partial.reshape(ways, rows // ways, rank), TENSOR_AXES, 0, 0, tiled=True
    )


def project(index, total, blocks, weights, tile, last=None, rows=256):
    tokens = blocks[0].shape[0]
    counts = [b.shape[1] // rows for b in blocks]
    pieces = sum(counts)
    kinds = len(weights)
    first = total is None
    tail, tail_operands, tail_specs, dtype = last or (None, [], [], f32)

    def body(index_ref, meta_ref, *refs):
        x_refs = refs[: len(blocks)]
        w_refs = refs[len(blocks) : len(blocks) + kinds * pieces]
        rest = refs[len(blocks) + kinds * pieces :]
        outs = rest[len(rest) - kinds :]
        for kind in range(kinds):
            mine = w_refs[kind * pieces : (kind + 1) * pieces]
            acc = None if first else rest[kind][...]
            at = 0
            for x_ref, n in zip(x_refs, counts):
                w = jnp.concatenate([r[...] for r in mine[at : at + n]], axis=0)
                add = jnp.dot(x_ref[...], w, preferred_element_type=f32)
                acc = add if acc is None else acc + add
                at += n
            if tail is not None:
                acc = tail(meta_ref, acc, rest[kinds : len(rest) - kinds])
            outs[kind][...] = acc

    def weight(k, width):
        return pl.BlockSpec((rows, width), lambda i, p, m: (p[k], 0))

    widths = [w.shape[1] for w in weights]
    row_specs = [pl.BlockSpec((tile, w), lambda i, p, m: (i, 0)) for w in widths]
    in_specs = [pl.BlockSpec((tile, b.shape[1]), lambda i, p, m: (i, 0)) for b in blocks]
    operands = list(blocks)
    for w in weights:
        in_specs += [weight(k, w.shape[1]) for k in range(pieces)]
        operands += [w] * pieces
    aliases = {}
    if not first:
        if tail is None:
            aliases = {2 + len(operands) + k: k for k in range(kinds)}
        in_specs += row_specs
        operands += list(total)
    index, meta = index
    depth = pieces * rows
    return pl.pallas_call(
        body,
        out_shape=tuple(jax.ShapeDtypeStruct((tokens, w), dtype) for w in widths),
        grid_spec=pltpu.PrefetchScalarGridSpec(
            num_scalar_prefetch=2,
            grid=(tokens // tile,),
            in_specs=in_specs + tail_specs,
            out_specs=row_specs,
        ),
        input_output_aliases=aliases,
        compiler_params=params(),
        cost_estimate=cost(
            2 * tokens * depth * sum(widths),
            2 * depth * (tokens + sum(widths)) + 8 * tokens * sum(widths),
        ),
    )(index, meta, *operands, *tail_operands)


def key_value_tail(shrunk, up, cosine, sine, wide, narrow, tile):
    rank = shrunk.shape[1] // 3
    per = tile // BLOCK

    def tail(meta_ref, acc, refs):
        s_ref, up_ref, c_ref, n_ref = refs
        i = pl.program_id(0)
        is_key = meta_ref[3, 0] == 1
        done = []
        for k in range(per):
            at = slice(k * BLOCK, (k + 1) * BLOCK)
            s = s_ref[at, :].astype(f32)
            rank_in = jnp.where(is_key, s[:, rank : 2 * rank], s[:, 2 * rank :]).astype(bf16)
            u = acc[at, :] + jnp.dot(
                rank_in, up_ref[meta_ref[0, i * per + k]], preferred_element_type=f32
            )
            place = meta_ref[1, i * per + k]
            turned = u * c_ref[place] + pltpu.roll(u, HEAD // 2, 1) * n_ref[place]
            done.append(jnp.where(is_key, turned, u).astype(bf16))
        return jnp.concatenate(done, axis=0)

    specs = [
        pl.BlockSpec((tile, 3 * rank), lambda i, p, m: (i, 0)),
        pl.BlockSpec((up.shape[0], rank, narrow), lambda i, p, m: (0, 0, 2 * wide // narrow)),
        pl.BlockSpec(cosine.shape, lambda i, p, m: (0, 0, 0)),
        pl.BlockSpec(sine.shape, lambda i, p, m: (0, 0, 0)),
    ]
    return tail, [shrunk, up, cosine, sine], specs, bf16


def rotation_tables():
    freq = np.exp(-(2.0 * np.arange(HEAD // 2, dtype=np.float32) / HEAD) * math.log(ROPE_BASE))
    angle = np.arange(3 * BLOCK, dtype=np.float32)[:, None] * freq.astype(np.float32)[None, :]
    cosine = np.concatenate([np.cos(angle)] * 2, axis=1)
    sine = np.concatenate([-np.sin(angle), np.sin(angle)], axis=1)
    shape = (3, BLOCK, HEAD)
    return (
        jnp.asarray(cosine.reshape(shape), f32),
        jnp.asarray(sine.reshape(shape), f32),
    )


def attention(meta, q, shrunk, up, down, mine, other, cosine, sine, begin, count):
    tokens, wide = q.shape
    rank = shrunk.shape[1] // 3
    heads = wide // HEAD
    window = min(3 * BLOCK, tokens)
    scale = 1.0 / math.sqrt(HEAD)

    def body(meta_ref, q_ref, s_ref, up_ref, d_ref, m_ref, o_ref, c_ref, n_ref, att, head):
        i = begin + pl.program_id(0)
        is_key = meta_ref[3, 0] == 1
        first = meta_ref[2, i]
        limit = meta_ref[4, i]
        u = q_ref[...] + jnp.dot(
            s_ref[...][:, :rank], up_ref[0], preferred_element_type=f32
        )
        start = pl.multiple_of(jnp.maximum(i - 2, 0) * BLOCK, BLOCK)
        own = m_ref[pl.ds(start, window), :]
        far = o_ref[pl.ds(start, window), :]
        keys = jnp.where(is_key, own, far)
        values = jnp.where(is_key, far, own)
        row = i * BLOCK + lax.broadcasted_iota(i32, (BLOCK, window), 0)
        col = start + lax.broadcasted_iota(i32, (BLOCK, window), 1)
        allowed = (col >= first) & (col <= row) & (col < limit)
        cosines = c_ref[0]
        sines = n_ref[0]
        turned = []
        for h in range(heads):
            part = u[:, h * HEAD : (h + 1) * HEAD]
            turned.append(
                (part * cosines + pltpu.roll(part, HEAD // 2, 1) * sines).astype(bf16)
            )
        scores = lax.dot_general(
            jnp.concatenate(turned, axis=0),
            keys,
            (((1,), (1,)), ((), ())),
            preferred_element_type=f32,
        )
        for h in range(heads):
            at = slice(h * HEAD, (h + 1) * HEAD)
            weights = jnp.where(allowed, jnp.exp(scores[at, :] * scale), 0.0)
            weights = weights * (1.0 / jnp.sum(weights, axis=1, keepdims=True))
            mixed = jnp.dot(weights.astype(bf16), values, preferred_element_type=f32)
            att[:, at] = mixed.astype(bf16)
        head[...] = lax.dot_general(
            att[...], d_ref[0], (((1,), (1,)), ((), ())), preferred_element_type=f32
        )

    table = pl.BlockSpec((1, BLOCK, HEAD), lambda i, m: (m[1, i + begin], 0, 0))
    whole = pl.BlockSpec((tokens, HEAD), lambda i, m: (0, 0))
    return pl.pallas_call(
        body,
        out_shape=(
            jax.ShapeDtypeStruct((count * BLOCK, wide), bf16),
            jax.ShapeDtypeStruct((count * BLOCK, rank), f32),
        ),
        grid_spec=pltpu.PrefetchScalarGridSpec(
            num_scalar_prefetch=1,
            grid=(count,),
            in_specs=[
                pl.BlockSpec((BLOCK, wide), lambda i, m: (i + begin, 0)),
                pl.BlockSpec((BLOCK, 3 * rank), lambda i, m: (i + begin, 0)),
                pl.BlockSpec((1, rank, wide), lambda i, m: (m[0, i + begin], 0, 0)),
                pl.BlockSpec((1, rank, down.shape[2]), lambda i, m: (m[0, i + begin], 3, 0)),
                whole,
                whole,
                table,
                table,
            ],
            out_specs=[
                pl.BlockSpec((BLOCK, wide), lambda i, m: (i, 0)),
                pl.BlockSpec((BLOCK, rank), lambda i, m: (i, 0)),
            ],
        ),
        compiler_params=params(),
        cost_estimate=cost(
            4 * count * BLOCK * window * wide, 8 * count * BLOCK * wide, heads * count * BLOCK * window
        ),
    )(meta, q, shrunk, up, down, mine, other, cosine, sine)


def output_partial(index, pieces, weights, dtypes, after):
    tokens = pieces[0].shape[0]
    depth, width = weights.shape[1:]
    unit = depth // SIDE
    count = len(dtypes)
    places = [(0, 0), (1, 0), (2, 0), (3, 0), (3, unit // 2)]

    def body(index_ref, *refs):
        x_refs, w_ref, outs = refs[: len(pieces)], refs[len(pieces)], refs[-count:]
        total = None
        for x_ref, (place, offset) in zip(x_refs, places):
            start = pl.multiple_of(index_ref[place] * unit + offset, 128)
            rows = w_ref[0, pl.ds(start, x_ref.shape[1]), :]
            add = jnp.dot(x_ref[...], rows, preferred_element_type=f32)
            total = add if total is None else total + add
        for k, out in enumerate(outs):

            @pl.when(pl.program_id(0) == k)
            def _():
                out[...] = total.astype(out.dtype)

    return pl.pallas_call(
        body,
        out_shape=tuple(jax.ShapeDtypeStruct((tokens, width), d) for d in dtypes),
        grid_spec=pltpu.PrefetchScalarGridSpec(
            num_scalar_prefetch=1,
            grid=(count,),
            in_specs=[pl.BlockSpec(p.shape, lambda j, d: (0, 0)) for p in pieces]
            + [pl.BlockSpec((1, depth, width), lambda j, d: (d[SIDE + j], 0, 0))]
            + passive(after),
            out_specs=[pl.BlockSpec((tokens, width), lambda j, d: (0, 0))] * count,
        ),
        compiler_params=params(),
        cost_estimate=cost(
            2 * tokens * depth * count * width, 2 * depth * (tokens + count * width)
        ),
    )(index, *pieces, weights, *after)


def add_pairs(pairs, after):
    rows, width = pairs[0][0].shape
    count = len(pairs)

    def body(*refs):
        for k in range(count):
            total = refs[2 * k][...].astype(f32) + refs[2 * k + 1][...].astype(f32)
            refs[len(refs) - count + k][...] = total.astype(bf16)

    spec = pl.BlockSpec((rows, width), lambda i: (0, 0))
    return pl.pallas_call(
        body,
        out_shape=tuple(jax.ShapeDtypeStruct((rows, width), bf16) for _ in pairs),
        grid=(1,),
        in_specs=[spec] * (2 * count) + passive(after),
        out_specs=[spec] * count,
        compiler_params=params(),
        cost_estimate=cost(count * rows * width, 6 * count * rows * width),
    )(*[a for pair in pairs for a in pair], *after)


def output_ring(pieces, weights, axis, places):
    me, behind, ahead, far = ring_order(lax.axis_index(axis))

    def partial(shards, dtypes, after=()):
        index = jnp.stack(places + shards).astype(i32)
        return output_partial(index, pieces, weights, dtypes, after)

    far_low, far_high = partial([2 * far, 2 * far + 1], [bf16] * 2)

    def rest(after, later):
        via_behind = shift(far_low, axis, 1)
        via_ahead = shift(far_high, axis, -1)
        ahead_high, behind_low, ahead_low, behind_high, low, high = partial(
            [2 * ahead + 1, 2 * behind, 2 * ahead, 2 * behind + 1, 2 * me, 2 * me + 1],
            [bf16] * 4 + [f32] * 2,
            after,
        )
        to_ahead, to_behind = add_pairs(
            [(ahead_low, via_behind), (behind_high, via_ahead)], later
        )
        return (
            (low, shift(behind_low, axis, -1), shift(to_ahead, axis, 1)),
            (high, shift(ahead_high, axis, 1), shift(to_behind, axis, -1)),
        )

    return (far_low, far_high), rest


def finish(meta, parts, head_rank, up, wide):
    cuts = len(parts)
    rows, width = parts[0][0][0].shape
    per = 2
    steps = rows // (per * BLOCK)
    rank = head_rank.shape[1] // cuts
    terms = [t for cut in parts for side in cut for t in side]
    each = len(parts[0][0])

    def body(meta_ref, *refs):
        h_ref, up_ref, out = refs[len(terms) :]
        i = pl.program_id(0)

        def put(cut):
            for k in range(per):
                at = slice(k * BLOCK, (k + 1) * BLOCK)
                block = i * per + k
                extra = jnp.dot(
                    h_ref[at, cut * rank : (cut + 1) * rank],
                    up_ref[meta_ref[0, block]],
                    preferred_element_type=f32,
                )
                row = block * BLOCK + lax.broadcasted_iota(i32, (BLOCK, width), 0)
                valid = row < meta_ref[4, block]
                for side in range(2):
                    cols = slice(side * width, (side + 1) * width)
                    total = extra[:, cols]
                    begin = (cut * 2 + side) * each
                    for ref in refs[begin : begin + each]:
                        total = total + ref[at, :].astype(f32)
                    out[at, cols] = jnp.where(valid, total, 0.0)

        for cut in range(cuts):

            @pl.when(i // steps == cut)
            def _():
                put(cut)

    def term_spec(cut):
        return pl.BlockSpec(
            (per * BLOCK, width), lambda i, m: (jnp.clip(i - cut * steps, 0, steps - 1), 0)
        )

    return pl.pallas_call(
        body,
        out_shape=jax.ShapeDtypeStruct((cuts * rows, 2 * width), f32),
        grid_spec=pltpu.PrefetchScalarGridSpec(
            num_scalar_prefetch=1,
            grid=(cuts * steps,),
            in_specs=[term_spec(cut) for cut in range(cuts) for _ in range(2 * each)]
            + [
                pl.BlockSpec((per * BLOCK, cuts * rank), lambda i, m: (lax.rem(i, steps), 0)),
                pl.BlockSpec((up.shape[0], rank, wide), lambda i, m: (0, 0, 1)),
            ],
            out_specs=pl.BlockSpec((per * BLOCK, 2 * width), lambda i, m: (i, 0)),
        ),
        compiler_params=params(),
        cost_estimate=cost(4 * cuts * rows * rank * width, 28 * cuts * rows * width),
    )(meta, *terms, head_rank, up)


def on_device(x, wq, wkv, wo, down_qkv, up_q, up_kv, down_o, up_o, choice, counts, tails):
    z, c, y, xi = (lax.axis_index(n) for n in ADAPTER_AXES + TENSOR_AXES)
    group = z * CORES + c
    tokens, local = x.shape
    holders = down_qkv.shape[0]
    requests = choice.shape[1]
    wide = wq.shape[1]
    rank = up_q.shape[1]
    blocks = tokens // BLOCK

    owners = choice // holders
    pick = jnp.sum(jnp.where(owners == group, choice % holders, 0), axis=1).astype(i32)
    own_owner = lax.dynamic_index_in_dim(owners, group, 0, keepdims=False)
    req = jnp.arange(requests, dtype=i32)
    starts = jnp.sum(jnp.where(req[None, :] < req[:, None], counts[0][None, :], 0), axis=1)
    block = jnp.arange(blocks, dtype=i32)
    of_block = (starts[None, :] <= block[:, None]) & (
        block[:, None] < (starts + counts[0])[None, :]
    )

    def lookup(values):
        return jnp.sum(jnp.where(of_block, values[None, :], 0), axis=1).astype(i32)

    slot = lookup(own_owner)
    first = lookup(starts)
    limit = (first + lookup(counts[0]) - 1) * BLOCK + lookup(tails[0])
    is_key = jnp.broadcast_to(1 - xi % 2, (blocks,)).astype(i32)
    meta = jnp.stack([slot, block - first, first * BLOCK, is_key, limit]).astype(i32)

    cosine, sine = rotation_tables()

    stores = (jnp.swapaxes(down_qkv, 1, 2), up_q, up_kv, jnp.swapaxes(down_o, 1, 2), up_o)
    ys, xs = ring_order(y), ring_order(xi)
    unit = wo.shape[1] // (SIDE * SIDE * 2)
    wo_cols = jnp.stack(ys) * (2 * SIDE) + group
    down_out, up_out, x_a, x_b, *sent = pick_local(
        jnp.concatenate([pick, wo_cols.astype(i32)]), *stores, x, wo, unit
    )
    down = lax.all_to_all(down_out, ADAPTER_AXES, 0, 0, tiled=True)

    first_a = ring_gather(x_a, "x")
    first_b = ring_gather(x_b, "y")

    got = [sent[0], shift(sent[2], "y", 1), shift(sent[1], "y", -1), shift(sent[3], "y", 2)]
    low_a, high_a, low_b, high_b = join(
        [first_a[:2], first_a[2:], first_b[:2], first_b[2:]], got[1:]
    )
    wo_mine = stack_rows(got, [down, low_a])
    wo_all = lax.all_gather(wo_mine, ADAPTER_AXES, axis=0)
    far_a, next_a = second_gather(low_a, high_a, "y")
    far_b, next_b = second_gather(low_b, high_b, "x")

    def rows_a(k, cols):
        return [(ys[k] * SIDE + xs[j]) * 2 for j in cols]

    def rows_b(k, cols):
        return [(ys[j] * SIDE + xs[k]) * 2 + 1 for j in cols]

    def index_of(rows):
        return jnp.stack(rows).astype(i32)

    every = range(SIDE)
    low, high = (0, 1), (2, 3)
    total = project(
        (index_of(rows_a(0, every) + rows_b(0, every)), meta),
        None,
        [low_a, high_a, low_b, high_b],
        [wq, wkv],
        512,
    )

    pieces = scatter_rows(rank_partial(meta, x, down, 3 * rank, [low_a]))
    copies = share_sum(pieces, [total[1]])
    shrunk = lax.all_to_all(copies, TENSOR_AXES, 0, 0, tiled=True).reshape(tokens, 3 * rank)
    up = lax.all_to_all(up_out, ADAPTER_AXES, 0, 0, tiled=True)

    a_low, a_high = shift(far_a[0], "y", 1), shift(far_a[1], "y", -1)
    b_low, b_high = shift(far_b[0], "x", 1), shift(far_b[1], "x", -1)
    total = project(
        (
            index_of(rows_a(1, low) + rows_a(2, high) + rows_b(1, low) + rows_b(2, high)),
            meta,
        ),
        total,
        [*far_a, *far_b],
        [wq, wkv],
        512,
    )
    total = project(
        (
            index_of(rows_a(1, high) + rows_a(2, low) + rows_b(1, high) + rows_b(2, low)),
            meta,
        ),
        total,
        [*next_a, *next_b],
        [wq, wkv],
        512,
    )
    final = (index_of(rows_a(3, every) + rows_b(3, every)), meta)
    far = [a_low, a_high, b_low, b_high]
    tail = key_value_tail(shrunk, up, cosine, sine, wide, wkv.shape[1], 512)
    (mine,) = project(final, total[1:], far, [wkv], 512, tail)
    other = lax.ppermute(mine, "x", [(i, i ^ 1) for i in range(SIDE)])
    (q,) = project(final, total[:1], far, [wq], 512)

    cuts = 2
    pieces, ranks = [], []
    for cut in range(cuts):
        attended, head = attention(
            meta, q, shrunk, up, down, mine, other, cosine, sine, cut * blocks // cuts, blocks // cuts
        )
        ranks.append(head)
        pieces.append(ring_gather(attended, "y"))
    places = [jnp.int32(k) for k in range(SIDE)]
    rings = [output_ring(p, wo_all, "x", places) for p in pieces]
    (first_far, first_rest), (last_far, last_rest) = rings
    copies = share_sum(scatter_rows(side_by_side(ranks, [first_far[0]])), [])
    head_rank = lax.all_to_all(copies, TENSOR_AXES, 0, 0, tiled=True).reshape(tokens // 2, 2 * rank)
    parts = [first_rest([], []), last_rest([copies], [head_rank])]
    return finish(meta, parts, head_rank, up, wide)


def solution(mesh):
    fine = Mesh(mesh.devices.reshape(SIDE, CORES, SIDE, SIDE), ADAPTER_AXES + TENSOR_AXES)
    placed = (
        P(ADAPTER_AXES, TENSOR_AXES),
        P(None, TENSOR_AXES),
        P(None, TENSOR_AXES),
        P(TENSOR_AXES, None),
        P(ADAPTER_AXES, TENSOR_AXES, None),
        P(ADAPTER_AXES, None, TENSOR_AXES),
        P(ADAPTER_AXES, None, TENSOR_AXES),
        P(ADAPTER_AXES, TENSOR_AXES, None),
        P(ADAPTER_AXES, None, TENSOR_AXES),
        P(),
        P(ADAPTER_AXES, None),
        P(ADAPTER_AXES, None),
    )
    return jax.shard_map(
        on_device,
        mesh=fine,
        in_specs=placed,
        out_specs=P(ADAPTER_AXES, TENSOR_AXES),
        check_vma=False,
    )
```

```python
import math

import jax
import jax.numpy as jnp
import numpy as np
from jax import lax
from jax.experimental import pallas as pl
from jax.experimental.pallas import tpu as pltpu
from jax.sharding import Mesh, PartitionSpec as P

HEAD = 128
BLOCK = 128
SIDE = 4
CORES = 2
ADAPTER_AXES = ("z", "c")
TENSOR_AXES = ("y", "x")
ROPE_BASE = 500000.0
VMEM = 56 * 1024 * 1024
bf16 = jnp.bfloat16
f32 = jnp.float32
i32 = jnp.int32


def params():
    return pltpu.CompilerParams(vmem_limit_bytes=VMEM)


def passive(arrays):
    return [pl.BlockSpec(memory_space=pl.ANY)] * len(arrays)


def cost(flops, moved, exps=0):
    return pl.CostEstimate(flops=flops, bytes_accessed=moved, transcendentals=exps)


def shift(block, axis, step):
    return lax.ppermute(block, axis, [(i, (i + step) % SIDE) for i in range(SIDE)])


def ring_gather(block, axis, half):
    behind = shift(block, axis, 1)
    ahead = shift(block, axis, -1)
    far_low = shift(behind[:, :half], axis, 1)
    far_high = shift(ahead[:, half:], axis, -1)
    return block, behind, ahead, far_low, far_high


def second_gather(low, high, axis):
    onward = shift(low, axis, 1), shift(high, axis, -1)
    return onward, (shift(high, axis, 1), shift(low, axis, -1))


def ring_order(index):
    return [index, (index + SIDE - 1) % SIDE, (index + 1) % SIDE, (index + 2) % SIDE]


def pick_local(pick, down_qkv, up_q, up_kv, down_o, up_o, x, wo, unit):
    tokens, local = x.shape
    groups = pick.shape[0] - SIDE
    rank3, depth = down_qkv.shape[1:]
    rank, wide = up_q.shape[1:]
    narrow = up_kv.shape[2]
    rows = wo.shape[0] // groups

    def body(pick_ref, dq, uq, ukv, do, uo, x_ref, *refs):
        w_refs, (down, up, left, right), w_outs = refs[:SIDE], refs[SIDE : SIDE + 4], refs[SIDE + 4 :]
        left[...] = x_ref[:, : local // 2]
        right[...] = x_ref[:, local // 2 :]
        down[0, :rank3, :] = dq[0]
        down[0, rank3:, :] = do[0]
        up[0, :, :wide] = uq[0]
        up[0, :, wide : 2 * wide] = uo[0]
        up[0, :, 2 * wide :] = ukv[0]
        for w_ref, w_out in zip(w_refs, w_outs):
            w_out[...] = w_ref[...]

    def chosen(a):
        return pl.BlockSpec((1,) + a.shape[1:], lambda i, p: (p[i], 0, 0))

    def columns(k):
        return pl.BlockSpec((rows, unit), lambda i, p: (i, p[groups + k]))

    down_shape = (groups, rank3 + rank, depth)
    up_shape = (groups, rank, 2 * wide + narrow)
    half = (tokens, local // 2)
    share = (wo.shape[0], unit)
    return pl.pallas_call(
        body,
        out_shape=tuple(
            jax.ShapeDtypeStruct(s, bf16)
            for s in (down_shape, up_shape, half, half, share, share, share, share)
        ),
        grid_spec=pltpu.PrefetchScalarGridSpec(
            num_scalar_prefetch=1,
            grid=(groups,),
            in_specs=[chosen(a) for a in (down_qkv, up_q, up_kv, down_o, up_o)]
            + [pl.BlockSpec((tokens // groups, local), lambda i, p: (i, 0))]
            + [columns(k) for k in range(SIDE)],
            out_specs=[
                pl.BlockSpec((1,) + s[1:], lambda i, p: (i, 0, 0)) for s in (down_shape, up_shape)
            ]
            + [pl.BlockSpec((tokens // groups, local // 2), lambda i, p: (i, 0))] * 2
            + [pl.BlockSpec((rows, unit), lambda i, p: (i, 0))] * SIDE,
        ),
        compiler_params=params(),
        cost_estimate=cost(0, 2 * 2 * (math.prod(down_shape) + math.prod(up_shape))),
    )(pick, down_qkv, up_q, up_kv, down_o, up_o, x, wo, wo, wo, wo)


def stack_rows(blocks, after):
    rows, width = blocks[0].shape
    count = len(blocks)

    def body(*refs):
        out = refs[-1]
        for k in range(count):
            out[k * rows : (k + 1) * rows, :] = refs[k][...]

    spec = pl.BlockSpec((rows, width), lambda i: (0, 0))
    return pl.pallas_call(
        body,
        out_shape=jax.ShapeDtypeStruct((count * rows, width), bf16),
        grid=(1,),
        in_specs=[spec] * count + passive(after),
        out_specs=pl.BlockSpec((count * rows, width), lambda i: (0, 0)),
        compiler_params=params(),
        cost_estimate=cost(0, 4 * count * rows * width),
    )(*blocks, *after)


def rank_partial(meta, x, down, rank3, after):
    tokens, depth = x.shape
    per = 2
    rows = per * BLOCK

    def body(meta_ref, x_ref, *rest):
        d_refs, out = rest[:per], rest[-1]
        for k in range(per):
            at = slice(k * BLOCK, (k + 1) * BLOCK)
            out[at, :] = lax.dot_general(
                x_ref[at, :], d_refs[k][0], (((1,), (1,)), ((), ())), preferred_element_type=f32
            )

    def chosen(k):
        return pl.BlockSpec((1, rank3, depth), lambda i, m: (m[0, i * per + k], 0, 0))

    return pl.pallas_call(
        body,
        out_shape=jax.ShapeDtypeStruct((tokens, rank3), f32),
        grid_spec=pltpu.PrefetchScalarGridSpec(
            num_scalar_prefetch=1,
            grid=(tokens // rows,),
            in_specs=[pl.BlockSpec((rows, depth), lambda i, m: (i, 0))]
            + [chosen(k) for k in range(per)]
            + passive(after),
            out_specs=pl.BlockSpec((rows, rank3), lambda i, m: (i, 0)),
        ),
        compiler_params=params(),
        cost_estimate=cost(2 * tokens * depth * rank3, 2 * tokens * depth + 8 * tokens * rank3),
    )(meta, x, *[down] * per, *after)


def join(groups, after):
    tokens = groups[0][0].shape[0]
    rows = 256
    flat = [b for group in groups for b in group]
    widths = [sum(b.shape[1] for b in group) for group in groups]

    def body(*refs):
        ins, outs = refs[: len(flat)], refs[len(flat) + len(after) :]
        at = 0
        for out, group in zip(outs, groups):
            col = 0
            for b in group:
                out[:, col : col + b.shape[1]] = ins[at][...]
                col += b.shape[1]
                at += 1

    return pl.pallas_call(
        body,
        out_shape=tuple(jax.ShapeDtypeStruct((tokens, w), bf16) for w in widths),
        grid=(tokens // rows,),
        in_specs=[pl.BlockSpec((rows, b.shape[1]), lambda i: (i, 0)) for b in flat]
        + passive(after),
        out_specs=[pl.BlockSpec((rows, w), lambda i: (i, 0)) for w in widths],
        compiler_params=params(),
        cost_estimate=cost(0, 4 * tokens * sum(widths)),
    )(*flat, *after)


def share_sum(pieces, after):
    ways, rows, rank = pieces.shape

    def body(p_ref, *refs):
        total = p_ref[0]
        for k in range(1, ways):
            total = total + p_ref[k]
        for k in range(ways):
            refs[-1][k] = total.astype(bf16)

    whole = pl.BlockSpec(pieces.shape, lambda i: (0, 0, 0))
    return pl.pallas_call(
        body,
        out_shape=jax.ShapeDtypeStruct(pieces.shape, bf16),
        grid=(1,),
        in_specs=[whole] + passive(after),
        out_specs=whole,
        compiler_params=params(),
        cost_estimate=cost(ways * rows * rank, 6 * ways * rows * rank),
    )(pieces, *after)


def scatter_rows(partial):
    rows, rank = partial.shape
    ways = SIDE * SIDE
    return lax.all_to_all(
        partial.reshape(ways, rows // ways, rank), TENSOR_AXES, 0, 0, tiled=True
    )


def project(index, total, blocks, weights, tile, last=None, after=(), rows=256):
    tokens = blocks[0].shape[0]
    counts = [b.shape[1] // rows for b in blocks]
    pieces = sum(counts)
    kinds = len(weights)
    first = total is None
    tail, tail_operands, tail_specs, dtype = last or (None, [], [], f32)

    def body(index_ref, meta_ref, *refs):
        x_refs = refs[: len(blocks)]
        w_refs = refs[len(blocks) : len(blocks) + kinds * pieces]
        rest = refs[len(blocks) + kinds * pieces :]
        outs = rest[len(rest) - kinds :]
        for kind in range(kinds):
            mine = w_refs[kind * pieces : (kind + 1) * pieces]
            acc = None if first else rest[kind][...]
            at = 0
            for x_ref, n in zip(x_refs, counts):
                w = jnp.concatenate([r[...] for r in mine[at : at + n]], axis=0)
                add = jnp.dot(x_ref[...], w, preferred_element_type=f32)
                acc = add if acc is None else acc + add
                at += n
            if tail is not None:
                acc = tail(meta_ref, acc, rest[kinds : kinds + len(tail_operands)])
            outs[kind][...] = acc

    def weight(k, width):
        return pl.BlockSpec((rows, width), lambda i, p, m: (p[k], 0))

    widths = [w.shape[1] for w in weights]
    row_specs = [pl.BlockSpec((tile, w), lambda i, p, m: (i, 0)) for w in widths]
    in_specs = [pl.BlockSpec((tile, b.shape[1]), lambda i, p, m: (i, 0)) for b in blocks]
    operands = list(blocks)
    for w in weights:
        in_specs += [weight(k, w.shape[1]) for k in range(pieces)]
        operands += [w] * pieces
    aliases = {}
    if not first:
        if tail is None:
            aliases = {2 + len(operands) + k: k for k in range(kinds)}
        in_specs += row_specs
        operands += list(total)
    index, meta = index
    depth = pieces * rows
    return pl.pallas_call(
        body,
        out_shape=tuple(jax.ShapeDtypeStruct((tokens, w), dtype) for w in widths),
        grid_spec=pltpu.PrefetchScalarGridSpec(
            num_scalar_prefetch=2,
            grid=(tokens // tile,),
            in_specs=in_specs + tail_specs + passive(after),
            out_specs=row_specs,
        ),
        input_output_aliases=aliases,
        compiler_params=params(),
        cost_estimate=cost(
            2 * tokens * depth * sum(widths),
            2 * depth * (tokens + sum(widths)) + 8 * tokens * sum(widths),
        ),
    )(index, meta, *operands, *tail_operands, *after)


def key_value_tail(shrunk, up, cosine, sine, wide, narrow, tile):
    rank = shrunk.shape[1] // 3
    per = tile // BLOCK

    def tail(meta_ref, acc, refs):
        s_ref, up_ref, c_ref, n_ref = refs
        i = pl.program_id(0)
        is_key = meta_ref[3, 0] == 1
        done = []
        for k in range(per):
            at = slice(k * BLOCK, (k + 1) * BLOCK)
            s = s_ref[at, :].astype(f32)
            rank_in = jnp.where(is_key, s[:, rank : 2 * rank], s[:, 2 * rank :]).astype(bf16)
            u = acc[at, :] + jnp.dot(
                rank_in, up_ref[meta_ref[0, i * per + k]], preferred_element_type=f32
            )
            place = meta_ref[1, i * per + k]
            turned = u * c_ref[place] + pltpu.roll(u, HEAD // 2, 1) * n_ref[place]
            done.append(jnp.where(is_key, turned, u).astype(bf16))
        return jnp.concatenate(done, axis=0)

    specs = [
        pl.BlockSpec((tile, 3 * rank), lambda i, p, m: (i, 0)),
        pl.BlockSpec((up.shape[0], rank, narrow), lambda i, p, m: (0, 0, 2 * wide // narrow)),
        pl.BlockSpec(cosine.shape, lambda i, p, m: (0, 0, 0)),
        pl.BlockSpec(sine.shape, lambda i, p, m: (0, 0, 0)),
    ]
    return tail, [shrunk, up, cosine, sine], specs, bf16


def rotation_tables():
    freq = np.exp(-(2.0 * np.arange(HEAD // 2, dtype=np.float32) / HEAD) * math.log(ROPE_BASE))
    angle = np.arange(3 * BLOCK, dtype=np.float32)[:, None] * freq.astype(np.float32)[None, :]
    cosine = np.concatenate([np.cos(angle)] * 2, axis=1)
    sine = np.concatenate([-np.sin(angle), np.sin(angle)], axis=1)
    shape = (3, BLOCK, HEAD)
    return (
        jnp.asarray(cosine.reshape(shape), f32),
        jnp.asarray(sine.reshape(shape), f32),
    )


def attention(meta, q, shrunk, up, down, mine, other, cosine, sine, begin, count):
    tokens, wide = q.shape
    rank = shrunk.shape[1] // 3
    heads = wide // HEAD
    window = min(3 * BLOCK, tokens)
    scale = 1.0 / math.sqrt(HEAD)

    def body(meta_ref, q_ref, s_ref, up_ref, d_ref, m_ref, o_ref, c_ref, n_ref, att):
        i = begin + pl.program_id(0)
        is_key = meta_ref[3, 0] == 1
        first = meta_ref[2, i]
        limit = meta_ref[4, i]
        u = q_ref[...] + jnp.dot(
            s_ref[...][:, :rank], up_ref[0], preferred_element_type=f32
        )
        start = pl.multiple_of(jnp.maximum(i - 2, 0) * BLOCK, BLOCK)
        own = m_ref[pl.ds(start, window), :]
        far = o_ref[pl.ds(start, window), :]
        keys = jnp.where(is_key, own, far)
        values = jnp.where(is_key, far, own)
        row = i * BLOCK + lax.broadcasted_iota(i32, (BLOCK, window), 0)
        col = start + lax.broadcasted_iota(i32, (BLOCK, window), 1)
        allowed = (col >= first) & (col <= row) & (col < limit)
        cosines = c_ref[0]
        sines = n_ref[0]
        turned = []
        for h in range(heads):
            part = u[:, h * HEAD : (h + 1) * HEAD]
            turned.append(
                (part * cosines + pltpu.roll(part, HEAD // 2, 1) * sines).astype(bf16)
            )
        scores = lax.dot_general(
            jnp.concatenate(turned, axis=0),
            keys,
            (((1,), (1,)), ((), ())),
            preferred_element_type=f32,
        )
        for h in range(heads):
            at = slice(h * HEAD, (h + 1) * HEAD)
            weights = jnp.where(allowed, jnp.exp(scores[at, :] * scale), 0.0)
            weights = weights * (1.0 / jnp.sum(weights, axis=1, keepdims=True))
            mixed = jnp.dot(weights.astype(bf16), values, preferred_element_type=f32)
            att[:, at] = mixed.astype(bf16)
        head = lax.dot_general(
            att[:, :wide], d_ref[0], (((1,), (1,)), ((), ())), preferred_element_type=f32
        )
        att[:, wide : wide + rank] = head.astype(bf16)
        att[:, wide + rank :] = jnp.zeros((BLOCK, HEAD - rank), bf16)

    table = pl.BlockSpec((1, BLOCK, HEAD), lambda i, m: (m[1, i + begin], 0, 0))
    whole = pl.BlockSpec((tokens, HEAD), lambda i, m: (0, 0))
    return pl.pallas_call(
        body,
        out_shape=jax.ShapeDtypeStruct((count * BLOCK, wide + HEAD), bf16),
        grid_spec=pltpu.PrefetchScalarGridSpec(
            num_scalar_prefetch=1,
            grid=(count,),
            in_specs=[
                pl.BlockSpec((BLOCK, wide), lambda i, m: (i + begin, 0)),
                pl.BlockSpec((BLOCK, 3 * rank), lambda i, m: (i + begin, 0)),
                pl.BlockSpec((1, rank, wide), lambda i, m: (m[0, i + begin], 0, 0)),
                pl.BlockSpec((1, rank, down.shape[2]), lambda i, m: (m[0, i + begin], 3, 0)),
                whole,
                whole,
                table,
                table,
            ],
            out_specs=pl.BlockSpec((BLOCK, wide + HEAD), lambda i, m: (i, 0)),
        ),
        compiler_params=params(),
        cost_estimate=cost(
            4 * count * BLOCK * window * wide, 8 * count * BLOCK * wide, heads * count * BLOCK * window
        ),
    )(meta, q, shrunk, up, down, mine, other, cosine, sine)


def output_partial(shards, pieces, weights):
    tokens = pieces[0].shape[0]
    count, (depth, width) = len(shards), weights.shape[1:]
    unit = depth // SIDE
    far_cut = pieces[3].shape[1]
    whole = 2 * width + HEAD

    def body(index_ref, *refs):
        own, behind, ahead, far_low, far_high, w_ref = refs[:6]
        out_far_low, out_far_high, out_ahead, out_behind, out_mine, x_all = refs[6:]
        step = pl.program_id(0)

        @pl.when(step == 0)
        def _():
            for k, ref in enumerate((own, behind, ahead)):
                x_all[:, k * unit : (k + 1) * unit] = ref[:, :unit]
            x_all[:, 3 * unit : 3 * unit + far_cut] = far_low[...]
            x_all[:, 3 * unit + far_cut :] = far_high[:, : unit - far_cut]
            rank = (
                own[:, unit:].astype(f32)
                + behind[:, unit:].astype(f32)
                + ahead[:, unit:].astype(f32)
                + far_high[:, unit - far_cut :].astype(f32)
            )
            for out in (out_far_low, out_ahead, out_behind, out_mine):
                out[:, width : width + HEAD] = rank.astype(out.dtype)

        total = jnp.dot(x_all[...], w_ref[0], preferred_element_type=f32)
        low, high = slice(0, width), slice(width + HEAD, whole)
        targets = [(out_far_low, low), (out_far_high, low)]
        targets += [(out, at) for out in (out_ahead, out_behind, out_mine) for at in (low, high)]
        for k, (out, at) in enumerate(targets):

            @pl.when(step == k)
            def _():
                out[:, at] = total.astype(out.dtype)

    shapes = [(width + HEAD, bf16), (width, bf16), (whole, bf16), (whole, bf16), (whole, f32)]
    return pl.pallas_call(
        body,
        out_shape=tuple(jax.ShapeDtypeStruct((tokens, w), d) for w, d in shapes),
        grid_spec=pltpu.PrefetchScalarGridSpec(
            num_scalar_prefetch=1,
            grid=(count,),
            in_specs=[pl.BlockSpec(p.shape, lambda j, d: (0, 0)) for p in pieces]
            + [pl.BlockSpec((1, depth, width), lambda j, d: (d[j], 0, 0))],
            out_specs=[pl.BlockSpec((tokens, w), lambda j, d: (0, 0)) for w, _ in shapes],
            scratch_shapes=[pltpu.VMEM((tokens, depth), bf16)],
        ),
        compiler_params=params(),
        cost_estimate=cost(
            2 * tokens * depth * count * width, 2 * depth * (tokens + count * width)
        ),
    )(jnp.stack(shards).astype(i32), *pieces, weights)


def add_far(ahead, via_behind, behind, via_ahead):
    rows, whole = ahead.shape
    low = via_behind.shape[1]

    def body(a_ref, va_ref, b_ref, vb_ref, out_a, out_b):
        out_a[:, :low] = (a_ref[:, :low].astype(f32) + va_ref[...].astype(f32)).astype(bf16)
        out_a[:, low:] = a_ref[:, low:]
        out_b[:, :low] = b_ref[:, :low]
        out_b[:, low:] = (b_ref[:, low:].astype(f32) + vb_ref[...].astype(f32)).astype(bf16)

    arrays = (ahead, via_behind, behind, via_ahead)
    return pl.pallas_call(
        body,
        out_shape=(jax.ShapeDtypeStruct((rows, whole), bf16),) * 2,
        grid=(1,),
        in_specs=[pl.BlockSpec(a.shape, lambda i: (0, 0)) for a in arrays],
        out_specs=[pl.BlockSpec((rows, whole), lambda i: (0, 0))] * 2,
        compiler_params=params(),
        cost_estimate=cost(2 * rows * whole, 10 * rows * whole),
    )(*arrays)


def output_ring(pieces, weights, axis):
    me, behind, ahead, far = ring_order(lax.axis_index(axis))
    shards = [2 * place + side for place in (far, ahead, behind, me) for side in range(2)]
    far_low, far_high, to_ahead, to_behind, mine = output_partial(shards, pieces, weights)
    to_ahead, to_behind = add_far(
        to_ahead, shift(far_low, axis, 1), to_behind, shift(far_high, axis, -1)
    )
    return mine, shift(to_behind, axis, -1), shift(to_ahead, axis, 1)


def finish(meta, parts, up, rank, wide):
    cuts = len(parts)
    rows, whole = parts[0][0].shape
    width = (whole - HEAD) // 2
    per = 2
    steps = rows // (per * BLOCK)
    terms = [t for cut in parts for t in cut]
    each = len(parts[0])

    def body(meta_ref, *refs):
        up_ref, out = refs[len(terms) :]
        i = pl.program_id(0)

        def put(mine):
            for k in range(per):
                at = slice(k * BLOCK, (k + 1) * BLOCK)
                block = i * per + k
                total = mine[0][at, :].astype(f32)
                for ref in mine[1:]:
                    total = total + ref[at, :].astype(f32)
                extra = jnp.dot(
                    total[:, width : width + rank].astype(bf16),
                    up_ref[meta_ref[0, block]],
                    preferred_element_type=f32,
                )
                row = block * BLOCK + lax.broadcasted_iota(i32, (BLOCK, width), 0)
                valid = row < meta_ref[4, block]
                for side, begin in enumerate((0, width + HEAD)):
                    cols = slice(side * width, (side + 1) * width)
                    out[at, cols] = jnp.where(
                        valid, total[:, begin : begin + width] + extra[:, cols], 0.0
                    )

        for cut in range(cuts):

            @pl.when(i // steps == cut)
            def _():
                put(refs[cut * each : (cut + 1) * each])

    def term_spec(cut):
        return pl.BlockSpec(
            (per * BLOCK, whole), lambda i, m: (jnp.clip(i - cut * steps, 0, steps - 1), 0)
        )

    return pl.pallas_call(
        body,
        out_shape=jax.ShapeDtypeStruct((cuts * rows, 2 * width), f32),
        grid_spec=pltpu.PrefetchScalarGridSpec(
            num_scalar_prefetch=1,
            grid=(cuts * steps,),
            in_specs=[term_spec(cut) for cut in range(cuts) for _ in range(each)]
            + [pl.BlockSpec((up.shape[0], rank, wide), lambda i, m: (0, 0, 1))],
            out_specs=pl.BlockSpec((per * BLOCK, 2 * width), lambda i, m: (i, 0)),
        ),
        compiler_params=params(),
        cost_estimate=cost(4 * cuts * rows * rank * width, 28 * cuts * rows * width),
    )(meta, *terms, up)


def on_device(x, wq, wkv, wo, down_qkv, up_q, up_kv, down_o, up_o, choice, counts, tails):
    z, c, y, xi = (lax.axis_index(n) for n in ADAPTER_AXES + TENSOR_AXES)
    group = z * CORES + c
    tokens, local = x.shape
    holders = down_qkv.shape[0]
    requests = choice.shape[1]
    wide = wq.shape[1]
    rank = up_q.shape[1]
    blocks = tokens // BLOCK

    owners = choice // holders
    pick = jnp.sum(jnp.where(owners == group, choice % holders, 0), axis=1).astype(i32)
    own_owner = lax.dynamic_index_in_dim(owners, group, 0, keepdims=False)
    req = jnp.arange(requests, dtype=i32)
    starts = jnp.sum(jnp.where(req[None, :] < req[:, None], counts[0][None, :], 0), axis=1)
    block = jnp.arange(blocks, dtype=i32)
    of_block = (starts[None, :] <= block[:, None]) & (
        block[:, None] < (starts + counts[0])[None, :]
    )

    def lookup(values):
        return jnp.sum(jnp.where(of_block, values[None, :], 0), axis=1).astype(i32)

    slot = lookup(own_owner)
    first = lookup(starts)
    limit = (first + lookup(counts[0]) - 1) * BLOCK + lookup(tails[0])
    is_key = jnp.broadcast_to(1 - xi % 2, (blocks,)).astype(i32)
    meta = jnp.stack([slot, block - first, first * BLOCK, is_key, limit]).astype(i32)

    cosine, sine = rotation_tables()

    stores = (jnp.swapaxes(down_qkv, 1, 2), up_q, up_kv, jnp.swapaxes(down_o, 1, 2), up_o)
    ys, xs = ring_order(y), ring_order(xi)
    unit = wo.shape[1] // (SIDE * SIDE * 2)
    wo_cols = jnp.stack(ys) * (2 * SIDE) + group
    down_out, up_out, x_a, x_b, *sent = pick_local(
        jnp.concatenate([pick, wo_cols.astype(i32)]), *stores, x, wo, unit
    )
    down = lax.all_to_all(down_out, ADAPTER_AXES, 0, 0, tiled=True)

    first_a = ring_gather(x_a, "x", x_a.shape[1] // 2)
    first_b = ring_gather(x_b, "y", x_b.shape[1] // 2)

    got = [sent[0], shift(sent[2], "y", 1), shift(sent[1], "y", -1), shift(sent[3], "y", 2)]
    low_a, high_a, low_b, high_b = join(
        [first_a[:2], first_a[2:], first_b[:2], first_b[2:]], got[1:]
    )
    wo_mine = stack_rows(got, [down, low_a])
    wo_all = lax.all_gather(wo_mine, ADAPTER_AXES, axis=0)
    far_a, next_a = second_gather(low_a, high_a, "y")
    far_b, next_b = second_gather(low_b, high_b, "x")

    def rows_a(k, cols):
        return [(ys[k] * SIDE + xs[j]) * 2 for j in cols]

    def rows_b(k, cols):
        return [(ys[j] * SIDE + xs[k]) * 2 + 1 for j in cols]

    def index_of(rows):
        return jnp.stack(rows).astype(i32)

    every = range(SIDE)
    low, high = (0, 1), (2, 3)
    pieces = scatter_rows(rank_partial(meta, x, down, 3 * rank, [low_a]))
    up = lax.all_to_all(up_out, ADAPTER_AXES, 0, 0, tiled=True)

    copies = share_sum(pieces, [])

    a_low, a_high = shift(far_a[0], "y", 1), shift(far_a[1], "y", -1)
    b_low, b_high = shift(far_b[0], "x", 1), shift(far_b[1], "x", -1)
    total = project(
        (
            index_of(
                rows_a(0, every) + rows_b(0, every)
                + rows_a(1, low) + rows_a(2, high) + rows_b(1, low) + rows_b(2, high)
            ),
            meta,
        ),
        None,
        [low_a, high_a, low_b, high_b, *far_a, *far_b],
        [wq, wkv],
        512,
        after=[copies],
    )
    total = project(
        (
            index_of(rows_a(1, high) + rows_a(2, low) + rows_b(1, high) + rows_b(2, low)),
            meta,
        ),
        total,
        [*next_a, *next_b],
        [wq, wkv],
        512,
    )
    shrunk = lax.all_to_all(copies, TENSOR_AXES, 0, 0, tiled=True).reshape(tokens, 3 * rank)
    final = (index_of(rows_a(3, every) + rows_b(3, every)), meta)
    far = [a_low, a_high, b_low, b_high]
    tail = key_value_tail(shrunk, up, cosine, sine, wide, wkv.shape[1], 512)
    (mine,) = project(final, total[1:], far, [wkv], 512, tail)
    other = lax.ppermute(mine, "x", [(i, i ^ 1) for i in range(SIDE)])
    (q,) = project(final, total[:1], far, [wq], 512)

    cuts = 2
    each = blocks // cuts
    parts = []
    for cut in range(cuts):
        attended = attention(
            meta, q, shrunk, up, down, mine, other, cosine, sine, cut * each, each
        )
        parts.append(output_ring(ring_gather(attended, "y", wide // 2), wo_all, "x"))
    return finish(meta, parts, up, rank, wide)


def solution(mesh):
    fine = Mesh(mesh.devices.reshape(SIDE, CORES, SIDE, SIDE), ADAPTER_AXES + TENSOR_AXES)
    placed = (
        P(ADAPTER_AXES, TENSOR_AXES),
        P(None, TENSOR_AXES),
        P(None, TENSOR_AXES),
        P(TENSOR_AXES, None),
        P(ADAPTER_AXES, TENSOR_AXES, None),
        P(ADAPTER_AXES, None, TENSOR_AXES),
        P(ADAPTER_AXES, None, TENSOR_AXES),
        P(ADAPTER_AXES, TENSOR_AXES, None),
        P(ADAPTER_AXES, None, TENSOR_AXES),
        P(),
        P(ADAPTER_AXES, None),
        P(ADAPTER_AXES, None),
    )
    return jax.shard_map(
        on_device,
        mesh=fine,
        in_specs=placed,
        out_specs=P(ADAPTER_AXES, TENSOR_AXES),
        check_vma=False,
    )
```

```python
import math

import jax
import jax.numpy as jnp
import numpy as np
from jax import lax
from jax.experimental import pallas as pl
from jax.experimental.pallas import tpu as pltpu
from jax.sharding import Mesh, PartitionSpec as P

HEAD = 128
BLOCK = 128
SIDE = 4
CORES = 2
ADAPTER_AXES = ("z", "c")
TENSOR_AXES = ("y", "x")
ROPE_BASE = 500000.0
VMEM = 56 * 1024 * 1024
bf16 = jnp.bfloat16
f32 = jnp.float32
i32 = jnp.int32


def params():
    return pltpu.CompilerParams(vmem_limit_bytes=VMEM)


def passive(arrays):
    return [pl.BlockSpec(memory_space=pl.ANY)] * len(arrays)


def cost(flops, moved, exps=0):
    return pl.CostEstimate(flops=flops, bytes_accessed=moved, transcendentals=exps)


def shift(block, axis, step):
    return lax.ppermute(block, axis, [(i, (i + step) % SIDE) for i in range(SIDE)])


def ring_gather(block, axis, half):
    behind = shift(block, axis, 1)
    ahead = shift(block, axis, -1)
    far_low = shift(behind[:, :half], axis, 1)
    far_high = shift(ahead[:, half:], axis, -1)
    return block, behind, ahead, far_low, far_high


def second_gather(low, high, axis):
    onward = shift(low, axis, 1), shift(high, axis, -1)
    return onward, (shift(high, axis, 1), shift(low, axis, -1))


def ring_order(index):
    return [index, (index + SIDE - 1) % SIDE, (index + 1) % SIDE, (index + 2) % SIDE]


def pick_local(pick, down_qkv, up_q, up_kv, down_o, up_o, wo, unit, after):
    groups = pick.shape[0] - SIDE
    rank3, depth = down_qkv.shape[1:]
    rank, wide = up_q.shape[1:]
    narrow = up_kv.shape[2]
    rows = wo.shape[0] // groups

    def body(pick_ref, dq, uq, ukv, do, uo, *refs):
        w_refs, w_outs = refs[:SIDE], refs[-SIDE:]
        down, up = refs[-SIDE - 2 : -SIDE]
        down[0, :rank3, :] = dq[0]
        down[0, rank3:, :] = do[0]
        up[0, :, :wide] = uq[0]
        up[0, :, wide : 2 * wide] = uo[0]
        up[0, :, 2 * wide :] = ukv[0]
        for w_ref, w_out in zip(w_refs, w_outs):
            w_out[...] = w_ref[...]

    def chosen(a):
        return pl.BlockSpec((1,) + a.shape[1:], lambda i, p: (p[i], 0, 0))

    def columns(k):
        return pl.BlockSpec((rows, unit), lambda i, p: (i, p[groups + k]))

    down_shape = (groups, rank3 + rank, depth)
    up_shape = (groups, rank, 2 * wide + narrow)
    share = (wo.shape[0], unit)
    return pl.pallas_call(
        body,
        out_shape=tuple(
            jax.ShapeDtypeStruct(s, bf16)
            for s in (down_shape, up_shape, share, share, share, share)
        ),
        grid_spec=pltpu.PrefetchScalarGridSpec(
            num_scalar_prefetch=1,
            grid=(groups,),
            in_specs=[chosen(a) for a in (down_qkv, up_q, up_kv, down_o, up_o)]
            + [columns(k) for k in range(SIDE)]
            + passive(after),
            out_specs=[
                pl.BlockSpec((1,) + s[1:], lambda i, p: (i, 0, 0)) for s in (down_shape, up_shape)
            ]
            + [pl.BlockSpec((rows, unit), lambda i, p: (i, 0))] * SIDE,
        ),
        compiler_params=params(),
        cost_estimate=cost(0, 2 * 2 * (math.prod(down_shape) + math.prod(up_shape))),
    )(pick, down_qkv, up_q, up_kv, down_o, up_o, wo, wo, wo, wo, *after)


def stack_rows(blocks, after):
    rows, width = blocks[0].shape
    count = len(blocks)

    def body(*refs):
        out = refs[-1]
        for k in range(count):
            out[k * rows : (k + 1) * rows, :] = refs[k][...]

    spec = pl.BlockSpec((rows, width), lambda i: (0, 0))
    return pl.pallas_call(
        body,
        out_shape=jax.ShapeDtypeStruct((count * rows, width), bf16),
        grid=(1,),
        in_specs=[spec] * count + passive(after),
        out_specs=pl.BlockSpec((count * rows, width), lambda i: (0, 0)),
        compiler_params=params(),
        cost_estimate=cost(0, 4 * count * rows * width),
    )(*blocks, *after)


def rank_partial(meta, x, down, rank3, after):
    tokens, depth = x.shape
    per = 2
    rows = per * BLOCK

    def body(meta_ref, x_ref, *rest):
        d_refs, out = rest[:per], rest[-1]
        for k in range(per):
            at = slice(k * BLOCK, (k + 1) * BLOCK)
            out[at, :] = lax.dot_general(
                x_ref[at, :], d_refs[k][0], (((1,), (1,)), ((), ())), preferred_element_type=f32
            )

    def chosen(k):
        return pl.BlockSpec((1, rank3, depth), lambda i, m: (m[0, i * per + k], 0, 0))

    return pl.pallas_call(
        body,
        out_shape=jax.ShapeDtypeStruct((tokens, rank3), f32),
        grid_spec=pltpu.PrefetchScalarGridSpec(
            num_scalar_prefetch=1,
            grid=(tokens // rows,),
            in_specs=[pl.BlockSpec((rows, depth), lambda i, m: (i, 0))]
            + [chosen(k) for k in range(per)]
            + passive(after),
            out_specs=pl.BlockSpec((rows, rank3), lambda i, m: (i, 0)),
        ),
        compiler_params=params(),
        cost_estimate=cost(2 * tokens * depth * rank3, 2 * tokens * depth + 8 * tokens * rank3),
    )(meta, x, *[down] * per, *after)


def join(groups, after):
    tokens = groups[0][0].shape[0]
    rows = 256
    flat = [b for group in groups for b in group]
    widths = [sum(b.shape[1] for b in group) for group in groups]

    def body(*refs):
        ins, outs = refs[: len(flat)], refs[len(flat) + len(after) :]
        at = 0
        for out, group in zip(outs, groups):
            col = 0
            for b in group:
                out[:, col : col + b.shape[1]] = ins[at][...]
                col += b.shape[1]
                at += 1

    return pl.pallas_call(
        body,
        out_shape=tuple(jax.ShapeDtypeStruct((tokens, w), bf16) for w in widths),
        grid=(tokens // rows,),
        in_specs=[pl.BlockSpec((rows, b.shape[1]), lambda i: (i, 0)) for b in flat]
        + passive(after),
        out_specs=[pl.BlockSpec((rows, w), lambda i: (i, 0)) for w in widths],
        compiler_params=params(),
        cost_estimate=cost(0, 4 * tokens * sum(widths)),
    )(*flat, *after)


def share_sum(pieces, after):
    ways, rows, rank = pieces.shape

    def body(p_ref, *refs):
        total = p_ref[0]
        for k in range(1, ways):
            total = total + p_ref[k]
        for k in range(ways):
            refs[-1][k] = total.astype(bf16)

    whole = pl.BlockSpec(pieces.shape, lambda i: (0, 0, 0))
    return pl.pallas_call(
        body,
        out_shape=jax.ShapeDtypeStruct(pieces.shape, bf16),
        grid=(1,),
        in_specs=[whole] + passive(after),
        out_specs=whole,
        compiler_params=params(),
        cost_estimate=cost(ways * rows * rank, 6 * ways * rows * rank),
    )(pieces, *after)


def scatter_rows(partial):
    rows, rank = partial.shape
    ways = SIDE * SIDE
    return lax.all_to_all(
        partial.reshape(ways, rows // ways, rank), TENSOR_AXES, 0, 0, tiled=True
    )


def project(index, total, blocks, weights, tile, last=None, after=(), rows=256):
    tokens = blocks[0].shape[0]
    counts = [b.shape[1] // rows for b in blocks]
    pieces = sum(counts)
    kinds = len(weights)
    first = total is None
    tail, tail_operands, tail_specs, dtype = last or (None, [], [], f32)

    def body(index_ref, meta_ref, *refs):
        x_refs = refs[: len(blocks)]
        w_refs = refs[len(blocks) : len(blocks) + kinds * pieces]
        rest = refs[len(blocks) + kinds * pieces :]
        outs = rest[len(rest) - kinds :]
        for kind in range(kinds):
            mine = w_refs[kind * pieces : (kind + 1) * pieces]
            acc = None if first else rest[kind][...]
            at = 0
            for x_ref, n in zip(x_refs, counts):
                w = jnp.concatenate([r[...] for r in mine[at : at + n]], axis=0)
                add = jnp.dot(x_ref[...], w, preferred_element_type=f32)
                acc = add if acc is None else acc + add
                at += n
            if tail is not None:
                acc = tail(meta_ref, acc, rest[kinds : kinds + len(tail_operands)])
            outs[kind][...] = acc

    def weight(k, width):
        return pl.BlockSpec((rows, width), lambda i, p, m: (p[k], 0))

    widths = [w.shape[1] for w in weights]
    row_specs = [pl.BlockSpec((tile, w), lambda i, p, m: (i, 0)) for w in widths]
    in_specs = [pl.BlockSpec((tile, b.shape[1]), lambda i, p, m: (i, 0)) for b in blocks]
    operands = list(blocks)
    for w in weights:
        in_specs += [weight(k, w.shape[1]) for k in range(pieces)]
        operands += [w] * pieces
    aliases = {}
    if not first:
        if tail is None:
            aliases = {2 + len(operands) + k: k for k in range(kinds)}
        in_specs += row_specs
        operands += list(total)
    index, meta = index
    depth = pieces * rows
    return pl.pallas_call(
        body,
        out_shape=tuple(jax.ShapeDtypeStruct((tokens, w), dtype) for w in widths),
        grid_spec=pltpu.PrefetchScalarGridSpec(
            num_scalar_prefetch=2,
            grid=(tokens // tile,),
            in_specs=in_specs + tail_specs + passive(after),
            out_specs=row_specs,
        ),
        input_output_aliases=aliases,
        compiler_params=params(),
        cost_estimate=cost(
            2 * tokens * depth * sum(widths),
            2 * depth * (tokens + sum(widths)) + 8 * tokens * sum(widths),
        ),
    )(index, meta, *operands, *tail_operands, *after)


def key_value_tail(shrunk, up, cosine, sine, wide, narrow, tile):
    rank = shrunk.shape[1] // 3
    per = tile // BLOCK

    def tail(meta_ref, acc, refs):
        s_ref, up_ref, c_ref, n_ref = refs
        i = pl.program_id(0)
        is_key = meta_ref[3, 0] == 1
        done = []
        for k in range(per):
            at = slice(k * BLOCK, (k + 1) * BLOCK)
            s = s_ref[at, :].astype(f32)
            rank_in = jnp.where(is_key, s[:, rank : 2 * rank], s[:, 2 * rank :]).astype(bf16)
            u = acc[at, :] + jnp.dot(
                rank_in, up_ref[meta_ref[0, i * per + k]], preferred_element_type=f32
            )
            place = meta_ref[1, i * per + k]
            turned = u * c_ref[place] + pltpu.roll(u, HEAD // 2, 1) * n_ref[place]
            done.append(jnp.where(is_key, turned, u).astype(bf16))
        return jnp.concatenate(done, axis=0)

    specs = [
        pl.BlockSpec((tile, 3 * rank), lambda i, p, m: (i, 0)),
        pl.BlockSpec((up.shape[0], rank, narrow), lambda i, p, m: (0, 0, 2 * wide // narrow)),
        pl.BlockSpec(cosine.shape, lambda i, p, m: (0, 0, 0)),
        pl.BlockSpec(sine.shape, lambda i, p, m: (0, 0, 0)),
    ]
    return tail, [shrunk, up, cosine, sine], specs, bf16


def rotation_tables():
    freq = np.exp(-(2.0 * np.arange(HEAD // 2, dtype=np.float32) / HEAD) * math.log(ROPE_BASE))
    angle = np.arange(3 * BLOCK, dtype=np.float32)[:, None] * freq.astype(np.float32)[None, :]
    cosine = np.concatenate([np.cos(angle)] * 2, axis=1)
    sine = np.concatenate([-np.sin(angle), np.sin(angle)], axis=1)
    shape = (3, BLOCK, HEAD)
    return (
        jnp.asarray(cosine.reshape(shape), f32),
        jnp.asarray(sine.reshape(shape), f32),
    )


def attention(meta, q, shrunk, up, down, mine, other, cosine, sine, begin, count):
    tokens, wide = q.shape
    rank = shrunk.shape[1] // 3
    heads = wide // HEAD
    window = min(3 * BLOCK, tokens)
    scale = 1.0 / math.sqrt(HEAD)

    def body(meta_ref, q_ref, s_ref, up_ref, d_ref, m_ref, o_ref, c_ref, n_ref, att):
        i = begin + pl.program_id(0)
        is_key = meta_ref[3, 0] == 1
        first = meta_ref[2, i]
        limit = meta_ref[4, i]
        u = q_ref[...] + jnp.dot(
            s_ref[...][:, :rank], up_ref[0], preferred_element_type=f32
        )
        start = pl.multiple_of(jnp.maximum(i - 2, 0) * BLOCK, BLOCK)
        own = m_ref[pl.ds(start, window), :]
        far = o_ref[pl.ds(start, window), :]
        keys = jnp.where(is_key, own, far)
        values = jnp.where(is_key, far, own)
        row = i * BLOCK + lax.broadcasted_iota(i32, (BLOCK, window), 0)
        col = start + lax.broadcasted_iota(i32, (BLOCK, window), 1)
        allowed = (col >= first) & (col <= row) & (col < limit)
        cosines = c_ref[0]
        sines = n_ref[0]
        turned = []
        for h in range(heads):
            part = u[:, h * HEAD : (h + 1) * HEAD]
            turned.append(
                (part * cosines + pltpu.roll(part, HEAD // 2, 1) * sines).astype(bf16)
            )
        scores = lax.dot_general(
            jnp.concatenate(turned, axis=0),
            keys,
            (((1,), (1,)), ((), ())),
            preferred_element_type=f32,
        )
        for h in range(heads):
            at = slice(h * HEAD, (h + 1) * HEAD)
            weights = jnp.where(allowed, jnp.exp(scores[at, :] * scale), 0.0)
            weights = weights * (1.0 / jnp.sum(weights, axis=1, keepdims=True))
            mixed = jnp.dot(weights.astype(bf16), values, preferred_element_type=f32)
            att[:, at] = mixed.astype(bf16)
        head = lax.dot_general(
            att[:, :wide], d_ref[0], (((1,), (1,)), ((), ())), preferred_element_type=f32
        )
        att[:, wide : wide + rank] = head.astype(bf16)
        att[:, wide + rank :] = jnp.zeros((BLOCK, HEAD - rank), bf16)

    table = pl.BlockSpec((1, BLOCK, HEAD), lambda i, m: (m[1, i + begin], 0, 0))
    whole = pl.BlockSpec((tokens, HEAD), lambda i, m: (0, 0))
    return pl.pallas_call(
        body,
        out_shape=jax.ShapeDtypeStruct((count * BLOCK, wide + HEAD), bf16),
        grid_spec=pltpu.PrefetchScalarGridSpec(
            num_scalar_prefetch=1,
            grid=(count,),
            in_specs=[
                pl.BlockSpec((BLOCK, wide), lambda i, m: (i + begin, 0)),
                pl.BlockSpec((BLOCK, 3 * rank), lambda i, m: (i + begin, 0)),
                pl.BlockSpec((1, rank, wide), lambda i, m: (m[0, i + begin], 0, 0)),
                pl.BlockSpec((1, rank, down.shape[2]), lambda i, m: (m[0, i + begin], 3, 0)),
                whole,
                whole,
                table,
                table,
            ],
            out_specs=pl.BlockSpec((BLOCK, wide + HEAD), lambda i, m: (i, 0)),
        ),
        compiler_params=params(),
        cost_estimate=cost(
            4 * count * BLOCK * window * wide, 8 * count * BLOCK * wide, heads * count * BLOCK * window
        ),
    )(meta, q, shrunk, up, down, mine, other, cosine, sine)


def output_partial(shards, pieces, weights):
    tokens = pieces[0].shape[0]
    count, (depth, width) = len(shards), weights.shape[1:]
    unit = depth // SIDE
    far_cut = pieces[3].shape[1]
    whole = 2 * width + HEAD

    def body(index_ref, *refs):
        own, behind, ahead, far_low, far_high, w_low, w_high = refs[:7]
        out_far_low, out_far_high, out_ahead, out_behind, out_mine, x_all = refs[7:]
        step = pl.program_id(0)

        @pl.when(step == 0)
        def _():
            for k, ref in enumerate((own, behind, ahead)):
                x_all[:, k * unit : (k + 1) * unit] = ref[:, :unit]
            x_all[:, 3 * unit : 3 * unit + far_cut] = far_low[...]
            x_all[:, 3 * unit + far_cut :] = far_high[:, : unit - far_cut]
            rank = (
                own[:, unit:].astype(f32)
                + behind[:, unit:].astype(f32)
                + ahead[:, unit:].astype(f32)
                + far_high[:, unit - far_cut :].astype(f32)
            )
            for out in (out_far_low, out_ahead, out_behind, out_mine):
                out[:, width : width + HEAD] = rank.astype(out.dtype)

        first = jnp.dot(x_all[...], w_low[0], preferred_element_type=f32)
        second = jnp.dot(x_all[...], w_high[0], preferred_element_type=f32)
        low, high = slice(0, width), slice(width + HEAD, whole)

        @pl.when(step == 0)
        def _():
            out_far_low[:, low] = first.astype(bf16)
            out_far_high[...] = second.astype(bf16)

        for k, out in enumerate((out_ahead, out_behind, out_mine)):

            @pl.when(step == k + 1)
            def _():
                out[:, low] = first.astype(out.dtype)
                out[:, high] = second.astype(out.dtype)

    shapes = [(width + HEAD, bf16), (width, bf16), (whole, bf16), (whole, bf16), (whole, f32)]
    return pl.pallas_call(
        body,
        out_shape=tuple(jax.ShapeDtypeStruct((tokens, w), d) for w, d in shapes),
        grid_spec=pltpu.PrefetchScalarGridSpec(
            num_scalar_prefetch=1,
            grid=(count // 2,),
            in_specs=[pl.BlockSpec(p.shape, lambda j, d: (0, 0)) for p in pieces]
            + [pl.BlockSpec((1, depth, width), lambda j, d: (d[2 * j], 0, 0))]
            + [pl.BlockSpec((1, depth, width), lambda j, d: (d[2 * j + 1], 0, 0))],
            out_specs=[pl.BlockSpec((tokens, w), lambda j, d: (0, 0)) for w, _ in shapes],
            scratch_shapes=[pltpu.VMEM((tokens, depth), bf16)],
        ),
        compiler_params=params(),
        cost_estimate=cost(
            2 * tokens * depth * count * width, 2 * depth * (tokens + count * width)
        ),
    )(jnp.stack(shards).astype(i32), *pieces, weights, weights)


def add_far(ahead, via_behind, behind, via_ahead):
    rows, whole = ahead.shape
    low = via_behind.shape[1]

    def body(a_ref, va_ref, b_ref, vb_ref, out_a, out_b):
        out_a[:, :low] = (a_ref[:, :low].astype(f32) + va_ref[...].astype(f32)).astype(bf16)
        out_a[:, low:] = a_ref[:, low:]
        out_b[:, :low] = b_ref[:, :low]
        out_b[:, low:] = (b_ref[:, low:].astype(f32) + vb_ref[...].astype(f32)).astype(bf16)

    arrays = (ahead, via_behind, behind, via_ahead)
    return pl.pallas_call(
        body,
        out_shape=(jax.ShapeDtypeStruct((rows, whole), bf16),) * 2,
        grid=(1,),
        in_specs=[pl.BlockSpec(a.shape, lambda i: (0, 0)) for a in arrays],
        out_specs=[pl.BlockSpec((rows, whole), lambda i: (0, 0))] * 2,
        compiler_params=params(),
        cost_estimate=cost(2 * rows * whole, 10 * rows * whole),
    )(*arrays)


def output_ring(pieces, weights, axis):
    me, behind, ahead, far = ring_order(lax.axis_index(axis))
    shards = [2 * place + side for place in (far, ahead, behind, me) for side in range(2)]
    far_low, far_high, to_ahead, to_behind, mine = output_partial(shards, pieces, weights)
    to_ahead, to_behind = add_far(
        to_ahead, shift(far_low, axis, 1), to_behind, shift(far_high, axis, -1)
    )
    return mine, shift(to_behind, axis, -1), shift(to_ahead, axis, 1)


def finish(meta, parts, up, rank, wide):
    cuts = len(parts)
    rows, whole = parts[0][0].shape
    width = (whole - HEAD) // 2
    per = 2
    steps = rows // (per * BLOCK)
    terms = [t for cut in parts for t in cut]
    each = len(parts[0])

    def body(meta_ref, *refs):
        up_ref, out = refs[len(terms) :]
        i = pl.program_id(0)

        def put(mine):
            for k in range(per):
                at = slice(k * BLOCK, (k + 1) * BLOCK)
                block = i * per + k
                total = mine[0][at, :].astype(f32)
                for ref in mine[1:]:
                    total = total + ref[at, :].astype(f32)
                extra = jnp.dot(
                    total[:, width : width + rank].astype(bf16),
                    up_ref[meta_ref[0, block]],
                    preferred_element_type=f32,
                )
                row = block * BLOCK + lax.broadcasted_iota(i32, (BLOCK, width), 0)
                valid = row < meta_ref[4, block]
                for side, begin in enumerate((0, width + HEAD)):
                    cols = slice(side * width, (side + 1) * width)
                    out[at, cols] = jnp.where(
                        valid, total[:, begin : begin + width] + extra[:, cols], 0.0
                    )

        for cut in range(cuts):

            @pl.when(i // steps == cut)
            def _():
                put(refs[cut * each : (cut + 1) * each])

    def term_spec(cut):
        return pl.BlockSpec(
            (per * BLOCK, whole), lambda i, m: (jnp.clip(i - cut * steps, 0, steps - 1), 0)
        )

    return pl.pallas_call(
        body,
        out_shape=jax.ShapeDtypeStruct((cuts * rows, 2 * width), f32),
        grid_spec=pltpu.PrefetchScalarGridSpec(
            num_scalar_prefetch=1,
            grid=(cuts * steps,),
            in_specs=[term_spec(cut) for cut in range(cuts) for _ in range(each)]
            + [pl.BlockSpec((up.shape[0], rank, wide), lambda i, m: (0, 0, 1))],
            out_specs=pl.BlockSpec((per * BLOCK, 2 * width), lambda i, m: (i, 0)),
        ),
        compiler_params=params(),
        cost_estimate=cost(4 * cuts * rows * rank * width, 28 * cuts * rows * width),
    )(meta, *terms, up)


def on_device(x, wq, wkv, wo, down_qkv, up_q, up_kv, down_o, up_o, choice, counts, tails):
    z, c, y, xi = (lax.axis_index(n) for n in ADAPTER_AXES + TENSOR_AXES)
    group = z * CORES + c
    tokens, local = x.shape
    holders = down_qkv.shape[0]
    requests = choice.shape[1]
    wide = wq.shape[1]
    rank = up_q.shape[1]
    blocks = tokens // BLOCK

    owners = choice // holders
    pick = jnp.sum(jnp.where(owners == group, choice % holders, 0), axis=1).astype(i32)
    own_owner = lax.dynamic_index_in_dim(owners, group, 0, keepdims=False)
    req = jnp.arange(requests, dtype=i32)
    starts = jnp.sum(jnp.where(req[None, :] < req[:, None], counts[0][None, :], 0), axis=1)
    block = jnp.arange(blocks, dtype=i32)
    of_block = (starts[None, :] <= block[:, None]) & (
        block[:, None] < (starts + counts[0])[None, :]
    )

    def lookup(values):
        return jnp.sum(jnp.where(of_block, values[None, :], 0), axis=1).astype(i32)

    slot = lookup(own_owner)
    first = lookup(starts)
    limit = (first + lookup(counts[0]) - 1) * BLOCK + lookup(tails[0])
    is_key = jnp.broadcast_to(1 - xi % 2, (blocks,)).astype(i32)
    meta = jnp.stack([slot, block - first, first * BLOCK, is_key, limit]).astype(i32)

    cosine, sine = rotation_tables()

    half = local // 2
    ys, xs = ring_order(y), ring_order(xi)
    first_a = ring_gather(x[:, :half], "x", half // 2)
    first_b = ring_gather(x[:, half:], "y", half // 2)
    low_a, high_a, low_b, high_b = join(
        [first_a[:2], first_a[2:], first_b[:2], first_b[2:]], []
    )
    far_a, next_a = second_gather(low_a, high_a, "y")
    far_b, next_b = second_gather(low_b, high_b, "x")

    stores = (jnp.swapaxes(down_qkv, 1, 2), up_q, up_kv, jnp.swapaxes(down_o, 1, 2), up_o)
    unit = wo.shape[1] // (SIDE * SIDE * 2)
    wo_cols = jnp.stack(ys) * (2 * SIDE) + group
    down_out, up_out, *sent = pick_local(
        jnp.concatenate([pick, wo_cols.astype(i32)]),
        *stores,
        wo,
        unit,
        first_a[1:3] + first_b[1:3],
    )
    down = lax.all_to_all(down_out, ADAPTER_AXES, 0, 0, tiled=True)

    got = [sent[0], shift(sent[2], "y", 1), shift(sent[1], "y", -1), shift(sent[3], "y", 2)]
    wo_mine = stack_rows(got, [down, *far_a, *far_b])
    wo_all = lax.all_gather(wo_mine, ADAPTER_AXES, axis=0)

    def rows_a(k, cols):
        return [(ys[k] * SIDE + xs[j]) * 2 for j in cols]

    def rows_b(k, cols):
        return [(ys[j] * SIDE + xs[k]) * 2 + 1 for j in cols]

    def index_of(rows):
        return jnp.stack(rows).astype(i32)

    every = range(SIDE)
    low, high = (0, 1), (2, 3)
    total = project(
        (index_of(rows_a(0, every) + rows_b(0, every)), meta),
        None,
        [low_a, high_a, low_b, high_b],
        [wq, wkv],
        512,
    )

    pieces = scatter_rows(
        rank_partial(meta, x, down, 3 * rank, [*far_a, *far_b, total[1]])
    )
    up = lax.all_to_all(up_out, ADAPTER_AXES, 0, 0, tiled=True)
    total = project(
        (
            index_of(rows_a(1, low) + rows_a(2, high) + rows_b(1, low) + rows_b(2, high)),
            meta,
        ),
        total,
        [*far_a, *far_b],
        [wq, wkv],
        512,
    )
    copies = share_sum(pieces, [total[1]])

    a_low, a_high = shift(far_a[0], "y", 1), shift(far_a[1], "y", -1)
    b_low, b_high = shift(far_b[0], "x", 1), shift(far_b[1], "x", -1)
    total = project(
        (
            index_of(rows_a(1, high) + rows_a(2, low) + rows_b(1, high) + rows_b(2, low)),
            meta,
        ),
        total,
        [*next_a, *next_b],
        [wq, wkv],
        512,
    )
    shrunk = lax.all_to_all(copies, TENSOR_AXES, 0, 0, tiled=True).reshape(tokens, 3 * rank)
    final = (index_of(rows_a(3, every) + rows_b(3, every)), meta)
    far = [a_low, a_high, b_low, b_high]
    tail = key_value_tail(shrunk, up, cosine, sine, wide, wkv.shape[1], 512)
    (mine,) = project(final, total[1:], far, [wkv], 512, tail)
    other = lax.ppermute(mine, "x", [(i, i ^ 1) for i in range(SIDE)])
    (q,) = project(final, total[:1], far, [wq], 512)

    cuts = 2
    each = blocks // cuts
    parts = []
    for cut in range(cuts):
        attended = attention(
            meta, q, shrunk, up, down, mine, other, cosine, sine, cut * each, each
        )
        parts.append(output_ring(ring_gather(attended, "y", wide // 2), wo_all, "x"))
    return finish(meta, parts, up, rank, wide)


def solution(mesh):
    fine = Mesh(mesh.devices.reshape(SIDE, CORES, SIDE, SIDE), ADAPTER_AXES + TENSOR_AXES)
    placed = (
        P(ADAPTER_AXES, TENSOR_AXES),
        P(None, TENSOR_AXES),
        P(None, TENSOR_AXES),
        P(TENSOR_AXES, None),
        P(ADAPTER_AXES, TENSOR_AXES, None),
        P(ADAPTER_AXES, None, TENSOR_AXES),
        P(ADAPTER_AXES, None, TENSOR_AXES),
        P(ADAPTER_AXES, TENSOR_AXES, None),
        P(ADAPTER_AXES, None, TENSOR_AXES),
        P(),
        P(ADAPTER_AXES, None),
        P(ADAPTER_AXES, None),
    )
    return jax.shard_map(
        on_device,
        mesh=fine,
        in_specs=placed,
        out_specs=P(ADAPTER_AXES, TENSOR_AXES),
        check_vma=False,
    )
```

```python
import math

import jax
import jax.numpy as jnp
import numpy as np
from jax import lax
from jax.experimental import pallas as pl
from jax.experimental.pallas import tpu as pltpu
from jax.sharding import Mesh, PartitionSpec as P

HEAD = 128
BLOCK = 128
SIDE = 4
CORES = 2
ADAPTER_AXES = ("z", "c")
TENSOR_AXES = ("y", "x")
ROPE_BASE = 500000.0
VMEM = 56 * 1024 * 1024
bf16 = jnp.bfloat16
f32 = jnp.float32
i32 = jnp.int32


def params():
    return pltpu.CompilerParams(vmem_limit_bytes=VMEM)


def passive(arrays):
    return [pl.BlockSpec(memory_space=pl.ANY)] * len(arrays)


def cost(flops, moved, exps=0):
    return pl.CostEstimate(flops=flops, bytes_accessed=moved, transcendentals=exps)


def shift(block, axis, step):
    return lax.ppermute(block, axis, [(i, (i + step) % SIDE) for i in range(SIDE)])


def ring_gather(block, axis, half):
    behind = shift(block, axis, 1)
    ahead = shift(block, axis, -1)
    far_low = shift(behind[:, :half], axis, 1)
    far_high = shift(ahead[:, half:], axis, -1)
    return block, behind, ahead, far_low, far_high


def second_gather(low, high, axis):
    onward = shift(low, axis, 1), shift(high, axis, -1)
    return onward, (shift(high, axis, 1), shift(low, axis, -1))


def ring_order(index):
    return [index, (index + SIDE - 1) % SIDE, (index + 1) % SIDE, (index + 2) % SIDE]


def pick_local(pick, down_qkv, up_q, up_kv, down_o, up_o, x, wo, unit):
    tokens, local = x.shape
    groups = pick.shape[0] - SIDE
    rank3, depth = down_qkv.shape[1:]
    rank, wide = up_q.shape[1:]
    narrow = up_kv.shape[2]
    rows = wo.shape[0] // groups

    def body(pick_ref, dq, uq, ukv, do, uo, x_ref, *refs):
        w_refs, (down, up, left, right), w_outs = refs[:SIDE], refs[SIDE : SIDE + 4], refs[SIDE + 4 :]
        left[...] = x_ref[:, : local // 2]
        right[...] = x_ref[:, local // 2 :]
        down[0, :rank3, :] = dq[0]
        down[0, rank3:, :] = do[0]
        up[0, :, :wide] = uq[0]
        up[0, :, wide : 2 * wide] = uo[0]
        up[0, :, 2 * wide :] = ukv[0]
        for w_ref, w_out in zip(w_refs, w_outs):
            w_out[...] = w_ref[...]

    def chosen(a):
        return pl.BlockSpec((1,) + a.shape[1:], lambda i, p: (p[i], 0, 0))

    def columns(k):
        return pl.BlockSpec((rows, unit), lambda i, p: (i, p[groups + k]))

    down_shape = (groups, rank3 + rank, depth)
    up_shape = (groups, rank, 2 * wide + narrow)
    half = (tokens, local // 2)
    share = (wo.shape[0], unit)
    return pl.pallas_call(
        body,
        out_shape=tuple(
            jax.ShapeDtypeStruct(s, bf16)
            for s in (down_shape, up_shape, half, half, share, share, share, share)
        ),
        grid_spec=pltpu.PrefetchScalarGridSpec(
            num_scalar_prefetch=1,
            grid=(groups,),
            in_specs=[chosen(a) for a in (down_qkv, up_q, up_kv, down_o, up_o)]
            + [pl.BlockSpec((tokens // groups, local), lambda i, p: (i, 0))]
            + [columns(k) for k in range(SIDE)],
            out_specs=[
                pl.BlockSpec((1,) + s[1:], lambda i, p: (i, 0, 0)) for s in (down_shape, up_shape)
            ]
            + [pl.BlockSpec((tokens // groups, local // 2), lambda i, p: (i, 0))] * 2
            + [pl.BlockSpec((rows, unit), lambda i, p: (i, 0))] * SIDE,
        ),
        compiler_params=params(),
        cost_estimate=cost(0, 2 * 2 * (math.prod(down_shape) + math.prod(up_shape))),
    )(pick, down_qkv, up_q, up_kv, down_o, up_o, x, wo, wo, wo, wo)


def stack_rows(blocks, after):
    rows, width = blocks[0].shape
    count = len(blocks)

    def body(*refs):
        out = refs[-1]
        for k in range(count):
            out[k * rows : (k + 1) * rows, :] = refs[k][...]

    spec = pl.BlockSpec((rows, width), lambda i: (0, 0))
    return pl.pallas_call(
        body,
        out_shape=jax.ShapeDtypeStruct((count * rows, width), bf16),
        grid=(1,),
        in_specs=[spec] * count + passive(after),
        out_specs=pl.BlockSpec((count * rows, width), lambda i: (0, 0)),
        compiler_params=params(),
        cost_estimate=cost(0, 4 * count * rows * width),
    )(*blocks, *after)


def rank_partial(meta, x, down, rank3, after):
    tokens, depth = x.shape
    per = 2
    rows = per * BLOCK

    def body(meta_ref, x_ref, *rest):
        d_refs, out = rest[:per], rest[-1]
        for k in range(per):
            at = slice(k * BLOCK, (k + 1) * BLOCK)
            out[at, :] = lax.dot_general(
                x_ref[at, :], d_refs[k][0], (((1,), (1,)), ((), ())), preferred_element_type=f32
            )

    def chosen(k):
        return pl.BlockSpec((1, rank3, depth), lambda i, m: (m[0, i * per + k], 0, 0))

    return pl.pallas_call(
        body,
        out_shape=jax.ShapeDtypeStruct((tokens, rank3), f32),
        grid_spec=pltpu.PrefetchScalarGridSpec(
            num_scalar_prefetch=1,
            grid=(tokens // rows,),
            in_specs=[pl.BlockSpec((rows, depth), lambda i, m: (i, 0))]
            + [chosen(k) for k in range(per)]
            + passive(after),
            out_specs=pl.BlockSpec((rows, rank3), lambda i, m: (i, 0)),
        ),
        compiler_params=params(),
        cost_estimate=cost(2 * tokens * depth * rank3, 2 * tokens * depth + 8 * tokens * rank3),
    )(meta, x, *[down] * per, *after)


def join(groups, after):
    tokens = groups[0][0].shape[0]
    rows = 256
    flat = [b for group in groups for b in group]
    widths = [sum(b.shape[1] for b in group) for group in groups]

    def body(*refs):
        ins, outs = refs[: len(flat)], refs[len(flat) + len(after) :]
        at = 0
        for out, group in zip(outs, groups):
            col = 0
            for b in group:
                out[:, col : col + b.shape[1]] = ins[at][...]
                col += b.shape[1]
                at += 1

    return pl.pallas_call(
        body,
        out_shape=tuple(jax.ShapeDtypeStruct((tokens, w), bf16) for w in widths),
        grid=(tokens // rows,),
        in_specs=[pl.BlockSpec((rows, b.shape[1]), lambda i: (i, 0)) for b in flat]
        + passive(after),
        out_specs=[pl.BlockSpec((rows, w), lambda i: (i, 0)) for w in widths],
        compiler_params=params(),
        cost_estimate=cost(0, 4 * tokens * sum(widths)),
    )(*flat, *after)


def share_sum(pieces, onward, after):
    ways, rows, rank = pieces.shape

    def body(p_ref, *refs):
        out = refs[-2]
        total = p_ref[0]
        for k in range(1, ways):
            total = total + p_ref[k]
        for k in range(ways):
            out[k] = total.astype(bf16)

    whole = pl.BlockSpec(pieces.shape, lambda i: (0, 0, 0))
    return pl.pallas_call(
        body,
        out_shape=(
            jax.ShapeDtypeStruct(pieces.shape, bf16),
            jax.ShapeDtypeStruct(onward.shape, onward.dtype),
        ),
        grid=(1,),
        in_specs=[whole] + passive([onward, *after]),
        out_specs=[whole] + passive([onward]),
        input_output_aliases={1: 1},
        compiler_params=params(),
        cost_estimate=cost(ways * rows * rank, 6 * ways * rows * rank),
    )(pieces, onward, *after)


def scatter_rows(partial):
    rows, rank = partial.shape
    ways = SIDE * SIDE
    return lax.all_to_all(
        partial.reshape(ways, rows // ways, rank), TENSOR_AXES, 0, 0, tiled=True
    )


def project(index, total, blocks, weights, tile, last=None, after=(), rows=256):
    tokens = blocks[0].shape[0]
    counts = [b.shape[1] // rows for b in blocks]
    pieces = sum(counts)
    kinds = len(weights)
    first = total is None
    tail, tail_operands, tail_specs, dtype = last or (None, [], [], f32)

    def body(index_ref, meta_ref, *refs):
        x_refs = refs[: len(blocks)]
        w_refs = refs[len(blocks) : len(blocks) + kinds * pieces]
        rest = refs[len(blocks) + kinds * pieces :]
        outs = rest[len(rest) - kinds :]
        for kind in range(kinds):
            mine = w_refs[kind * pieces : (kind + 1) * pieces]
            acc = None if first else rest[kind][...]
            at = 0
            for x_ref, n in zip(x_refs, counts):
                w = jnp.concatenate([r[...] for r in mine[at : at + n]], axis=0)
                add = jnp.dot(x_ref[...], w, preferred_element_type=f32)
                acc = add if acc is None else acc + add
                at += n
            if tail is not None:
                acc = tail(meta_ref, acc, rest[kinds : kinds + len(tail_operands)])
            outs[kind][...] = acc

    def weight(k, width):
        return pl.BlockSpec((rows, width), lambda i, p, m: (p[k], 0))

    widths = [w.shape[1] for w in weights]
    row_specs = [pl.BlockSpec((tile, w), lambda i, p, m: (i, 0)) for w in widths]
    in_specs = [pl.BlockSpec((tile, b.shape[1]), lambda i, p, m: (i, 0)) for b in blocks]
    operands = list(blocks)
    for w in weights:
        in_specs += [weight(k, w.shape[1]) for k in range(pieces)]
        operands += [w] * pieces
    aliases = {}
    if not first:
        if tail is None:
            aliases = {2 + len(operands) + k: k for k in range(kinds)}
        in_specs += row_specs
        operands += list(total)
    index, meta = index
    depth = pieces * rows
    return pl.pallas_call(
        body,
        out_shape=tuple(jax.ShapeDtypeStruct((tokens, w), dtype) for w in widths),
        grid_spec=pltpu.PrefetchScalarGridSpec(
            num_scalar_prefetch=2,
            grid=(tokens // tile,),
            in_specs=in_specs + tail_specs + passive(after),
            out_specs=row_specs,
        ),
        input_output_aliases=aliases,
        compiler_params=params(),
        cost_estimate=cost(
            2 * tokens * depth * sum(widths),
            2 * depth * (tokens + sum(widths)) + 8 * tokens * sum(widths),
        ),
    )(index, meta, *operands, *tail_operands, *after)


def key_value_tail(shrunk, up, cosine, sine, wide, narrow, tile):
    rank = shrunk.shape[1] // 3
    per = tile // BLOCK

    def tail(meta_ref, acc, refs):
        s_ref, up_ref, c_ref, n_ref = refs
        i = pl.program_id(0)
        is_key = meta_ref[3, 0] == 1
        done = []
        for k in range(per):
            at = slice(k * BLOCK, (k + 1) * BLOCK)
            s = s_ref[at, :].astype(f32)
            rank_in = jnp.where(is_key, s[:, rank : 2 * rank], s[:, 2 * rank :]).astype(bf16)
            u = acc[at, :] + jnp.dot(
                rank_in, up_ref[meta_ref[0, i * per + k]], preferred_element_type=f32
            )
            place = meta_ref[1, i * per + k]
            turned = u * c_ref[place] + pltpu.roll(u, HEAD // 2, 1) * n_ref[place]
            done.append(jnp.where(is_key, turned, u).astype(bf16))
        return jnp.concatenate(done, axis=0)

    specs = [
        pl.BlockSpec((tile, 3 * rank), lambda i, p, m: (i, 0)),
        pl.BlockSpec((up.shape[0], rank, narrow), lambda i, p, m: (0, 0, 2 * wide // narrow)),
        pl.BlockSpec(cosine.shape, lambda i, p, m: (0, 0, 0)),
        pl.BlockSpec(sine.shape, lambda i, p, m: (0, 0, 0)),
    ]
    return tail, [shrunk, up, cosine, sine], specs, bf16


def rotation_tables():
    freq = np.exp(-(2.0 * np.arange(HEAD // 2, dtype=np.float32) / HEAD) * math.log(ROPE_BASE))
    angle = np.arange(3 * BLOCK, dtype=np.float32)[:, None] * freq.astype(np.float32)[None, :]
    cosine = np.concatenate([np.cos(angle)] * 2, axis=1)
    sine = np.concatenate([-np.sin(angle), np.sin(angle)], axis=1)
    shape = (3, BLOCK, HEAD)
    return (
        jnp.asarray(cosine.reshape(shape), f32),
        jnp.asarray(sine.reshape(shape), f32),
    )


def attention(meta, q, shrunk, up, down, mine, other, cosine, sine, begin, count):
    tokens, wide = q.shape
    rank = shrunk.shape[1] // 3
    heads = wide // HEAD
    window = min(3 * BLOCK, tokens)
    scale = 1.0 / math.sqrt(HEAD)

    def body(meta_ref, q_ref, s_ref, up_ref, d_ref, m_ref, o_ref, c_ref, n_ref, att):
        i = begin + pl.program_id(0)
        is_key = meta_ref[3, 0] == 1
        first = meta_ref[2, i]
        limit = meta_ref[4, i]
        u = q_ref[...] + jnp.dot(
            s_ref[...][:, :rank], up_ref[0], preferred_element_type=f32
        )
        start = pl.multiple_of(jnp.maximum(i - 2, 0) * BLOCK, BLOCK)
        own = m_ref[pl.ds(start, window), :]
        far = o_ref[pl.ds(start, window), :]
        keys = jnp.where(is_key, own, far)
        values = jnp.where(is_key, far, own)
        row = i * BLOCK + lax.broadcasted_iota(i32, (BLOCK, window), 0)
        col = start + lax.broadcasted_iota(i32, (BLOCK, window), 1)
        allowed = (col >= first) & (col <= row) & (col < limit)
        cosines = c_ref[0]
        sines = n_ref[0]
        turned = []
        for h in range(heads):
            part = u[:, h * HEAD : (h + 1) * HEAD]
            turned.append(
                (part * cosines + pltpu.roll(part, HEAD // 2, 1) * sines).astype(bf16)
            )
        scores = lax.dot_general(
            jnp.concatenate(turned, axis=0),
            keys,
            (((1,), (1,)), ((), ())),
            preferred_element_type=f32,
        )
        for h in range(heads):
            at = slice(h * HEAD, (h + 1) * HEAD)
            weights = jnp.where(allowed, jnp.exp(scores[at, :] * scale), 0.0)
            weights = weights * (1.0 / jnp.sum(weights, axis=1, keepdims=True))
            mixed = jnp.dot(weights.astype(bf16), values, preferred_element_type=f32)
            att[:, at] = mixed.astype(bf16)
        head = lax.dot_general(
            att[:, :wide], d_ref[0], (((1,), (1,)), ((), ())), preferred_element_type=f32
        )
        att[:, wide : wide + rank] = head.astype(bf16)
        att[:, wide + rank :] = jnp.zeros((BLOCK, HEAD - rank), bf16)

    table = pl.BlockSpec((1, BLOCK, HEAD), lambda i, m: (m[1, i + begin], 0, 0))
    whole = pl.BlockSpec((tokens, HEAD), lambda i, m: (0, 0))
    return pl.pallas_call(
        body,
        out_shape=jax.ShapeDtypeStruct((count * BLOCK, wide + HEAD), bf16),
        grid_spec=pltpu.PrefetchScalarGridSpec(
            num_scalar_prefetch=1,
            grid=(count,),
            in_specs=[
                pl.BlockSpec((BLOCK, wide), lambda i, m: (i + begin, 0)),
                pl.BlockSpec((BLOCK, 3 * rank), lambda i, m: (i + begin, 0)),
                pl.BlockSpec((1, rank, wide), lambda i, m: (m[0, i + begin], 0, 0)),
                pl.BlockSpec((1, rank, down.shape[2]), lambda i, m: (m[0, i + begin], 3, 0)),
                whole,
                whole,
                table,
                table,
            ],
            out_specs=pl.BlockSpec((BLOCK, wide + HEAD), lambda i, m: (i, 0)),
        ),
        compiler_params=params(),
        cost_estimate=cost(
            4 * count * BLOCK * window * wide, 8 * count * BLOCK * wide, heads * count * BLOCK * window
        ),
    )(meta, q, shrunk, up, down, mine, other, cosine, sine)


def output_partial(shards, pieces, weights):
    tokens = pieces[0].shape[0]
    count, (depth, width) = len(shards), weights.shape[1:]
    unit = depth // SIDE
    far_cut = pieces[3].shape[1]
    whole = 2 * width + HEAD

    def body(index_ref, *refs):
        own, behind, ahead, far_low, far_high, w_low, w_high = refs[:7]
        out_far_low, out_far_high, out_ahead, out_behind, out_mine, x_all = refs[7:]
        step = pl.program_id(0)

        @pl.when(step == 0)
        def _():
            for k, ref in enumerate((own, behind, ahead)):
                x_all[:, k * unit : (k + 1) * unit] = ref[:, :unit]
            x_all[:, 3 * unit : 3 * unit + far_cut] = far_low[...]
            x_all[:, 3 * unit + far_cut :] = far_high[:, : unit - far_cut]
            rank = (
                own[:, unit:].astype(f32)
                + behind[:, unit:].astype(f32)
                + ahead[:, unit:].astype(f32)
                + far_high[:, unit - far_cut :].astype(f32)
            )
            for out in (out_far_low, out_ahead, out_behind, out_mine):
                out[:, width : width + HEAD] = rank.astype(out.dtype)

        first = jnp.dot(x_all[...], w_low[0], preferred_element_type=f32)
        second = jnp.dot(x_all[...], w_high[0], preferred_element_type=f32)
        low, high = slice(0, width), slice(width + HEAD, whole)

        @pl.when(step == 0)
        def _():
            out_far_low[:, low] = first.astype(bf16)
            out_far_high[...] = second.astype(bf16)

        for k, out in enumerate((out_ahead, out_behind, out_mine)):

            @pl.when(step == k + 1)
            def _():
                out[:, low] = first.astype(out.dtype)
                out[:, high] = second.astype(out.dtype)

    shapes = [(width + HEAD, bf16), (width, bf16), (whole, bf16), (whole, bf16), (whole, f32)]
    return pl.pallas_call(
        body,
        out_shape=tuple(jax.ShapeDtypeStruct((tokens, w), d) for w, d in shapes),
        grid_spec=pltpu.PrefetchScalarGridSpec(
            num_scalar_prefetch=1,
            grid=(count // 2,),
            in_specs=[pl.BlockSpec(p.shape, lambda j, d: (0, 0)) for p in pieces]
            + [pl.BlockSpec((1, depth, width), lambda j, d: (d[2 * j], 0, 0))]
            + [pl.BlockSpec((1, depth, width), lambda j, d: (d[2 * j + 1], 0, 0))],
            out_specs=[pl.BlockSpec((tokens, w), lambda j, d: (0, 0)) for w, _ in shapes],
            scratch_shapes=[pltpu.VMEM((tokens, depth), bf16)],
        ),
        compiler_params=params(),
        cost_estimate=cost(
            2 * tokens * depth * count * width, 2 * depth * (tokens + count * width)
        ),
    )(jnp.stack(shards).astype(i32), *pieces, weights, weights)


def add_far(ahead, via_behind, behind, via_ahead):
    rows, whole = ahead.shape
    low = via_behind.shape[1]

    def body(a_ref, va_ref, b_ref, vb_ref, out_a, out_b):
        out_a[:, :low] = (a_ref[:, :low].astype(f32) + va_ref[...].astype(f32)).astype(bf16)
        out_a[:, low:] = a_ref[:, low:]
        out_b[:, :low] = b_ref[:, :low]
        out_b[:, low:] = (b_ref[:, low:].astype(f32) + vb_ref[...].astype(f32)).astype(bf16)

    arrays = (ahead, via_behind, behind, via_ahead)
    return pl.pallas_call(
        body,
        out_shape=(jax.ShapeDtypeStruct((rows, whole), bf16),) * 2,
        grid=(1,),
        in_specs=[pl.BlockSpec(a.shape, lambda i: (0, 0)) for a in arrays],
        out_specs=[pl.BlockSpec((rows, whole), lambda i: (0, 0))] * 2,
        compiler_params=params(),
        cost_estimate=cost(2 * rows * whole, 10 * rows * whole),
    )(*arrays)


def output_ring(pieces, weights, axis):
    me, behind, ahead, far = ring_order(lax.axis_index(axis))
    shards = [2 * place + side for place in (far, ahead, behind, me) for side in range(2)]
    far_low, far_high, to_ahead, to_behind, mine = output_partial(shards, pieces, weights)
    to_ahead, to_behind = add_far(
        to_ahead, shift(far_low, axis, 1), to_behind, shift(far_high, axis, -1)
    )
    return mine, shift(to_behind, axis, -1), shift(to_ahead, axis, 1)


def finish(meta, parts, up, rank, wide):
    cuts = len(parts)
    rows, whole = parts[0][0].shape
    width = (whole - HEAD) // 2
    per = 2
    steps = rows // (per * BLOCK)
    terms = [t for cut in parts for t in cut]
    each = len(parts[0])

    def body(meta_ref, *refs):
        up_ref, out = refs[len(terms) :]
        i = pl.program_id(0)

        def put(mine):
            for k in range(per):
                at = slice(k * BLOCK, (k + 1) * BLOCK)
                block = i * per + k
                total = mine[0][at, :].astype(f32)
                for ref in mine[1:]:
                    total = total + ref[at, :].astype(f32)
                extra = jnp.dot(
                    total[:, width : width + rank].astype(bf16),
                    up_ref[meta_ref[0, block]],
                    preferred_element_type=f32,
                )
                row = block * BLOCK + lax.broadcasted_iota(i32, (BLOCK, width), 0)
                valid = row < meta_ref[4, block]
                for side, begin in enumerate((0, width + HEAD)):
                    cols = slice(side * width, (side + 1) * width)
                    out[at, cols] = jnp.where(
                        valid, total[:, begin : begin + width] + extra[:, cols], 0.0
                    )

        for cut in range(cuts):

            @pl.when(i // steps == cut)
            def _():
                put(refs[cut * each : (cut + 1) * each])

    def term_spec(cut):
        return pl.BlockSpec(
            (per * BLOCK, whole), lambda i, m: (jnp.clip(i - cut * steps, 0, steps - 1), 0)
        )

    return pl.pallas_call(
        body,
        out_shape=jax.ShapeDtypeStruct((cuts * rows, 2 * width), f32),
        grid_spec=pltpu.PrefetchScalarGridSpec(
            num_scalar_prefetch=1,
            grid=(cuts * steps,),
            in_specs=[term_spec(cut) for cut in range(cuts) for _ in range(each)]
            + [pl.BlockSpec((up.shape[0], rank, wide), lambda i, m: (0, 0, 1))],
            out_specs=pl.BlockSpec((per * BLOCK, 2 * width), lambda i, m: (i, 0)),
        ),
        compiler_params=params(),
        cost_estimate=cost(4 * cuts * rows * rank * width, 28 * cuts * rows * width),
    )(meta, *terms, up)


def on_device(x, wq, wkv, wo, down_qkv, up_q, up_kv, down_o, up_o, choice, counts, tails):
    z, c, y, xi = (lax.axis_index(n) for n in ADAPTER_AXES + TENSOR_AXES)
    group = z * CORES + c
    tokens, local = x.shape
    holders = down_qkv.shape[0]
    requests = choice.shape[1]
    wide = wq.shape[1]
    rank = up_q.shape[1]
    blocks = tokens // BLOCK

    owners = choice // holders
    pick = jnp.sum(jnp.where(owners == group, choice % holders, 0), axis=1).astype(i32)
    own_owner = lax.dynamic_index_in_dim(owners, group, 0, keepdims=False)
    req = jnp.arange(requests, dtype=i32)
    starts = jnp.sum(jnp.where(req[None, :] < req[:, None], counts[0][None, :], 0), axis=1)
    block = jnp.arange(blocks, dtype=i32)
    of_block = (starts[None, :] <= block[:, None]) & (
        block[:, None] < (starts + counts[0])[None, :]
    )

    def lookup(values):
        return jnp.sum(jnp.where(of_block, values[None, :], 0), axis=1).astype(i32)

    slot = lookup(own_owner)
    first = lookup(starts)
    limit = (first + lookup(counts[0]) - 1) * BLOCK + lookup(tails[0])
    is_key = jnp.broadcast_to(1 - xi % 2, (blocks,)).astype(i32)
    meta = jnp.stack([slot, block - first, first * BLOCK, is_key, limit]).astype(i32)

    cosine, sine = rotation_tables()

    stores = (jnp.swapaxes(down_qkv, 1, 2), up_q, up_kv, jnp.swapaxes(down_o, 1, 2), up_o)
    ys, xs = ring_order(y), ring_order(xi)
    unit = wo.shape[1] // (SIDE * SIDE * 2)
    wo_cols = jnp.stack(ys) * (2 * SIDE) + group
    down_out, up_out, x_a, x_b, *sent = pick_local(
        jnp.concatenate([pick, wo_cols.astype(i32)]), *stores, x, wo, unit
    )
    down = lax.all_to_all(down_out, ADAPTER_AXES, 0, 0, tiled=True)

    first_a = ring_gather(x_a, "x", x_a.shape[1] // 2)
    first_b = ring_gather(x_b, "y", x_b.shape[1] // 2)

    got = [sent[0], shift(sent[2], "y", 1), shift(sent[1], "y", -1), shift(sent[3], "y", 2)]
    low_a, high_a, low_b, high_b = join(
        [first_a[:2], first_a[2:], first_b[:2], first_b[2:]], got[1:]
    )
    wo_mine = stack_rows(got, [down, low_a])
    wo_all = lax.all_gather(wo_mine, ADAPTER_AXES, axis=0)
    far_a, next_a = second_gather(low_a, high_a, "y")
    far_b, next_b = second_gather(low_b, high_b, "x")

    def rows_a(k, cols):
        return [(ys[k] * SIDE + xs[j]) * 2 for j in cols]

    def rows_b(k, cols):
        return [(ys[j] * SIDE + xs[k]) * 2 + 1 for j in cols]

    def index_of(rows):
        return jnp.stack(rows).astype(i32)

    every = range(SIDE)
    low, high = (0, 1), (2, 3)
    total = project(
        (index_of(rows_a(0, every) + rows_b(0, every)), meta),
        None,
        [low_a, high_a, low_b, high_b],
        [wq, wkv],
        512,
    )

    pieces = scatter_rows(rank_partial(meta, x, down, 3 * rank, [low_a]))
    copies, up_out = share_sum(pieces, up_out, [total[1]])
    up = lax.all_to_all(up_out, ADAPTER_AXES, 0, 0, tiled=True)

    a_low, a_high = shift(far_a[0], "y", 1), shift(far_a[1], "y", -1)
    b_low, b_high = shift(far_b[0], "x", 1), shift(far_b[1], "x", -1)
    total = project(
        (
            index_of(rows_a(1, low) + rows_a(2, high) + rows_b(1, low) + rows_b(2, high)),
            meta,
        ),
        total,
        [*far_a, *far_b],
        [wq, wkv],
        512,
    )
    total = project(
        (
            index_of(rows_a(1, high) + rows_a(2, low) + rows_b(1, high) + rows_b(2, low)),
            meta,
        ),
        total,
        [*next_a, *next_b],
        [wq, wkv],
        512,
    )
    shrunk = lax.all_to_all(copies, TENSOR_AXES, 0, 0, tiled=True).reshape(tokens, 3 * rank)
    final = (index_of(rows_a(3, every) + rows_b(3, every)), meta)
    far = [a_low, a_high, b_low, b_high]
    tail = key_value_tail(shrunk, up, cosine, sine, wide, wkv.shape[1], 512)
    (mine,) = project(final, total[1:], far, [wkv], 512, tail)
    other = lax.ppermute(mine, "x", [(i, i ^ 1) for i in range(SIDE)])
    (q,) = project(final, total[:1], far, [wq], 512)

    cuts = 2
    each = blocks // cuts
    parts = []
    for cut in range(cuts):
        attended = attention(
            meta, q, shrunk, up, down, mine, other, cosine, sine, cut * each, each
        )
        parts.append(output_ring(ring_gather(attended, "y", wide // 2), wo_all, "x"))
    return finish(meta, parts, up, rank, wide)


def solution(mesh):
    fine = Mesh(mesh.devices.reshape(SIDE, CORES, SIDE, SIDE), ADAPTER_AXES + TENSOR_AXES)
    placed = (
        P(ADAPTER_AXES, TENSOR_AXES),
        P(None, TENSOR_AXES),
        P(None, TENSOR_AXES),
        P(TENSOR_AXES, None),
        P(ADAPTER_AXES, TENSOR_AXES, None),
        P(ADAPTER_AXES, None, TENSOR_AXES),
        P(ADAPTER_AXES, None, TENSOR_AXES),
        P(ADAPTER_AXES, TENSOR_AXES, None),
        P(ADAPTER_AXES, None, TENSOR_AXES),
        P(),
        P(ADAPTER_AXES, None),
        P(ADAPTER_AXES, None),
    )
    return jax.shard_map(
        on_device,
        mesh=fine,
        in_specs=placed,
        out_specs=P(ADAPTER_AXES, TENSOR_AXES),
        check_vma=False,
    )
```

```python
import math

import jax
import jax.numpy as jnp
import numpy as np
from jax import lax
from jax.experimental import pallas as pl
from jax.experimental.pallas import tpu as pltpu
from jax.sharding import Mesh, PartitionSpec as P

HEAD = 128
BLOCK = 128
SIDE = 4
CORES = 2
ADAPTER_AXES = ("z", "c")
TENSOR_AXES = ("y", "x")
ROPE_BASE = 500000.0
VMEM = 56 * 1024 * 1024
bf16 = jnp.bfloat16
f32 = jnp.float32
i32 = jnp.int32


def params():
    return pltpu.CompilerParams(vmem_limit_bytes=VMEM)


def passive(arrays):
    return [pl.BlockSpec(memory_space=pl.ANY)] * len(arrays)


def cost(flops, moved, exps=0):
    return pl.CostEstimate(flops=flops, bytes_accessed=moved, transcendentals=exps)


def shift(block, axis, step):
    return lax.ppermute(block, axis, [(i, (i + step) % SIDE) for i in range(SIDE)])


def ring_gather(block, axis, half):
    behind = shift(block, axis, 1)
    ahead = shift(block, axis, -1)
    far_low = shift(behind[:, :half], axis, 1)
    far_high = shift(ahead[:, half:], axis, -1)
    return block, behind, ahead, far_low, far_high


def gather_onward(low, high, axis):
    return shift(low, axis, 1), shift(high, axis, -1)


def gather_next(low, high, axis):
    return shift(high, axis, 1), shift(low, axis, -1)


def ring_gather_whole(block, axis, step):
    behind = shift(block, axis, 1)
    ahead = shift(block, axis, -1)
    return block, behind, ahead, shift(behind if step == 1 else ahead, axis, step)


def ring_order(index):
    return [index, (index + SIDE - 1) % SIDE, (index + 1) % SIDE, (index + 2) % SIDE]


def pick_local(pick, down_qkv, up_q, up_kv, down_o, up_o, x, wo, unit):
    tokens, local = x.shape
    groups = pick.shape[0] - SIDE
    rank3, depth = down_qkv.shape[1:]
    rank, wide = up_q.shape[1:]
    narrow = up_kv.shape[2]
    rows = wo.shape[0] // groups

    def body(pick_ref, dq, uq, ukv, do, uo, x_ref, *refs):
        w_refs, (down, up, left, right), w_outs = refs[:SIDE], refs[SIDE : SIDE + 4], refs[SIDE + 4 :]
        left[...] = x_ref[:, : local // 2]
        right[...] = x_ref[:, local // 2 :]
        down[0, :rank3, :] = dq[0]
        down[0, rank3:, :] = do[0]
        up[0, :, :wide] = uq[0]
        up[0, :, wide : 2 * wide] = uo[0]
        up[0, :, 2 * wide :] = ukv[0]
        for w_ref, w_out in zip(w_refs, w_outs):
            w_out[...] = w_ref[...]

    def chosen(a):
        return pl.BlockSpec((1,) + a.shape[1:], lambda i, p: (p[i], 0, 0))

    def columns(k):
        return pl.BlockSpec((rows, unit), lambda i, p: (i, p[groups + k]))

    down_shape = (groups, rank3 + rank, depth)
    up_shape = (groups, rank, 2 * wide + narrow)
    half = (tokens, local // 2)
    share = (wo.shape[0], unit)
    return pl.pallas_call(
        body,
        out_shape=tuple(
            jax.ShapeDtypeStruct(s, bf16)
            for s in (down_shape, up_shape, half, half, share, share, share, share)
        ),
        grid_spec=pltpu.PrefetchScalarGridSpec(
            num_scalar_prefetch=1,
            grid=(groups,),
            in_specs=[chosen(a) for a in (down_qkv, up_q, up_kv, down_o, up_o)]
            + [pl.BlockSpec((tokens // groups, local), lambda i, p: (i, 0))]
            + [columns(k) for k in range(SIDE)],
            out_specs=[
                pl.BlockSpec((1,) + s[1:], lambda i, p: (i, 0, 0)) for s in (down_shape, up_shape)
            ]
            + [pl.BlockSpec((tokens // groups, local // 2), lambda i, p: (i, 0))] * 2
            + [pl.BlockSpec((rows, unit), lambda i, p: (i, 0))] * SIDE,
        ),
        compiler_params=params(),
        cost_estimate=cost(0, 2 * 2 * (math.prod(down_shape) + math.prod(up_shape))),
    )(pick, down_qkv, up_q, up_kv, down_o, up_o, x, wo, wo, wo, wo)


def stack_rows(blocks, after):
    rows, width = blocks[0].shape
    count = len(blocks)

    def body(*refs):
        out = refs[-1]
        for k in range(count):
            out[k * rows : (k + 1) * rows, :] = refs[k][...]

    spec = pl.BlockSpec((rows, width), lambda i: (0, 0))
    return pl.pallas_call(
        body,
        out_shape=jax.ShapeDtypeStruct((count * rows, width), bf16),
        grid=(1,),
        in_specs=[spec] * count + passive(after),
        out_specs=pl.BlockSpec((count * rows, width), lambda i: (0, 0)),
        compiler_params=params(),
        cost_estimate=cost(0, 4 * count * rows * width),
    )(*blocks, *after)


def rank_partial(meta, x, down, rank3, after):
    tokens, depth = x.shape
    per = 2
    rows = per * BLOCK

    def body(meta_ref, x_ref, *rest):
        d_refs, out = rest[:per], rest[-1]
        for k in range(per):
            at = slice(k * BLOCK, (k + 1) * BLOCK)
            out[at, :] = lax.dot_general(
                x_ref[at, :], d_refs[k][0], (((1,), (1,)), ((), ())), preferred_element_type=f32
            )

    def chosen(k):
        return pl.BlockSpec((1, rank3, depth), lambda i, m: (m[0, i * per + k], 0, 0))

    return pl.pallas_call(
        body,
        out_shape=jax.ShapeDtypeStruct((tokens, rank3), f32),
        grid_spec=pltpu.PrefetchScalarGridSpec(
            num_scalar_prefetch=1,
            grid=(tokens // rows,),
            in_specs=[pl.BlockSpec((rows, depth), lambda i, m: (i, 0))]
            + [chosen(k) for k in range(per)]
            + passive(after),
            out_specs=pl.BlockSpec((rows, rank3), lambda i, m: (i, 0)),
        ),
        compiler_params=params(),
        cost_estimate=cost(2 * tokens * depth * rank3, 2 * tokens * depth + 8 * tokens * rank3),
    )(meta, x, *[down] * per, *after)


def join(groups, after):
    tokens = groups[0][0].shape[0]
    rows = 256
    flat = [b for group in groups for b in group]
    widths = [sum(b.shape[1] for b in group) for group in groups]

    def body(*refs):
        ins, outs = refs[: len(flat)], refs[len(flat) + len(after) :]
        at = 0
        for out, group in zip(outs, groups):
            col = 0
            for b in group:
                out[:, col : col + b.shape[1]] = ins[at][...]
                col += b.shape[1]
                at += 1

    return pl.pallas_call(
        body,
        out_shape=tuple(jax.ShapeDtypeStruct((tokens, w), bf16) for w in widths),
        grid=(tokens // rows,),
        in_specs=[pl.BlockSpec((rows, b.shape[1]), lambda i: (i, 0)) for b in flat]
        + passive(after),
        out_specs=[pl.BlockSpec((rows, w), lambda i: (i, 0)) for w in widths],
        compiler_params=params(),
        cost_estimate=cost(0, 4 * tokens * sum(widths)),
    )(*flat, *after)


def share_sum(pieces, onward, after):
    ways, rows, rank = pieces.shape

    def body(p_ref, *refs):
        out = refs[-2]
        total = p_ref[0]
        for k in range(1, ways):
            total = total + p_ref[k]
        for k in range(ways):
            out[k] = total.astype(bf16)

    whole = pl.BlockSpec(pieces.shape, lambda i: (0, 0, 0))
    return pl.pallas_call(
        body,
        out_shape=(
            jax.ShapeDtypeStruct(pieces.shape, bf16),
            jax.ShapeDtypeStruct(onward.shape, onward.dtype),
        ),
        grid=(1,),
        in_specs=[whole] + passive([onward, *after]),
        out_specs=[whole] + passive([onward]),
        input_output_aliases={1: 1},
        compiler_params=params(),
        cost_estimate=cost(ways * rows * rank, 6 * ways * rows * rank),
    )(pieces, onward, *after)


def scatter_rows(partial):
    rows, rank = partial.shape
    ways = SIDE * SIDE
    return lax.all_to_all(
        partial.reshape(ways, rows // ways, rank), TENSOR_AXES, 0, 0, tiled=True
    )


def project(index, total, blocks, weights, tile, last=None, after=(), rows=256):
    tokens = blocks[0].shape[0]
    counts = [b.shape[1] // rows for b in blocks]
    pieces = sum(counts)
    kinds = len(weights)
    first = total is None
    tail, tail_operands, tail_specs, dtype = last or (None, [], [], f32)

    def body(index_ref, meta_ref, *refs):
        x_refs = refs[: len(blocks)]
        w_refs = refs[len(blocks) : len(blocks) + kinds * pieces]
        rest = refs[len(blocks) + kinds * pieces :]
        outs = rest[len(rest) - kinds :]
        for kind in range(kinds):
            mine = w_refs[kind * pieces : (kind + 1) * pieces]
            acc = None if first else rest[kind][...]
            at = 0
            for x_ref, n in zip(x_refs, counts):
                w = jnp.concatenate([r[...] for r in mine[at : at + n]], axis=0)
                add = jnp.dot(x_ref[...], w, preferred_element_type=f32)
                acc = add if acc is None else acc + add
                at += n
            if tail is not None:
                acc = tail(meta_ref, acc, rest[kinds : kinds + len(tail_operands)])
            outs[kind][...] = acc

    def weight(k, width):
        return pl.BlockSpec((rows, width), lambda i, p, m: (p[k], 0))

    widths = [w.shape[1] for w in weights]
    row_specs = [pl.BlockSpec((tile, w), lambda i, p, m: (i, 0)) for w in widths]
    in_specs = [pl.BlockSpec((tile, b.shape[1]), lambda i, p, m: (i, 0)) for b in blocks]
    operands = list(blocks)
    for w in weights:
        in_specs += [weight(k, w.shape[1]) for k in range(pieces)]
        operands += [w] * pieces
    aliases = {}
    if not first:
        if tail is None:
            aliases = {2 + len(operands) + k: k for k in range(kinds)}
        in_specs += row_specs
        operands += list(total)
    index, meta = index
    depth = pieces * rows
    return pl.pallas_call(
        body,
        out_shape=tuple(jax.ShapeDtypeStruct((tokens, w), dtype) for w in widths),
        grid_spec=pltpu.PrefetchScalarGridSpec(
            num_scalar_prefetch=2,
            grid=(tokens // tile,),
            in_specs=in_specs + tail_specs + passive(after),
            out_specs=row_specs,
        ),
        input_output_aliases=aliases,
        compiler_params=params(),
        cost_estimate=cost(
            2 * tokens * depth * sum(widths),
            2 * depth * (tokens + sum(widths)) + 8 * tokens * sum(widths),
        ),
    )(index, meta, *operands, *tail_operands, *after)


def key_value_tail(shrunk, up, cosine, sine, wide, narrow, tile):
    rank = shrunk.shape[1] // 3
    per = tile // BLOCK

    def tail(meta_ref, acc, refs):
        s_ref, up_ref, c_ref, n_ref = refs
        i = pl.program_id(0)
        is_key = meta_ref[3, 0] == 1
        done = []
        for k in range(per):
            at = slice(k * BLOCK, (k + 1) * BLOCK)
            s = s_ref[at, :].astype(f32)
            rank_in = jnp.where(is_key, s[:, rank : 2 * rank], s[:, 2 * rank :]).astype(bf16)
            u = acc[at, :] + jnp.dot(
                rank_in, up_ref[meta_ref[0, i * per + k]], preferred_element_type=f32
            )
            place = meta_ref[1, i * per + k]
            turned = u * c_ref[place] + pltpu.roll(u, HEAD // 2, 1) * n_ref[place]
            done.append(jnp.where(is_key, turned, u).astype(bf16))
        return jnp.concatenate(done, axis=0)

    specs = [
        pl.BlockSpec((tile, 3 * rank), lambda i, p, m: (i, 0)),
        pl.BlockSpec((up.shape[0], rank, narrow), lambda i, p, m: (0, 0, 2 * wide // narrow)),
        pl.BlockSpec(cosine.shape, lambda i, p, m: (0, 0, 0)),
        pl.BlockSpec(sine.shape, lambda i, p, m: (0, 0, 0)),
    ]
    return tail, [shrunk, up, cosine, sine], specs, bf16


def rotation_tables():
    freq = np.exp(-(2.0 * np.arange(HEAD // 2, dtype=np.float32) / HEAD) * math.log(ROPE_BASE))
    angle = np.arange(3 * BLOCK, dtype=np.float32)[:, None] * freq.astype(np.float32)[None, :]
    cosine = np.concatenate([np.cos(angle)] * 2, axis=1)
    sine = np.concatenate([-np.sin(angle), np.sin(angle)], axis=1)
    shape = (3, BLOCK, HEAD)
    return (
        jnp.asarray(cosine.reshape(shape), f32),
        jnp.asarray(sine.reshape(shape), f32),
    )


def attention(meta, q, shrunk, up, down, mine, other, cosine, sine, begin, count):
    tokens, wide = q.shape
    rank = shrunk.shape[1] // 3
    heads = wide // HEAD
    window = min(3 * BLOCK, tokens)
    scale = 1.0 / math.sqrt(HEAD)

    def body(meta_ref, q_ref, s_ref, up_ref, d_ref, m_ref, o_ref, c_ref, n_ref, att):
        i = begin + pl.program_id(0)
        is_key = meta_ref[3, 0] == 1
        first = meta_ref[2, i]
        limit = meta_ref[4, i]
        u = q_ref[...] + jnp.dot(
            s_ref[...][:, :rank], up_ref[0], preferred_element_type=f32
        )
        start = pl.multiple_of(jnp.maximum(i - 2, 0) * BLOCK, BLOCK)
        own = m_ref[pl.ds(start, window), :]
        far = o_ref[pl.ds(start, window), :]
        keys = jnp.where(is_key, own, far)
        values = jnp.where(is_key, far, own)
        row = i * BLOCK + lax.broadcasted_iota(i32, (BLOCK, window), 0)
        col = start + lax.broadcasted_iota(i32, (BLOCK, window), 1)
        allowed = (col >= first) & (col <= row) & (col < limit)
        cosines = c_ref[0]
        sines = n_ref[0]
        turned = []
        for h in range(heads):
            part = u[:, h * HEAD : (h + 1) * HEAD]
            turned.append(
                (part * cosines + pltpu.roll(part, HEAD // 2, 1) * sines).astype(bf16)
            )
        scores = lax.dot_general(
            jnp.concatenate(turned, axis=0),
            keys,
            (((1,), (1,)), ((), ())),
            preferred_element_type=f32,
        )
        for h in range(heads):
            at = slice(h * HEAD, (h + 1) * HEAD)
            weights = jnp.where(allowed, jnp.exp(scores[at, :] * scale), 0.0)
            weights = weights * (1.0 / jnp.sum(weights, axis=1, keepdims=True))
            mixed = jnp.dot(weights.astype(bf16), values, preferred_element_type=f32)
            att[:, at] = mixed.astype(bf16)
        head = lax.dot_general(
            att[:, :wide], d_ref[0], (((1,), (1,)), ((), ())), preferred_element_type=f32
        )
        att[:, wide : wide + rank] = head.astype(bf16)
        att[:, wide + rank :] = jnp.zeros((BLOCK, HEAD - rank), bf16)

    table = pl.BlockSpec((1, BLOCK, HEAD), lambda i, m: (m[1, i + begin], 0, 0))
    whole = pl.BlockSpec((tokens, HEAD), lambda i, m: (0, 0))
    return pl.pallas_call(
        body,
        out_shape=jax.ShapeDtypeStruct((count * BLOCK, wide + HEAD), bf16),
        grid_spec=pltpu.PrefetchScalarGridSpec(
            num_scalar_prefetch=1,
            grid=(count,),
            in_specs=[
                pl.BlockSpec((BLOCK, wide), lambda i, m: (i + begin, 0)),
                pl.BlockSpec((BLOCK, 3 * rank), lambda i, m: (i + begin, 0)),
                pl.BlockSpec((1, rank, wide), lambda i, m: (m[0, i + begin], 0, 0)),
                pl.BlockSpec((1, rank, down.shape[2]), lambda i, m: (m[0, i + begin], 3, 0)),
                whole,
                whole,
                table,
                table,
            ],
            out_specs=pl.BlockSpec((BLOCK, wide + HEAD), lambda i, m: (i, 0)),
        ),
        compiler_params=params(),
        cost_estimate=cost(
            4 * count * BLOCK * window * wide, 8 * count * BLOCK * wide, heads * count * BLOCK * window
        ),
    )(meta, q, shrunk, up, down, mine, other, cosine, sine)


def output_partial(shards, pieces, weights):
    tokens = pieces[0].shape[0]
    count, (depth, width) = len(shards) // 2, weights.shape[1:]
    unit = depth // SIDE
    whole = 2 * width + HEAD
    low, high = slice(0, width), slice(width + HEAD, whole)

    def body(index_ref, *refs):
        x_refs, (w_low, w_high) = refs[:SIDE], refs[SIDE : SIDE + 2]
        outs, x_all = refs[SIDE + 2 : -1], refs[-1]
        step = pl.program_id(0)

        @pl.when(step == 0)
        def _():
            for k, ref in enumerate(x_refs):
                x_all[:, k * unit : (k + 1) * unit] = ref[:, :unit]
            rank = x_refs[0][:, unit:].astype(f32)
            for ref in x_refs[1:]:
                rank = rank + ref[:, unit:].astype(f32)
            for out in outs:
                out[:, width : width + HEAD] = rank.astype(out.dtype)

        first = jnp.dot(x_all[...], w_low[0], preferred_element_type=f32)
        second = jnp.dot(x_all[...], w_high[0], preferred_element_type=f32)
        for k, out in enumerate(outs):

            @pl.when(step == k)
            def _():
                out[:, low] = first.astype(out.dtype)
                out[:, high] = second.astype(out.dtype)

    dtypes = [bf16] * (count - 1) + [f32]
    return pl.pallas_call(
        body,
        out_shape=tuple(jax.ShapeDtypeStruct((tokens, whole), d) for d in dtypes),
        grid_spec=pltpu.PrefetchScalarGridSpec(
            num_scalar_prefetch=1,
            grid=(count,),
            in_specs=[pl.BlockSpec(p.shape, lambda j, d: (0, 0)) for p in pieces]
            + [pl.BlockSpec((1, depth, width), lambda j, d: (d[2 * j], 0, 0))]
            + [pl.BlockSpec((1, depth, width), lambda j, d: (d[2 * j + 1], 0, 0))],
            out_specs=[pl.BlockSpec((tokens, whole), lambda j, d: (0, 0))] * count,
            scratch_shapes=[pltpu.VMEM((tokens, depth), bf16)],
        ),
        compiler_params=params(),
        cost_estimate=cost(
            4 * tokens * depth * count * width, 2 * depth * (tokens + 2 * count * width)
        ),
    )(jnp.stack(shards).astype(i32), *pieces, weights, weights)


def output_ring(pieces, weights, axis, step):
    me, behind, ahead, far = ring_order(lax.axis_index(axis))
    shards = [2 * place + side for place in (far, ahead, behind, me) for side in range(2)]
    to_far, to_ahead, to_behind, mine = output_partial(shards, pieces, weights)
    passing = shift(to_far, axis, step)
    if step == 1:
        to_ahead = to_ahead + passing
    else:
        to_behind = to_behind + passing
    return mine, shift(to_behind, axis, -1), shift(to_ahead, axis, 1)


def finish(meta, parts, up, rank, wide):
    cuts = len(parts)
    rows, whole = parts[0][0].shape
    width = (whole - HEAD) // 2
    per = 2
    steps = rows // (per * BLOCK)
    terms = [t for cut in parts for t in cut]
    each = len(parts[0])

    def body(meta_ref, *refs):
        up_ref, out = refs[len(terms) :]
        i = pl.program_id(0)

        def put(mine):
            for k in range(per):
                at = slice(k * BLOCK, (k + 1) * BLOCK)
                block = i * per + k
                total = mine[0][at, :].astype(f32)
                for ref in mine[1:]:
                    total = total + ref[at, :].astype(f32)
                extra = jnp.dot(
                    total[:, width : width + rank].astype(bf16),
                    up_ref[meta_ref[0, block]],
                    preferred_element_type=f32,
                )
                row = block * BLOCK + lax.broadcasted_iota(i32, (BLOCK, width), 0)
                valid = row < meta_ref[4, block]
                for side, begin in enumerate((0, width + HEAD)):
                    cols = slice(side * width, (side + 1) * width)
                    out[at, cols] = jnp.where(
                        valid, total[:, begin : begin + width] + extra[:, cols], 0.0
                    )

        for cut in range(cuts):

            @pl.when(i // steps == cut)
            def _():
                put(refs[cut * each : (cut + 1) * each])

    def term_spec(cut):
        return pl.BlockSpec(
            (per * BLOCK, whole), lambda i, m: (jnp.clip(i - cut * steps, 0, steps - 1), 0)
        )

    return pl.pallas_call(
        body,
        out_shape=jax.ShapeDtypeStruct((cuts * rows, 2 * width), f32),
        grid_spec=pltpu.PrefetchScalarGridSpec(
            num_scalar_prefetch=1,
            grid=(cuts * steps,),
            in_specs=[term_spec(cut) for cut in range(cuts) for _ in range(each)]
            + [pl.BlockSpec((up.shape[0], rank, wide), lambda i, m: (0, 0, 1))],
            out_specs=pl.BlockSpec((per * BLOCK, 2 * width), lambda i, m: (i, 0)),
        ),
        compiler_params=params(),
        cost_estimate=cost(4 * cuts * rows * rank * width, 28 * cuts * rows * width),
    )(meta, *terms, up)


def on_device(x, wq, wkv, wo, down_qkv, up_q, up_kv, down_o, up_o, choice, counts, tails):
    z, c, y, xi = (lax.axis_index(n) for n in ADAPTER_AXES + TENSOR_AXES)
    group = z * CORES + c
    tokens, local = x.shape
    holders = down_qkv.shape[0]
    requests = choice.shape[1]
    wide = wq.shape[1]
    rank = up_q.shape[1]
    blocks = tokens // BLOCK

    owners = choice // holders
    pick = jnp.sum(jnp.where(owners == group, choice % holders, 0), axis=1).astype(i32)
    own_owner = lax.dynamic_index_in_dim(owners, group, 0, keepdims=False)
    req = jnp.arange(requests, dtype=i32)
    starts = jnp.sum(jnp.where(req[None, :] < req[:, None], counts[0][None, :], 0), axis=1)
    block = jnp.arange(blocks, dtype=i32)
    of_block = (starts[None, :] <= block[:, None]) & (
        block[:, None] < (starts + counts[0])[None, :]
    )

    def lookup(values):
        return jnp.sum(jnp.where(of_block, values[None, :], 0), axis=1).astype(i32)

    slot = lookup(own_owner)
    first = lookup(starts)
    limit = (first + lookup(counts[0]) - 1) * BLOCK + lookup(tails[0])
    is_key = jnp.broadcast_to(1 - xi % 2, (blocks,)).astype(i32)
    meta = jnp.stack([slot, block - first, first * BLOCK, is_key, limit]).astype(i32)

    cosine, sine = rotation_tables()

    stores = (jnp.swapaxes(down_qkv, 1, 2), up_q, up_kv, jnp.swapaxes(down_o, 1, 2), up_o)
    ys, xs = ring_order(y), ring_order(xi)
    unit = wo.shape[1] // (SIDE * SIDE * 2)
    wo_cols = jnp.stack(ys) * (2 * SIDE) + group
    down_out, up_out, x_a, x_b, *sent = pick_local(
        jnp.concatenate([pick, wo_cols.astype(i32)]), *stores, x, wo, unit
    )
    down = lax.all_to_all(down_out, ADAPTER_AXES, 0, 0, tiled=True)

    first_a = ring_gather(x_a, "x", x_a.shape[1] // 2)
    first_b = ring_gather(x_b, "y", x_b.shape[1] // 2)

    got = [sent[0], shift(sent[2], "y", 1), shift(sent[1], "y", -1), shift(sent[3], "y", 2)]
    halves = [first_a[:2], first_a[2:], first_b[:2], first_b[2:]]
    low_a, high_a, low_b, high_b = join(halves, got[1:])
    far_a = gather_onward(low_a, high_a, "y")
    far_b = gather_onward(low_b, high_b, "x")
    wo_mine = stack_rows(got, [down, low_a])
    wo_all = lax.all_gather(wo_mine, ADAPTER_AXES, axis=0)

    def rows_a(k, cols):
        return [(ys[k] * SIDE + xs[j]) * 2 for j in cols]

    def rows_b(k, cols):
        return [(ys[j] * SIDE + xs[k]) * 2 + 1 for j in cols]

    def index_of(rows):
        return jnp.stack(rows).astype(i32)

    every = range(SIDE)
    low, high = (0, 1), (2, 3)
    total = project(
        (index_of(rows_a(0, every) + rows_b(0, every)), meta),
        None,
        [low_a, high_a, low_b, high_b],
        [wq, wkv],
        512,
    )

    again = join(halves, [total[1]])
    next_a = gather_next(again[0], again[1], "y")
    next_b = gather_next(again[2], again[3], "x")

    pieces = scatter_rows(rank_partial(meta, x, down, 3 * rank, [low_a]))
    copies, up_out = share_sum(pieces, up_out, [total[1]])
    up = lax.all_to_all(up_out, ADAPTER_AXES, 0, 0, tiled=True)

    a_low, a_high = shift(far_a[0], "y", 1), shift(far_a[1], "y", -1)
    b_low, b_high = shift(far_b[0], "x", 1), shift(far_b[1], "x", -1)
    total = project(
        (
            index_of(rows_a(1, low) + rows_a(2, high) + rows_b(1, low) + rows_b(2, high)),
            meta,
        ),
        total,
        [*far_a, *far_b],
        [wq, wkv],
        512,
    )
    total = project(
        (
            index_of(rows_a(1, high) + rows_a(2, low) + rows_b(1, high) + rows_b(2, low)),
            meta,
        ),
        total,
        [*next_a, *next_b],
        [wq, wkv],
        512,
    )
    shrunk = lax.all_to_all(copies, TENSOR_AXES, 0, 0, tiled=True).reshape(tokens, 3 * rank)
    final = (index_of(rows_a(3, every) + rows_b(3, every)), meta)
    far = [a_low, a_high, b_low, b_high]
    tail = key_value_tail(shrunk, up, cosine, sine, wide, wkv.shape[1], 512)
    (mine,) = project(final, total[1:], far, [wkv], 512, tail)
    other = lax.ppermute(mine, "x", [(i, i ^ 1) for i in range(SIDE)])
    (q,) = project(final, total[:1], far, [wq], 512)

    cuts = 2
    each = blocks // cuts
    parts = []
    for cut in range(cuts):
        attended = attention(
            meta, q, shrunk, up, down, mine, other, cosine, sine, cut * each, each
        )
        step = 1 - 2 * cut
        parts.append(output_ring(ring_gather_whole(attended, "y", step), wo_all, "x", step))
    return finish(meta, parts, up, rank, wide)


def solution(mesh):
    fine = Mesh(mesh.devices.reshape(SIDE, CORES, SIDE, SIDE), ADAPTER_AXES + TENSOR_AXES)
    placed = (
        P(ADAPTER_AXES, TENSOR_AXES),
        P(None, TENSOR_AXES),
        P(None, TENSOR_AXES),
        P(TENSOR_AXES, None),
        P(ADAPTER_AXES, TENSOR_AXES, None),
        P(ADAPTER_AXES, None, TENSOR_AXES),
        P(ADAPTER_AXES, None, TENSOR_AXES),
        P(ADAPTER_AXES, TENSOR_AXES, None),
        P(ADAPTER_AXES, None, TENSOR_AXES),
        P(),
        P(ADAPTER_AXES, None),
        P(ADAPTER_AXES, None),
    )
    return jax.shard_map(
        on_device,
        mesh=fine,
        in_specs=placed,
        out_specs=P(ADAPTER_AXES, TENSOR_AXES),
        check_vma=False,
    )
```

```python
import math

import jax
import jax.numpy as jnp
import numpy as np
from jax import lax
from jax.experimental import pallas as pl
from jax.experimental.pallas import tpu as pltpu
from jax.sharding import Mesh, PartitionSpec as P

HEAD = 128
BLOCK = 128
SIDE = 4
CORES = 2
ADAPTER_AXES = ("z", "c")
TENSOR_AXES = ("y", "x")
ROPE_BASE = 500000.0
VMEM = 56 * 1024 * 1024
bf16 = jnp.bfloat16
f32 = jnp.float32
i32 = jnp.int32


def params():
    return pltpu.CompilerParams(vmem_limit_bytes=VMEM)


def passive(arrays):
    return [pl.BlockSpec(memory_space=pl.ANY)] * len(arrays)


def cost(flops, moved, exps=0):
    return pl.CostEstimate(flops=flops, bytes_accessed=moved, transcendentals=exps)


def shift(block, axis, step):
    return lax.ppermute(block, axis, [(i, (i + step) % SIDE) for i in range(SIDE)])


def ring_gather(block, axis, half):
    behind = shift(block, axis, 1)
    ahead = shift(block, axis, -1)
    far_low = shift(behind[:, :half], axis, 1)
    far_high = shift(ahead[:, half:], axis, -1)
    return block, behind, ahead, far_low, far_high


def ring_gather_rows(block, axis):
    half = block.shape[0] // 2
    behind = shift(block, axis, 1)
    ahead = shift(block, axis, -1)
    return block, behind, ahead, (shift(behind[:half], axis, 1), shift(ahead[half:], axis, -1))


def ring_gather_whole(block, axis, step):
    behind = shift(block, axis, 1)
    ahead = shift(block, axis, -1)
    return block, behind, ahead, shift(behind if step == 1 else ahead, axis, step)


def ring_order(index):
    return [index, (index + SIDE - 1) % SIDE, (index + 1) % SIDE, (index + 2) % SIDE]


def pick_local(pick, down_qkv, up_q, up_kv, down_o, up_o, x, wo, unit):
    tokens, local = x.shape
    groups = pick.shape[0] - SIDE
    rank3, depth = down_qkv.shape[1:]
    rank, wide = up_q.shape[1:]
    narrow = up_kv.shape[2]
    rows = wo.shape[0] // groups

    def body(pick_ref, dq, uq, ukv, do, uo, x_ref, *refs):
        w_refs, (down, up, left, right), w_outs = refs[:SIDE], refs[SIDE : SIDE + 4], refs[SIDE + 4 :]
        left[...] = x_ref[:, : local // 2]
        right[...] = x_ref[:, local // 2 :]
        down[0, :rank3, :] = dq[0]
        down[0, rank3:, :] = do[0]
        up[0, :, :wide] = uq[0]
        up[0, :, wide : 2 * wide] = uo[0]
        up[0, :, 2 * wide :] = ukv[0]
        for w_ref, w_out in zip(w_refs, w_outs):
            w_out[...] = w_ref[...]

    def chosen(a):
        return pl.BlockSpec((1,) + a.shape[1:], lambda i, p: (p[i], 0, 0))

    def columns(k):
        return pl.BlockSpec((rows, unit), lambda i, p: (i, p[groups + k]))

    down_shape = (groups, rank3 + rank, depth)
    up_shape = (groups, rank, 2 * wide + narrow)
    half = (tokens, local // 2)
    share = (wo.shape[0], unit)
    return pl.pallas_call(
        body,
        out_shape=tuple(
            jax.ShapeDtypeStruct(s, bf16)
            for s in (down_shape, up_shape, half, half, share, share, share, share)
        ),
        grid_spec=pltpu.PrefetchScalarGridSpec(
            num_scalar_prefetch=1,
            grid=(groups,),
            in_specs=[chosen(a) for a in (down_qkv, up_q, up_kv, down_o, up_o)]
            + [pl.BlockSpec((tokens // groups, local), lambda i, p: (i, 0))]
            + [columns(k) for k in range(SIDE)],
            out_specs=[
                pl.BlockSpec((1,) + s[1:], lambda i, p: (i, 0, 0)) for s in (down_shape, up_shape)
            ]
            + [pl.BlockSpec((tokens // groups, local // 2), lambda i, p: (i, 0))] * 2
            + [pl.BlockSpec((rows, unit), lambda i, p: (i, 0))] * SIDE,
        ),
        compiler_params=params(),
        cost_estimate=cost(0, 2 * 2 * (math.prod(down_shape) + math.prod(up_shape))),
    )(pick, down_qkv, up_q, up_kv, down_o, up_o, x, wo, wo, wo, wo)


def stack_rows(blocks, after):
    rows, width = blocks[0].shape
    count = len(blocks)

    def body(*refs):
        out = refs[-1]
        for k in range(count):
            out[k * rows : (k + 1) * rows, :] = refs[k][...]

    spec = pl.BlockSpec((rows, width), lambda i: (0, 0))
    return pl.pallas_call(
        body,
        out_shape=jax.ShapeDtypeStruct((count * rows, width), bf16),
        grid=(1,),
        in_specs=[spec] * count + passive(after),
        out_specs=pl.BlockSpec((count * rows, width), lambda i: (0, 0)),
        compiler_params=params(),
        cost_estimate=cost(0, 4 * count * rows * width),
    )(*blocks, *after)


def rank_partial(meta, x, down, rank3, after):
    tokens, depth = x.shape
    per = 2
    rows = per * BLOCK

    def body(meta_ref, x_ref, *rest):
        d_refs, out = rest[:per], rest[-1]
        for k in range(per):
            at = slice(k * BLOCK, (k + 1) * BLOCK)
            out[at, :] = lax.dot_general(
                x_ref[at, :], d_refs[k][0], (((1,), (1,)), ((), ())), preferred_element_type=f32
            )

    def chosen(k):
        return pl.BlockSpec((1, rank3, depth), lambda i, m: (m[0, i * per + k], 0, 0))

    return pl.pallas_call(
        body,
        out_shape=jax.ShapeDtypeStruct((tokens, rank3), f32),
        grid_spec=pltpu.PrefetchScalarGridSpec(
            num_scalar_prefetch=1,
            grid=(tokens // rows,),
            in_specs=[pl.BlockSpec((rows, depth), lambda i, m: (i, 0))]
            + [chosen(k) for k in range(per)]
            + passive(after),
            out_specs=pl.BlockSpec((rows, rank3), lambda i, m: (i, 0)),
        ),
        compiler_params=params(),
        cost_estimate=cost(2 * tokens * depth * rank3, 2 * tokens * depth + 8 * tokens * rank3),
    )(meta, x, *[down] * per, *after)


def join(groups, after):
    tokens = groups[0][0].shape[0]
    rows = 256
    flat = [b for group in groups for b in group]
    widths = [sum(b.shape[1] for b in group) for group in groups]

    def body(*refs):
        ins, outs = refs[: len(flat)], refs[len(flat) + len(after) :]
        at = 0
        for out, group in zip(outs, groups):
            col = 0
            for b in group:
                out[:, col : col + b.shape[1]] = ins[at][...]
                col += b.shape[1]
                at += 1

    return pl.pallas_call(
        body,
        out_shape=tuple(jax.ShapeDtypeStruct((tokens, w), bf16) for w in widths),
        grid=(tokens // rows,),
        in_specs=[pl.BlockSpec((rows, b.shape[1]), lambda i: (i, 0)) for b in flat]
        + passive(after),
        out_specs=[pl.BlockSpec((rows, w), lambda i: (i, 0)) for w in widths],
        compiler_params=params(),
        cost_estimate=cost(0, 4 * tokens * sum(widths)),
    )(*flat, *after)


def share_sum(pieces, onward, after):
    ways, rows, rank = pieces.shape

    def body(p_ref, *refs):
        out = refs[-2]
        total = p_ref[0]
        for k in range(1, ways):
            total = total + p_ref[k]
        for k in range(ways):
            out[k] = total.astype(bf16)

    whole = pl.BlockSpec(pieces.shape, lambda i: (0, 0, 0))
    return pl.pallas_call(
        body,
        out_shape=(
            jax.ShapeDtypeStruct(pieces.shape, bf16),
            jax.ShapeDtypeStruct(onward.shape, onward.dtype),
        ),
        grid=(1,),
        in_specs=[whole] + passive([onward, *after]),
        out_specs=[whole] + passive([onward]),
        input_output_aliases={1: 1},
        compiler_params=params(),
        cost_estimate=cost(ways * rows * rank, 6 * ways * rows * rank),
    )(pieces, onward, *after)


def scatter_rows(partial):
    rows, rank = partial.shape
    ways = SIDE * SIDE
    return lax.all_to_all(
        partial.reshape(ways, rows // ways, rank), TENSOR_AXES, 0, 0, tiled=True
    )


def project(index, total, blocks, weights, tile, last=None, after=(), rows=256):
    split = isinstance(blocks[0], tuple)
    columns = [b[0] if split else b for b in blocks]
    tokens = columns[0].shape[0] * (2 if split else 1)
    counts = [b.shape[1] // rows for b in columns]
    pieces = sum(counts)
    inputs = [h for b in blocks for h in b] if split else list(blocks)
    kinds = len(weights)
    first = total is None
    tail, tail_operands, tail_specs, dtype = last or (None, [], [], f32)

    def body(index_ref, meta_ref, *refs):
        x_refs = refs[: len(inputs)]
        w_refs = refs[len(inputs) : len(inputs) + kinds * pieces]
        rest = refs[len(inputs) + kinds * pieces :]
        if split:
            top = pl.program_id(0) == 0
            xs = [
                jnp.where(top, x_refs[2 * k][...], x_refs[2 * k + 1][...])
                for k in range(len(blocks))
            ]
        else:
            xs = [ref[...] for ref in x_refs]
        outs = rest[len(rest) - kinds :]
        for kind in range(kinds):
            mine = w_refs[kind * pieces : (kind + 1) * pieces]
            acc = None if first else rest[kind][...]
            at = 0
            for x, n in zip(xs, counts):
                w = jnp.concatenate([r[...] for r in mine[at : at + n]], axis=0)
                add = jnp.dot(x, w, preferred_element_type=f32)
                acc = add if acc is None else acc + add
                at += n
            if tail is not None:
                acc = tail(meta_ref, acc, rest[kinds : kinds + len(tail_operands)])
            outs[kind][...] = acc

    def weight(k, width):
        return pl.BlockSpec((rows, width), lambda i, p, m: (p[k], 0))

    widths = [w.shape[1] for w in weights]
    row_specs = [pl.BlockSpec((tile, w), lambda i, p, m: (i, 0)) for w in widths]
    def row_block(b):
        return pl.BlockSpec((tile, b.shape[1]), lambda i, p, m: (0 if split else i, 0))

    in_specs = [row_block(b) for b in inputs]
    operands = list(inputs)
    for w in weights:
        in_specs += [weight(k, w.shape[1]) for k in range(pieces)]
        operands += [w] * pieces
    aliases = {}
    if not first:
        if tail is None:
            aliases = {2 + len(operands) + k: k for k in range(kinds)}
        in_specs += row_specs
        operands += list(total)
    index, meta = index
    depth = pieces * rows
    return pl.pallas_call(
        body,
        out_shape=tuple(jax.ShapeDtypeStruct((tokens, w), dtype) for w in widths),
        grid_spec=pltpu.PrefetchScalarGridSpec(
            num_scalar_prefetch=2,
            grid=(tokens // tile,),
            in_specs=in_specs + tail_specs + passive(after),
            out_specs=row_specs,
        ),
        input_output_aliases=aliases,
        compiler_params=params(),
        cost_estimate=cost(
            2 * tokens * depth * sum(widths),
            2 * depth * (tokens + sum(widths)) + 8 * tokens * sum(widths),
        ),
    )(index, meta, *operands, *tail_operands, *after)


def key_value_tail(shrunk, up, cosine, sine, wide, narrow, tile):
    rank = shrunk.shape[1] // 3
    per = tile // BLOCK

    def tail(meta_ref, acc, refs):
        s_ref, up_ref, c_ref, n_ref = refs
        i = pl.program_id(0)
        is_key = meta_ref[3, 0] == 1
        done = []
        for k in range(per):
            at = slice(k * BLOCK, (k + 1) * BLOCK)
            s = s_ref[at, :].astype(f32)
            rank_in = jnp.where(is_key, s[:, rank : 2 * rank], s[:, 2 * rank :]).astype(bf16)
            u = acc[at, :] + jnp.dot(
                rank_in, up_ref[meta_ref[0, i * per + k]], preferred_element_type=f32
            )
            place = meta_ref[1, i * per + k]
            turned = u * c_ref[place] + pltpu.roll(u, HEAD // 2, 1) * n_ref[place]
            done.append(jnp.where(is_key, turned, u).astype(bf16))
        return jnp.concatenate(done, axis=0)

    specs = [
        pl.BlockSpec((tile, 3 * rank), lambda i, p, m: (i, 0)),
        pl.BlockSpec((up.shape[0], rank, narrow), lambda i, p, m: (0, 0, 2 * wide // narrow)),
        pl.BlockSpec(cosine.shape, lambda i, p, m: (0, 0, 0)),
        pl.BlockSpec(sine.shape, lambda i, p, m: (0, 0, 0)),
    ]
    return tail, [shrunk, up, cosine, sine], specs, bf16


def rotation_tables():
    freq = np.exp(-(2.0 * np.arange(HEAD // 2, dtype=np.float32) / HEAD) * math.log(ROPE_BASE))
    angle = np.arange(3 * BLOCK, dtype=np.float32)[:, None] * freq.astype(np.float32)[None, :]
    cosine = np.concatenate([np.cos(angle)] * 2, axis=1)
    sine = np.concatenate([-np.sin(angle), np.sin(angle)], axis=1)
    shape = (3, BLOCK, HEAD)
    return (
        jnp.asarray(cosine.reshape(shape), f32),
        jnp.asarray(sine.reshape(shape), f32),
    )


def attention(meta, q, shrunk, up, down, mine, other, cosine, sine, begin, count):
    tokens, wide = q.shape
    rank = shrunk.shape[1] // 3
    heads = wide // HEAD
    window = min(3 * BLOCK, tokens)
    scale = 1.0 / math.sqrt(HEAD)

    def body(meta_ref, q_ref, s_ref, up_ref, d_ref, m_ref, o_ref, c_ref, n_ref, att):
        i = begin + pl.program_id(0)
        is_key = meta_ref[3, 0] == 1
        first = meta_ref[2, i]
        limit = meta_ref[4, i]
        u = q_ref[...] + jnp.dot(
            s_ref[...][:, :rank], up_ref[0], preferred_element_type=f32
        )
        start = pl.multiple_of(jnp.maximum(i - 2, 0) * BLOCK, BLOCK)
        own = m_ref[pl.ds(start, window), :]
        far = o_ref[pl.ds(start, window), :]
        keys = jnp.where(is_key, own, far)
        values = jnp.where(is_key, far, own)
        row = i * BLOCK + lax.broadcasted_iota(i32, (BLOCK, window), 0)
        col = start + lax.broadcasted_iota(i32, (BLOCK, window), 1)
        allowed = (col >= first) & (col <= row) & (col < limit)
        cosines = c_ref[0]
        sines = n_ref[0]
        turned = []
        for h in range(heads):
            part = u[:, h * HEAD : (h + 1) * HEAD]
            turned.append(
                (part * cosines + pltpu.roll(part, HEAD // 2, 1) * sines).astype(bf16)
            )
        scores = lax.dot_general(
            jnp.concatenate(turned, axis=0),
            keys,
            (((1,), (1,)), ((), ())),
            preferred_element_type=f32,
        )
        for h in range(heads):
            at = slice(h * HEAD, (h + 1) * HEAD)
            weights = jnp.where(allowed, jnp.exp(scores[at, :] * scale), 0.0)
            weights = weights * (1.0 / jnp.sum(weights, axis=1, keepdims=True))
            mixed = jnp.dot(weights.astype(bf16), values, preferred_element_type=f32)
            att[:, at] = mixed.astype(bf16)
        head = lax.dot_general(
            att[:, :wide], d_ref[0], (((1,), (1,)), ((), ())), preferred_element_type=f32
        )
        att[:, wide : wide + rank] = head.astype(bf16)
        att[:, wide + rank :] = jnp.zeros((BLOCK, HEAD - rank), bf16)

    table = pl.BlockSpec((1, BLOCK, HEAD), lambda i, m: (m[1, i + begin], 0, 0))
    whole = pl.BlockSpec((tokens, HEAD), lambda i, m: (0, 0))
    return pl.pallas_call(
        body,
        out_shape=jax.ShapeDtypeStruct((count * BLOCK, wide + HEAD), bf16),
        grid_spec=pltpu.PrefetchScalarGridSpec(
            num_scalar_prefetch=1,
            grid=(count,),
            in_specs=[
                pl.BlockSpec((BLOCK, wide), lambda i, m: (i + begin, 0)),
                pl.BlockSpec((BLOCK, 3 * rank), lambda i, m: (i + begin, 0)),
                pl.BlockSpec((1, rank, wide), lambda i, m: (m[0, i + begin], 0, 0)),
                pl.BlockSpec((1, rank, down.shape[2]), lambda i, m: (m[0, i + begin], 3, 0)),
                whole,
                whole,
                table,
                table,
            ],
            out_specs=pl.BlockSpec((BLOCK, wide + HEAD), lambda i, m: (i, 0)),
        ),
        compiler_params=params(),
        cost_estimate=cost(
            4 * count * BLOCK * window * wide, 8 * count * BLOCK * wide, heads * count * BLOCK * window
        ),
    )(meta, q, shrunk, up, down, mine, other, cosine, sine)


def output_partial(shards, pieces, weights, after):
    tokens = pieces[0].shape[0]
    count, (depth, width) = len(shards) // 2, weights.shape[1:]
    unit = depth // SIDE
    whole = 2 * width + HEAD
    low, high = slice(0, width), slice(width + HEAD, whole)

    def body(index_ref, *refs):
        x_refs, (w_low, w_high) = refs[:SIDE], refs[SIDE : SIDE + 2]
        outs, x_all = refs[-1 - count : -1], refs[-1]
        step = pl.program_id(0)

        @pl.when(step == 0)
        def _():
            for k, ref in enumerate(x_refs):
                x_all[:, k * unit : (k + 1) * unit] = ref[:, :unit]
            rank = x_refs[0][:, unit:].astype(f32)
            for ref in x_refs[1:]:
                rank = rank + ref[:, unit:].astype(f32)
            for out in outs:
                out[:, width : width + HEAD] = rank.astype(out.dtype)

        first = jnp.dot(x_all[...], w_low[0], preferred_element_type=f32)
        second = jnp.dot(x_all[...], w_high[0], preferred_element_type=f32)
        for k, out in enumerate(outs):

            @pl.when(step == k)
            def _():
                out[:, low] = first.astype(out.dtype)
                out[:, high] = second.astype(out.dtype)

    dtypes = [bf16] * (count - 1) + [f32]
    return pl.pallas_call(
        body,
        out_shape=tuple(jax.ShapeDtypeStruct((tokens, whole), d) for d in dtypes),
        grid_spec=pltpu.PrefetchScalarGridSpec(
            num_scalar_prefetch=1,
            grid=(count,),
            in_specs=[pl.BlockSpec(p.shape, lambda j, d: (0, 0)) for p in pieces]
            + [pl.BlockSpec((1, depth, width), lambda j, d: (d[2 * j], 0, 0))]
            + [pl.BlockSpec((1, depth, width), lambda j, d: (d[2 * j + 1], 0, 0))]
            + passive(after),
            out_specs=[pl.BlockSpec((tokens, whole), lambda j, d: (0, 0))] * count,
            scratch_shapes=[pltpu.VMEM((tokens, depth), bf16)],
        ),
        compiler_params=params(),
        cost_estimate=cost(
            4 * tokens * depth * count * width, 2 * depth * (tokens + 2 * count * width)
        ),
    )(jnp.stack(shards).astype(i32), *pieces, weights, weights, *after)


def handed_on(block, after):
    return pl.pallas_call(
        lambda *refs: None,
        out_shape=jax.ShapeDtypeStruct(block.shape, block.dtype),
        in_specs=passive([block, *after]),
        out_specs=pl.BlockSpec(memory_space=pl.ANY),
        input_output_aliases={0: 0},
        compiler_params=params(),
        cost_estimate=cost(0, 0),
    )(block, *after)


def output_ring(pieces, weights, axis, step, after):
    me, behind, ahead, far = ring_order(lax.axis_index(axis))
    shards = [2 * place + side for place in (far, ahead, behind, me) for side in range(2)]
    to_far, to_ahead, to_behind, mine = output_partial(shards, pieces, weights, after)
    passing = shift(to_far, axis, step)
    if step == 1:
        to_ahead = to_ahead + passing
    else:
        to_behind = to_behind + passing
    return (mine, shift(to_behind, axis, -1), shift(to_ahead, axis, 1)), to_far


def finish(meta, parts, up, rank, wide):
    cuts = len(parts)
    rows, whole = parts[0][0].shape
    width = (whole - HEAD) // 2
    per = 2
    steps = rows // (per * BLOCK)
    terms = [t for cut in parts for t in cut]
    each = len(parts[0])

    def body(meta_ref, *refs):
        up_ref, out = refs[len(terms) :]
        i = pl.program_id(0)

        def put(mine):
            for k in range(per):
                at = slice(k * BLOCK, (k + 1) * BLOCK)
                block = i * per + k
                total = mine[0][at, :].astype(f32)
                for ref in mine[1:]:
                    total = total + ref[at, :].astype(f32)
                extra = jnp.dot(
                    total[:, width : width + rank].astype(bf16),
                    up_ref[meta_ref[0, block]],
                    preferred_element_type=f32,
                )
                row = block * BLOCK + lax.broadcasted_iota(i32, (BLOCK, width), 0)
                valid = row < meta_ref[4, block]
                for side, begin in enumerate((0, width + HEAD)):
                    cols = slice(side * width, (side + 1) * width)
                    out[at, cols] = jnp.where(
                        valid, total[:, begin : begin + width] + extra[:, cols], 0.0
                    )

        for cut in range(cuts):

            @pl.when(i // steps == cut)
            def _():
                put(refs[cut * each : (cut + 1) * each])

    def term_spec(cut):
        return pl.BlockSpec(
            (per * BLOCK, whole), lambda i, m: (jnp.clip(i - cut * steps, 0, steps - 1), 0)
        )

    return pl.pallas_call(
        body,
        out_shape=jax.ShapeDtypeStruct((cuts * rows, 2 * width), f32),
        grid_spec=pltpu.PrefetchScalarGridSpec(
            num_scalar_prefetch=1,
            grid=(cuts * steps,),
            in_specs=[term_spec(cut) for cut in range(cuts) for _ in range(each)]
            + [pl.BlockSpec((up.shape[0], rank, wide), lambda i, m: (0, 0, 1))],
            out_specs=pl.BlockSpec((per * BLOCK, 2 * width), lambda i, m: (i, 0)),
        ),
        compiler_params=params(),
        cost_estimate=cost(4 * cuts * rows * rank * width, 28 * cuts * rows * width),
    )(meta, *terms, up)


def on_device(x, wq, wkv, wo, down_qkv, up_q, up_kv, down_o, up_o, choice, counts, tails):
    z, c, y, xi = (lax.axis_index(n) for n in ADAPTER_AXES + TENSOR_AXES)
    group = z * CORES + c
    tokens, local = x.shape
    holders = down_qkv.shape[0]
    requests = choice.shape[1]
    wide = wq.shape[1]
    rank = up_q.shape[1]
    blocks = tokens // BLOCK

    owners = choice // holders
    pick = jnp.sum(jnp.where(owners == group, choice % holders, 0), axis=1).astype(i32)
    own_owner = lax.dynamic_index_in_dim(owners, group, 0, keepdims=False)
    req = jnp.arange(requests, dtype=i32)
    starts = jnp.sum(jnp.where(req[None, :] < req[:, None], counts[0][None, :], 0), axis=1)
    block = jnp.arange(blocks, dtype=i32)
    of_block = (starts[None, :] <= block[:, None]) & (
        block[:, None] < (starts + counts[0])[None, :]
    )

    def lookup(values):
        return jnp.sum(jnp.where(of_block, values[None, :], 0), axis=1).astype(i32)

    slot = lookup(own_owner)
    first = lookup(starts)
    limit = (first + lookup(counts[0]) - 1) * BLOCK + lookup(tails[0])
    is_key = jnp.broadcast_to(1 - xi % 2, (blocks,)).astype(i32)
    meta = jnp.stack([slot, block - first, first * BLOCK, is_key, limit]).astype(i32)

    cosine, sine = rotation_tables()

    stores = (jnp.swapaxes(down_qkv, 1, 2), up_q, up_kv, jnp.swapaxes(down_o, 1, 2), up_o)
    ys, xs = ring_order(y), ring_order(xi)
    unit = wo.shape[1] // (SIDE * SIDE * 2)
    wo_cols = jnp.stack(ys) * (2 * SIDE) + group
    down_out, up_out, x_a, x_b, *sent = pick_local(
        jnp.concatenate([pick, wo_cols.astype(i32)]), *stores, x, wo, unit
    )
    down = lax.all_to_all(down_out, ADAPTER_AXES, 0, 0, tiled=True)

    first_a = ring_gather(x_a, "x", x_a.shape[1] // 2)
    first_b = ring_gather(x_b, "y", x_b.shape[1] // 2)

    got = [sent[0], shift(sent[2], "y", 1), shift(sent[1], "y", -1), shift(sent[3], "y", 2)]
    flat_a, flat_b = join([first_a, first_b], got[1:])
    a = ring_gather_rows(flat_a, "y")
    b = ring_gather_rows(flat_b, "x")
    wo_mine = stack_rows(got, [down, flat_a])
    wo_all = lax.all_gather(wo_mine, ADAPTER_AXES, axis=0)

    def rows_a(k, cols):
        return [(ys[k] * SIDE + xs[j]) * 2 for j in cols]

    def rows_b(k, cols):
        return [(ys[j] * SIDE + xs[k]) * 2 + 1 for j in cols]

    def index_of(rows):
        return jnp.stack(rows).astype(i32)

    every = range(SIDE)
    total = project(
        (index_of(rows_a(0, every) + rows_b(0, every)), meta), None, [a[0], b[0]], [wq, wkv], 512
    )

    pieces = scatter_rows(rank_partial(meta, x, down, 3 * rank, [flat_a]))
    copies, up_out = share_sum(pieces, up_out, [total[1]])
    up = lax.all_to_all(up_out, ADAPTER_AXES, 0, 0, tiled=True)

    total = project(
        (
            index_of(rows_a(1, every) + rows_a(2, every) + rows_b(1, every) + rows_b(2, every)),
            meta,
        ),
        total,
        [*a[1:3], *b[1:3]],
        [wq, wkv],
        512,
    )
    shrunk = lax.all_to_all(copies, TENSOR_AXES, 0, 0, tiled=True).reshape(tokens, 3 * rank)
    final = (index_of(rows_a(3, every) + rows_b(3, every)), meta)
    far = [a[3], b[3]]
    tail = key_value_tail(shrunk, up, cosine, sine, wide, wkv.shape[1], 512)
    (mine,) = project(final, total[1:], far, [wkv], 512, tail)
    other = lax.ppermute(mine, "x", [(i, i ^ 1) for i in range(SIDE)])
    (q,) = project(final, total[:1], far, [wq], 512)

    cuts = 2
    each = blocks // cuts
    parts = []
    for cut in range(cuts):
        attended = attention(
            meta, q, shrunk, up, down, mine, other, cosine, sine, cut * each, each
        )
        step = 1 - 2 * cut
        if cut > 0:
            attended = handed_on(attended, near)
        gathered = ring_gather_whole(attended, "y", step)
        near = gathered[1:3]
        terms, away = output_ring(gathered, wo_all, "x", step, [away] if cut > 0 else [])
        parts.append(terms)
    return finish(meta, parts, up, rank, wide)


def solution(mesh):
    fine = Mesh(mesh.devices.reshape(SIDE, CORES, SIDE, SIDE), ADAPTER_AXES + TENSOR_AXES)
    placed = (
        P(ADAPTER_AXES, TENSOR_AXES),
        P(None, TENSOR_AXES),
        P(None, TENSOR_AXES),
        P(TENSOR_AXES, None),
        P(ADAPTER_AXES, TENSOR_AXES, None),
        P(ADAPTER_AXES, None, TENSOR_AXES),
        P(ADAPTER_AXES, None, TENSOR_AXES),
        P(ADAPTER_AXES, TENSOR_AXES, None),
        P(ADAPTER_AXES, None, TENSOR_AXES),
        P(),
        P(ADAPTER_AXES, None),
        P(ADAPTER_AXES, None),
    )
    return jax.shard_map(
        on_device,
        mesh=fine,
        in_specs=placed,
        out_specs=P(ADAPTER_AXES, TENSOR_AXES),
        check_vma=False,
    )
```

```python
import math

import jax
import jax.numpy as jnp
import numpy as np
from jax import lax
from jax.experimental import pallas as pl
from jax.experimental.pallas import tpu as pltpu
from jax.sharding import Mesh, PartitionSpec as P

HEAD = 128
BLOCK = 128
SIDE = 4
CORES = 2
ADAPTER_AXES = ("z", "c")
TENSOR_AXES = ("y", "x")
ROPE_BASE = 500000.0
VMEM = 56 * 1024 * 1024
bf16 = jnp.bfloat16
f32 = jnp.float32
i32 = jnp.int32


def params():
    return pltpu.CompilerParams(vmem_limit_bytes=VMEM)


def passive(arrays):
    return [pl.BlockSpec(memory_space=pl.ANY)] * len(arrays)


def cost(flops, moved, exps=0):
    return pl.CostEstimate(flops=flops, bytes_accessed=moved, transcendentals=exps)


def shift(block, axis, step):
    return lax.ppermute(block, axis, [(i, (i + step) % SIDE) for i in range(SIDE)])


def ring_gather(block, axis, half):
    behind = shift(block, axis, 1)
    ahead = shift(block, axis, -1)
    far_low = shift(behind[:, :half], axis, 1)
    far_high = shift(ahead[:, half:], axis, -1)
    return block, behind, ahead, far_low, far_high


def gather_onward(low, high, axis):
    return shift(low, axis, 1), shift(high, axis, -1)


def gather_next(low, high, axis):
    return shift(high, axis, 1), shift(low, axis, -1)


def ring_order(index):
    return [index, (index + SIDE - 1) % SIDE, (index + 1) % SIDE, (index + 2) % SIDE]


def pick_local(pick, down_qkv, up_q, up_kv, down_o, up_o, x, wo, unit):
    tokens, local = x.shape
    groups = pick.shape[0] - SIDE
    rank3, depth = down_qkv.shape[1:]
    rank, wide = up_q.shape[1:]
    narrow = up_kv.shape[2]
    rows = wo.shape[0] // groups

    def body(pick_ref, dq, uq, ukv, do, uo, x_ref, *refs):
        w_refs, (down, up, left, right), w_outs = refs[:SIDE], refs[SIDE : SIDE + 4], refs[SIDE + 4 :]
        left[...] = x_ref[:, : local // 2]
        right[...] = x_ref[:, local // 2 :]
        down[0, :rank3, :] = dq[0]
        down[0, rank3:, :] = do[0]
        up[0, :, :wide] = uq[0]
        up[0, :, wide : 2 * wide] = uo[0]
        up[0, :, 2 * wide :] = ukv[0]
        for w_ref, w_out in zip(w_refs, w_outs):
            w_out[...] = w_ref[...]

    def chosen(a):
        return pl.BlockSpec((1,) + a.shape[1:], lambda i, p: (p[i], 0, 0))

    def columns(k):
        return pl.BlockSpec((rows, unit), lambda i, p: (i, p[groups + k]))

    down_shape = (groups, rank3 + rank, depth)
    up_shape = (groups, rank, 2 * wide + narrow)
    half = (tokens, local // 2)
    share = (wo.shape[0], unit)
    return pl.pallas_call(
        body,
        out_shape=tuple(
            jax.ShapeDtypeStruct(s, bf16)
            for s in (down_shape, up_shape, half, half, share, share, share, share)
        ),
        grid_spec=pltpu.PrefetchScalarGridSpec(
            num_scalar_prefetch=1,
            grid=(groups,),
            in_specs=[chosen(a) for a in (down_qkv, up_q, up_kv, down_o, up_o)]
            + [pl.BlockSpec((tokens // groups, local), lambda i, p: (i, 0))]
            + [columns(k) for k in range(SIDE)],
            out_specs=[
                pl.BlockSpec((1,) + s[1:], lambda i, p: (i, 0, 0)) for s in (down_shape, up_shape)
            ]
            + [pl.BlockSpec((tokens // groups, local // 2), lambda i, p: (i, 0))] * 2
            + [pl.BlockSpec((rows, unit), lambda i, p: (i, 0))] * SIDE,
        ),
        compiler_params=params(),
        cost_estimate=cost(0, 2 * 2 * (math.prod(down_shape) + math.prod(up_shape))),
    )(pick, down_qkv, up_q, up_kv, down_o, up_o, x, wo, wo, wo, wo)


def stack_rows(blocks, after):
    rows, width = blocks[0].shape
    count = len(blocks)

    def body(*refs):
        out = refs[-1]
        for k in range(count):
            out[k * rows : (k + 1) * rows, :] = refs[k][...]

    spec = pl.BlockSpec((rows, width), lambda i: (0, 0))
    return pl.pallas_call(
        body,
        out_shape=jax.ShapeDtypeStruct((count * rows, width), bf16),
        grid=(1,),
        in_specs=[spec] * count + passive(after),
        out_specs=pl.BlockSpec((count * rows, width), lambda i: (0, 0)),
        compiler_params=params(),
        cost_estimate=cost(0, 4 * count * rows * width),
    )(*blocks, *after)


def rank_partial(meta, x, down, rank3, after):
    tokens, depth = x.shape
    per = 2
    rows = per * BLOCK

    def body(meta_ref, x_ref, *rest):
        d_refs, out = rest[:per], rest[-1]
        for k in range(per):
            at = slice(k * BLOCK, (k + 1) * BLOCK)
            out[at, :] = lax.dot_general(
                x_ref[at, :], d_refs[k][0], (((1,), (1,)), ((), ())), preferred_element_type=f32
            )

    def chosen(k):
        return pl.BlockSpec((1, rank3, depth), lambda i, m: (m[0, i * per + k], 0, 0))

    return pl.pallas_call(
        body,
        out_shape=jax.ShapeDtypeStruct((tokens, rank3), f32),
        grid_spec=pltpu.PrefetchScalarGridSpec(
            num_scalar_prefetch=1,
            grid=(tokens // rows,),
            in_specs=[pl.BlockSpec((rows, depth), lambda i, m: (i, 0))]
            + [chosen(k) for k in range(per)]
            + passive(after),
            out_specs=pl.BlockSpec((rows, rank3), lambda i, m: (i, 0)),
        ),
        compiler_params=params(),
        cost_estimate=cost(2 * tokens * depth * rank3, 2 * tokens * depth + 8 * tokens * rank3),
    )(meta, x, *[down] * per, *after)


def join(groups, after):
    tokens = groups[0][0].shape[0]
    rows = 256
    flat = [b for group in groups for b in group]
    widths = [sum(b.shape[1] for b in group) for group in groups]

    def body(*refs):
        ins, outs = refs[: len(flat)], refs[len(flat) + len(after) :]
        at = 0
        for out, group in zip(outs, groups):
            col = 0
            for b in group:
                out[:, col : col + b.shape[1]] = ins[at][...]
                col += b.shape[1]
                at += 1

    return pl.pallas_call(
        body,
        out_shape=tuple(jax.ShapeDtypeStruct((tokens, w), bf16) for w in widths),
        grid=(tokens // rows,),
        in_specs=[pl.BlockSpec((rows, b.shape[1]), lambda i: (i, 0)) for b in flat]
        + passive(after),
        out_specs=[pl.BlockSpec((rows, w), lambda i: (i, 0)) for w in widths],
        compiler_params=params(),
        cost_estimate=cost(0, 4 * tokens * sum(widths)),
    )(*flat, *after)


def share_sum(pieces, onward, after):
    ways, rows, rank = pieces.shape

    def body(p_ref, *refs):
        out = refs[-2]
        total = p_ref[0]
        for k in range(1, ways):
            total = total + p_ref[k]
        for k in range(ways):
            out[k] = total.astype(bf16)

    whole = pl.BlockSpec(pieces.shape, lambda i: (0, 0, 0))
    return pl.pallas_call(
        body,
        out_shape=(
            jax.ShapeDtypeStruct(pieces.shape, bf16),
            jax.ShapeDtypeStruct(onward.shape, onward.dtype),
        ),
        grid=(1,),
        in_specs=[whole] + passive([onward, *after]),
        out_specs=[whole] + passive([onward]),
        input_output_aliases={1: 1},
        compiler_params=params(),
        cost_estimate=cost(ways * rows * rank, 6 * ways * rows * rank),
    )(pieces, onward, *after)


def scatter_rows(partial):
    rows, rank = partial.shape
    ways = SIDE * SIDE
    return lax.all_to_all(
        partial.reshape(ways, rows // ways, rank), TENSOR_AXES, 0, 0, tiled=True
    )


def project(index, total, blocks, weights, tile, last=None, after=(), rows=256):
    tokens = blocks[0].shape[0]
    counts = [b.shape[1] // rows for b in blocks]
    pieces = sum(counts)
    kinds = len(weights)
    first = total is None
    tail, tail_operands, tail_specs, dtype = last or (None, [], [], f32)

    def body(index_ref, meta_ref, *refs):
        x_refs = refs[: len(blocks)]
        w_refs = refs[len(blocks) : len(blocks) + kinds * pieces]
        rest = refs[len(blocks) + kinds * pieces :]
        outs = rest[len(rest) - kinds :]
        for kind in range(kinds):
            mine = w_refs[kind * pieces : (kind + 1) * pieces]
            acc = None if first else rest[kind][...]
            at = 0
            for x_ref, n in zip(x_refs, counts):
                w = jnp.concatenate([r[...] for r in mine[at : at + n]], axis=0)
                add = jnp.dot(x_ref[...], w, preferred_element_type=f32)
                acc = add if acc is None else acc + add
                at += n
            if tail is not None:
                acc = tail(meta_ref, acc, rest[kinds : kinds + len(tail_operands)])
            outs[kind][...] = acc

    def weight(k, width):
        return pl.BlockSpec((rows, width), lambda i, p, m: (p[k], 0))

    widths = [w.shape[1] for w in weights]
    row_specs = [pl.BlockSpec((tile, w), lambda i, p, m: (i, 0)) for w in widths]
    in_specs = [pl.BlockSpec((tile, b.shape[1]), lambda i, p, m: (i, 0)) for b in blocks]
    operands = list(blocks)
    for w in weights:
        in_specs += [weight(k, w.shape[1]) for k in range(pieces)]
        operands += [w] * pieces
    aliases = {}
    if not first:
        if tail is None:
            aliases = {2 + len(operands) + k: k for k in range(kinds)}
        in_specs += row_specs
        operands += list(total)
    index, meta = index
    depth = pieces * rows
    return pl.pallas_call(
        body,
        out_shape=tuple(jax.ShapeDtypeStruct((tokens, w), dtype) for w in widths),
        grid_spec=pltpu.PrefetchScalarGridSpec(
            num_scalar_prefetch=2,
            grid=(tokens // tile,),
            in_specs=in_specs + tail_specs + passive(after),
            out_specs=row_specs,
        ),
        input_output_aliases=aliases,
        compiler_params=params(),
        cost_estimate=cost(
            2 * tokens * depth * sum(widths),
            2 * depth * (tokens + sum(widths)) + 8 * tokens * sum(widths),
        ),
    )(index, meta, *operands, *tail_operands, *after)


def key_value_tail(shrunk, up, cosine, sine, wide, narrow, tile):
    rank = shrunk.shape[1] // 3
    per = tile // BLOCK

    def tail(meta_ref, acc, refs):
        s_ref, up_ref, c_ref, n_ref = refs
        i = pl.program_id(0)
        is_key = meta_ref[3, 0] == 1
        done = []
        for k in range(per):
            at = slice(k * BLOCK, (k + 1) * BLOCK)
            s = s_ref[at, :].astype(f32)
            rank_in = jnp.where(is_key, s[:, rank : 2 * rank], s[:, 2 * rank :]).astype(bf16)
            u = acc[at, :] + jnp.dot(
                rank_in, up_ref[meta_ref[0, i * per + k]], preferred_element_type=f32
            )
            place = meta_ref[1, i * per + k]
            turned = u * c_ref[place] + pltpu.roll(u, HEAD // 2, 1) * n_ref[place]
            done.append(jnp.where(is_key, turned, u).astype(bf16))
        return jnp.concatenate(done, axis=0)

    specs = [
        pl.BlockSpec((tile, 3 * rank), lambda i, p, m: (i, 0)),
        pl.BlockSpec((up.shape[0], rank, narrow), lambda i, p, m: (0, 0, 2 * wide // narrow)),
        pl.BlockSpec(cosine.shape, lambda i, p, m: (0, 0, 0)),
        pl.BlockSpec(sine.shape, lambda i, p, m: (0, 0, 0)),
    ]
    return tail, [shrunk, up, cosine, sine], specs, bf16


def rotation_tables():
    freq = np.exp(-(2.0 * np.arange(HEAD // 2, dtype=np.float32) / HEAD) * math.log(ROPE_BASE))
    angle = np.arange(3 * BLOCK, dtype=np.float32)[:, None] * freq.astype(np.float32)[None, :]
    cosine = np.concatenate([np.cos(angle)] * 2, axis=1)
    sine = np.concatenate([-np.sin(angle), np.sin(angle)], axis=1)
    shape = (3, BLOCK, HEAD)
    return (
        jnp.asarray(cosine.reshape(shape), f32),
        jnp.asarray(sine.reshape(shape), f32),
    )


def attention(meta, q, shrunk, up, down, mine, other, cosine, sine, begin, count):
    tokens, wide = q.shape
    rank = shrunk.shape[1] // 3
    heads = wide // HEAD
    window = min(3 * BLOCK, tokens)
    scale = 1.0 / math.sqrt(HEAD)

    def body(meta_ref, q_ref, s_ref, up_ref, d_ref, m_ref, o_ref, c_ref, n_ref, att):
        i = begin + pl.program_id(0)
        is_key = meta_ref[3, 0] == 1
        first = meta_ref[2, i]
        limit = meta_ref[4, i]
        u = q_ref[...] + jnp.dot(
            s_ref[...][:, :rank], up_ref[0], preferred_element_type=f32
        )
        start = pl.multiple_of(jnp.maximum(i - 2, 0) * BLOCK, BLOCK)
        own = m_ref[pl.ds(start, window), :]
        far = o_ref[pl.ds(start, window), :]
        keys = jnp.where(is_key, own, far)
        values = jnp.where(is_key, far, own)
        row = i * BLOCK + lax.broadcasted_iota(i32, (BLOCK, window), 0)
        col = start + lax.broadcasted_iota(i32, (BLOCK, window), 1)
        allowed = (col >= first) & (col <= row) & (col < limit)
        cosines = c_ref[0]
        sines = n_ref[0]
        turned = []
        for h in range(heads):
            part = u[:, h * HEAD : (h + 1) * HEAD]
            turned.append(
                (part * cosines + pltpu.roll(part, HEAD // 2, 1) * sines).astype(bf16)
            )
        scores = lax.dot_general(
            jnp.concatenate(turned, axis=0),
            keys,
            (((1,), (1,)), ((), ())),
            preferred_element_type=f32,
        )
        for h in range(heads):
            at = slice(h * HEAD, (h + 1) * HEAD)
            weights = jnp.where(allowed, jnp.exp(scores[at, :] * scale), 0.0)
            weights = weights * (1.0 / jnp.sum(weights, axis=1, keepdims=True))
            mixed = jnp.dot(weights.astype(bf16), values, preferred_element_type=f32)
            att[:, at] = mixed.astype(bf16)
        head = lax.dot_general(
            att[:, :wide], d_ref[0], (((1,), (1,)), ((), ())), preferred_element_type=f32
        )
        att[:, wide : wide + rank] = head.astype(bf16)
        att[:, wide + rank :] = jnp.zeros((BLOCK, HEAD - rank), bf16)

    table = pl.BlockSpec((1, BLOCK, HEAD), lambda i, m: (m[1, i + begin], 0, 0))
    whole = pl.BlockSpec((tokens, HEAD), lambda i, m: (0, 0))
    return pl.pallas_call(
        body,
        out_shape=jax.ShapeDtypeStruct((count * BLOCK, wide + HEAD), bf16),
        grid_spec=pltpu.PrefetchScalarGridSpec(
            num_scalar_prefetch=1,
            grid=(count,),
            in_specs=[
                pl.BlockSpec((BLOCK, wide), lambda i, m: (i + begin, 0)),
                pl.BlockSpec((BLOCK, 3 * rank), lambda i, m: (i + begin, 0)),
                pl.BlockSpec((1, rank, wide), lambda i, m: (m[0, i + begin], 0, 0)),
                pl.BlockSpec((1, rank, down.shape[2]), lambda i, m: (m[0, i + begin], 3, 0)),
                whole,
                whole,
                table,
                table,
            ],
            out_specs=pl.BlockSpec((BLOCK, wide + HEAD), lambda i, m: (i, 0)),
        ),
        compiler_params=params(),
        cost_estimate=cost(
            4 * count * BLOCK * window * wide, 8 * count * BLOCK * wide, heads * count * BLOCK * window
        ),
    )(meta, q, shrunk, up, down, mine, other, cosine, sine)


def output_partial(shards, pieces, weights):
    tokens = pieces[0].shape[0]
    count, (depth, width) = len(shards) // 2, weights.shape[1:]
    unit = depth // SIDE
    whole = 2 * width + HEAD
    cut = pieces[3].shape[1]
    low, high = slice(0, width), slice(width + HEAD, whole)

    def body(index_ref, *refs):
        x_refs, (w_low, w_high) = refs[: SIDE + 1], refs[SIDE + 1 : SIDE + 3]
        outs, x_all = refs[SIDE + 3 : -1], refs[-1]
        step = pl.program_id(0)

        @pl.when(step == 0)
        def _():
            rank = jnp.zeros((tokens, HEAD), f32)
            for ref, begin in zip(x_refs, (0, unit, 2 * unit, 3 * unit, 3 * unit + cut)):
                held = min(ref.shape[1], depth - begin, unit)
                x_all[:, begin : begin + held] = ref[:, :held]
                if held < ref.shape[1]:
                    rank = rank + ref[:, held:].astype(f32)
            for out in outs:
                out[:, width : width + HEAD] = rank.astype(out.dtype)

        first = jnp.dot(x_all[...], w_low[0], preferred_element_type=f32)
        second = jnp.dot(x_all[...], w_high[0], preferred_element_type=f32)
        for k, out in enumerate(outs):

            @pl.when(step == k)
            def _():
                out[:, low] = first.astype(out.dtype)
                out[:, high] = second.astype(out.dtype)

    dtypes = [bf16] * (count - 1) + [f32]
    return pl.pallas_call(
        body,
        out_shape=tuple(jax.ShapeDtypeStruct((tokens, whole), d) for d in dtypes),
        grid_spec=pltpu.PrefetchScalarGridSpec(
            num_scalar_prefetch=1,
            grid=(count,),
            in_specs=[pl.BlockSpec(p.shape, lambda j, d: (0, 0)) for p in pieces]
            + [pl.BlockSpec((1, depth, width), lambda j, d: (d[2 * j], 0, 0))]
            + [pl.BlockSpec((1, depth, width), lambda j, d: (d[2 * j + 1], 0, 0))],
            out_specs=[pl.BlockSpec((tokens, whole), lambda j, d: (0, 0))] * count,
            scratch_shapes=[pltpu.VMEM((tokens, depth), bf16)],
        ),
        compiler_params=params(),
        cost_estimate=cost(
            4 * tokens * depth * count * width, 2 * depth * (tokens + 2 * count * width)
        ),
    )(jnp.stack(shards).astype(i32), *pieces, weights, weights)


def output_ring(pieces, weights, axis, step):
    me, behind, ahead, far = ring_order(lax.axis_index(axis))
    shards = [2 * place + side for place in (far, ahead, behind, me) for side in range(2)]
    to_far, to_ahead, to_behind, mine = output_partial(shards, pieces, weights)
    passing = shift(to_far, axis, step)
    if step == 1:
        to_ahead = to_ahead + passing
    else:
        to_behind = to_behind + passing
    return mine, shift(to_behind, axis, -1), shift(to_ahead, axis, 1)


def finish(meta, parts, up, rank, wide):
    cuts = len(parts)
    rows, whole = parts[0][0].shape
    width = (whole - HEAD) // 2
    per = 2
    steps = rows // (per * BLOCK)
    terms = [t for cut in parts for t in cut]
    each = len(parts[0])

    def body(meta_ref, *refs):
        up_ref, out = refs[len(terms) :]
        i = pl.program_id(0)

        def put(mine):
            for k in range(per):
                at = slice(k * BLOCK, (k + 1) * BLOCK)
                block = i * per + k
                total = mine[0][at, :].astype(f32)
                for ref in mine[1:]:
                    total = total + ref[at, :].astype(f32)
                extra = jnp.dot(
                    total[:, width : width + rank].astype(bf16),
                    up_ref[meta_ref[0, block]],
                    preferred_element_type=f32,
                )
                row = block * BLOCK + lax.broadcasted_iota(i32, (BLOCK, width), 0)
                valid = row < meta_ref[4, block]
                for side, begin in enumerate((0, width + HEAD)):
                    cols = slice(side * width, (side + 1) * width)
                    out[at, cols] = jnp.where(
                        valid, total[:, begin : begin + width] + extra[:, cols], 0.0
                    )

        for cut in range(cuts):

            @pl.when(i // steps == cut)
            def _():
                put(refs[cut * each : (cut + 1) * each])

    def term_spec(cut):
        return pl.BlockSpec(
            (per * BLOCK, whole), lambda i, m: (jnp.clip(i - cut * steps, 0, steps - 1), 0)
        )

    return pl.pallas_call(
        body,
        out_shape=jax.ShapeDtypeStruct((cuts * rows, 2 * width), f32),
        grid_spec=pltpu.PrefetchScalarGridSpec(
            num_scalar_prefetch=1,
            grid=(cuts * steps,),
            in_specs=[term_spec(cut) for cut in range(cuts) for _ in range(each)]
            + [pl.BlockSpec((up.shape[0], rank, wide), lambda i, m: (0, 0, 1))],
            out_specs=pl.BlockSpec((per * BLOCK, 2 * width), lambda i, m: (i, 0)),
        ),
        compiler_params=params(),
        cost_estimate=cost(4 * cuts * rows * rank * width, 28 * cuts * rows * width),
    )(meta, *terms, up)


def on_device(x, wq, wkv, wo, down_qkv, up_q, up_kv, down_o, up_o, choice, counts, tails):
    z, c, y, xi = (lax.axis_index(n) for n in ADAPTER_AXES + TENSOR_AXES)
    group = z * CORES + c
    tokens, local = x.shape
    holders = down_qkv.shape[0]
    requests = choice.shape[1]
    wide = wq.shape[1]
    rank = up_q.shape[1]
    blocks = tokens // BLOCK

    owners = choice // holders
    pick = jnp.sum(jnp.where(owners == group, choice % holders, 0), axis=1).astype(i32)
    own_owner = lax.dynamic_index_in_dim(owners, group, 0, keepdims=False)
    req = jnp.arange(requests, dtype=i32)
    starts = jnp.sum(jnp.where(req[None, :] < req[:, None], counts[0][None, :], 0), axis=1)
    block = jnp.arange(blocks, dtype=i32)
    of_block = (starts[None, :] <= block[:, None]) & (
        block[:, None] < (starts + counts[0])[None, :]
    )

    def lookup(values):
        return jnp.sum(jnp.where(of_block, values[None, :], 0), axis=1).astype(i32)

    slot = lookup(own_owner)
    first = lookup(starts)
    limit = (first + lookup(counts[0]) - 1) * BLOCK + lookup(tails[0])
    is_key = jnp.broadcast_to(1 - xi % 2, (blocks,)).astype(i32)
    meta = jnp.stack([slot, block - first, first * BLOCK, is_key, limit]).astype(i32)

    cosine, sine = rotation_tables()

    stores = (jnp.swapaxes(down_qkv, 1, 2), up_q, up_kv, jnp.swapaxes(down_o, 1, 2), up_o)
    ys, xs = ring_order(y), ring_order(xi)
    unit = wo.shape[1] // (SIDE * SIDE * 2)
    wo_cols = jnp.stack(ys) * (2 * SIDE) + group
    down_out, up_out, x_a, x_b, *sent = pick_local(
        jnp.concatenate([pick, wo_cols.astype(i32)]), *stores, x, wo, unit
    )
    down = lax.all_to_all(down_out, ADAPTER_AXES, 0, 0, tiled=True)

    first_a = ring_gather(x_a, "x", x_a.shape[1] // 2)
    first_b = ring_gather(x_b, "y", x_b.shape[1] // 2)

    got = [sent[0], shift(sent[2], "y", 1), shift(sent[1], "y", -1), shift(sent[3], "y", 2)]
    halves = [first_a[:2], first_a[2:], first_b[:2], first_b[2:]]
    low_a, high_a, low_b, high_b = join(halves, got[1:])
    far_a = gather_onward(low_a, high_a, "y")
    far_b = gather_onward(low_b, high_b, "x")
    wo_mine = stack_rows(got, [down, low_a])
    wo_all = lax.all_gather(wo_mine, ADAPTER_AXES, axis=0)

    def rows_a(k, cols):
        return [(ys[k] * SIDE + xs[j]) * 2 for j in cols]

    def rows_b(k, cols):
        return [(ys[j] * SIDE + xs[k]) * 2 + 1 for j in cols]

    def index_of(rows):
        return jnp.stack(rows).astype(i32)

    every = range(SIDE)
    low, high = (0, 1), (2, 3)
    total = project(
        (index_of(rows_a(0, every) + rows_b(0, every)), meta),
        None,
        [low_a, high_a, low_b, high_b],
        [wq, wkv],
        512,
    )

    again = join(halves, [total[1]])
    next_a = gather_next(again[0], again[1], "y")
    next_b = gather_next(again[2], again[3], "x")

    pieces = scatter_rows(rank_partial(meta, x, down, 3 * rank, [low_a]))
    copies, up_out = share_sum(pieces, up_out, [total[1]])
    up = lax.all_to_all(up_out, ADAPTER_AXES, 0, 0, tiled=True)

    a_low, a_high = shift(far_a[0], "y", 1), shift(far_a[1], "y", -1)
    b_low, b_high = shift(far_b[0], "x", 1), shift(far_b[1], "x", -1)
    total = project(
        (
            index_of(rows_a(1, low) + rows_a(2, high) + rows_b(1, low) + rows_b(2, high)),
            meta,
        ),
        total,
        [*far_a, *far_b],
        [wq, wkv],
        512,
    )
    total = project(
        (
            index_of(rows_a(1, high) + rows_a(2, low) + rows_b(1, high) + rows_b(2, low)),
            meta,
        ),
        total,
        [*next_a, *next_b],
        [wq, wkv],
        512,
    )
    shrunk = lax.all_to_all(copies, TENSOR_AXES, 0, 0, tiled=True).reshape(tokens, 3 * rank)
    final = (index_of(rows_a(3, every) + rows_b(3, every)), meta)
    far = [a_low, a_high, b_low, b_high]
    tail = key_value_tail(shrunk, up, cosine, sine, wide, wkv.shape[1], 512)
    (mine,) = project(final, total[1:], far, [wkv], 512, tail)
    other = lax.ppermute(mine, "x", [(i, i ^ 1) for i in range(SIDE)])
    (q,) = project(final, total[:1], far, [wq], 512)

    cuts = 2
    each = blocks // cuts
    parts = []
    for cut in range(cuts):
        attended = attention(
            meta, q, shrunk, up, down, mine, other, cosine, sine, cut * each, each
        )
        step = 1 - 2 * cut
        gathered = ring_gather(attended, "y", wide // 2)
        parts.append(output_ring(gathered, wo_all, "x", step))
    return finish(meta, parts, up, rank, wide)


def solution(mesh):
    fine = Mesh(mesh.devices.reshape(SIDE, CORES, SIDE, SIDE), ADAPTER_AXES + TENSOR_AXES)
    placed = (
        P(ADAPTER_AXES, TENSOR_AXES),
        P(None, TENSOR_AXES),
        P(None, TENSOR_AXES),
        P(TENSOR_AXES, None),
        P(ADAPTER_AXES, TENSOR_AXES, None),
        P(ADAPTER_AXES, None, TENSOR_AXES),
        P(ADAPTER_AXES, None, TENSOR_AXES),
        P(ADAPTER_AXES, TENSOR_AXES, None),
        P(ADAPTER_AXES, None, TENSOR_AXES),
        P(),
        P(ADAPTER_AXES, None),
        P(ADAPTER_AXES, None),
    )
    return jax.shard_map(
        on_device,
        mesh=fine,
        in_specs=placed,
        out_specs=P(ADAPTER_AXES, TENSOR_AXES),
        check_vma=False,
    )
```

```python
import math

import jax
import jax.numpy as jnp
import numpy as np
from jax import lax
from jax.experimental import pallas as pl
from jax.experimental.pallas import tpu as pltpu
from jax.sharding import Mesh, PartitionSpec as P

HEAD = 128
BLOCK = 128
SIDE = 4
CORES = 2
ADAPTER_AXES = ("z", "c")
TENSOR_AXES = ("y", "x")
ROPE_BASE = 500000.0
VMEM = 56 * 1024 * 1024
bf16 = jnp.bfloat16
f32 = jnp.float32
i32 = jnp.int32


def params():
    return pltpu.CompilerParams(vmem_limit_bytes=VMEM)


def passive(arrays):
    return [pl.BlockSpec(memory_space=pl.ANY)] * len(arrays)


def cost(flops, moved, exps=0):
    return pl.CostEstimate(flops=flops, bytes_accessed=moved, transcendentals=exps)


def shift(block, axis, step):
    return lax.ppermute(block, axis, [(i, (i + step) % SIDE) for i in range(SIDE)])


def ring_gather(block, axis, half):
    behind = shift(block, axis, 1)
    ahead = shift(block, axis, -1)
    far_low = shift(behind[:, :half], axis, 1)
    far_high = shift(ahead[:, half:], axis, -1)
    return block, behind, ahead, far_low, far_high


def gather_onward(low, high, axis):
    return shift(low, axis, 1), shift(high, axis, -1)


def gather_next(low, high, axis):
    return shift(high, axis, 1), shift(low, axis, -1)


def ring_order(index):
    return [index, (index + SIDE - 1) % SIDE, (index + 1) % SIDE, (index + 2) % SIDE]


def pick_local(pick, down_qkv, up_q, up_kv, down_o, up_o, x, wo, unit):
    tokens, local = x.shape
    groups = pick.shape[0] - SIDE
    rank3, depth = down_qkv.shape[1:]
    rank, wide = up_q.shape[1:]
    narrow = up_kv.shape[2]
    rows = wo.shape[0] // groups

    def body(pick_ref, dq, uq, ukv, do, uo, x_ref, *refs):
        w_refs, (down, up, left, right), w_outs = refs[:SIDE], refs[SIDE : SIDE + 4], refs[SIDE + 4 :]
        left[...] = x_ref[:, : local // 2]
        right[...] = x_ref[:, local // 2 :]
        down[0, :rank3, :] = dq[0]
        down[0, rank3:, :] = do[0]
        up[0, :, :wide] = uq[0]
        up[0, :, wide : 2 * wide] = uo[0]
        up[0, :, 2 * wide :] = ukv[0]
        for w_ref, w_out in zip(w_refs, w_outs):
            w_out[...] = w_ref[...]

    def chosen(a):
        return pl.BlockSpec((1,) + a.shape[1:], lambda i, p: (p[i], 0, 0))

    def columns(k):
        return pl.BlockSpec((rows, unit), lambda i, p: (i, p[groups + k]))

    down_shape = (groups, rank3 + rank, depth)
    up_shape = (groups, rank, 2 * wide + narrow)
    half = (tokens, local // 2)
    share = (wo.shape[0], unit)
    return pl.pallas_call(
        body,
        out_shape=tuple(
            jax.ShapeDtypeStruct(s, bf16)
            for s in (down_shape, up_shape, half, half, share, share, share, share)
        ),
        grid_spec=pltpu.PrefetchScalarGridSpec(
            num_scalar_prefetch=1,
            grid=(groups,),
            in_specs=[chosen(a) for a in (down_qkv, up_q, up_kv, down_o, up_o)]
            + [pl.BlockSpec((tokens // groups, local), lambda i, p: (i, 0))]
            + [columns(k) for k in range(SIDE)],
            out_specs=[
                pl.BlockSpec((1,) + s[1:], lambda i, p: (i, 0, 0)) for s in (down_shape, up_shape)
            ]
            + [pl.BlockSpec((tokens // groups, local // 2), lambda i, p: (i, 0))] * 2
            + [pl.BlockSpec((rows, unit), lambda i, p: (i, 0))] * SIDE,
        ),
        compiler_params=params(),
        cost_estimate=cost(0, 2 * 2 * (math.prod(down_shape) + math.prod(up_shape))),
    )(pick, down_qkv, up_q, up_kv, down_o, up_o, x, wo, wo, wo, wo)


def stack_rows(blocks, after):
    rows, width = blocks[0].shape
    count = len(blocks)

    def body(*refs):
        out = refs[-1]
        for k in range(count):
            out[k * rows : (k + 1) * rows, :] = refs[k][...]

    spec = pl.BlockSpec((rows, width), lambda i: (0, 0))
    return pl.pallas_call(
        body,
        out_shape=jax.ShapeDtypeStruct((count * rows, width), bf16),
        grid=(1,),
        in_specs=[spec] * count + passive(after),
        out_specs=pl.BlockSpec((count * rows, width), lambda i: (0, 0)),
        compiler_params=params(),
        cost_estimate=cost(0, 4 * count * rows * width),
    )(*blocks, *after)


def rank_partial(meta, x, down, rank3, after):
    tokens, depth = x.shape
    per = 2
    rows = per * BLOCK

    def body(meta_ref, x_ref, *rest):
        d_refs, out = rest[:per], rest[-1]
        for k in range(per):
            at = slice(k * BLOCK, (k + 1) * BLOCK)
            out[at, :] = lax.dot_general(
                x_ref[at, :], d_refs[k][0], (((1,), (1,)), ((), ())), preferred_element_type=f32
            )

    def chosen(k):
        return pl.BlockSpec((1, rank3, depth), lambda i, m: (m[0, i * per + k], 0, 0))

    return pl.pallas_call(
        body,
        out_shape=jax.ShapeDtypeStruct((tokens, rank3), f32),
        grid_spec=pltpu.PrefetchScalarGridSpec(
            num_scalar_prefetch=1,
            grid=(tokens // rows,),
            in_specs=[pl.BlockSpec((rows, depth), lambda i, m: (i, 0))]
            + [chosen(k) for k in range(per)]
            + passive(after),
            out_specs=pl.BlockSpec((rows, rank3), lambda i, m: (i, 0)),
        ),
        compiler_params=params(),
        cost_estimate=cost(2 * tokens * depth * rank3, 2 * tokens * depth + 8 * tokens * rank3),
    )(meta, x, *[down] * per, *after)


def join(groups, after):
    tokens = groups[0][0].shape[0]
    rows = 256
    flat = [b for group in groups for b in group]
    widths = [sum(b.shape[1] for b in group) for group in groups]

    def body(*refs):
        ins, outs = refs[: len(flat)], refs[len(flat) + len(after) :]
        at = 0
        for out, group in zip(outs, groups):
            col = 0
            for b in group:
                out[:, col : col + b.shape[1]] = ins[at][...]
                col += b.shape[1]
                at += 1

    return pl.pallas_call(
        body,
        out_shape=tuple(jax.ShapeDtypeStruct((tokens, w), bf16) for w in widths),
        grid=(tokens // rows,),
        in_specs=[pl.BlockSpec((rows, b.shape[1]), lambda i: (i, 0)) for b in flat]
        + passive(after),
        out_specs=[pl.BlockSpec((rows, w), lambda i: (i, 0)) for w in widths],
        compiler_params=params(),
        cost_estimate=cost(0, 4 * tokens * sum(widths)),
    )(*flat, *after)


def share_sum(pieces, onward, after):
    ways, rows, rank = pieces.shape

    def body(p_ref, *refs):
        out = refs[-2]
        total = p_ref[0]
        for k in range(1, ways):
            total = total + p_ref[k]
        for k in range(ways):
            out[k] = total.astype(bf16)

    whole = pl.BlockSpec(pieces.shape, lambda i: (0, 0, 0))
    return pl.pallas_call(
        body,
        out_shape=(
            jax.ShapeDtypeStruct(pieces.shape, bf16),
            jax.ShapeDtypeStruct(onward.shape, onward.dtype),
        ),
        grid=(1,),
        in_specs=[whole] + passive([onward, *after]),
        out_specs=[whole] + passive([onward]),
        input_output_aliases={1: 1},
        compiler_params=params(),
        cost_estimate=cost(ways * rows * rank, 6 * ways * rows * rank),
    )(pieces, onward, *after)


def scatter_rows(partial):
    rows, rank = partial.shape
    ways = SIDE * SIDE
    return lax.all_to_all(
        partial.reshape(ways, rows // ways, rank), TENSOR_AXES, 0, 0, tiled=True
    )


def project(index, total, blocks, weights, tile, last=None, after=(), rows=256):
    tokens = blocks[0].shape[0]
    counts = [b.shape[1] // rows for b in blocks]
    pieces = sum(counts)
    kinds = len(weights)
    first = total is None
    tail, tail_operands, tail_specs, dtype = last or (None, [], [], f32)

    def body(index_ref, meta_ref, *refs):
        x_refs = refs[: len(blocks)]
        w_refs = refs[len(blocks) : len(blocks) + kinds * pieces]
        rest = refs[len(blocks) + kinds * pieces :]
        outs = rest[len(rest) - kinds :]
        for kind in range(kinds):
            mine = w_refs[kind * pieces : (kind + 1) * pieces]
            acc = None if first else rest[kind][...]
            at = 0
            for x_ref, n in zip(x_refs, counts):
                w = jnp.concatenate([r[...] for r in mine[at : at + n]], axis=0)
                add = jnp.dot(x_ref[...], w, preferred_element_type=f32)
                acc = add if acc is None else acc + add
                at += n
            if tail is not None:
                acc = tail(meta_ref, acc, rest[kinds : kinds + len(tail_operands)])
            outs[kind][...] = acc

    def weight(k, width):
        return pl.BlockSpec((rows, width), lambda i, p, m: (p[k], 0))

    widths = [w.shape[1] for w in weights]
    row_specs = [pl.BlockSpec((tile, w), lambda i, p, m: (i, 0)) for w in widths]
    in_specs = [pl.BlockSpec((tile, b.shape[1]), lambda i, p, m: (i, 0)) for b in blocks]
    operands = list(blocks)
    for w in weights:
        in_specs += [weight(k, w.shape[1]) for k in range(pieces)]
        operands += [w] * pieces
    aliases = {}
    if not first:
        if tail is None:
            aliases = {2 + len(operands) + k: k for k in range(kinds)}
        in_specs += row_specs
        operands += list(total)
    index, meta = index
    depth = pieces * rows
    return pl.pallas_call(
        body,
        out_shape=tuple(jax.ShapeDtypeStruct((tokens, w), dtype) for w in widths),
        grid_spec=pltpu.PrefetchScalarGridSpec(
            num_scalar_prefetch=2,
            grid=(tokens // tile,),
            in_specs=in_specs + tail_specs + passive(after),
            out_specs=row_specs,
        ),
        input_output_aliases=aliases,
        compiler_params=params(),
        cost_estimate=cost(
            2 * tokens * depth * sum(widths),
            2 * depth * (tokens + sum(widths)) + 8 * tokens * sum(widths),
        ),
    )(index, meta, *operands, *tail_operands, *after)


def key_value_tail(shrunk, up, cosine, sine, wide, narrow, tile):
    rank = shrunk.shape[1] // 3
    per = tile // BLOCK

    def tail(meta_ref, acc, refs):
        s_ref, up_ref, c_ref, n_ref = refs
        i = pl.program_id(0)
        is_key = meta_ref[3, 0] == 1
        done = []
        for k in range(per):
            at = slice(k * BLOCK, (k + 1) * BLOCK)
            s = s_ref[at, :].astype(f32)
            rank_in = jnp.where(is_key, s[:, rank : 2 * rank], s[:, 2 * rank :]).astype(bf16)
            u = acc[at, :] + jnp.dot(
                rank_in, up_ref[meta_ref[0, i * per + k]], preferred_element_type=f32
            )
            place = meta_ref[1, i * per + k]
            turned = u * c_ref[place] + pltpu.roll(u, HEAD // 2, 1) * n_ref[place]
            done.append(jnp.where(is_key, turned, u).astype(bf16))
        return jnp.concatenate(done, axis=0)

    specs = [
        pl.BlockSpec((tile, 3 * rank), lambda i, p, m: (i, 0)),
        pl.BlockSpec((up.shape[0], rank, narrow), lambda i, p, m: (0, 0, 2 * wide // narrow)),
        pl.BlockSpec(cosine.shape, lambda i, p, m: (0, 0, 0)),
        pl.BlockSpec(sine.shape, lambda i, p, m: (0, 0, 0)),
    ]
    return tail, [shrunk, up, cosine, sine], specs, bf16


def rotation_tables():
    freq = np.exp(-(2.0 * np.arange(HEAD // 2, dtype=np.float32) / HEAD) * math.log(ROPE_BASE))
    angle = np.arange(3 * BLOCK, dtype=np.float32)[:, None] * freq.astype(np.float32)[None, :]
    cosine = np.concatenate([np.cos(angle)] * 2, axis=1)
    sine = np.concatenate([-np.sin(angle), np.sin(angle)], axis=1)
    shape = (3, BLOCK, HEAD)
    return (
        jnp.asarray(cosine.reshape(shape), f32),
        jnp.asarray(sine.reshape(shape), f32),
    )


def attention(meta, q, shrunk, up, down, mine, other, cosine, sine, begin, count):
    tokens, wide = q.shape
    rank = shrunk.shape[1] // 3
    heads = wide // HEAD
    window = min(3 * BLOCK, tokens)
    scale = 1.0 / math.sqrt(HEAD)

    def body(meta_ref, q_ref, s_ref, up_ref, d_ref, m_ref, o_ref, c_ref, n_ref, att):
        i = begin + pl.program_id(0)
        is_key = meta_ref[3, 0] == 1
        first = meta_ref[2, i]
        limit = meta_ref[4, i]
        u = q_ref[...] + jnp.dot(
            s_ref[...][:, :rank], up_ref[0], preferred_element_type=f32
        )
        start = pl.multiple_of(jnp.maximum(i - 2, 0) * BLOCK, BLOCK)
        own = m_ref[pl.ds(start, window), :]
        far = o_ref[pl.ds(start, window), :]
        keys = jnp.where(is_key, own, far)
        values = jnp.where(is_key, far, own)
        row = i * BLOCK + lax.broadcasted_iota(i32, (BLOCK, window), 0)
        col = start + lax.broadcasted_iota(i32, (BLOCK, window), 1)
        allowed = (col >= first) & (col <= row) & (col < limit)
        cosines = c_ref[0]
        sines = n_ref[0]
        turned = []
        for h in range(heads):
            part = u[:, h * HEAD : (h + 1) * HEAD]
            turned.append(
                (part * cosines + pltpu.roll(part, HEAD // 2, 1) * sines).astype(bf16)
            )
        scores = lax.dot_general(
            jnp.concatenate(turned, axis=0),
            keys,
            (((1,), (1,)), ((), ())),
            preferred_element_type=f32,
        )
        for h in range(heads):
            at = slice(h * HEAD, (h + 1) * HEAD)
            weights = jnp.where(allowed, jnp.exp(scores[at, :] * scale), 0.0)
            weights = weights * (1.0 / jnp.sum(weights, axis=1, keepdims=True))
            mixed = jnp.dot(weights.astype(bf16), values, preferred_element_type=f32)
            att[:, at] = mixed.astype(bf16)
        head = lax.dot_general(
            att[:, :wide], d_ref[0], (((1,), (1,)), ((), ())), preferred_element_type=f32
        )
        att[:, wide : wide + rank] = head.astype(bf16)
        att[:, wide + rank :] = jnp.zeros((BLOCK, HEAD - rank), bf16)

    table = pl.BlockSpec((1, BLOCK, HEAD), lambda i, m: (m[1, i + begin], 0, 0))
    whole = pl.BlockSpec((tokens, HEAD), lambda i, m: (0, 0))
    return pl.pallas_call(
        body,
        out_shape=jax.ShapeDtypeStruct((count * BLOCK, wide + HEAD), bf16),
        grid_spec=pltpu.PrefetchScalarGridSpec(
            num_scalar_prefetch=1,
            grid=(count,),
            in_specs=[
                pl.BlockSpec((BLOCK, wide), lambda i, m: (i + begin, 0)),
                pl.BlockSpec((BLOCK, 3 * rank), lambda i, m: (i + begin, 0)),
                pl.BlockSpec((1, rank, wide), lambda i, m: (m[0, i + begin], 0, 0)),
                pl.BlockSpec((1, rank, down.shape[2]), lambda i, m: (m[0, i + begin], 3, 0)),
                whole,
                whole,
                table,
                table,
            ],
            out_specs=pl.BlockSpec((BLOCK, wide + HEAD), lambda i, m: (i, 0)),
        ),
        compiler_params=params(),
        cost_estimate=cost(
            4 * count * BLOCK * window * wide, 8 * count * BLOCK * wide, heads * count * BLOCK * window
        ),
    )(meta, q, shrunk, up, down, mine, other, cosine, sine)


def output_partial(shards, pieces, weights):
    tokens = pieces[0].shape[0]
    count, (depth, width) = len(shards) // 2, weights.shape[1:]
    unit = depth // SIDE
    whole = 2 * width + HEAD
    cut = pieces[3].shape[1]
    low, high = slice(0, width), slice(width + HEAD, whole)

    def body(index_ref, *refs):
        x_refs, (w_low, w_high) = refs[: SIDE + 1], refs[SIDE + 1 : SIDE + 3]
        outs, x_all = refs[SIDE + 3 : -1], refs[-1]
        step = pl.program_id(0)

        @pl.when(step == 0)
        def _():
            rank = jnp.zeros((tokens, HEAD), f32)
            for ref, begin in zip(x_refs, (0, unit, 2 * unit, 3 * unit, 3 * unit + cut)):
                held = min(ref.shape[1], depth - begin, unit)
                x_all[:, begin : begin + held] = ref[:, :held]
                if held < ref.shape[1]:
                    rank = rank + ref[:, held:].astype(f32)
            for out in outs:
                out[:, width : width + HEAD] = rank.astype(out.dtype)

        first = jnp.dot(x_all[...], w_low[0], preferred_element_type=f32)
        second = jnp.dot(x_all[...], w_high[0], preferred_element_type=f32)
        for k, out in enumerate(outs):

            @pl.when(step == k)
            def _():
                out[:, low] = first.astype(out.dtype)
                out[:, high] = second.astype(out.dtype)

    dtypes = [bf16] * (count - 1) + [f32]
    return pl.pallas_call(
        body,
        out_shape=tuple(jax.ShapeDtypeStruct((tokens, whole), d) for d in dtypes),
        grid_spec=pltpu.PrefetchScalarGridSpec(
            num_scalar_prefetch=1,
            grid=(count,),
            in_specs=[pl.BlockSpec(p.shape, lambda j, d: (0, 0)) for p in pieces]
            + [pl.BlockSpec((1, depth, width), lambda j, d: (d[2 * j], 0, 0))]
            + [pl.BlockSpec((1, depth, width), lambda j, d: (d[2 * j + 1], 0, 0))],
            out_specs=[pl.BlockSpec((tokens, whole), lambda j, d: (0, 0))] * count,
            scratch_shapes=[pltpu.VMEM((tokens, depth), bf16)],
        ),
        compiler_params=params(),
        cost_estimate=cost(
            4 * tokens * depth * count * width, 2 * depth * (tokens + 2 * count * width)
        ),
    )(jnp.stack(shards).astype(i32), *pieces, weights, weights)


def add_blocks(a, b, after):
    rows, width = a.shape
    tile = rows // 2

    def body(a_ref, b_ref, *refs):
        refs[-1][...] = (a_ref[...].astype(f32) + b_ref[...].astype(f32)).astype(bf16)

    spec = pl.BlockSpec((tile, width), lambda i: (i, 0))
    return pl.pallas_call(
        body,
        out_shape=jax.ShapeDtypeStruct(a.shape, bf16),
        grid=(2,),
        in_specs=[spec, spec] + passive(after),
        out_specs=spec,
        compiler_params=params(),
        cost_estimate=cost(rows * width, 6 * rows * width),
    )(a, b, *after)


def output_ring(pieces, weights, axis, step):
    me, behind, ahead, far = ring_order(lax.axis_index(axis))
    shards = [2 * place + side for place in (far, ahead, behind, me) for side in range(2)]
    to_far, to_ahead, to_behind, mine = output_partial(shards, pieces, weights)
    passing = shift(to_far, axis, step)
    if step == 1:
        to_ahead = add_blocks(to_ahead, passing, [])
        return mine, shift(to_behind, axis, -1), shift(to_ahead, axis, 1)
    from_behind = shift(to_ahead, axis, 1)
    to_behind = add_blocks(to_behind, passing, [from_behind])
    return mine, shift(to_behind, axis, -1), from_behind


def finish(meta, parts, up, rank, wide):
    cuts = len(parts)
    rows, whole = parts[0][0].shape
    width = (whole - HEAD) // 2
    per = 2
    steps = rows // (per * BLOCK)
    terms = [t for cut in parts for t in cut]
    each = len(parts[0])

    def body(meta_ref, *refs):
        up_ref, out = refs[len(terms) :]
        i = pl.program_id(0)

        def put(mine):
            for k in range(per):
                at = slice(k * BLOCK, (k + 1) * BLOCK)
                block = i * per + k
                total = mine[0][at, :].astype(f32)
                for ref in mine[1:]:
                    total = total + ref[at, :].astype(f32)
                extra = jnp.dot(
                    total[:, width : width + rank].astype(bf16),
                    up_ref[meta_ref[0, block]],
                    preferred_element_type=f32,
                )
                row = block * BLOCK + lax.broadcasted_iota(i32, (BLOCK, width), 0)
                valid = row < meta_ref[4, block]
                for side, begin in enumerate((0, width + HEAD)):
                    cols = slice(side * width, (side + 1) * width)
                    out[at, cols] = jnp.where(
                        valid, total[:, begin : begin + width] + extra[:, cols], 0.0
                    )

        for cut in range(cuts):

            @pl.when(i // steps == cut)
            def _():
                put(refs[cut * each : (cut + 1) * each])

    def term_spec(cut):
        return pl.BlockSpec(
            (per * BLOCK, whole), lambda i, m: (jnp.clip(i - cut * steps, 0, steps - 1), 0)
        )

    return pl.pallas_call(
        body,
        out_shape=jax.ShapeDtypeStruct((cuts * rows, 2 * width), f32),
        grid_spec=pltpu.PrefetchScalarGridSpec(
            num_scalar_prefetch=1,
            grid=(cuts * steps,),
            in_specs=[term_spec(cut) for cut in range(cuts) for _ in range(each)]
            + [pl.BlockSpec((up.shape[0], rank, wide), lambda i, m: (0, 0, 1))],
            out_specs=pl.BlockSpec((per * BLOCK, 2 * width), lambda i, m: (i, 0)),
        ),
        compiler_params=params(),
        cost_estimate=cost(4 * cuts * rows * rank * width, 28 * cuts * rows * width),
    )(meta, *terms, up)


def on_device(x, wq, wkv, wo, down_qkv, up_q, up_kv, down_o, up_o, choice, counts, tails):
    z, c, y, xi = (lax.axis_index(n) for n in ADAPTER_AXES + TENSOR_AXES)
    group = z * CORES + c
    tokens, local = x.shape
    holders = down_qkv.shape[0]
    requests = choice.shape[1]
    wide = wq.shape[1]
    rank = up_q.shape[1]
    blocks = tokens // BLOCK

    owners = choice // holders
    pick = jnp.sum(jnp.where(owners == group, choice % holders, 0), axis=1).astype(i32)
    own_owner = lax.dynamic_index_in_dim(owners, group, 0, keepdims=False)
    req = jnp.arange(requests, dtype=i32)
    starts = jnp.sum(jnp.where(req[None, :] < req[:, None], counts[0][None, :], 0), axis=1)
    block = jnp.arange(blocks, dtype=i32)
    of_block = (starts[None, :] <= block[:, None]) & (
        block[:, None] < (starts + counts[0])[None, :]
    )

    def lookup(values):
        return jnp.sum(jnp.where(of_block, values[None, :], 0), axis=1).astype(i32)

    slot = lookup(own_owner)
    first = lookup(starts)
    limit = (first + lookup(counts[0]) - 1) * BLOCK + lookup(tails[0])
    is_key = jnp.broadcast_to(1 - xi % 2, (blocks,)).astype(i32)
    meta = jnp.stack([slot, block - first, first * BLOCK, is_key, limit]).astype(i32)

    cosine, sine = rotation_tables()

    stores = (jnp.swapaxes(down_qkv, 1, 2), up_q, up_kv, jnp.swapaxes(down_o, 1, 2), up_o)
    ys, xs = ring_order(y), ring_order(xi)
    unit = wo.shape[1] // (SIDE * SIDE * 2)
    wo_cols = jnp.stack(ys) * (2 * SIDE) + group
    down_out, up_out, x_a, x_b, *sent = pick_local(
        jnp.concatenate([pick, wo_cols.astype(i32)]), *stores, x, wo, unit
    )
    down = lax.all_to_all(down_out, ADAPTER_AXES, 0, 0, tiled=True)

    first_a = ring_gather(x_a, "x", x_a.shape[1] // 2)
    first_b = ring_gather(x_b, "y", x_b.shape[1] // 2)

    got = [sent[0], shift(sent[2], "y", 1), shift(sent[1], "y", -1), shift(sent[3], "y", 2)]
    halves = [first_a[:2], first_a[2:], first_b[:2], first_b[2:]]
    low_a, high_a, low_b, high_b = join(halves, got[1:])
    far_a = gather_onward(low_a, high_a, "y")
    far_b = gather_onward(low_b, high_b, "x")
    wo_mine = stack_rows(got, [down, low_a])
    wo_all = lax.all_gather(wo_mine, ADAPTER_AXES, axis=0)

    def rows_a(k, cols):
        return [(ys[k] * SIDE + xs[j]) * 2 for j in cols]

    def rows_b(k, cols):
        return [(ys[j] * SIDE + xs[k]) * 2 + 1 for j in cols]

    def index_of(rows):
        return jnp.stack(rows).astype(i32)

    every = range(SIDE)
    low, high = (0, 1), (2, 3)
    total = project(
        (index_of(rows_a(0, every) + rows_b(0, every)), meta),
        None,
        [low_a, high_a, low_b, high_b],
        [wq, wkv],
        512,
    )

    again = join(halves, [total[1]])
    next_a = gather_next(again[0], again[1], "y")
    next_b = gather_next(again[2], again[3], "x")

    pieces = scatter_rows(rank_partial(meta, x, down, 3 * rank, [low_a]))
    copies, up_out = share_sum(pieces, up_out, [total[1]])
    up = lax.all_to_all(up_out, ADAPTER_AXES, 0, 0, tiled=True)

    a_low, a_high = shift(far_a[0], "y", 1), shift(far_a[1], "y", -1)
    b_low, b_high = shift(far_b[0], "x", 1), shift(far_b[1], "x", -1)
    total = project(
        (
            index_of(rows_a(1, low) + rows_a(2, high) + rows_b(1, low) + rows_b(2, high)),
            meta,
        ),
        total,
        [*far_a, *far_b],
        [wq, wkv],
        512,
    )
    total = project(
        (
            index_of(rows_a(1, high) + rows_a(2, low) + rows_b(1, high) + rows_b(2, low)),
            meta,
        ),
        total,
        [*next_a, *next_b],
        [wq, wkv],
        512,
    )
    shrunk = lax.all_to_all(copies, TENSOR_AXES, 0, 0, tiled=True).reshape(tokens, 3 * rank)
    final = (index_of(rows_a(3, every) + rows_b(3, every)), meta)
    far = [a_low, a_high, b_low, b_high]
    tail = key_value_tail(shrunk, up, cosine, sine, wide, wkv.shape[1], 512)
    (mine,) = project(final, total[1:], far, [wkv], 512, tail)
    other = lax.ppermute(mine, "x", [(i, i ^ 1) for i in range(SIDE)])
    (q,) = project(final, total[:1], far, [wq], 512)

    cuts = 2
    each = blocks // cuts
    parts = []
    for cut in range(cuts):
        attended = attention(
            meta, q, shrunk, up, down, mine, other, cosine, sine, cut * each, each
        )
        step = 1 - 2 * cut
        gathered = ring_gather(attended, "y", wide // 2)
        parts.append(output_ring(gathered, wo_all, "x", step))
    return finish(meta, parts, up, rank, wide)


def solution(mesh):
    fine = Mesh(mesh.devices.reshape(SIDE, CORES, SIDE, SIDE), ADAPTER_AXES + TENSOR_AXES)
    placed = (
        P(ADAPTER_AXES, TENSOR_AXES),
        P(None, TENSOR_AXES),
        P(None, TENSOR_AXES),
        P(TENSOR_AXES, None),
        P(ADAPTER_AXES, TENSOR_AXES, None),
        P(ADAPTER_AXES, None, TENSOR_AXES),
        P(ADAPTER_AXES, None, TENSOR_AXES),
        P(ADAPTER_AXES, TENSOR_AXES, None),
        P(ADAPTER_AXES, None, TENSOR_AXES),
        P(),
        P(ADAPTER_AXES, None),
        P(ADAPTER_AXES, None),
    )
    return jax.shard_map(
        on_device,
        mesh=fine,
        in_specs=placed,
        out_specs=P(ADAPTER_AXES, TENSOR_AXES),
        check_vma=False,
    )
```

```python
import math

import jax
import jax.numpy as jnp
import numpy as np
from jax import lax
from jax.experimental import pallas as pl
from jax.experimental.pallas import tpu as pltpu
from jax.sharding import Mesh, PartitionSpec as P

HEAD = 128
BLOCK = 128
SIDE = 4
CORES = 2
ADAPTER_AXES = ("z", "c")
TENSOR_AXES = ("y", "x")
ROPE_BASE = 500000.0
VMEM = 56 * 1024 * 1024
bf16 = jnp.bfloat16
f32 = jnp.float32
i32 = jnp.int32


def params():
    return pltpu.CompilerParams(vmem_limit_bytes=VMEM)


def passive(arrays):
    return [pl.BlockSpec(memory_space=pl.ANY)] * len(arrays)


def cost(flops, moved, exps=0):
    return pl.CostEstimate(flops=flops, bytes_accessed=moved, transcendentals=exps)


def shift(block, axis, step):
    return lax.ppermute(block, axis, [(i, (i + step) % SIDE) for i in range(SIDE)])


def ring_gather(block, axis, half):
    behind = shift(block, axis, 1)
    ahead = shift(block, axis, -1)
    far_low = shift(behind[:, :half], axis, 1)
    far_high = shift(ahead[:, half:], axis, -1)
    return block, behind, ahead, far_low, far_high


def gather_onward(low, high, axis):
    return shift(low, axis, 1), shift(high, axis, -1)


def gather_next(low, high, axis):
    return shift(high, axis, 1), shift(low, axis, -1)


def ring_order(index):
    return [index, (index + SIDE - 1) % SIDE, (index + 1) % SIDE, (index + 2) % SIDE]


def pick_local(pick, down_qkv, up_q, up_kv, down_o, up_o, x, wo, unit):
    tokens, local = x.shape
    groups = pick.shape[0] - SIDE
    rank3, depth = down_qkv.shape[1:]
    rank, wide = up_q.shape[1:]
    narrow = up_kv.shape[2]
    rows = wo.shape[0] // groups

    def body(pick_ref, dq, uq, ukv, do, uo, x_ref, *refs):
        w_refs, (down, up, left, right), w_outs = refs[:SIDE], refs[SIDE : SIDE + 4], refs[SIDE + 4 :]
        left[...] = x_ref[:, : local // 2]
        right[...] = x_ref[:, local // 2 :]
        down[0, :rank3, :] = dq[0]
        down[0, rank3:, :] = do[0]
        up[0, :, :wide] = uq[0]
        up[0, :, wide : 2 * wide] = uo[0]
        up[0, :, 2 * wide :] = ukv[0]
        for w_ref, w_out in zip(w_refs, w_outs):
            w_out[...] = w_ref[...]

    def chosen(a):
        return pl.BlockSpec((1,) + a.shape[1:], lambda i, p: (p[i], 0, 0))

    def columns(k):
        return pl.BlockSpec((rows, unit), lambda i, p: (i, p[groups + k]))

    down_shape = (groups, rank3 + rank, depth)
    up_shape = (groups, rank, 2 * wide + narrow)
    half = (tokens, local // 2)
    share = (wo.shape[0], unit)
    return pl.pallas_call(
        body,
        out_shape=tuple(
            jax.ShapeDtypeStruct(s, bf16)
            for s in (down_shape, up_shape, half, half, share, share, share, share)
        ),
        grid_spec=pltpu.PrefetchScalarGridSpec(
            num_scalar_prefetch=1,
            grid=(groups,),
            in_specs=[chosen(a) for a in (down_qkv, up_q, up_kv, down_o, up_o)]
            + [pl.BlockSpec((tokens // groups, local), lambda i, p: (i, 0))]
            + [columns(k) for k in range(SIDE)],
            out_specs=[
                pl.BlockSpec((1,) + s[1:], lambda i, p: (i, 0, 0)) for s in (down_shape, up_shape)
            ]
            + [pl.BlockSpec((tokens // groups, local // 2), lambda i, p: (i, 0))] * 2
            + [pl.BlockSpec((rows, unit), lambda i, p: (i, 0))] * SIDE,
        ),
        compiler_params=params(),
        cost_estimate=cost(0, 2 * 2 * (math.prod(down_shape) + math.prod(up_shape))),
    )(pick, down_qkv, up_q, up_kv, down_o, up_o, x, wo, wo, wo, wo)


def stack_rows(blocks, after):
    rows, width = blocks[0].shape
    count = len(blocks)

    def body(*refs):
        out = refs[-1]
        for k in range(count):
            out[k * rows : (k + 1) * rows, :] = refs[k][...]

    spec = pl.BlockSpec((rows, width), lambda i: (0, 0))
    return pl.pallas_call(
        body,
        out_shape=jax.ShapeDtypeStruct((count * rows, width), bf16),
        grid=(1,),
        in_specs=[spec] * count + passive(after),
        out_specs=pl.BlockSpec((count * rows, width), lambda i: (0, 0)),
        compiler_params=params(),
        cost_estimate=cost(0, 4 * count * rows * width),
    )(*blocks, *after)


def rank_partial(meta, x, down, rank3, after):
    tokens, depth = x.shape
    per = 2
    rows = per * BLOCK

    def body(meta_ref, x_ref, *rest):
        d_refs, out = rest[:per], rest[-1]
        for k in range(per):
            at = slice(k * BLOCK, (k + 1) * BLOCK)
            out[at, :] = lax.dot_general(
                x_ref[at, :], d_refs[k][0], (((1,), (1,)), ((), ())), preferred_element_type=f32
            )

    def chosen(k):
        return pl.BlockSpec((1, rank3, depth), lambda i, m: (m[0, i * per + k], 0, 0))

    return pl.pallas_call(
        body,
        out_shape=jax.ShapeDtypeStruct((tokens, rank3), f32),
        grid_spec=pltpu.PrefetchScalarGridSpec(
            num_scalar_prefetch=1,
            grid=(tokens // rows,),
            in_specs=[pl.BlockSpec((rows, depth), lambda i, m: (i, 0))]
            + [chosen(k) for k in range(per)]
            + passive(after),
            out_specs=pl.BlockSpec((rows, rank3), lambda i, m: (i, 0)),
        ),
        compiler_params=params(),
        cost_estimate=cost(2 * tokens * depth * rank3, 2 * tokens * depth + 8 * tokens * rank3),
    )(meta, x, *[down] * per, *after)


def join(groups, after):
    tokens = groups[0][0].shape[0]
    rows = 256
    flat = [b for group in groups for b in group]
    widths = [sum(b.shape[1] for b in group) for group in groups]

    def body(*refs):
        ins, outs = refs[: len(flat)], refs[len(flat) + len(after) :]
        at = 0
        for out, group in zip(outs, groups):
            col = 0
            for b in group:
                out[:, col : col + b.shape[1]] = ins[at][...]
                col += b.shape[1]
                at += 1

    return pl.pallas_call(
        body,
        out_shape=tuple(jax.ShapeDtypeStruct((tokens, w), bf16) for w in widths),
        grid=(tokens // rows,),
        in_specs=[pl.BlockSpec((rows, b.shape[1]), lambda i: (i, 0)) for b in flat]
        + passive(after),
        out_specs=[pl.BlockSpec((rows, w), lambda i: (i, 0)) for w in widths],
        compiler_params=params(),
        cost_estimate=cost(0, 4 * tokens * sum(widths)),
    )(*flat, *after)


def share_sum(pieces, onward, after):
    ways, rows, rank = pieces.shape

    def body(p_ref, *refs):
        out = refs[-2]
        total = p_ref[0]
        for k in range(1, ways):
            total = total + p_ref[k]
        for k in range(ways):
            out[k] = total.astype(bf16)

    whole = pl.BlockSpec(pieces.shape, lambda i: (0, 0, 0))
    return pl.pallas_call(
        body,
        out_shape=(
            jax.ShapeDtypeStruct(pieces.shape, bf16),
            jax.ShapeDtypeStruct(onward.shape, onward.dtype),
        ),
        grid=(1,),
        in_specs=[whole] + passive([onward, *after]),
        out_specs=[whole] + passive([onward]),
        input_output_aliases={1: 1},
        compiler_params=params(),
        cost_estimate=cost(ways * rows * rank, 6 * ways * rows * rank),
    )(pieces, onward, *after)


def scatter_rows(partial):
    rows, rank = partial.shape
    ways = SIDE * SIDE
    return lax.all_to_all(
        partial.reshape(ways, rows // ways, rank), TENSOR_AXES, 0, 0, tiled=True
    )


def project(index, total, blocks, weights, tile, last=None, after=(), rows=256):
    tokens = blocks[0].shape[0]
    counts = [b.shape[1] // rows for b in blocks]
    pieces = sum(counts)
    kinds = len(weights)
    first = total is None
    tail, tail_operands, tail_specs, dtype = last or (None, [], [], f32)

    def body(index_ref, meta_ref, *refs):
        x_refs = refs[: len(blocks)]
        w_refs = refs[len(blocks) : len(blocks) + kinds * pieces]
        rest = refs[len(blocks) + kinds * pieces :]
        outs = rest[len(rest) - kinds :]
        for kind in range(kinds):
            mine = w_refs[kind * pieces : (kind + 1) * pieces]
            acc = None if first else rest[kind][...]
            at = 0
            for x_ref, n in zip(x_refs, counts):
                w = jnp.concatenate([r[...] for r in mine[at : at + n]], axis=0)
                add = jnp.dot(x_ref[...], w, preferred_element_type=f32)
                acc = add if acc is None else acc + add
                at += n
            if tail is not None:
                acc = tail(meta_ref, acc, rest[kinds : kinds + len(tail_operands)])
            outs[kind][...] = acc

    def weight(k, width):
        return pl.BlockSpec((rows, width), lambda i, p, m: (p[k], 0))

    widths = [w.shape[1] for w in weights]
    row_specs = [pl.BlockSpec((tile, w), lambda i, p, m: (i, 0)) for w in widths]
    in_specs = [pl.BlockSpec((tile, b.shape[1]), lambda i, p, m: (i, 0)) for b in blocks]
    operands = list(blocks)
    for w in weights:
        in_specs += [weight(k, w.shape[1]) for k in range(pieces)]
        operands += [w] * pieces
    aliases = {}
    if not first:
        if tail is None:
            aliases = {2 + len(operands) + k: k for k in range(kinds)}
        in_specs += row_specs
        operands += list(total)
    index, meta = index
    depth = pieces * rows
    return pl.pallas_call(
        body,
        out_shape=tuple(jax.ShapeDtypeStruct((tokens, w), dtype) for w in widths),
        grid_spec=pltpu.PrefetchScalarGridSpec(
            num_scalar_prefetch=2,
            grid=(tokens // tile,),
            in_specs=in_specs + tail_specs + passive(after),
            out_specs=row_specs,
        ),
        input_output_aliases=aliases,
        compiler_params=params(),
        cost_estimate=cost(
            2 * tokens * depth * sum(widths),
            2 * depth * (tokens + sum(widths)) + 8 * tokens * sum(widths),
        ),
    )(index, meta, *operands, *tail_operands, *after)


def key_value_tail(shrunk, up, cosine, sine, wide, narrow, tile):
    rank = shrunk.shape[1] // 3
    per = tile // BLOCK

    def tail(meta_ref, acc, refs):
        s_ref, up_ref, c_ref, n_ref = refs
        i = pl.program_id(0)
        is_key = meta_ref[3, 0] == 1
        done = []
        for k in range(per):
            at = slice(k * BLOCK, (k + 1) * BLOCK)
            s = s_ref[at, :].astype(f32)
            rank_in = jnp.where(is_key, s[:, rank : 2 * rank], s[:, 2 * rank :]).astype(bf16)
            u = acc[at, :] + jnp.dot(
                rank_in, up_ref[meta_ref[0, i * per + k]], preferred_element_type=f32
            )
            place = meta_ref[1, i * per + k]
            turned = u * c_ref[place] + pltpu.roll(u, HEAD // 2, 1) * n_ref[place]
            done.append(jnp.where(is_key, turned, u).astype(bf16))
        return jnp.concatenate(done, axis=0)

    specs = [
        pl.BlockSpec((tile, 3 * rank), lambda i, p, m: (i, 0)),
        pl.BlockSpec((up.shape[0], rank, narrow), lambda i, p, m: (0, 0, 2 * wide // narrow)),
        pl.BlockSpec(cosine.shape, lambda i, p, m: (0, 0, 0)),
        pl.BlockSpec(sine.shape, lambda i, p, m: (0, 0, 0)),
    ]
    return tail, [shrunk, up, cosine, sine], specs, bf16


def rotation_tables():
    freq = np.exp(-(2.0 * np.arange(HEAD // 2, dtype=np.float32) / HEAD) * math.log(ROPE_BASE))
    angle = np.arange(3 * BLOCK, dtype=np.float32)[:, None] * freq.astype(np.float32)[None, :]
    cosine = np.concatenate([np.cos(angle)] * 2, axis=1)
    sine = np.concatenate([-np.sin(angle), np.sin(angle)], axis=1)
    shape = (3, BLOCK, HEAD)
    return (
        jnp.asarray(cosine.reshape(shape), f32),
        jnp.asarray(sine.reshape(shape), f32),
    )


def attention(meta, q, shrunk, up, down, mine, other, cosine, sine, begin, count):
    tokens, wide = q.shape
    rank = shrunk.shape[1] // 3
    heads = wide // HEAD
    window = min(3 * BLOCK, tokens)
    scale = 1.0 / math.sqrt(HEAD)

    def body(meta_ref, q_ref, s_ref, up_ref, d_ref, m_ref, o_ref, c_ref, n_ref, att):
        i = begin + pl.program_id(0)
        is_key = meta_ref[3, 0] == 1
        first = meta_ref[2, i]
        limit = meta_ref[4, i]
        u = q_ref[...] + jnp.dot(
            s_ref[...][:, :rank], up_ref[0], preferred_element_type=f32
        )
        start = pl.multiple_of(jnp.maximum(i - 2, 0) * BLOCK, BLOCK)
        own = m_ref[pl.ds(start, window), :]
        far = o_ref[pl.ds(start, window), :]
        keys = jnp.where(is_key, own, far)
        values = jnp.where(is_key, far, own)
        row = i * BLOCK + lax.broadcasted_iota(i32, (BLOCK, window), 0)
        col = start + lax.broadcasted_iota(i32, (BLOCK, window), 1)
        allowed = (col >= first) & (col <= row) & (col < limit)
        cosines = c_ref[0]
        sines = n_ref[0]
        turned = []
        for h in range(heads):
            part = u[:, h * HEAD : (h + 1) * HEAD]
            turned.append(
                (part * cosines + pltpu.roll(part, HEAD // 2, 1) * sines).astype(bf16)
            )
        scores = lax.dot_general(
            jnp.concatenate(turned, axis=0),
            keys,
            (((1,), (1,)), ((), ())),
            preferred_element_type=f32,
        )
        for h in range(heads):
            at = slice(h * HEAD, (h + 1) * HEAD)
            weights = jnp.where(allowed, jnp.exp(scores[at, :] * scale), 0.0)
            weights = weights / jnp.sum(weights, axis=1, keepdims=True)
            mixed = jnp.dot(weights.astype(bf16), values, preferred_element_type=f32)
            att[:, at] = mixed.astype(bf16)
        head = lax.dot_general(
            att[:, :wide], d_ref[0], (((1,), (1,)), ((), ())), preferred_element_type=f32
        )
        att[:, wide : wide + rank] = head.astype(bf16)
        att[:, wide + rank :] = jnp.zeros((BLOCK, HEAD - rank), bf16)

    table = pl.BlockSpec((1, BLOCK, HEAD), lambda i, m: (m[1, i + begin], 0, 0))
    whole = pl.BlockSpec((tokens, HEAD), lambda i, m: (0, 0))
    return pl.pallas_call(
        body,
        out_shape=jax.ShapeDtypeStruct((count * BLOCK, wide + HEAD), bf16),
        grid_spec=pltpu.PrefetchScalarGridSpec(
            num_scalar_prefetch=1,
            grid=(count,),
            in_specs=[
                pl.BlockSpec((BLOCK, wide), lambda i, m: (i + begin, 0)),
                pl.BlockSpec((BLOCK, 3 * rank), lambda i, m: (i + begin, 0)),
                pl.BlockSpec((1, rank, wide), lambda i, m: (m[0, i + begin], 0, 0)),
                pl.BlockSpec((1, rank, down.shape[2]), lambda i, m: (m[0, i + begin], 3, 0)),
                whole,
                whole,
                table,
                table,
            ],
            out_specs=pl.BlockSpec((BLOCK, wide + HEAD), lambda i, m: (i, 0)),
        ),
        compiler_params=params(),
        cost_estimate=cost(
            4 * count * BLOCK * window * wide, 8 * count * BLOCK * wide, heads * count * BLOCK * window
        ),
    )(meta, q, shrunk, up, down, mine, other, cosine, sine)


def output_partial(shards, pieces, weights):
    tokens = pieces[0].shape[0]
    count, (depth, width) = len(shards) // 2, weights.shape[1:]
    unit = depth // SIDE
    whole = 2 * width + HEAD
    cut = pieces[3].shape[1]
    low, high = slice(0, width), slice(width + HEAD, whole)

    def body(index_ref, *refs):
        x_refs, (w_low, w_high) = refs[: SIDE + 1], refs[SIDE + 1 : SIDE + 3]
        outs, x_all = refs[SIDE + 3 : -1], refs[-1]
        step = pl.program_id(0)

        @pl.when(step == 0)
        def _():
            rank = jnp.zeros((tokens, HEAD), f32)
            for ref, begin in zip(x_refs, (0, unit, 2 * unit, 3 * unit, 3 * unit + cut)):
                held = min(ref.shape[1], depth - begin, unit)
                x_all[:, begin : begin + held] = ref[:, :held]
                if held < ref.shape[1]:
                    rank = rank + ref[:, held:].astype(f32)
            for out in outs:
                out[:, width : width + HEAD] = rank.astype(out.dtype)

        first = jnp.dot(x_all[...], w_low[0], preferred_element_type=f32)
        second = jnp.dot(x_all[...], w_high[0], preferred_element_type=f32)
        for k, out in enumerate(outs):

            @pl.when(step == k)
            def _():
                out[:, low] = first.astype(out.dtype)
                out[:, high] = second.astype(out.dtype)

    dtypes = [bf16] * (count - 1) + [f32]
    return pl.pallas_call(
        body,
        out_shape=tuple(jax.ShapeDtypeStruct((tokens, whole), d) for d in dtypes),
        grid_spec=pltpu.PrefetchScalarGridSpec(
            num_scalar_prefetch=1,
            grid=(count,),
            in_specs=[pl.BlockSpec(p.shape, lambda j, d: (0, 0)) for p in pieces]
            + [pl.BlockSpec((1, depth, width), lambda j, d: (d[2 * j], 0, 0))]
            + [pl.BlockSpec((1, depth, width), lambda j, d: (d[2 * j + 1], 0, 0))],
            out_specs=[pl.BlockSpec((tokens, whole), lambda j, d: (0, 0))] * count,
            scratch_shapes=[pltpu.VMEM((tokens, depth), bf16)],
        ),
        compiler_params=params(),
        cost_estimate=cost(
            4 * tokens * depth * count * width, 2 * depth * (tokens + 2 * count * width)
        ),
    )(jnp.stack(shards).astype(i32), *pieces, weights, weights)


def add_blocks(a, b, after):
    rows, width = a.shape
    tile = rows // 2

    def body(a_ref, b_ref, *refs):
        refs[-1][...] = (a_ref[...].astype(f32) + b_ref[...].astype(f32)).astype(bf16)

    spec = pl.BlockSpec((tile, width), lambda i: (i, 0))
    return pl.pallas_call(
        body,
        out_shape=jax.ShapeDtypeStruct(a.shape, bf16),
        grid=(2,),
        in_specs=[spec, spec] + passive(after),
        out_specs=spec,
        compiler_params=params(),
        cost_estimate=cost(rows * width, 6 * rows * width),
    )(a, b, *after)


def output_ring(pieces, weights, axis, step):
    me, behind, ahead, far = ring_order(lax.axis_index(axis))
    shards = [2 * place + side for place in (far, ahead, behind, me) for side in range(2)]
    to_far, to_ahead, to_behind, mine = output_partial(shards, pieces, weights)
    passing = shift(to_far, axis, step)
    if step == 1:
        to_ahead = add_blocks(to_ahead, passing, [])
        return mine, shift(to_behind, axis, -1), shift(to_ahead, axis, 1)
    from_behind = shift(to_ahead, axis, 1)
    to_behind = add_blocks(to_behind, passing, [from_behind])
    return mine, shift(to_behind, axis, -1), from_behind


def finish(meta, parts, up, rank, wide):
    cuts = len(parts)
    rows, whole = parts[0][0].shape
    width = (whole - HEAD) // 2
    per = 2
    steps = rows // (per * BLOCK)
    terms = [t for cut in parts for t in cut]
    each = len(parts[0])

    def body(meta_ref, *refs):
        up_ref, out = refs[len(terms) :]
        i = pl.program_id(0)

        def put(mine):
            for k in range(per):
                at = slice(k * BLOCK, (k + 1) * BLOCK)
                block = i * per + k
                total = mine[0][at, :].astype(f32)
                for ref in mine[1:]:
                    total = total + ref[at, :].astype(f32)
                extra = jnp.dot(
                    total[:, width : width + rank].astype(bf16),
                    up_ref[meta_ref[0, block]],
                    preferred_element_type=f32,
                )
                row = block * BLOCK + lax.broadcasted_iota(i32, (BLOCK, width), 0)
                valid = row < meta_ref[4, block]
                for side, begin in enumerate((0, width + HEAD)):
                    cols = slice(side * width, (side + 1) * width)
                    out[at, cols] = jnp.where(
                        valid, total[:, begin : begin + width] + extra[:, cols], 0.0
                    )

        for cut in range(cuts):

            @pl.when(i // steps == cut)
            def _():
                put(refs[cut * each : (cut + 1) * each])

    def term_spec(cut):
        return pl.BlockSpec(
            (per * BLOCK, whole), lambda i, m: (jnp.clip(i - cut * steps, 0, steps - 1), 0)
        )

    return pl.pallas_call(
        body,
        out_shape=jax.ShapeDtypeStruct((cuts * rows, 2 * width), f32),
        grid_spec=pltpu.PrefetchScalarGridSpec(
            num_scalar_prefetch=1,
            grid=(cuts * steps,),
            in_specs=[term_spec(cut) for cut in range(cuts) for _ in range(each)]
            + [pl.BlockSpec((up.shape[0], rank, wide), lambda i, m: (0, 0, 1))],
            out_specs=pl.BlockSpec((per * BLOCK, 2 * width), lambda i, m: (i, 0)),
        ),
        compiler_params=params(),
        cost_estimate=cost(4 * cuts * rows * rank * width, 28 * cuts * rows * width),
    )(meta, *terms, up)


def on_device(x, wq, wkv, wo, down_qkv, up_q, up_kv, down_o, up_o, choice, counts, tails):
    z, c, y, xi = (lax.axis_index(n) for n in ADAPTER_AXES + TENSOR_AXES)
    group = z * CORES + c
    tokens, local = x.shape
    holders = down_qkv.shape[0]
    requests = choice.shape[1]
    wide = wq.shape[1]
    rank = up_q.shape[1]
    blocks = tokens // BLOCK

    owners = choice // holders
    pick = jnp.sum(jnp.where(owners == group, choice % holders, 0), axis=1).astype(i32)
    own_owner = lax.dynamic_index_in_dim(owners, group, 0, keepdims=False)
    req = jnp.arange(requests, dtype=i32)
    starts = jnp.sum(jnp.where(req[None, :] < req[:, None], counts[0][None, :], 0), axis=1)
    block = jnp.arange(blocks, dtype=i32)
    of_block = (starts[None, :] <= block[:, None]) & (
        block[:, None] < (starts + counts[0])[None, :]
    )

    def lookup(values):
        return jnp.sum(jnp.where(of_block, values[None, :], 0), axis=1).astype(i32)

    slot = lookup(own_owner)
    first = lookup(starts)
    limit = (first + lookup(counts[0]) - 1) * BLOCK + lookup(tails[0])
    is_key = jnp.broadcast_to(1 - xi % 2, (blocks,)).astype(i32)
    meta = jnp.stack([slot, block - first, first * BLOCK, is_key, limit]).astype(i32)

    cosine, sine = rotation_tables()

    stores = (jnp.swapaxes(down_qkv, 1, 2), up_q, up_kv, jnp.swapaxes(down_o, 1, 2), up_o)
    ys, xs = ring_order(y), ring_order(xi)
    unit = wo.shape[1] // (SIDE * SIDE * 2)
    wo_cols = jnp.stack(ys) * (2 * SIDE) + group
    down_out, up_out, x_a, x_b, *sent = pick_local(
        jnp.concatenate([pick, wo_cols.astype(i32)]), *stores, x, wo, unit
    )
    down = lax.all_to_all(down_out, ADAPTER_AXES, 0, 0, tiled=True)

    first_a = ring_gather(x_a, "x", x_a.shape[1] // 2)
    first_b = ring_gather(x_b, "y", x_b.shape[1] // 2)

    got = [sent[0], shift(sent[2], "y", 1), shift(sent[1], "y", -1), shift(sent[3], "y", 2)]
    halves = [first_a[:2], first_a[2:], first_b[:2], first_b[2:]]
    low_a, high_a, low_b, high_b = join(halves, got[1:])
    far_a = gather_onward(low_a, high_a, "y")
    far_b = gather_onward(low_b, high_b, "x")
    wo_mine = stack_rows(got, [down, low_a])
    wo_all = lax.all_gather(wo_mine, ADAPTER_AXES, axis=0)

    def rows_a(k, cols):
        return [(ys[k] * SIDE + xs[j]) * 2 for j in cols]

    def rows_b(k, cols):
        return [(ys[j] * SIDE + xs[k]) * 2 + 1 for j in cols]

    def index_of(rows):
        return jnp.stack(rows).astype(i32)

    every = range(SIDE)
    low, high = (0, 1), (2, 3)
    total = project(
        (index_of(rows_a(0, every) + rows_b(0, every)), meta),
        None,
        [low_a, high_a, low_b, high_b],
        [wq, wkv],
        512,
    )

    again = join(halves, [total[1]])
    next_a = gather_next(again[0], again[1], "y")
    next_b = gather_next(again[2], again[3], "x")

    pieces = scatter_rows(rank_partial(meta, x, down, 3 * rank, [low_a]))
    copies, up_out = share_sum(pieces, up_out, [total[1]])
    up = lax.all_to_all(up_out, ADAPTER_AXES, 0, 0, tiled=True)

    a_low, a_high = shift(far_a[0], "y", 1), shift(far_a[1], "y", -1)
    b_low, b_high = shift(far_b[0], "x", 1), shift(far_b[1], "x", -1)
    total = project(
        (
            index_of(rows_a(1, low) + rows_a(2, high) + rows_b(1, low) + rows_b(2, high)),
            meta,
        ),
        total,
        [*far_a, *far_b],
        [wq, wkv],
        512,
    )
    total = project(
        (
            index_of(rows_a(1, high) + rows_a(2, low) + rows_b(1, high) + rows_b(2, low)),
            meta,
        ),
        total,
        [*next_a, *next_b],
        [wq, wkv],
        512,
    )
    shrunk = lax.all_to_all(copies, TENSOR_AXES, 0, 0, tiled=True).reshape(tokens, 3 * rank)
    final = (index_of(rows_a(3, every) + rows_b(3, every)), meta)
    far = [a_low, a_high, b_low, b_high]
    tail = key_value_tail(shrunk, up, cosine, sine, wide, wkv.shape[1], 512)
    (mine,) = project(final, total[1:], far, [wkv], 512, tail)
    other = lax.ppermute(mine, "x", [(i, i ^ 1) for i in range(SIDE)])
    (q,) = project(final, total[:1], far, [wq], 512)

    cuts = 2
    each = blocks // cuts
    parts = []
    for cut in range(cuts):
        attended = attention(
            meta, q, shrunk, up, down, mine, other, cosine, sine, cut * each, each
        )
        step = 1 - 2 * cut
        gathered = ring_gather(attended, "y", wide // 2)
        parts.append(output_ring(gathered, wo_all, "x", step))
    return finish(meta, parts, up, rank, wide)


def solution(mesh):
    fine = Mesh(mesh.devices.reshape(SIDE, CORES, SIDE, SIDE), ADAPTER_AXES + TENSOR_AXES)
    placed = (
        P(ADAPTER_AXES, TENSOR_AXES),
        P(None, TENSOR_AXES),
        P(None, TENSOR_AXES),
        P(TENSOR_AXES, None),
        P(ADAPTER_AXES, TENSOR_AXES, None),
        P(ADAPTER_AXES, None, TENSOR_AXES),
        P(ADAPTER_AXES, None, TENSOR_AXES),
        P(ADAPTER_AXES, TENSOR_AXES, None),
        P(ADAPTER_AXES, None, TENSOR_AXES),
        P(),
        P(ADAPTER_AXES, None),
        P(ADAPTER_AXES, None),
    )
    return jax.shard_map(
        on_device,
        mesh=fine,
        in_specs=placed,
        out_specs=P(ADAPTER_AXES, TENSOR_AXES),
        check_vma=False,
    )
```
